32 devices in a mesh: seq: 4 (over y, x), mem: 8 (over z, core).
Axes of the slice: x: 2, y: 2, z: 4, core: 2. Of those that a mesh axis runs over, the one named last changes fastest.
Arguments:
- tokens: bfloat16 [8, 1024, 1024], P('mem', 'seq'), may hold values from -6 to 6
- cached_keys: bfloat16 [8, 8192, 1024], P(None, 'mem'), may hold values from -6 to 6
- cached_values: bfloat16 [8, 8192, 1024], P(None, 'mem'), may hold values from -6 to 6
- knn_index: int32 [8, 1024, 128], P('mem', 'seq'), may hold values from 0 to 8191, as said below
- has_memory: int32 [8], P('mem'), may hold values from 0 to 1, as said below
- w_query: bfloat16 [1024, 1024], P(('seq', 'mem')), may hold values from -0.1875 to 0.1875
- w_key: bfloat16 [1024, 1024], P(('seq', 'mem')), may hold values from -0.1875 to 0.1875
- w_value: bfloat16 [1024, 1024], P(('seq', 'mem')), may hold values from -0.1875 to 0.1875
- w_out: bfloat16 [1024, 1024], P(('seq', 'mem')), may hold values from -1.5 to 1.5
- gain_attn: bfloat16 [1024], P(('seq', 'mem')), may hold values from 0.099609375 to 1.8984375
- w_gate: bfloat16 [1024, 2816], P(('seq', 'mem')), may hold values from -0.1875 to 0.1875
- w_up: bfloat16 [1024, 2816], P(('seq', 'mem')), may hold values from -0.1875 to 0.1875
- w_down: bfloat16 [2816, 1024], P(('seq', 'mem')), may hold values from -0.109375 to 0.109375
- gain_ffn: bfloat16 [1024], P(('seq', 'mem')), may hold values from 0.099609375 to 1.8984375
- cotangent: bfloat16 [8, 1024, 1024], P('mem', 'seq'), may hold values from -6 to 6
Outputs:
- mixed: float32 [8, 1024, 1024], P('mem', 'seq')
- grad_tokens: float32 [8, 1024, 1024], P('mem', 'seq')
- grad_w_query: float32 [1024, 1024], P(('seq', 'mem'))
- grad_w_key: float32 [1024, 1024], P(('seq', 'mem'))
- grad_w_value: float32 [1024, 1024], P(('seq', 'mem'))
- grad_w_out: float32 [1024, 1024], P(('seq', 'mem'))
- grad_gain_attn: float32 [1024], P(('seq', 'mem'))
- grad_w_gate: float32 [1024, 2816], P(('seq', 'mem'))
- grad_w_up: float32 [1024, 2816], P(('seq', 'mem'))
- grad_w_down: float32 [2816, 1024], P(('seq', 'mem'))
- grad_gain_ffn: float32 [1024], P(('seq', 'mem'))
The draws below stay inside these ranges and needn't reach their ends.
Inputs may be any that keep to these rules, and one draw needn't show every extreme that they name: `knn_index`: each row holds 128 different indices of the 8192 cached keys of its segment. `has_memory`: exactly half of the 8 segments have 1.
All inputs are finite; a program needn't handle non-finite values.
Results may differ from the reference program's by a relative error of at most 0.03.
Values may be sent and summed in bfloat16 or wider, within the bound.
A program may use at most 640 MiB of HBM per device.

```python
import jax
import jax.numpy as jnp
from jax import lax

D = 1024
HEADS = 8
HEAD = 128
FF = 2816
MEMORY = 8192
KNN = 128
SEG = 1024
SEGMENTS = 8


def draw_knn_index(key, part):
    key = jax.random.fold_in(key, 11)
    stride = MEMORY // KNN
    first_key, second_key = jax.random.split(key)
    starting = jax.random.randint(first_key, (SEGMENTS, SEG, 1), 0, MEMORY)
    jitter = jax.random.randint(second_key, (SEGMENTS, SEG, KNN), 0, stride)
    slots = jnp.arange(KNN, dtype=jnp.int32)[None, None, :]
    anchor = (jnp.arange(SEGMENTS)[:, None, None] == 0) & (jnp.arange(SEG)[None, :, None] == 0)
    starting = jnp.where(anchor, 0, starting)
    jitter = jnp.where(anchor & (slots == 0), 0, jitter)
    jitter = jnp.where(anchor & (slots == KNN - 1), stride - 1, jitter)
    return ((starting + slots * stride + jitter) % MEMORY).astype(jnp.int32)


def draw_has_memory(key, part):
    key = jax.random.fold_in(key, 23)
    ordering = jax.random.permutation(key, SEGMENTS)
    return (ordering % 2).astype(jnp.int32)


def shard_levels(key, dims, cuts, smallest, top_value):
    factor_of = 1.0
    for dim, blocks in cuts:
        heights = jax.random.uniform(jax.random.fold_in(jax.random.fold_in(key, 6), dim), (blocks,), jnp.float32, smallest / len(cuts), top_value / len(cuts))
        factor_of = factor_of * jnp.repeat(jnp.exp(heights), dims[dim] // blocks).reshape((-1,) + (1,) * (len(dims) - 1 - dim))
    return factor_of


def gaussian(key, shape, scale, reach, cuts=(), held_as=jnp.bfloat16):
    loudness = shard_levels(key, shape, cuts, -0.22, 0.18) if cuts else 1.0
    result = jax.random.normal(key, shape, jnp.float32) * scale * loudness
    return jnp.minimum(jnp.maximum(result, -reach), reach).astype(held_as)


def setup_inputs(seed: int = 0) -> dict:
    streams_of = jax.random.split(jax.random.key(seed), 16)
    tokens = gaussian(streams_of[0], (SEGMENTS, SEG, D), 1.0, 6.0, ((0, 8), (1, 4)))
    cached_keys = gaussian(streams_of[1], (SEGMENTS, MEMORY, D), 1.0, 6.0, ((1, 8),))
    cached_values = gaussian(streams_of[2], (SEGMENTS, MEMORY, D), 1.0, 6.0, ((1, 8),))
    knn_index = draw_knn_index(jax.random.fold_in(streams_of[15], 71), 0)
    has_memory = draw_has_memory(jax.random.fold_in(streams_of[15], 71), 0)
    w_query = gaussian(streams_of[5], (D, D), D ** -0.5, 0.1875, ((0, 32),))
    w_key = gaussian(streams_of[6], (D, D), D ** -0.5, 0.1875, ((0, 32),))
    w_value = gaussian(streams_of[7], (D, D), D ** -0.5, 0.1875, ((0, 32),))
    w_out = gaussian(streams_of[8], (D, D), (max(D // 64, 1)) ** -0.5, 1.5, ((0, 32),))
    gain_attn = jnp.clip(1.0 + 0.18 * jax.random.normal(streams_of[9], (D,), jnp.float32), 0.099609375, 1.8984375).astype(jnp.bfloat16)
    w_gate = gaussian(streams_of[10], (D, FF), D ** -0.5, 0.1875, ((0, 32),))
    w_up = gaussian(streams_of[11], (D, FF), D ** -0.5, 0.1875, ((0, 32),))
    w_down = gaussian(streams_of[12], (FF, D), FF ** -0.5, 0.109375, ((0, 32),))
    gain_ffn = jnp.clip(1.0 + 0.18 * jax.random.normal(streams_of[13], (D,), jnp.float32), 0.099609375, 1.8984375).astype(jnp.bfloat16)
    cotangent = gaussian(streams_of[14], (SEGMENTS, SEG, D), 1.0, 6.0, ((0, 8), (1, 4)))
    return dict(tokens=tokens, cached_keys=cached_keys, cached_values=cached_values, knn_index=knn_index, has_memory=has_memory, w_query=w_query, w_key=w_key, w_value=w_value, w_out=w_out, gain_attn=gain_attn, w_gate=w_gate, w_up=w_up, w_down=w_down, gain_ffn=gain_ffn, cotangent=cotangent)


FLOOR_SCORE = -1e+30
EPSILON = 1e-05
PRECISE = lax.Precision.HIGHEST

@jax.custom_vjp
def low(v):
    return lax.optimization_barrier(v.astype(jnp.bfloat16)).astype(jnp.float32)

@jax.custom_vjp
def low_back(v):
    return v

def low_keep(v):
    return (low(v), None)

def low_pass(kept, grad):
    return (grad,)

def back_keep(v):
    return (v, None)

def back_low(kept, grad):
    return (low(grad),)
low.defvjp(low_keep, low_pass)
low_back.defvjp(back_keep, back_low)

def rms_norm(values, gain):
    return values * lax.rsqrt(lax.optimization_barrier(jnp.mean(values * values, axis=-1, keepdims=True)) + EPSILON) * gain

def angles_for(positions, head_width):
    exponent = jnp.arange(head_width // 2, dtype=jnp.float32) * (2.0 / head_width)
    frequency = jnp.power(10000.0, -exponent)
    turned = positions.astype(jnp.float32)[:, None] * frequency[None, :]
    return (jnp.cos(turned), jnp.sin(turned))

def rotate(values, cosine, sine, head_count):
    leading = values.shape[:-1]
    split = values.reshape(leading + (head_count, values.shape[-1] // head_count))
    middle = split.shape[-1] // 2
    first_half = split[..., :middle]
    second_half = split[..., middle:]
    cos_rows = cosine[:, None, :]
    sin_rows = sine[:, None, :]
    turned = jnp.concatenate([first_half * cos_rows - second_half * sin_rows, second_half * cos_rows + first_half * sin_rows], axis=-1)
    return turned.reshape(values.shape)

def project(left, right):
    return jnp.einsum('std,de->ste', left, right, precision=PRECISE)

def by_heads(values):
    split = values.reshape(values.shape[:-1] + (HEADS, HEAD))
    return jnp.moveaxis(split, -2, -3)

def attend_head(query_part, key_part, value_part, mem_key_part, mem_value_part, allowed, causal):
    score_scale = HEAD ** (-0.5)
    local_scores = low_back(jnp.dot(query_part, key_part.T, precision=PRECISE)) * score_scale
    memory_scores = low_back(jnp.dot(query_part, mem_key_part.T, precision=PRECISE)) * score_scale
    scores = jnp.concatenate([jnp.where(causal, local_scores, FLOOR_SCORE), jnp.where(allowed, memory_scores, FLOOR_SCORE)], axis=1)
    weights = low(jax.nn.softmax(scores, axis=-1))
    return jnp.dot(weights, jnp.concatenate([value_part, mem_value_part], axis=0), precision=PRECISE)

def reference(tokens, cached_keys, cached_values, knn_index, has_memory, w_query, w_key, w_value, w_out, gain_attn, w_gate, w_up, w_down, gain_ffn, cotangent):
    positions = jnp.arange(SEG)
    cosine, sine = angles_for(positions, HEAD)
    causal = positions[None, :] <= positions[:, None]
    live_index = jnp.where(has_memory[:, None, None] > 0, knn_index, MEMORY).astype(jnp.int32)
    memory_keys = by_heads(cached_keys.astype(jnp.float32))
    memory_values = by_heads(cached_values.astype(jnp.float32))

    def forward(inputs, query_weight, key_weight, value_weight, out_weight, gain_one, gate_weight, up_weight, down_weight, gain_two):
        norm_one = low(rms_norm(inputs, gain_one))
        queries = low(rotate(low_back(project(norm_one, query_weight)), cosine, sine, HEADS))
        keys = low(rotate(low_back(project(norm_one, key_weight)), cosine, sine, HEADS))
        values = low(low_back(project(norm_one, value_weight)))

        def segment(items):
            query_heads, key_heads, value_heads, mem_key_heads, mem_value_heads, index_rows = items
            allowed = jnp.zeros((SEG, MEMORY), jnp.bool_).at[positions[:, None], index_rows].set(True, mode='drop')

            def one_head(query_part, key_part, value_part, mem_key_part, mem_value_part):
                return attend_head(query_part, key_part, value_part, mem_key_part, mem_value_part, allowed, causal)
            checked = jax.checkpoint(one_head)
            return lax.map(lambda parts: checked(parts[0], parts[1], parts[2], parts[3], parts[4]), (query_heads, key_heads, value_heads, mem_key_heads, mem_value_heads))
        head_outputs = lax.map(segment, (by_heads(queries), by_heads(keys), by_heads(values), memory_keys, memory_values, live_index))
        attention = jnp.moveaxis(head_outputs, 1, 2).reshape(inputs.shape)
        attention_used = low_back(low(attention))
        mid = inputs + low_back(project(attention_used, out_weight))
        norm_two = low(rms_norm(mid, gain_two))
        gate = low_back(project(norm_two, gate_weight))
        upward = low_back(project(norm_two, up_weight))
        hidden = low(jax.nn.silu(gate) * upward)
        return mid + low_back(project(hidden, down_weight))
    primals = (tokens.astype(jnp.float32), w_query.astype(jnp.float32), w_key.astype(jnp.float32), w_value.astype(jnp.float32), w_out.astype(jnp.float32), gain_attn.astype(jnp.float32), w_gate.astype(jnp.float32), w_up.astype(jnp.float32), w_down.astype(jnp.float32), gain_ffn.astype(jnp.float32))
    mixed, pullback = jax.vjp(forward, *primals)
    grads = pullback(cotangent.astype(jnp.float32))
    return (mixed, grads[0], grads[1], grads[2], grads[3], grads[4], grads[5], grads[6], grads[7], grads[8], grads[9])
```

```python
import functools

import jax
import jax.numpy as jnp
from jax import lax
from jax.experimental import pallas as pl
from jax.experimental.pallas import tpu as pltpu
from jax.sharding import PartitionSpec as P

HEADS = 8
EPSILON = 1e-05
FLOOR = -1e30
LOW = -1e29
LOG2E = 1.4426950408889634
STATS = 16
F32 = jnp.float32
BF16 = jnp.bfloat16
VMEM_LIMIT = 56 * 1024 * 1024
NT = (((1,), (1,)), ((), ()))
TN = (((0,), (0,)), ((), ()))


def dot(left, right, dims=(((1,), (0,)), ((), ()))):
    return lax.dot_general(left, right, dims, preferred_element_type=F32)


def rms_norm(values, gain):
    return values * lax.rsqrt(jnp.mean(values * values, axis=-1, keepdims=True) + EPSILON) * gain


def swiglu(gate_in, up_in):
    return jax.nn.silu(gate_in) * up_in


def angles_for(positions, head_width):
    exponent = jnp.arange(head_width // 2, dtype=F32) * (2.0 / head_width)
    frequency = jnp.power(10000.0, -exponent)
    turned = positions.astype(F32)[:, None] * frequency[None, :]
    return (jnp.cos(turned), jnp.sin(turned))


def rotate(values, cosine, sine):
    rows, width = values.shape
    split = values.reshape(rows, HEADS, width // HEADS)
    middle = split.shape[-1] // 2
    first, second = split[..., :middle], split[..., middle:]
    cos_rows, sin_rows = cosine[:, None, :], sine[:, None, :]
    turned = jnp.concatenate(
        [first * cos_rows - second * sin_rows, second * cos_rows + first * sin_rows], axis=-1
    )
    return turned.reshape(values.shape)


def params(**more):
    return pltpu.CompilerParams(vmem_limit_bytes=VMEM_LIMIT, **more)


def spread(columns, width=128):
    lanes = lax.broadcasted_iota(jnp.int32, (columns[0].shape[0], width), 1)
    result = jnp.zeros((columns[0].shape[0], width), F32)
    for place, column in enumerate(columns):
        result = jnp.where(lanes == place, column, result)
    return result


def columns_of(rows_by_stat):
    count, width = rows_by_stat.shape
    padded = jnp.concatenate([rows_by_stat, jnp.zeros((128 - count, width), F32)], axis=0)
    return padded.T


def mask_kernel(blocks, order_ref, base_ref, index_ref, bits_ref):
    del order_ref
    rows = index_ref.shape[1]
    lanes = lax.broadcasted_iota(jnp.int32, (8, 128), 1)

    def group(g, carry):
        start = pl.multiple_of(g * 8, 8)
        relative = index_ref[0, pl.ds(start, 8), :] - base_ref[0]
        inside = (relative >= 0) & (relative < blocks * 128)
        place = jnp.where(inside, relative & 127, 0)
        bit = jnp.where(inside, lax.shift_left(jnp.ones_like(relative), relative >> 7), 0)
        code = place | (bit << 7)
        word = jnp.zeros((8, 128), jnp.int32)
        for j in range(index_ref.shape[2]):
            one = jnp.broadcast_to(code[:, j : j + 1], (8, 128))
            word = word | jnp.where((one & 127) == lanes, one >> 7, 0)
        bits_ref[0, pl.ds(start, 8), :] = word
        return carry

    lax.fori_loop(0, rows // 8, group, 0)


def mask_bits(order, base, all_index, mem_dev):
    active = order.shape[0]
    _, rows, count = all_index.shape
    return pl.pallas_call(
        functools.partial(mask_kernel, mem_dev // 128),
        grid_spec=pltpu.PrefetchScalarGridSpec(
            num_scalar_prefetch=2,
            grid=(active,),
            in_specs=[pl.BlockSpec((1, rows, count), lambda a, o, b: (o[a], 0, 0))],
            out_specs=pl.BlockSpec((1, rows, 128), lambda a, o, b: (a, 0, 0)),
        ),
        out_shape=jax.ShapeDtypeStruct((active, rows, 128), jnp.int32),
        compiler_params=params(),
        name="mask_bits",
    )(order, base, all_index)


def fill_bias(bits_ref, bias_ref):
    bits = bits_ref[0]
    for b in range(bias_ref.shape[1] // 128):
        bias_ref[:, b * 128 : (b + 1) * 128] = jnp.where(((bits >> b) & 1) != 0, 0.0, FLOOR)


def owner_forward_kernel(scale, order_ref, q_ref, bits_ref, k_ref, v_ref, o_ref, st_ref, bias_ref):
    del order_ref
    fill_bias(bits_ref, bias_ref)
    maxima, sums = [], []
    for h in range(HEADS):
        span = slice(h * 128, (h + 1) * 128)
        scores = dot(q_ref[0, :, span], k_ref[0, :, span], NT) * scale + bias_ref[...]
        top = jnp.maximum(jnp.max(scores, axis=1, keepdims=True), LOW)
        weights = jnp.exp2(scores - top)
        maxima.append(top)
        sums.append(jnp.sum(weights, axis=1, keepdims=True))
        o_ref[0, :, span] = dot(weights.astype(BF16), v_ref[0, :, span]).astype(BF16)
    st_ref[0] = spread(maxima + sums).T[:STATS]


def owner_forward(order, queries, bits, cached_keys, cached_values, scale):
    segments, rows, width = queries.shape
    mem_dev = cached_keys.shape[1]
    active = order.shape[0]
    picked = lambda a, o: (o[a], 0, 0)
    return pl.pallas_call(
        functools.partial(owner_forward_kernel, scale),
        grid_spec=pltpu.PrefetchScalarGridSpec(
            num_scalar_prefetch=1,
            grid=(active,),
            in_specs=[
                pl.BlockSpec((1, rows, width), picked),
                pl.BlockSpec((1, rows, 128), lambda a, o: (a, 0, 0)),
                pl.BlockSpec((1, mem_dev, width), picked),
                pl.BlockSpec((1, mem_dev, width), picked),
            ],
            out_specs=[
                pl.BlockSpec((1, rows, width), picked),
                pl.BlockSpec((1, STATS, rows), picked),
            ],
            scratch_shapes=[pltpu.VMEM((rows, mem_dev), F32)],
        ),
        out_shape=[
            jax.ShapeDtypeStruct((segments, rows, width), BF16),
            jax.ShapeDtypeStruct((segments, STATS, rows), F32),
        ],
        compiler_params=params(),
        name="owner_forward",
    )(order, queries, bits, cached_keys, cached_values)


def owner_backward_kernel(
    scale, order_ref, q_ref, g_ref, st_ref, bits_ref, k_ref, v_ref, dq_ref, bias_ref
):
    del order_ref
    fill_bias(bits_ref, bias_ref)
    stats = columns_of(st_ref[0])
    for h in range(HEADS):
        span = slice(h * 128, (h + 1) * 128)
        scores = dot(q_ref[0, :, span], k_ref[0, :, span], NT) * scale + bias_ref[...]
        weights = jnp.exp2(scores - stats[:, h : h + 1])
        dweights = dot(g_ref[0, :, span], v_ref[0, :, span], NT)
        dscore = weights * (dweights - stats[:, HEADS + h : HEADS + h + 1])
        dq_ref[0, :, span] = (
            dot(dscore.astype(BF16), k_ref[0, :, span]) * (scale / LOG2E)
        ).astype(BF16)


def owner_backward(order, queries, grads, stats, bits, cached_keys, cached_values, scale):
    segments, rows, width = queries.shape
    mem_dev = cached_keys.shape[1]
    active = order.shape[0]
    picked = lambda a, o: (o[a], 0, 0)
    return pl.pallas_call(
        functools.partial(owner_backward_kernel, scale),
        grid_spec=pltpu.PrefetchScalarGridSpec(
            num_scalar_prefetch=1,
            grid=(active,),
            in_specs=[
                pl.BlockSpec((1, rows, width), picked),
                pl.BlockSpec((1, rows, width), picked),
                pl.BlockSpec((1, STATS, rows), picked),
                pl.BlockSpec((1, rows, 128), lambda a, o: (a, 0, 0)),
                pl.BlockSpec((1, mem_dev, width), picked),
                pl.BlockSpec((1, mem_dev, width), picked),
            ],
            out_specs=pl.BlockSpec((1, rows, width), picked),
            scratch_shapes=[pltpu.VMEM((rows, mem_dev), F32)],
        ),
        out_shape=jax.ShapeDtypeStruct((segments, rows, width), BF16),
        compiler_params=params(),
        name="owner_backward",
    )(order, queries, grads, stats, bits, cached_keys, cached_values)


def causal_bias(place_ref, rows, keys):
    row = place_ref[0] * rows + lax.broadcasted_iota(jnp.int32, (rows, keys), 0)
    return jnp.where(lax.broadcasted_iota(jnp.int32, (rows, keys), 1) <= row, 0.0, FLOOR)


def local_forward_kernel(scale, place_ref, q_ref, k_ref, v_ref, o_ref, st_ref):
    bias = causal_bias(place_ref, q_ref.shape[0], k_ref.shape[0])
    maxima, sums = [], []
    for h in range(HEADS):
        span = slice(h * 128, (h + 1) * 128)
        scores = dot(q_ref[:, span], k_ref[:, span], NT) * scale + bias
        top = jnp.max(scores, axis=1, keepdims=True)
        weights = jnp.exp2(scores - top)
        maxima.append(top)
        sums.append(jnp.sum(weights, axis=1, keepdims=True))
        o_ref[:, span] = dot(weights.astype(BF16), v_ref[:, span])
    st_ref[...] = spread(maxima + sums).T[:STATS]


def whole(*shape):
    return pl.BlockSpec(shape, lambda *_: (0,) * len(shape))


def local_forward(place, queries, keys, values, scale):
    rows, width = queries.shape
    length = keys.shape[0]
    return pl.pallas_call(
        functools.partial(local_forward_kernel, scale),
        grid_spec=pltpu.PrefetchScalarGridSpec(
            num_scalar_prefetch=1,
            grid=(1,),
            in_specs=[whole(rows, width), whole(length, width), whole(length, width)],
            out_specs=[whole(rows, width), whole(STATS, rows)],
        ),
        out_shape=[
            jax.ShapeDtypeStruct((rows, width), F32),
            jax.ShapeDtypeStruct((STATS, rows), F32),
        ],
        compiler_params=params(),
        name="local_forward",
    )(place, queries, keys, values)


def local_backward_kernel(
    scale, place_ref, q_ref, g_ref, st_ref, k_ref, v_ref, dq_ref, dk_ref, dv_ref
):
    bias = causal_bias(place_ref, q_ref.shape[0], k_ref.shape[0])
    stats = columns_of(st_ref[...])
    for h in range(HEADS):
        span = slice(h * 128, (h + 1) * 128)
        query, key, grad = q_ref[:, span], k_ref[:, span], g_ref[:, span]
        scores = dot(query, key, NT) * scale + bias
        weights = jnp.exp2(scores - stats[:, h : h + 1])
        dweights = dot(grad, v_ref[:, span], NT)
        dscore = (weights * (dweights - stats[:, HEADS + h : HEADS + h + 1])).astype(BF16)
        dq_ref[:, span] = dot(dscore, key) * (scale / LOG2E)
        dk_ref[:, span] = (dot(dscore, query, TN) * (scale / LOG2E)).astype(BF16)
        dv_ref[:, span] = dot(weights.astype(BF16), grad, TN).astype(BF16)


def local_backward(place, queries, grads, stats, keys, values, scale):
    rows, width = queries.shape
    length = keys.shape[0]
    return pl.pallas_call(
        functools.partial(local_backward_kernel, scale),
        grid_spec=pltpu.PrefetchScalarGridSpec(
            num_scalar_prefetch=1,
            grid=(1,),
            in_specs=[
                whole(rows, width),
                whole(rows, width),
                whole(STATS, rows),
                whole(length, width),
                whole(length, width),
            ],
            out_specs=[whole(rows, width), whole(length, width), whole(length, width)],
        ),
        out_shape=[
            jax.ShapeDtypeStruct((rows, width), F32),
            jax.ShapeDtypeStruct((length, width), BF16),
            jax.ShapeDtypeStruct((length, width), BF16),
        ],
        compiler_params=params(),
        name="local_backward",
    )(place, queries, grads, stats, keys, values)


def per_device(
    tokens,
    cached_keys,
    cached_values,
    knn_index,
    has_memory,
    w_query,
    w_key,
    w_value,
    w_out,
    gain_attn,
    w_gate,
    w_up,
    w_down,
    gain_ffn,
    cotangent,
):
    both = ("seq", "mem")
    gather = functools.partial(lax.all_gather, axis=0, tiled=True)
    scatter = functools.partial(lax.psum_scatter, scatter_dimension=0, tiled=True)
    inputs = tokens[0].astype(F32)
    rows, width = inputs.shape
    hidden_width = w_gate.shape[1]
    head_width = width // HEADS
    scale = head_width ** (-0.5) * LOG2E
    mem_dev = cached_keys.shape[1]
    place = lax.axis_index("seq").astype(jnp.int32)[None]
    base = (lax.axis_index("mem") * mem_dev).astype(jnp.int32)[None]

    gains = jnp.zeros((w_query.shape[0], 128), BF16)
    gains = gains.at[:, 0].set(gain_attn).at[:, 1].set(gain_ffn)
    first_weights = gather(jnp.concatenate([w_query, w_key, w_value, gains], axis=1), both)
    flag_rows = jnp.broadcast_to(has_memory[:, None], (8, 128))
    shared = gather(jnp.concatenate([knn_index[0], flag_rows], axis=0)[None], "mem")
    all_index, flags = shared[:, :rows], shared[:, rows, 0]
    segments = flags.shape[0]
    order = jnp.argsort(jnp.where(flags > 0, 0, 1), stable=True)[: segments // 2].astype(jnp.int32)
    bits = mask_bits(order, base, all_index, mem_dev)

    qkv_weight = first_weights[:, : 3 * width]
    gain_first = first_weights[:, 3 * width].astype(F32)
    gain_second = first_weights[:, 3 * width + 1].astype(F32)
    out_gate_up = gather(jnp.concatenate([w_out, w_gate, w_up], axis=1), both)
    down_weight = gather(w_down, both)
    out_weight = out_gate_up[:, :width]
    gate_weight = out_gate_up[:, width : width + hidden_width]
    up_weight = out_gate_up[:, width + hidden_width :]

    positions = lax.axis_index("seq") * rows + jnp.arange(rows)
    cosine, sine = angles_for(positions, head_width)
    normed_one, norm_one_back = jax.vjp(rms_norm, inputs, gain_first)
    norm_one = normed_one.astype(BF16)
    qkv = dot(norm_one, qkv_weight)
    queries = rotate(qkv[:, :width], cosine, sine).astype(BF16)
    keys = rotate(qkv[:, width : 2 * width], cosine, sine).astype(BF16)
    values = qkv[:, 2 * width :].astype(BF16)
    all_queries = gather(queries[None], "mem")
    segment_keys, segment_values = gather(keys, "seq"), gather(values, "seq")

    owner_out, owner_stats = owner_forward(
        order, all_queries, bits, cached_keys, cached_values, scale
    )
    local_out, local_stats = local_forward(place, queries, segment_keys, segment_values, scale)
    exchange = functools.partial(
        lax.all_to_all, axis_name="mem", split_axis=0, concat_axis=0, tiled=True
    )
    peer_out, peer_stats = exchange(owner_out), exchange(owner_stats)
    live = has_memory[0] > 0
    peer_max = jnp.where(live, peer_stats[:, :HEADS], LOW)
    peer_sum = jnp.where(live, peer_stats[:, HEADS:], 0.0)
    local_max, local_sum = local_stats[:HEADS], local_stats[HEADS:]
    row_max = jnp.maximum(local_max, jnp.max(peer_max, axis=0))
    peer_share = jnp.exp2(peer_max - row_max)
    local_share = jnp.exp2(local_max - row_max)
    row_sum = local_sum * local_share + jnp.sum(peer_sum * peer_share, axis=0)
    log_total = row_max + jnp.log2(row_sum)

    def wide(stat):
        return jnp.broadcast_to(
            jnp.swapaxes(stat, -1, -2)[..., None], stat.shape[:-2] + (rows, HEADS, head_width)
        ).reshape(stat.shape[:-2] + (rows, width))

    peer_sums = jnp.sum(
        jnp.where(live, peer_out.astype(F32), 0.0) * wide(peer_share / row_sum), axis=0
    )
    attention = local_out * wide(local_share / row_sum) + peer_sums
    attention_low = attention.astype(BF16)
    mid = inputs + dot(attention_low, out_weight)
    normed_two, norm_two_back = jax.vjp(rms_norm, mid, gain_second)
    norm_two = normed_two.astype(BF16)
    gate = dot(norm_two, gate_weight)
    upward = dot(norm_two, up_weight)
    gated, gated_back = jax.vjp(swiglu, gate, upward)
    hidden = gated.astype(BF16)
    mixed = mid + dot(hidden, down_weight)
    grad_out = cotangent[0]
    grad_hidden = dot(grad_out, down_weight, NT)
    grad_gate_full, grad_up_full = gated_back(grad_hidden)
    grad_gate, grad_upward = grad_gate_full.astype(BF16), grad_up_full.astype(BF16)
    grad_norm_two = dot(grad_gate, gate_weight, NT) + dot(grad_upward, up_weight, NT)
    grad_mid_norm, grad_gain_second = norm_two_back(grad_norm_two)
    grad_mid = grad_out.astype(F32) + grad_mid_norm
    grad_mid_low = grad_mid.astype(BF16)
    grad_attention = dot(grad_mid_low, out_weight, NT).astype(BF16)
    grad_dots = jnp.sum(
        (grad_attention.astype(F32) * attention).reshape(rows, HEADS, head_width), axis=2
    ).T
    back_stats = jnp.concatenate([log_total, grad_dots], axis=0)
    all_grads, all_stats = gather(grad_attention[None], "mem"), gather(back_stats[None], "mem")

    early = jnp.concatenate(
        [
            dot(attention_low, grad_mid_low, TN),
            dot(norm_two, grad_gate, TN),
            dot(norm_two, grad_upward, TN),
        ],
        axis=1,
    ).astype(BF16)
    early_sum = scatter(early, both)
    down_sum = scatter(dot(hidden, grad_out, TN).astype(BF16), both)

    local_dq, local_dk, local_dv = local_backward(
        place, queries, grad_attention, back_stats, segment_keys, segment_values, scale
    )
    owner_grads = owner_backward(
        order, all_queries, all_grads, all_stats, bits, cached_keys, cached_values, scale
    )
    peer_grads = exchange(owner_grads)
    grad_queries = local_dq + jnp.sum(jnp.where(live, peer_grads.astype(F32), 0.0), axis=0)
    grad_keys_mine = scatter(local_dk, "seq").astype(F32)
    grad_value_in = scatter(local_dv, "seq")
    grad_query_in = rotate(grad_queries, cosine, -sine).astype(BF16)
    grad_key_in = rotate(grad_keys_mine, cosine, -sine).astype(BF16)
    grad_in = jnp.concatenate([grad_query_in, grad_key_in, grad_value_in], axis=1)
    grad_norm_one = dot(grad_in, qkv_weight, NT)
    grad_in_norm, grad_gain_first = norm_one_back(grad_norm_one)
    grad_inputs = grad_mid + grad_in_norm
    late = jnp.concatenate(
        [
            dot(norm_one, grad_in, TN).astype(BF16),
            jnp.zeros((width, 128), BF16)
            .at[:, 0]
            .set(grad_gain_first.astype(BF16))
            .at[:, 1]
            .set(grad_gain_second.astype(BF16)),
        ],
        axis=1,
    )
    late_sum = scatter(late, both).astype(F32)
    early_sum = early_sum.astype(F32)
    return (
        mixed[None],
        grad_inputs[None],
        late_sum[:, :width],
        late_sum[:, width : 2 * width],
        late_sum[:, 2 * width : 3 * width],
        early_sum[:, :width],
        late_sum[:, 3 * width],
        early_sum[:, width : width + hidden_width],
        early_sum[:, width + hidden_width :],
        down_sum.astype(F32),
        late_sum[:, 3 * width + 1],
    )


def solution(mesh):
    rows, owned, feature = P("mem", "seq", None), P(None, "mem", None), P(("seq", "mem"), None)
    gain = P(("seq", "mem"))
    return jax.shard_map(
        per_device,
        mesh=mesh,
        in_specs=(
            (rows, owned, owned, rows, P("mem"))
            + (feature,) * 4
            + (gain,)
            + (feature,) * 3
            + (gain, rows)
        ),
        out_specs=(rows, rows) + (feature,) * 4 + (gain,) + (feature,) * 3 + (gain,),
        check_vma=False,
    )
```

```python
import functools

import jax
import jax.numpy as jnp
from jax import lax
from jax.experimental import pallas as pl
from jax.experimental.pallas import tpu as pltpu
from jax.sharding import PartitionSpec as P

HEADS = 8
EPSILON = 1e-05
FLOOR = -1e30
LOW = -1e29
LOG2E = 1.4426950408889634
STATS = 16
PIECES = 4
F32 = jnp.float32
BF16 = jnp.bfloat16
VMEM_LIMIT = 56 * 1024 * 1024
NT = (((1,), (1,)), ((), ()))
TN = (((0,), (0,)), ((), ()))


def dot(left, right, dims=(((1,), (0,)), ((), ()))):
    return lax.dot_general(left, right, dims, preferred_element_type=F32)


def rms_norm(values, gain):
    return values * lax.rsqrt(jnp.mean(values * values, axis=-1, keepdims=True) + EPSILON) * gain


def swiglu(gate_in, up_in):
    return jax.nn.silu(gate_in) * up_in


def angles_for(positions, head_width):
    exponent = jnp.arange(head_width // 2, dtype=F32) * (2.0 / head_width)
    frequency = jnp.power(10000.0, -exponent)
    turned = positions.astype(F32)[:, None] * frequency[None, :]
    return (jnp.cos(turned), jnp.sin(turned))


def rotate(values, cosine, sine):
    rows, width = values.shape
    split = values.reshape(rows, HEADS, width // HEADS)
    middle = split.shape[-1] // 2
    first, second = split[..., :middle], split[..., middle:]
    cos_rows, sin_rows = cosine[:, None, :], sine[:, None, :]
    turned = jnp.concatenate(
        [first * cos_rows - second * sin_rows, second * cos_rows + first * sin_rows], axis=-1
    )
    return turned.reshape(values.shape)


def params(**more):
    return pltpu.CompilerParams(vmem_limit_bytes=VMEM_LIMIT, **more)


def spread(columns, width=128):
    lanes = lax.broadcasted_iota(jnp.int32, (columns[0].shape[0], width), 1)
    result = jnp.zeros((columns[0].shape[0], width), F32)
    for place, column in enumerate(columns):
        result = jnp.where(lanes == place, column, result)
    return result


def columns_of(rows_by_stat):
    count, width = rows_by_stat.shape
    padded = jnp.concatenate([rows_by_stat, jnp.zeros((128 - count, width), F32)], axis=0)
    return padded.T


MESH = pl.DeviceIdType.MESH


class Net:
    def __init__(self, line):
        self.line = line
        self.s, self.m = lax.axis_index("seq"), lax.axis_index("mem")
        self.c, self.z = self.m % 2, self.m // 2
        self.x, self.y, self.core = (self.s ^ 1, self.m), (self.s ^ 2, self.m), (self.s, self.m ^ 1)
        self.right = (self.s, (self.m + 2) % (2 * line))
        self.left = (self.s, (self.m + 2 * line - 2) % (2 * line))

    def greet(self, others):
        barrier = pltpu.get_barrier_semaphore()
        for other in others:
            pl.semaphore_signal(barrier, inc=1, device_id=other, device_id_type=MESH)
        pl.semaphore_wait(barrier, len(others))


def remote(src, dst, sends, recvs, place, device):
    return pltpu.make_async_remote_copy(
        src_ref=src,
        dst_ref=dst,
        send_sem=sends.at[place],
        recv_sem=recvs.at[place],
        device_id=device,
        device_id_type=MESH,
    )


def row_halves(ref, part):
    half = ref.shape[-2] // 2
    return ref.at[pl.ds(part * half, half)]


def column_halves(ref, part):
    half = ref.shape[-1] // 2
    return ref.at[:, pl.ds(part * half, half)]


class Gather:
    def __init__(self, net, src, out, sends, recvs, own, index, halves, line=True, square=True, core=True):
        self.net, self.src, self.out, self.sends, self.recvs, self.own = net, src, out, sends, recvs, own
        self.index, self.halves = index, halves
        self.line, self.square, self.core = line, square, core

    def slot(self, s, z):
        return self.out.at[self.index(s, z, self.net.c)]

    def send(self, block, target, place, device):
        copy = remote(block, target, self.sends, self.recvs, place, device)
        copy.start()

    def sent(self, block, place):
        remote(block, block, self.sends, self.recvs, place, self.net.core).wait_send()

    def arrived(self, block, place):
        remote(block, block, self.sends, self.recvs, place, self.net.core).wait_recv()

    def places(self):
        z = self.net.line
        right, left, square, core = 0, z, 2 * z, 8 * z
        return right, left, square, core

    def steps(self, body):
        net = self.net
        body(0, net.z, None)
        if self.line:
            for k in range(1, net.line):
                self.step(k, body)

    def step(self, k, body):
        net = self.net
        if k == 0:
            body(0, net.z, None)
            return
        if not self.line:
            return
        pl.when(net.z >= k)(lambda: body(k, net.z - k, True))
        pl.when(net.z + k < net.line)(lambda: body(k, net.z + k, False))

    def have(self, k, z, from_left):
        net = self.net
        right, left, square, core = self.places()
        target = self.slot(net.s, z)
        block = self.src if k == 0 else target
        if k == 0:
            pltpu.make_async_copy(self.src, target, self.own).start()
        else:
            self.arrived(target, (right if from_left else left) + z)
        if self.line:
            if from_left is not False:
                pl.when(net.z < net.line - 1)(lambda: self.send(block, target, right + z, net.right))
            if from_left is not True:
                pl.when(net.z > 0)(lambda: self.send(block, target, left + z, net.left))
        if self.square:
            for kind, part, device in ((0, 0, net.x), (2, 1, net.y), (1, 0, net.y), (3, 1, net.x)):
                self.send(
                    self.halves(block, part),
                    self.halves(target, part),
                    square + kind * net.line + z,
                    device,
                )
        if self.core:
            self.send(block, target, core + z, net.core)

    def pass_square(self, k, z, from_left):
        net = self.net
        _, _, square, core = self.places()
        for kind, part, other, then, device, mirror in (
            (0, 0, net.s ^ 1, 4, net.y, 1),
            (2, 1, net.s ^ 2, 5, net.x, 2),
        ):
            block = self.halves(self.slot(other, z), part)
            self.arrived(block, square + kind * net.line + z)
            self.send(block, block, square + then * net.line + z, device)
            if self.core:
                self.send(block, block, core + mirror * net.line + z, net.core)

    def end_square(self, k, z, from_left):
        net = self.net
        _, _, square, core = self.places()
        for kind, part, other, mirror in self.last(net):
            block = self.halves(self.slot(other, z), part)
            self.arrived(block, square + kind * net.line + z)
            if self.core:
                self.send(block, block, core + mirror * net.line + z, net.core)

    def last(self, net):
        return (
            (1, 0, net.s ^ 2, 3),
            (3, 1, net.s ^ 1, 5),
            (4, 0, net.s ^ 3, 4),
            (5, 1, net.s ^ 3, 6),
        )

    def finish(self):
        net = self.net
        right, left, square, core = self.places()
        own = self.slot(net.s, net.z)
        pltpu.make_async_copy(self.src, own, self.own).wait()
        if self.core:
            for z in range(net.line if self.line else 1):
                z = z if self.line else net.z
                for mirror, part, other in (
                    (0, None, net.s),
                    (1, 0, net.s ^ 1),
                    (2, 1, net.s ^ 2),
                    (3, 0, net.s ^ 2),
                    (4, 0, net.s ^ 3),
                    (5, 1, net.s ^ 1),
                    (6, 1, net.s ^ 3),
                ):
                    if part is not None and not self.square:
                        continue
                    block = self.out.at[self.index(other, z, 1 - net.c)]
                    block = block if part is None else self.halves(block, part)
                    self.arrived(block, core + mirror * net.line + z)
                    self.sent(block, core + mirror * net.line + z)
        if self.square:
            half = [self.halves(own, 0), self.halves(own, 1)]
            for z in range(net.line if self.line else 1):
                z = z if self.line else net.z
                for kind, part in ((0, 0), (1, 0), (2, 1), (3, 1), (4, 0), (5, 1)):
                    self.sent(half[part], square + kind * net.line + z)
        if self.line:
            for z in range(net.line):
                pl.when((z <= net.z) & (net.z < net.line - 1))(lambda z=z: self.sent(own, right + z))
                pl.when((z >= net.z) & (net.z > 0))(lambda z=z: self.sent(own, left + z))


def run_gathers(gathers, line):
    for k in range(line):
        for gather in gathers:
            gather.step(k, gather.have)
        if k > 0:
            for gather in gathers:
                if gather.square:
                    gather.step(k - 1, gather.pass_square)
    for gather in gathers:
        if gather.square:
            gather.step(line - 1, gather.pass_square)
    for k in range(line):
        for gather in gathers:
            if gather.square:
                gather.step(k, gather.end_square)
    for gather in gathers:
        gather.finish()


def gather_kernel(line, plan, *refs):
    count = len(plan)
    sources, outs, sems = refs[:count], refs[count : 2 * count], refs[2 * count :]
    net = Net(line)
    net.greet([net.x, net.y, net.core, net.left, net.right])
    index = {
        "all": lambda s, z, c: (s * line + z) * 2 + c,
        "line": lambda s, z, c: z * 2 + c,
        "square": lambda s, z, c: s,
    }
    gathers = []
    for i, (halves, reach) in enumerate(plan):
        sends, recvs, own = sems[3 * i : 3 * i + 3]
        gathers.append(
            Gather(
                net,
                sources[i],
                outs[i],
                sends,
                recvs,
                own,
                index[reach],
                halves,
                line=reach != "square",
                square=reach != "line",
                core=reach != "square",
            )
        )
    run_gathers(gathers, line)


def gather_many(collective_id, name, sizes, arrays, plan):
    line = sizes["mem"] // 2
    slots = {"all": sizes["seq"] * sizes["mem"], "line": sizes["mem"], "square": sizes["seq"]}
    anywhere = pl.BlockSpec(memory_space=pl.ANY)
    scratch = []
    for _ in plan:
        scratch += [pltpu.SemaphoreType.DMA((15 * line,))] * 2 + [pltpu.SemaphoreType.DMA]
    moved = sum(a.size * a.dtype.itemsize * slots[reach] for a, (_, reach) in zip(arrays, plan))
    return pl.pallas_call(
        functools.partial(gather_kernel, line, plan),
        out_shape=[
            jax.ShapeDtypeStruct((slots[reach],) + a.shape, a.dtype)
            for a, (_, reach) in zip(arrays, plan)
        ],
        in_specs=[anywhere] * len(plan),
        out_specs=[anywhere] * len(plan),
        scratch_shapes=scratch,
        compiler_params=params(collective_id=collective_id, has_side_effects=True),
        cost_estimate=pl.CostEstimate(flops=0, bytes_accessed=2 * moved, transcendentals=0),
        name=name,
    )(*arrays)


class Scatter:
    def __init__(self, net, src, out, buffers, sems, halves, whole=True):
        self.net, self.src, self.out, self.halves = net, src, out, halves
        self.whole, self.count = whole, src.shape[1]
        self.held, self.twin, self.first, self.second, self.along = buffers
        self.sends, self.recvs, self.own = sems

    def send(self, block, target, place, device):
        remote(block, target, self.sends, self.recvs, place, device).start()

    def sent(self, block, place):
        remote(block, block, self.sends, self.recvs, place, self.net.core).wait_send()

    def arrived(self, block, place):
        remote(block, block, self.sends, self.recvs, place, self.net.core).wait_recv()

    def places(self):
        z = self.count
        return 0, 4 * z, 8 * z, 10 * z, 11 * z

    def loading(self, d):
        source = self.src.at[:, d, self.net.c] if self.whole else self.src.at[:, d]
        return pltpu.make_async_copy(source, self.held.at[:, d], self.own.at[d])

    def load(self, d):
        net = self.net
        self.loading(d).start()
        for s in range(4 if self.whole else 0):
            self.send(self.src.at[s, d, 1 - net.c], self.twin.at[s, d], s * self.count + d, net.core)

    def add_core(self, d):
        net = self.net
        _, first, _, _, _ = self.places()
        self.loading(d).wait()
        for turn in (3, 2, 1, 0):
            s = net.s ^ turn
            if self.whole:
                self.arrived(self.twin.at[s, d], s * self.count + d)
                self.held[s, d] = self.held[s, d] + self.twin[s, d]
            for part, device, slot, kind in {
                3: ((0, net.y, 1, 1), (1, net.x, 1, 3)),
                2: ((0, net.y, 0, 0),),
                1: ((1, net.x, 0, 2),),
                0: (),
            }[turn]:
                self.send(
                    self.halves(self.held.at[s, d], part),
                    self.first.at[part, slot, d],
                    first + kind * self.count + d,
                    device,
                )

    def add(self, block, other):
        block[...] = block[...] + other[...]

    def add_first(self, d):
        net = self.net
        _, first, second, _, _ = self.places()
        for part, slot, kind, turn in ((0, 1, 1, 1), (1, 1, 3, 2), (0, 0, 0, 0), (1, 0, 2, 0)):
            got = self.first.at[part, slot, d]
            self.arrived(got, first + kind * self.count + d)
            block = self.halves(self.held.at[net.s ^ turn, d], part)
            self.add(block, got)
            if turn:
                device = net.x if part == 0 else net.y
                self.send(block, self.second.at[part, d], second + part * self.count + d, device)

    def add_second(self, d):
        net = self.net
        _, _, second, _, _ = self.places()
        for part in range(2):
            self.arrived(self.second.at[part, d], second + part * self.count + d)
            self.add(self.halves(self.held.at[net.s, d], part), self.second.at[part, d])

    def line_step(self, d):
        net = self.net
        _, _, _, right, left = self.places()
        block = self.held.at[net.s, d]
        if not self.whole:
            self.out[d] = block[...].astype(self.out.dtype)
            return

        def from_left():
            self.arrived(self.along.at[0, d], right + d)
            self.add(block, self.along.at[0, d])

        def from_right():
            self.arrived(self.along.at[1, d], left + d)
            self.add(block, self.along.at[1, d])

        pl.when((net.z <= d) & (net.z > 0))(from_left)
        pl.when((net.z >= d) & (net.z < net.line - 1))(from_right)
        pl.when(net.z < d)(lambda: self.send(block, self.along.at[0, d], right + d, net.right))
        pl.when(net.z > d)(lambda: self.send(block, self.along.at[1, d], left + d, net.left))

        def keep():
            self.out[...] = block[...].astype(self.out.dtype)

        pl.when(net.z == d)(keep)

    def finish(self):
        net = self.net
        _, first, second, right, left = self.places()
        full = self.held.at[net.s, 0]
        for d in range(self.count):
            for s in range(4 if self.whole else 0):
                self.sent(full, s * self.count + d)
            for kind, part in enumerate((0, 0, 1, 1)):
                self.sent(self.halves(full, part), first + kind * self.count + d)
            for part in range(2):
                self.sent(self.halves(full, part), second + part * self.count + d)
            if self.whole:
                pl.when(net.z < d)(lambda d=d: self.sent(full, right + d))
                pl.when(net.z > d)(lambda d=d: self.sent(full, left + d))


def ends_first(line):
    return sorted(range(line), key=lambda d: min(d, line - 1 - d))


def run_scatters(scatters):
    lags = (("load", 0), ("add_core", 1), ("add_first", 2), ("add_second", 3), ("line_step", 4))
    for wave in range(max(scatter.count for scatter in scatters) + lags[-1][1]):
        for stage, lag in lags:
            for scatter in scatters:
                if 0 <= wave - lag < scatter.count:
                    getattr(scatter, stage)(ends_first(scatter.count)[wave - lag])
    for scatter in scatters:
        scatter.finish()


def scatter_scratch(count, rows, columns, halves, whole):
    half = (rows // 2, columns) if halves is row_halves else (rows, columns // 2)
    block = (rows, columns)
    return [
        pltpu.VMEM((4, count) + block, BF16),
        pltpu.VMEM((4, count) + block if whole else (16, 128), BF16),
        pltpu.VMEM((2, 2, count) + half, BF16),
        pltpu.VMEM((2, count) + half, BF16),
        pltpu.VMEM((2, count) + block if whole else (16, 128), BF16),
        pltpu.SemaphoreType.DMA((12 * count,)),
        pltpu.SemaphoreType.DMA((12 * count,)),
        pltpu.SemaphoreType.DMA((count,)),
    ]


def scatter_kernel(line, plan, *refs):
    count = len(plan)
    sources, outs, scratch = refs[:count], refs[count : 2 * count], refs[2 * count :]
    net = Net(line)
    net.greet([net.x, net.y, net.core, net.left, net.right])
    scatters = []
    for i, (halves, whole) in enumerate(plan):
        scatch = scratch[8 * i : 8 * i + 8]
        scatters.append(Scatter(net, sources[i], outs[i], scatch[:5], scatch[5:], halves, whole))
    run_scatters(scatters)


def scatter_many(collective_id, name, sizes, arrays, plan):
    square, line = sizes["seq"], sizes["mem"] // 2
    blocks, outs, scratch = [], [], []
    for array, (halves, whole) in zip(arrays, plan):
        columns = array.shape[1]
        if whole:
            rows = array.shape[0] // (2 * square * line)
            blocks.append(array.reshape(square, line, 2, rows, columns))
            outs.append(jax.ShapeDtypeStruct((rows, columns), F32))
            scratch += scatter_scratch(line, rows, columns, halves, True)
        else:
            rows = array.shape[0] // (square * PIECES)
            blocks.append(array.reshape(square, PIECES, rows, columns))
            outs.append(jax.ShapeDtypeStruct((PIECES, rows, columns), F32))
            scratch += scatter_scratch(PIECES, rows, columns, halves, False)
    moved = sum(a.size * a.dtype.itemsize for a in arrays)
    sums = pl.pallas_call(
        functools.partial(scatter_kernel, line, plan),
        out_shape=outs,
        in_specs=[pl.BlockSpec(memory_space=pl.ANY)] * len(plan),
        out_specs=[pl.BlockSpec(memory_space=pltpu.VMEM)] * len(plan),
        scratch_shapes=scratch,
        compiler_params=params(collective_id=collective_id, has_side_effects=True),
        cost_estimate=pl.CostEstimate(flops=0, bytes_accessed=2 * moved, transcendentals=0),
        name=name,
    )(*blocks)
    return [s.reshape(-1, s.shape[-1]) for s in sums]


def return_kernel(line, with_stats, *refs):
    kinds = 2 if with_stats else 1
    sources, outs = refs[:kinds], refs[kinds : 2 * kinds]
    held, twin = refs[2 * kinds : 3 * kinds], refs[3 * kinds : 4 * kinds]
    own, twin_sends, twin_recvs, sends, recvs = refs[4 * kinds :]
    net = Net(line)
    others = [(net.s, lax.rem(net.m + 2 * k, 2 * line)) for k in range(1, line)]
    net.greet([net.core] + others)
    places = [lax.rem(net.z + k, line) for k in (*range(1, line), 0)]
    for d in places:
        for i in range(kinds):
            pltpu.make_async_copy(sources[i].at[d, net.c], held[i].at[d], own.at[i, d]).start()
            remote(
                sources[i].at[d, 1 - net.c], twin[i].at[d], twin_sends.at[i], twin_recvs.at[i], d, net.core
            ).start()
    for k, d in enumerate(places):
        for i in range(kinds):
            pltpu.make_async_copy(sources[i].at[d, net.c], held[i].at[d], own.at[i, d]).wait()
            remote(
                twin[i].at[d], twin[i].at[d], twin_sends.at[i], twin_recvs.at[i], d, net.core
            ).wait_recv()
        if with_stats:
            mine, theirs = held[1][d], twin[1][d]
            top = jnp.maximum(mine[:HEADS], theirs[:HEADS])
            shares = [jnp.exp2(mine[:HEADS] - top), jnp.exp2(theirs[:HEADS] - top)]
            held[1][d] = jnp.concatenate(
                [top, mine[HEADS:] * shares[0] + theirs[HEADS:] * shares[1]], axis=0
            )
            shares = columns_of(jnp.concatenate(shares, axis=0))
            for h in range(HEADS):
                span = slice(h * 128, (h + 1) * 128)
                held[0][d, :, span] = (
                    held[0][d, :, span].astype(F32) * shares[:, h : h + 1]
                    + twin[0][d, :, span].astype(F32) * shares[:, HEADS + h : HEADS + h + 1]
                ).astype(BF16)
        else:
            held[0][d] = held[0][d] + twin[0][d]
        for i in range(kinds):
            if k < line - 1:
                pltpu.make_async_remote_copy(
                    src_ref=held[i].at[d],
                    dst_ref=outs[i].at[net.z],
                    send_sem=sends.at[i, k],
                    recv_sem=recvs.at[i, net.z],
                    device_id=(net.s, 2 * d + net.c),
                    device_id_type=MESH,
                ).start()
            else:
                pltpu.make_async_copy(held[i].at[d], outs[i].at[net.z], own.at[i, d]).start()
    for i in range(kinds):
        for k, d in enumerate(places):
            remote(twin[i].at[d], twin[i].at[d], twin_sends.at[i], twin_recvs.at[i], d, net.core).wait_send()
            if k < line - 1:
                here = outs[i].at[d]
                remote(here, here, sends.at[i], recvs.at[i], d, net.core).wait_recv()
                pltpu.make_async_remote_copy(
                    src_ref=held[i].at[d],
                    dst_ref=here,
                    send_sem=sends.at[i, k],
                    recv_sem=recvs.at[i, d],
                    device_id=net.core,
                    device_id_type=MESH,
                ).wait_send()
            else:
                pltpu.make_async_copy(held[i].at[d], outs[i].at[net.z], own.at[i, d]).wait()


def return_home(collective_id, name, sizes, arrays):
    line = sizes["mem"] // 2
    blocks = [a.reshape((line, 2) + a.shape[1:]) for a in arrays]
    kinds = len(arrays)
    anywhere = pl.BlockSpec(memory_space=pl.ANY)
    slots = [pltpu.VMEM((line,) + a.shape[1:], a.dtype) for a in arrays]
    moved = sum(a.size * a.dtype.itemsize for a in arrays)
    return pl.pallas_call(
        functools.partial(return_kernel, line, kinds == 2),
        out_shape=[jax.ShapeDtypeStruct((line,) + a.shape[1:], a.dtype) for a in arrays],
        in_specs=[anywhere] * kinds,
        out_specs=[anywhere] * kinds,
        scratch_shapes=slots
        + slots
        + [pltpu.SemaphoreType.DMA((kinds, line))] * 5,
        compiler_params=params(collective_id=collective_id, has_side_effects=True),
        cost_estimate=pl.CostEstimate(flops=0, bytes_accessed=2 * moved, transcendentals=0),
        name=name,
    )(*blocks)


def mask_kernel(blocks, order_ref, base_ref, index_ref, bits_ref):
    del order_ref
    rows = index_ref.shape[1]
    lanes = lax.broadcasted_iota(jnp.int32, (8, 128), 1)

    def group(g, carry):
        start = pl.multiple_of(g * 8, 8)
        relative = index_ref[0, pl.ds(start, 8), :] - base_ref[0]
        inside = (relative >= 0) & (relative < blocks * 128)
        place = jnp.where(inside, relative & 127, 0)
        bit = jnp.where(inside, lax.shift_left(jnp.ones_like(relative), relative >> 7), 0)
        code = place | (bit << 7)
        word = jnp.zeros((8, 128), jnp.int32)
        for j in range(index_ref.shape[2]):
            one = jnp.broadcast_to(code[:, j : j + 1], (8, 128))
            word = word | jnp.where((one & 127) == lanes, one >> 7, 0)
        bits_ref[0, pl.ds(start, 8), :] = word
        return carry

    lax.fori_loop(0, rows // 8, group, 0)


def mask_bits(order, base, all_index, mem_dev):
    active = order.shape[0]
    _, rows, count = all_index.shape
    return pl.pallas_call(
        functools.partial(mask_kernel, mem_dev // 128),
        grid_spec=pltpu.PrefetchScalarGridSpec(
            num_scalar_prefetch=2,
            grid=(active,),
            in_specs=[pl.BlockSpec((1, rows, count), lambda a, o, b: (o[a], 0, 0))],
            out_specs=pl.BlockSpec((1, rows, 128), lambda a, o, b: (a, 0, 0)),
        ),
        out_shape=jax.ShapeDtypeStruct((active, rows, 128), jnp.int32),
        compiler_params=params(),
        name="mask_bits",
    )(order, base, all_index)


def fill_bias(bits_ref, bias_ref):
    bits = bits_ref[0]
    for b in range(bias_ref.shape[1] // 128):
        bias_ref[:, b * 128 : (b + 1) * 128] = jnp.where(((bits >> b) & 1) != 0, 0.0, FLOOR)


def owner_forward_kernel(scale, order_ref, q_ref, bits_ref, k_ref, v_ref, o_ref, st_ref, bias_ref):
    del order_ref
    fill_bias(bits_ref, bias_ref)
    maxima, sums = [], []
    for h in range(HEADS):
        span = slice(h * 128, (h + 1) * 128)
        scores = dot(q_ref[0, :, span], k_ref[0, :, span], NT) * scale + bias_ref[...]
        top = jnp.maximum(jnp.max(scores, axis=1, keepdims=True), LOW)
        weights = jnp.exp2(scores - top)
        maxima.append(top)
        sums.append(jnp.sum(weights, axis=1, keepdims=True))
        o_ref[0, :, span] = dot(weights.astype(BF16), v_ref[0, :, span]).astype(BF16)
    st_ref[0] = spread(maxima + sums).T[:STATS]


def owner_forward(order, queries, bits, cached_keys, cached_values, scale):
    segments, rows, width = queries.shape
    mem_dev = cached_keys.shape[1]
    active = order.shape[0]
    picked = lambda a, o: (o[a], 0, 0)
    return pl.pallas_call(
        functools.partial(owner_forward_kernel, scale),
        grid_spec=pltpu.PrefetchScalarGridSpec(
            num_scalar_prefetch=1,
            grid=(active,),
            in_specs=[
                pl.BlockSpec((1, rows, width), picked),
                pl.BlockSpec((1, rows, 128), lambda a, o: (a, 0, 0)),
                pl.BlockSpec((1, mem_dev, width), picked),
                pl.BlockSpec((1, mem_dev, width), picked),
            ],
            out_specs=[
                pl.BlockSpec((1, rows, width), picked),
                pl.BlockSpec((1, STATS, rows), picked),
            ],
            scratch_shapes=[pltpu.VMEM((rows, mem_dev), F32)],
        ),
        out_shape=[
            jax.ShapeDtypeStruct((segments, rows, width), BF16),
            jax.ShapeDtypeStruct((segments, STATS, rows), F32),
        ],
        compiler_params=params(),
        name="owner_forward",
    )(order, queries, bits, cached_keys, cached_values)


def owner_backward_kernel(
    scale, order_ref, q_ref, g_ref, st_ref, bits_ref, k_ref, v_ref, dq_ref, bias_ref
):
    del order_ref
    fill_bias(bits_ref, bias_ref)
    stats = columns_of(st_ref[0])
    for h in range(HEADS):
        span = slice(h * 128, (h + 1) * 128)
        scores = dot(q_ref[0, :, span], k_ref[0, :, span], NT) * scale + bias_ref[...]
        weights = jnp.exp2(scores - stats[:, h : h + 1])
        dweights = dot(g_ref[0, :, span], v_ref[0, :, span], NT)
        dscore = weights * (dweights - stats[:, HEADS + h : HEADS + h + 1])
        dq_ref[0, :, span] = (
            dot(dscore.astype(BF16), k_ref[0, :, span]) * (scale / LOG2E)
        ).astype(BF16)


def owner_backward(order, queries, grads, stats, bits, cached_keys, cached_values, scale):
    segments, rows, width = queries.shape
    mem_dev = cached_keys.shape[1]
    active = order.shape[0]
    picked = lambda a, o: (o[a], 0, 0)
    return pl.pallas_call(
        functools.partial(owner_backward_kernel, scale),
        grid_spec=pltpu.PrefetchScalarGridSpec(
            num_scalar_prefetch=1,
            grid=(active,),
            in_specs=[
                pl.BlockSpec((1, rows, width), picked),
                pl.BlockSpec((1, rows, width), picked),
                pl.BlockSpec((1, STATS, rows), picked),
                pl.BlockSpec((1, rows, 128), lambda a, o: (a, 0, 0)),
                pl.BlockSpec((1, mem_dev, width), picked),
                pl.BlockSpec((1, mem_dev, width), picked),
            ],
            out_specs=pl.BlockSpec((1, rows, width), picked),
            scratch_shapes=[pltpu.VMEM((rows, mem_dev), F32)],
        ),
        out_shape=jax.ShapeDtypeStruct((segments, rows, width), BF16),
        compiler_params=params(),
        name="owner_backward",
    )(order, queries, grads, stats, bits, cached_keys, cached_values)


def causal_bias(place_ref, rows, keys):
    row = place_ref[0] * rows + lax.broadcasted_iota(jnp.int32, (rows, keys), 0)
    return jnp.where(lax.broadcasted_iota(jnp.int32, (rows, keys), 1) <= row, 0.0, FLOOR)


def local_forward_kernel(scale, place_ref, q_ref, kv_ref, o_ref, st_ref):
    width = q_ref.shape[1]
    k_ref, v_ref = kv_ref.at[:, :width], kv_ref.at[:, width:]
    bias = causal_bias(place_ref, q_ref.shape[0], k_ref.shape[0])
    maxima, sums = [], []
    for h in range(HEADS):
        span = slice(h * 128, (h + 1) * 128)
        scores = dot(q_ref[:, span], k_ref[:, span], NT) * scale + bias
        top = jnp.max(scores, axis=1, keepdims=True)
        weights = jnp.exp2(scores - top)
        maxima.append(top)
        sums.append(jnp.sum(weights, axis=1, keepdims=True))
        o_ref[:, span] = dot(weights.astype(BF16), v_ref[:, span])
    st_ref[...] = spread(maxima + sums).T[:STATS]


def whole(*shape):
    return pl.BlockSpec(shape, lambda *_: (0,) * len(shape))


def local_forward(place, queries, kv, scale):
    rows, width = queries.shape
    length = kv.shape[0]
    return pl.pallas_call(
        functools.partial(local_forward_kernel, scale),
        grid_spec=pltpu.PrefetchScalarGridSpec(
            num_scalar_prefetch=1,
            grid=(1,),
            in_specs=[whole(rows, width), whole(length, 2 * width)],
            out_specs=[whole(rows, width), whole(STATS, rows)],
        ),
        out_shape=[
            jax.ShapeDtypeStruct((rows, width), F32),
            jax.ShapeDtypeStruct((STATS, rows), F32),
        ],
        compiler_params=params(),
        name="local_forward",
    )(place, queries, kv)


def local_backward_kernel(
    scale, place_ref, q_ref, g_ref, st_ref, kv_ref, dq_ref, dkv_ref
):
    width = q_ref.shape[1]
    k_ref, v_ref = kv_ref.at[:, :width], kv_ref.at[:, width:]
    dk_ref, dv_ref = dkv_ref.at[:, :width], dkv_ref.at[:, width:]
    bias = causal_bias(place_ref, q_ref.shape[0], k_ref.shape[0])
    stats = columns_of(st_ref[...])
    for h in range(HEADS):
        span = slice(h * 128, (h + 1) * 128)
        query, key, grad = q_ref[:, span], k_ref[:, span], g_ref[:, span]
        scores = dot(query, key, NT) * scale + bias
        weights = jnp.exp2(scores - stats[:, h : h + 1])
        dweights = dot(grad, v_ref[:, span], NT)
        dscore = (weights * (dweights - stats[:, HEADS + h : HEADS + h + 1])).astype(BF16)
        dq_ref[:, span] = dot(dscore, key) * (scale / LOG2E)
        dk_ref[:, span] = (dot(dscore, query, TN) * (scale / LOG2E)).astype(BF16)
        dv_ref[:, span] = dot(weights.astype(BF16), grad, TN).astype(BF16)


def local_backward(place, queries, grads, stats, kv, scale):
    rows, width = queries.shape
    length = kv.shape[0]
    return pl.pallas_call(
        functools.partial(local_backward_kernel, scale),
        grid_spec=pltpu.PrefetchScalarGridSpec(
            num_scalar_prefetch=1,
            grid=(1,),
            in_specs=[
                whole(rows, width),
                whole(rows, width),
                whole(STATS, rows),
                whole(length, 2 * width),
            ],
            out_specs=[whole(rows, width), whole(length, 2 * width)],
        ),
        out_shape=[
            jax.ShapeDtypeStruct((rows, width), F32),
            jax.ShapeDtypeStruct((length, 2 * width), BF16),
        ],
        compiler_params=params(),
        name="local_backward",
    )(place, queries, grads, stats, kv)


REACH = {"all": ("seq", "mem"), "line": "mem", "square": "seq"}


def gather_plain(collective_id, name, sizes, arrays, plan):
    return [lax.all_gather(a, REACH[reach], axis=0) for a, (_, reach) in zip(arrays, plan)]


def scatter_plain(collective_id, name, sizes, arrays, plan):
    return [
        lax.psum_scatter(
            a, REACH["all"] if whole else REACH["square"], scatter_dimension=0, tiled=True
        ).astype(F32)
        for a, (_, whole) in zip(arrays, plan)
    ]


def return_plain(collective_id, name, sizes, arrays):
    return [
        lax.all_to_all(a, "mem", split_axis=0, concat_axis=0, tiled=True) for a in arrays
    ]


def per_device(
    sizes,
    tokens,
    cached_keys,
    cached_values,
    knn_index,
    has_memory,
    w_query,
    w_key,
    w_value,
    w_out,
    gain_attn,
    w_gate,
    w_up,
    w_down,
    gain_ffn,
    cotangent,
):
    near = sizes["seq"] == 4 and sizes["mem"] % 2 == 0 and 4 <= sizes["mem"] <= 16
    gather, scatter, send_home = (
        (gather_many, scatter_many, return_home)
        if near
        else (gather_plain, scatter_plain, return_plain)
    )
    inputs = tokens[0].astype(F32)
    rows, width = inputs.shape
    hidden_width = w_gate.shape[1]
    head_width = width // HEADS
    scale = head_width ** (-0.5) * LOG2E
    mem_dev = cached_keys.shape[1]
    place = lax.axis_index("seq").astype(jnp.int32)[None]
    base = (lax.axis_index("mem") * mem_dev).astype(jnp.int32)[None]

    gains = jnp.zeros((w_query.shape[0], 128), BF16)
    gains = gains.at[:, 0].set(gain_attn).at[:, 1].set(gain_ffn)
    first_shard = jnp.concatenate([w_query, w_key, w_value, gains], axis=1)
    flag_rows = jnp.broadcast_to(has_memory[:, None], (8, 128))
    first_weights, shared = gather(
        1,
        "gather_first",
        sizes,
        [first_shard, jnp.concatenate([knn_index[0], flag_rows], axis=0)],
        [(row_halves, "all"), (row_halves, "line")],
    )
    first_weights = first_weights.reshape(-1, first_shard.shape[1])
    all_index, flags = shared[:, :rows], shared[:, rows, 0]
    segments = flags.shape[0]
    order = jnp.argsort(jnp.where(flags > 0, 0, 1), stable=True)[: segments // 2].astype(jnp.int32)
    bits = mask_bits(order, base, all_index, mem_dev)

    qkv_weight = first_weights[:, : 3 * width]
    gain_first = first_weights[:, 3 * width].astype(F32)
    gain_second = first_weights[:, 3 * width + 1].astype(F32)
    positions = lax.axis_index("seq") * rows + jnp.arange(rows)
    cosine, sine = angles_for(positions, head_width)
    normed_one, norm_one_back = jax.vjp(rms_norm, inputs, gain_first)
    norm_one = normed_one.astype(BF16)
    qkv = dot(norm_one, qkv_weight)
    queries = rotate(qkv[:, :width], cosine, sine).astype(BF16)
    keys = rotate(qkv[:, width : 2 * width], cosine, sine).astype(BF16)
    keys_values = jnp.concatenate([keys, qkv[:, 2 * width :].astype(BF16)], axis=1)
    out_shard = jnp.concatenate([w_out, w_gate, w_up], axis=1)
    all_queries, segment_kv, out_gate_up, down_weight = gather(
        2,
        "gather_second",
        sizes,
        [queries, keys_values, out_shard, w_down],
        [(row_halves, "line"), (row_halves, "square"), (row_halves, "all"), (column_halves, "all")],
    )
    segment_kv = segment_kv.reshape(-1, 2 * width)
    down_weight = down_weight.reshape(-1, width)
    out_gate_up = out_gate_up.reshape(width, -1)
    out_weight = out_gate_up[:, :width]
    gate_weight = out_gate_up[:, width : width + hidden_width]
    up_weight = out_gate_up[:, width + hidden_width :]

    owner_out, owner_stats = owner_forward(
        order, all_queries, bits, cached_keys, cached_values, scale
    )
    local_out, local_stats = local_forward(place, queries, segment_kv, scale)
    peer_out, peer_stats = send_home(3, "return_outputs", sizes, [owner_out, owner_stats])
    live = has_memory[0] > 0
    peer_max = jnp.where(live, peer_stats[:, :HEADS], LOW)
    peer_sum = jnp.where(live, peer_stats[:, HEADS:], 0.0)
    local_max, local_sum = local_stats[:HEADS], local_stats[HEADS:]
    row_max = jnp.maximum(local_max, jnp.max(peer_max, axis=0))
    peer_share = jnp.exp2(peer_max - row_max)
    local_share = jnp.exp2(local_max - row_max)
    row_sum = local_sum * local_share + jnp.sum(peer_sum * peer_share, axis=0)
    log_total = row_max + jnp.log2(row_sum)

    def wide(stat):
        return jnp.broadcast_to(
            jnp.swapaxes(stat, -1, -2)[..., None], stat.shape[:-2] + (rows, HEADS, head_width)
        ).reshape(stat.shape[:-2] + (rows, width))

    peer_sums = jnp.sum(
        jnp.where(live, peer_out.astype(F32), 0.0) * wide(peer_share / row_sum), axis=0
    )
    attention = local_out * wide(local_share / row_sum) + peer_sums
    attention_low = attention.astype(BF16)
    mid = inputs + dot(attention_low, out_weight)
    normed_two, norm_two_back = jax.vjp(rms_norm, mid, gain_second)
    norm_two = normed_two.astype(BF16)
    gate = dot(norm_two, gate_weight)
    upward = dot(norm_two, up_weight)
    gated, gated_back = jax.vjp(swiglu, gate, upward)
    hidden = gated.astype(BF16)
    mixed = mid + dot(hidden, down_weight)
    grad_out = cotangent[0]
    grad_hidden = dot(grad_out, down_weight, NT)
    grad_gate_full, grad_up_full = gated_back(grad_hidden)
    grad_gate, grad_upward = grad_gate_full.astype(BF16), grad_up_full.astype(BF16)
    grad_norm_two = dot(grad_gate, gate_weight, NT) + dot(grad_upward, up_weight, NT)
    grad_mid_norm, grad_gain_second = norm_two_back(grad_norm_two)
    grad_mid = grad_out.astype(F32) + grad_mid_norm
    grad_mid_low = grad_mid.astype(BF16)
    grad_attention = dot(grad_mid_low, out_weight, NT).astype(BF16)
    grad_dots = jnp.sum(
        (grad_attention.astype(F32) * attention).reshape(rows, HEADS, head_width), axis=2
    ).T
    back_stats = jnp.concatenate([log_total, grad_dots], axis=0)
    all_grads, all_stats = gather(
        4,
        "gather_grads",
        sizes,
        [grad_attention, back_stats],
        [(row_halves, "line"), (row_halves, "line")],
    )

    early = jnp.concatenate(
        [
            dot(attention_low, grad_mid_low, TN),
            dot(norm_two, grad_gate, TN),
            dot(norm_two, grad_upward, TN),
        ],
        axis=1,
    ).astype(BF16)
    early_sum, down_sum = scatter(
        5,
        "scatter_early",
        sizes,
        [early, dot(hidden, grad_out, TN).astype(BF16)],
        [(row_halves, True), (column_halves, True)],
    )

    local_dq, local_dkv = local_backward(
        place, queries, grad_attention, back_stats, segment_kv, scale
    )
    owner_grads = owner_backward(
        order, all_queries, all_grads, all_stats, bits, cached_keys, cached_values, scale
    )
    (peer_grads,) = send_home(6, "return_grads", sizes, [owner_grads])
    grad_queries = local_dq + jnp.sum(jnp.where(live, peer_grads.astype(F32), 0.0), axis=0)
    (grad_kv,) = scatter(7, "scatter_keys", sizes, [local_dkv], [(row_halves, False)])
    grad_keys_mine, grad_value_in = grad_kv[:, :width], grad_kv[:, width:].astype(BF16)
    grad_query_in = rotate(grad_queries, cosine, -sine).astype(BF16)
    grad_key_in = rotate(grad_keys_mine, cosine, -sine).astype(BF16)
    grad_in = jnp.concatenate([grad_query_in, grad_key_in, grad_value_in], axis=1)
    grad_norm_one = dot(grad_in, qkv_weight, NT)
    grad_in_norm, grad_gain_first = norm_one_back(grad_norm_one)
    grad_inputs = grad_mid + grad_in_norm
    late = jnp.concatenate(
        [
            dot(norm_one, grad_in, TN).astype(BF16),
            jnp.zeros((width, 128), BF16)
            .at[:, 0]
            .set(grad_gain_first.astype(BF16))
            .at[:, 1]
            .set(grad_gain_second.astype(BF16)),
        ],
        axis=1,
    )
    (late_sum,) = scatter(8, "scatter_late", sizes, [late], [(row_halves, True)])
    return (
        mixed[None],
        grad_inputs[None],
        late_sum[:, :width],
        late_sum[:, width : 2 * width],
        late_sum[:, 2 * width : 3 * width],
        early_sum[:, :width],
        late_sum[:, 3 * width],
        early_sum[:, width : width + hidden_width],
        early_sum[:, width + hidden_width :],
        down_sum,
        late_sum[:, 3 * width + 1],
    )


def solution(mesh):
    rows, owned, feature = P("mem", "seq", None), P(None, "mem", None), P(("seq", "mem"), None)
    gain = P(("seq", "mem"))
    return jax.shard_map(
        functools.partial(per_device, dict(mesh.shape)),
        mesh=mesh,
        in_specs=(
            (rows, owned, owned, rows, P("mem"))
            + (feature,) * 4
            + (gain,)
            + (feature,) * 3
            + (gain, rows)
        ),
        out_specs=(rows, rows) + (feature,) * 4 + (gain,) + (feature,) * 3 + (gain,),
        check_vma=False,
    )
```

```python
import functools

import jax
import jax.numpy as jnp
from jax import lax
from jax.experimental import pallas as pl
from jax.experimental.pallas import tpu as pltpu
from jax.sharding import PartitionSpec as P

HEADS = 8
EPSILON = 1e-05
FLOOR = -1e30
LOW = -1e29
LOG2E = 1.4426950408889634
STATS = 16
PIECES = 4
ORDERS = {
    ("first", 4): (
        7, 0, 7, 8, 9, 1, 7, 8, 2, 10, 10, 3, 9, 11, 11, 12, 4, 10, 13, 12, 8, 13, 9, 11, 6, 5,
        13, 12,
    ),
    ("second", 4): (
        28, 29, 21, 36, 14, 36, 30, 7, 22, 0, 36, 23, 32, 31, 16, 15, 2, 9, 36, 34, 36, 1, 25, 36,
        17, 30, 33, 32, 8, 34, 4, 28, 36, 11, 27, 35, 3, 33, 36, 18, 29, 30, 35, 24, 19, 13, 34,
        26, 31, 12, 20, 33, 5, 32, 10, 6, 28, 29, 35, 31,
    ),
    ("third", 4): (
        4, 18, 6, 5, 18, 11, 1, 8, 6, 7, 25, 13, 12, 2, 25, 4, 3, 1, 25, 25, 10, 0, 10, 15, 10,
        19, 14, 0, 17, 20, 25, 7, 22, 25, 3, 14, 11, 12, 2, 16, 22, 8, 20, 7, 18, 16, 6, 21, 19,
        24, 4, 21, 17, 11, 13, 25, 15, 19, 17, 5, 22, 25, 24, 21, 9, 9, 13, 20, 12, 8, 5, 23, 9,
        23, 15, 24, 14, 16, 23,
    ),
    ("fourth", 4): (
        0, 7, 14, 21, 28, 35, 35, 1, 35, 2, 35, 8, 35, 9, 35, 15, 16, 35, 35, 22, 23, 29, 30, 3,
        4, 10, 11, 17, 18, 24, 25, 31, 32, 5, 6, 12, 13, 19, 20, 26, 27, 33, 34,
    ),
    ("fifth", 4): (
        4, 4, 2, 12, 8, 16, 8, 4, 12, 20, 20, 5, 0, 0, 8, 13, 21, 16, 13, 17, 20, 8, 16, 9, 5, 9,
        6, 10, 8, 12, 11, 4, 13, 10, 2, 9, 16, 1, 1, 21, 5, 14, 17, 18, 9, 12, 10, 4, 6, 5, 19,
        22, 21, 20, 13, 17, 22, 17, 16, 15, 3, 20, 10, 13, 19, 6, 22, 14, 19, 12, 5, 3, 14, 18,
        21, 15, 11, 23, 14, 9, 18, 10, 11, 17, 7, 15, 22, 7, 14, 15, 18, 21, 7, 6, 22, 11, 18, 23,
        15, 6, 7, 19, 23, 19, 7, 23, 23, 11,
    ),
    ("sixth", 4): (
        0, 0, 3, 2, 1, 0, 1, 0, 0, 1, 2, 1, 1, 2, 3, 2, 2, 3, 3, 3,
    ),
}
F32 = jnp.float32
BF16 = jnp.bfloat16
VMEM_LIMIT = 56 * 1024 * 1024
NT = (((1,), (1,)), ((), ()))
TN = (((0,), (0,)), ((), ()))


def dot(left, right, dims=(((1,), (0,)), ((), ()))):
    return lax.dot_general(left, right, dims, preferred_element_type=F32)


def angles_for(positions, head_width):
    exponent = jnp.arange(head_width // 2, dtype=F32) * (2.0 / head_width)
    frequency = jnp.power(10000.0, -exponent)
    turned = positions.astype(F32)[:, None] * frequency[None, :]
    return (jnp.cos(turned), jnp.sin(turned))


def params(**more):
    return pltpu.CompilerParams(vmem_limit_bytes=VMEM_LIMIT, **more)


def spread(columns, width=128):
    lanes = lax.broadcasted_iota(jnp.int32, (columns[0].shape[0], width), 1)
    result = jnp.zeros((columns[0].shape[0], width), F32)
    for place, column in enumerate(columns):
        result = jnp.where(lanes == place, column, result)
    return result


def columns_of(rows_by_stat):
    count, width = rows_by_stat.shape
    padded = jnp.concatenate([rows_by_stat, jnp.zeros((128 - count, width), F32)], axis=0)
    return padded.T


MESH = pl.DeviceIdType.MESH


class Net:
    def __init__(self, line):
        self.line = line
        self.s, self.m = lax.axis_index("seq"), lax.axis_index("mem")
        self.c, self.z = self.m % 2, self.m // 2
        self.x, self.y, self.core = (self.s ^ 1, self.m), (self.s ^ 2, self.m), (self.s, self.m ^ 1)
        self.right = (self.s, (self.m + 2) % (2 * line))
        self.left = (self.s, (self.m + 2 * line - 2) % (2 * line))

    def others(self):
        ring = 2 * self.line
        return [(self.s, lax.rem(self.m + 2 * k, ring)) for k in range(1, self.line)]

    def greet(self, others):
        barrier = pltpu.get_barrier_semaphore()
        for other in others:
            pl.semaphore_signal(barrier, inc=1, device_id=other, device_id_type=MESH)
        pl.semaphore_wait(barrier, len(others))


def remote(src, dst, sends, recvs, place, device):
    return pltpu.make_async_remote_copy(
        src_ref=src,
        dst_ref=dst,
        send_sem=sends.at[place],
        recv_sem=recvs.at[place],
        device_id=device,
        device_id_type=MESH,
    )


def row_halves(ref, part):
    half = ref.shape[-2] // 2
    return ref.at[pl.ds(part * half, half)]


def column_halves(ref, part):
    half = ref.shape[-1] // 2
    return ref.at[:, pl.ds(part * half, half)]


class Gather:
    def __init__(self, net, src, out, sends, recvs, own, index, halves, line=True, square=True, core=True):
        self.net, self.src, self.out, self.sends, self.recvs, self.own = net, src, out, sends, recvs, own
        self.index, self.halves = index, halves
        self.line, self.square, self.core = line, square, core

    def slot(self, s, z):
        return self.out.at[self.index(s, z, self.net.c)]

    def send(self, block, target, place, device):
        copy = remote(block, target, self.sends, self.recvs, place, device)
        copy.start()

    def sent(self, block, place):
        remote(block, block, self.sends, self.recvs, place, self.net.core).wait_send()

    def arrived(self, block, place):
        remote(block, block, self.sends, self.recvs, place, self.net.core).wait_recv()

    def places(self):
        z = self.net.line
        right, left, square, core = 0, z, 2 * z, 8 * z
        return right, left, square, core

    def chain(self, k, from_left):
        net = self.net
        z = net.z - k if from_left else net.z + k
        present = z >= 0 if from_left else z < net.line
        for stage in (self.have, self.pass_square, self.end_square) if self.square else (self.have,):
            if k == 0:
                stage(0, net.z, None)
            else:
                pl.when(present)(lambda stage=stage: stage(k, z, from_left))
            yield

    def chains(self):
        chains = [self.chain(0, True)]
        for k in range(1, self.net.line if self.line else 1):
            chains += [self.chain(k, True), self.chain(k, False)]
        return chains

    def have(self, k, z, from_left):
        net = self.net
        right, left, square, core = self.places()
        target = self.slot(net.s, z)
        block = self.src if k == 0 else target
        if k == 0:
            pltpu.make_async_copy(self.src, target, self.own).start()
        else:
            self.arrived(target, (right if from_left else left) + z)
        if self.line:
            if from_left is not False:
                pl.when(net.z < net.line - 1)(lambda: self.send(block, target, right + z, net.right))
            if from_left is not True:
                pl.when(net.z > 0)(lambda: self.send(block, target, left + z, net.left))
        if self.square:
            for kind, part, device in ((0, 0, net.x), (2, 1, net.y), (1, 0, net.y), (3, 1, net.x)):
                self.send(
                    self.halves(block, part),
                    self.halves(target, part),
                    square + kind * net.line + z,
                    device,
                )
        if self.core:
            self.send(block, target, core + z, net.core)

    def pass_square(self, k, z, from_left):
        net = self.net
        _, _, square, core = self.places()
        for kind, part, other, then, device, mirror in (
            (0, 0, net.s ^ 1, 4, net.y, 1),
            (2, 1, net.s ^ 2, 5, net.x, 2),
        ):
            block = self.halves(self.slot(other, z), part)
            self.arrived(block, square + kind * net.line + z)
            self.send(block, block, square + then * net.line + z, device)
            if self.core:
                self.send(block, block, core + mirror * net.line + z, net.core)

    def end_square(self, k, z, from_left):
        net = self.net
        _, _, square, core = self.places()
        for kind, part, other, mirror in self.last(net):
            block = self.halves(self.slot(other, z), part)
            self.arrived(block, square + kind * net.line + z)
            if self.core:
                self.send(block, block, core + mirror * net.line + z, net.core)

    def last(self, net):
        return (
            (1, 0, net.s ^ 2, 3),
            (3, 1, net.s ^ 1, 5),
            (4, 0, net.s ^ 3, 4),
            (5, 1, net.s ^ 3, 6),
        )

    def finish(self):
        net = self.net
        right, left, square, core = self.places()
        own = self.slot(net.s, net.z)
        pltpu.make_async_copy(self.src, own, self.own).wait()
        if self.core:
            for z in range(net.line if self.line else 1):
                z = z if self.line else net.z
                for mirror, part, other in (
                    (0, None, net.s),
                    (1, 0, net.s ^ 1),
                    (2, 1, net.s ^ 2),
                    (3, 0, net.s ^ 2),
                    (4, 0, net.s ^ 3),
                    (5, 1, net.s ^ 1),
                    (6, 1, net.s ^ 3),
                ):
                    if part is not None and not self.square:
                        continue
                    block = self.out.at[self.index(other, z, 1 - net.c)]
                    block = block if part is None else self.halves(block, part)
                    self.arrived(block, core + mirror * net.line + z)
                    self.sent(block, core + mirror * net.line + z)
        if self.square:
            half = [self.halves(own, 0), self.halves(own, 1)]
            for z in range(net.line if self.line else 1):
                z = z if self.line else net.z
                for kind, part in ((0, 0), (1, 0), (2, 1), (3, 1), (4, 0), (5, 1)):
                    self.sent(half[part], square + kind * net.line + z)
        if self.line:
            for z in range(net.line):
                pl.when((z <= net.z) & (net.z < net.line - 1))(lambda z=z: self.sent(own, right + z))
                pl.when((z >= net.z) & (net.z > 0))(lambda z=z: self.sent(own, left + z))


class Job:
    def __init__(self, arrays, outs, scratch, steps, where=pl.ANY, out_where=pl.ANY):
        self.arrays, self.outs, self.scratch, self.steps = arrays, outs, scratch, steps
        self.where, self.out_where = where, out_where


def together_kernel(line, jobs, order, *refs):
    refs = list(refs)
    take = lambda count: [refs.pop(0) for _ in range(count)]
    ins = [take(len(job.arrays)) for job in jobs]
    outs = [take(len(job.outs)) for job in jobs]
    scratch = [take(len(job.scratch)) for job in jobs]
    net = Net(line)
    net.greet([net.x, net.y, net.core] + net.others())
    chains, ends = [], []
    for job, *parts in zip(jobs, ins, outs, scratch):
        more, last = job.steps(net, *parts)
        chains += more
        ends += last
    for turn in order:
        next(chains[turn], None)
    while chains:
        chains = [chain for chain in chains if next(chain, True) is None]
    for end in ends:
        end()


def together(collective_id, name, sizes, jobs):
    line = sizes["mem"] // 2
    moved = sum(2 * a.size * a.dtype.itemsize for job in jobs for a in job.arrays)
    results = pl.pallas_call(
        functools.partial(together_kernel, line, jobs, ORDERS.get((name, line), ())),
        out_shape=[out for job in jobs for out in job.outs],
        in_specs=[pl.BlockSpec(memory_space=job.where) for job in jobs for _ in job.arrays],
        out_specs=[pl.BlockSpec(memory_space=job.out_where) for job in jobs for _ in job.outs],
        scratch_shapes=[s for job in jobs for s in job.scratch],
        compiler_params=params(collective_id=collective_id, has_side_effects=True),
        cost_estimate=pl.CostEstimate(flops=0, bytes_accessed=moved, transcendentals=0),
        name=name,
    )(*[a for job in jobs for a in job.arrays])
    results = list(results)
    return [[results.pop(0) for _ in job.outs] for job in jobs]


def gather_job(sizes, array, halves, reach, pieces=1):
    line = sizes["mem"] // 2
    slots = {"all": sizes["seq"] * sizes["mem"], "line": sizes["mem"], "square": sizes["seq"]}[reach]
    index = {
        "all": lambda s, z, c: (s * line + z) * 2 + c,
        "line": lambda s, z, c: z * 2 + c,
        "square": lambda s, z, c: s,
    }[reach]
    rows = array.shape[0] // pieces

    def steps(net, ins, outs, scratch):
        parts = []
        for i in range(pieces):
            span = pl.ds(i * rows, rows)
            src, out = (ins[0], outs[0]) if pieces == 1 else (ins[0].at[span], outs[0].at[:, span])
            parts.append(
                Gather(
                    net, src, out, *scratch[3 * i : 3 * i + 3], index, halves,
                    line=reach != "square", square=reach != "line", core=reach != "square",
                )
            )
        return [chain for part in parts for chain in part.chains()], [part.finish for part in parts]

    semaphores = [pltpu.SemaphoreType.DMA((15 * line,))] * 2 + [pltpu.SemaphoreType.DMA]
    out = jax.ShapeDtypeStruct((slots,) + array.shape, array.dtype)
    return Job([array], [out], semaphores * pieces, steps)


class Scatter:
    def __init__(self, net, src, out, buffers, sems, halves, whole=True):
        self.net, self.src, self.out, self.halves = net, src, out, halves
        self.whole, self.count = whole, src.shape[1]
        self.held, self.twin, self.first, self.second, self.along = buffers
        self.sends, self.recvs, self.own = sems

    def send(self, block, target, place, device):
        remote(block, target, self.sends, self.recvs, place, device).start()

    def sent(self, block, place):
        remote(block, block, self.sends, self.recvs, place, self.net.core).wait_send()

    def arrived(self, block, place):
        remote(block, block, self.sends, self.recvs, place, self.net.core).wait_recv()

    def places(self):
        z = self.count
        return 0, 4 * z, 8 * z, 10 * z, 11 * z

    def loading(self, d):
        source = self.src.at[:, d, self.net.c] if self.whole else self.src.at[:, d]
        return pltpu.make_async_copy(source, self.held.at[:, d], self.own.at[d])

    def load(self, d):
        net = self.net
        self.loading(d).start()
        for s in range(4 if self.whole else 0):
            self.send(self.src.at[s, d, 1 - net.c], self.twin.at[s, d], s * self.count + d, net.core)

    def add_core(self, d):
        net = self.net
        _, first, _, _, _ = self.places()
        self.loading(d).wait()
        for turn in (3, 2, 1, 0):
            s = net.s ^ turn
            if self.whole:
                self.arrived(self.twin.at[s, d], s * self.count + d)
                self.held[s, d] = self.held[s, d] + self.twin[s, d]
            for part, device, slot, kind in {
                3: ((0, net.y, 1, 1), (1, net.x, 1, 3)),
                2: ((0, net.y, 0, 0),),
                1: ((1, net.x, 0, 2),),
                0: (),
            }[turn]:
                self.send(
                    self.halves(self.held.at[s, d], part),
                    self.first.at[part, slot, d],
                    first + kind * self.count + d,
                    device,
                )

    def chain(self, k):
        d = lax.rem(self.net.z + k, self.net.line) if self.whole else k
        for stage in (self.load, self.add_core, self.add_first, self.add_second, self.line_step):
            stage(d)
            yield

    def add(self, block, other):
        block[...] = block[...] + other[...]

    def add_first(self, d):
        net = self.net
        _, first, second, _, _ = self.places()
        for part, slot, kind, turn in ((0, 1, 1, 1), (1, 1, 3, 2), (0, 0, 0, 0), (1, 0, 2, 0)):
            got = self.first.at[part, slot, d]
            self.arrived(got, first + kind * self.count + d)
            block = self.halves(self.held.at[net.s ^ turn, d], part)
            self.add(block, got)
            if turn:
                device = net.x if part == 0 else net.y
                self.send(block, self.second.at[part, d], second + part * self.count + d, device)

    def add_second(self, d):
        net = self.net
        _, _, second, _, _ = self.places()
        for part in range(2):
            self.arrived(self.second.at[part, d], second + part * self.count + d)
            self.add(self.halves(self.held.at[net.s, d], part), self.second.at[part, d])

    def line_step(self, d):
        net = self.net
        _, _, _, right, left = self.places()
        block = self.held.at[net.s, d]
        if not self.whole:
            self.out[d] = block[...].astype(self.out.dtype)
            return

        def go():
            pltpu.make_async_remote_copy(
                src_ref=block,
                dst_ref=self.along.at[net.z],
                send_sem=self.sends.at[right + d],
                recv_sem=self.recvs.at[left + net.z],
                device_id=(net.s, 2 * d + net.c),
                device_id_type=MESH,
            ).start()

        pl.when(net.z != d)(go)

    def keep(self):
        net = self.net
        _, _, _, _, left = self.places()
        total = self.held[net.s, net.z].astype(F32)
        for k in range(1, net.line):
            z = lax.rem(net.z + k, net.line)
            self.arrived(self.along.at[z], left + z)
            total = total + self.along[z].astype(F32)
        self.out[...] = total

    def finish(self):
        net = self.net
        _, first, second, right, left = self.places()
        full = self.held.at[net.s, 0]
        if self.whole:
            self.keep()
        for d in range(self.count):
            for s in range(4 if self.whole else 0):
                self.sent(full, s * self.count + d)
            for kind, part in enumerate((0, 0, 1, 1)):
                self.sent(self.halves(full, part), first + kind * self.count + d)
            for part in range(2):
                self.sent(self.halves(full, part), second + part * self.count + d)
            if self.whole:
                pl.when(net.z != d)(lambda d=d: self.sent(full, right + d))


def far_first(count):
    return sorted(range(count), key=lambda k: (k == 0, -min(k, count - k)))


def scatter_job(sizes, array, halves, whole=True):
    square, line = sizes["seq"], sizes["mem"] // 2
    columns = array.shape[1]
    if whole:
        count, rows = line, array.shape[0] // (2 * square * line)
        array = array.reshape(square, line, 2, rows, columns)
        out = jax.ShapeDtypeStruct((rows, columns), F32)
    else:
        count, rows = PIECES, array.shape[0] // (square * PIECES)
        array = array.reshape(square, count, rows, columns)
        out = jax.ShapeDtypeStruct((count, rows, columns), F32)
    half = (rows // 2, columns) if halves is row_halves else (rows, columns // 2)
    block, unused = (rows, columns), (16, 128)
    scratch = [
        pltpu.VMEM((4, count) + block, BF16),
        pltpu.VMEM((4, count) + block if whole else unused, BF16),
        pltpu.VMEM((2, 2, count) + half, BF16),
        pltpu.VMEM((2, count) + half, BF16),
        pltpu.VMEM((count,) + block if whole else unused, BF16),
        pltpu.SemaphoreType.DMA((12 * count,)),
        pltpu.SemaphoreType.DMA((12 * count,)),
        pltpu.SemaphoreType.DMA((count,)),
    ]

    def steps(net, ins, outs, scratch):
        scatter = Scatter(net, ins[0], outs[0], scratch[:5], scratch[5:], halves, whole)
        return [scatter.chain(k) for k in far_first(count)], [scatter.finish]

    return Job([array], [out], scratch, steps, out_where=pltpu.VMEM)


class Return:
    def __init__(self, net, sources, outs, scratch):
        kinds = len(sources)
        self.net, self.sources, self.outs, self.kinds = net, sources, outs, range(kinds)
        self.held, self.twin = scratch[:kinds], scratch[kinds : 2 * kinds]
        self.own, self.twin_sends, self.twin_recvs, self.sends, self.recvs = scratch[2 * kinds :]

    def loading(self, i, d):
        source = self.sources[i].at[d, self.net.c]
        return pltpu.make_async_copy(source, self.held[i].at[d], self.own.at[i, d])

    def pairing(self, i, d):
        net = self.net
        return remote(
            self.sources[i].at[d, 1 - net.c],
            self.twin[i].at[d],
            self.twin_sends.at[i],
            self.twin_recvs.at[i],
            d,
            net.core,
        )

    def giving(self, i, k, d, slot, device):
        return pltpu.make_async_remote_copy(
            src_ref=self.held[i].at[d],
            dst_ref=self.outs[i].at[slot],
            send_sem=self.sends.at[i, k],
            recv_sem=self.recvs.at[i, slot],
            device_id=device,
            device_id_type=MESH,
        )

    def keeping(self, i, d):
        return pltpu.make_async_copy(
            self.held[i].at[d], self.outs[i].at[self.net.z], self.own.at[i, d]
        )

    def chain(self, k):
        net = self.net
        d = lax.rem(net.z + k, net.line)
        for i in self.kinds:
            self.loading(i, d).start()
            self.pairing(i, d).start()
        yield
        for i in self.kinds:
            self.loading(i, d).wait()
            self.pairing(i, d).wait_recv()
        self.merge(d)
        for i in self.kinds:
            if k:
                self.giving(i, k, d, net.z, (net.s, 2 * d + net.c)).start()
            else:
                self.keeping(i, d).start()
        yield

    def merge(self, d):
        held, twin = self.held, self.twin
        if len(held) == 1:
            held[0][d] = held[0][d] + twin[0][d]
            return
        mine, theirs = held[1][d], twin[1][d]
        top = jnp.maximum(mine[:HEADS], theirs[:HEADS])
        shares = [jnp.exp2(mine[:HEADS] - top), jnp.exp2(theirs[:HEADS] - top)]
        held[1][d] = jnp.concatenate(
            [top, mine[HEADS:] * shares[0] + theirs[HEADS:] * shares[1]], axis=0
        )
        shares = columns_of(jnp.concatenate(shares, axis=0))
        for h in range(HEADS):
            span = slice(h * 128, (h + 1) * 128)
            held[0][d, :, span] = (
                held[0][d, :, span].astype(F32) * shares[:, h : h + 1]
                + twin[0][d, :, span].astype(F32) * shares[:, HEADS + h : HEADS + h + 1]
            ).astype(BF16)

    def finish(self):
        net = self.net
        for k in range(net.line):
            d = lax.rem(net.z + k, net.line)
            for i in self.kinds:
                self.pairing(i, d).wait_send()
                if k:
                    copy = self.giving(i, k, d, d, net.core)
                    copy.wait_recv()
                    copy.wait_send()
                else:
                    self.keeping(i, d).wait()


def return_job(sizes, arrays):
    line, kinds = sizes["mem"] // 2, len(arrays)
    blocks = [a.reshape((line, 2) + a.shape[1:]) for a in arrays]
    slots = [pltpu.VMEM((line,) + a.shape[1:], a.dtype) for a in arrays]
    outs = [jax.ShapeDtypeStruct((line,) + a.shape[1:], a.dtype) for a in arrays]
    scratch = slots + slots + [pltpu.SemaphoreType.DMA((kinds, line))] * 5
    def steps(net, ins, outs, scratch):
        back = Return(net, ins, outs, scratch)
        return [back.chain(k) for k in (*range(1, line), 0)], [back.finish]

    return Job(blocks, outs, scratch, steps)


def mask_words(index, base, mem_dev, place_ref, bit_ref):
    relative = index - base
    inside = (relative >= 0) & (relative < mem_dev)
    place = jnp.where(inside, relative & 127, 0)
    bit = jnp.where(inside, lax.shift_left(jnp.ones_like(relative), relative >> 7), 0)
    place_ref[...] = place.T
    bit_ref[...] = bit.T
    sought = lax.broadcasted_iota(jnp.int32, (128, 128), 0)
    halves = []
    for start in range(0, index.shape[0], 128):

        def eight(g, words, start=start):
            group = pl.ds(pl.multiple_of(g * 8, 8), 8)
            places = place_ref[group, start : start + 128]
            bits = bit_ref[group, start : start + 128]
            for j in range(8):
                words = words | jnp.where(places[j : j + 1] == sought, bits[j : j + 1], 0)
            return words

        none = jnp.zeros((128, 128), jnp.int32)
        words = lax.fori_loop(0, index.shape[1] // 8, eight, none)
        halves.append(words.T)
    return jnp.concatenate(halves, axis=0)


def mask_scratch(rows, count):
    return [pltpu.VMEM((count, rows), jnp.int32), pltpu.VMEM((count, rows), jnp.int32)]


def mask_kernel(mem_dev, base_ref, index_ref, bits_ref, place_ref, bit_ref):
    bits_ref[0] = mask_words(index_ref[0], base_ref[0], mem_dev, place_ref, bit_ref)


def mask_bits(base, all_index, mem_dev):
    segments, rows, count = all_index.shape
    return pl.pallas_call(
        functools.partial(mask_kernel, mem_dev),
        grid_spec=pltpu.PrefetchScalarGridSpec(
            num_scalar_prefetch=1,
            grid=(segments,),
            in_specs=[pl.BlockSpec((1, rows, count), lambda g, b: (g, 0, 0))],
            out_specs=pl.BlockSpec((1, rows, 128), lambda g, b: (g, 0, 0)),
            scratch_shapes=mask_scratch(rows, count),
        ),
        out_shape=jax.ShapeDtypeStruct((segments, rows, 128), jnp.int32),
        compiler_params=params(),
        name="mask_bits",
    )(base, all_index)


def mask_job(all_index, mem_dev):
    segments, rows, count = all_index.shape

    def steps(net, ins, outs, scratch):
        def chain():
            for g in range(segments):
                outs[0][g] = mask_words(ins[0][g], net.m * mem_dev, mem_dev, *scratch)
                yield

        return [chain()], []

    out = jax.ShapeDtypeStruct((segments, rows, 128), jnp.int32)
    return Job([all_index], [out], mask_scratch(rows, count), steps, pltpu.VMEM, pltpu.VMEM)


def fill_bias(bits_ref, bias_ref):
    bits = bits_ref[0]
    for b in range(bias_ref.shape[1] // 128):
        bias_ref[:, b * 128 : (b + 1) * 128] = jnp.where(((bits >> b) & 1) != 0, 0.0, FLOOR)


def owner_forward_kernel(scale, order_ref, q_ref, bits_ref, k_ref, v_ref, o_ref, st_ref, bias_ref):
    del order_ref
    fill_bias(bits_ref, bias_ref)
    maxima, sums = [], []
    for h in range(HEADS):
        span = slice(h * 128, (h + 1) * 128)
        scores = dot(q_ref[0, :, span], k_ref[0, :, span], NT) * scale + bias_ref[...]
        top = jnp.maximum(jnp.max(scores, axis=1, keepdims=True), LOW)
        weights = jnp.exp2(scores - top)
        maxima.append(top)
        sums.append(jnp.sum(weights, axis=1, keepdims=True))
        o_ref[0, :, span] = dot(weights.astype(BF16), v_ref[0, :, span]).astype(BF16)
    st_ref[0] = spread(maxima + sums).T[:STATS]


def owner_forward(order, queries, bits, cached_keys, cached_values, scale):
    segments, rows, width = queries.shape
    mem_dev = cached_keys.shape[1]
    active = order.shape[0]
    picked = lambda a, o: (o[a], 0, 0)
    return pl.pallas_call(
        functools.partial(owner_forward_kernel, scale),
        grid_spec=pltpu.PrefetchScalarGridSpec(
            num_scalar_prefetch=1,
            grid=(active,),
            in_specs=[
                pl.BlockSpec((1, rows, width), picked),
                pl.BlockSpec((1, rows, 128), picked),
                pl.BlockSpec((1, mem_dev, width), picked),
                pl.BlockSpec((1, mem_dev, width), picked),
            ],
            out_specs=[
                pl.BlockSpec((1, rows, width), picked),
                pl.BlockSpec((1, STATS, rows), picked),
            ],
            scratch_shapes=[pltpu.VMEM((rows, mem_dev), F32)],
        ),
        out_shape=[
            jax.ShapeDtypeStruct((segments, rows, width), BF16),
            jax.ShapeDtypeStruct((segments, STATS, rows), F32),
        ],
        compiler_params=params(),
        name="owner_forward",
    )(order, queries, bits, cached_keys, cached_values)


def owner_backward_kernel(
    scale, order_ref, q_ref, g_ref, st_ref, bits_ref, k_ref, v_ref, dq_ref, bias_ref
):
    del order_ref
    fill_bias(bits_ref, bias_ref)
    stats = columns_of(st_ref[0])
    for h in range(HEADS):
        span = slice(h * 128, (h + 1) * 128)
        scores = dot(q_ref[0, :, span], k_ref[0, :, span], NT) * scale + bias_ref[...]
        weights = jnp.exp2(scores - stats[:, h : h + 1])
        dweights = dot(g_ref[0, :, span], v_ref[0, :, span], NT)
        dscore = weights * (dweights - stats[:, HEADS + h : HEADS + h + 1])
        dq_ref[0, :, span] = (
            dot(dscore.astype(BF16), k_ref[0, :, span]) * (scale / LOG2E)
        ).astype(BF16)


def owner_backward(order, queries, grads, stats, bits, cached_keys, cached_values, scale):
    segments, rows, width = queries.shape
    mem_dev = cached_keys.shape[1]
    active = order.shape[0]
    picked = lambda a, o: (o[a], 0, 0)
    return pl.pallas_call(
        functools.partial(owner_backward_kernel, scale),
        grid_spec=pltpu.PrefetchScalarGridSpec(
            num_scalar_prefetch=1,
            grid=(active,),
            in_specs=[
                pl.BlockSpec((1, rows, width), picked),
                pl.BlockSpec((1, rows, width), picked),
                pl.BlockSpec((1, STATS, rows), picked),
                pl.BlockSpec((1, rows, 128), picked),
                pl.BlockSpec((1, mem_dev, width), picked),
                pl.BlockSpec((1, mem_dev, width), picked),
            ],
            out_specs=pl.BlockSpec((1, rows, width), picked),
            scratch_shapes=[pltpu.VMEM((rows, mem_dev), F32)],
        ),
        out_shape=jax.ShapeDtypeStruct((segments, rows, width), BF16),
        compiler_params=params(),
        name="owner_backward",
    )(order, queries, grads, stats, bits, cached_keys, cached_values)


def causal_bias(place, rows, keys):
    row = place * rows + lax.broadcasted_iota(jnp.int32, (rows, keys), 0)
    return jnp.where(lax.broadcasted_iota(jnp.int32, (rows, keys), 1) <= row, 0.0, FLOOR)


def local_forward_steps(scale, place, q_ref, kv_ref, o_ref, st_ref, bias_ref):
    rows, width = q_ref.shape
    bias_ref[...] = causal_bias(place, rows, kv_ref.shape[0])
    maxima, sums = [], []
    for h in range(HEADS):
        span, over = slice(h * 128, (h + 1) * 128), slice(width + h * 128, width + (h + 1) * 128)
        scores = dot(q_ref[:, span], kv_ref[:, span], NT) * scale + bias_ref[...]
        top = jnp.max(scores, axis=1, keepdims=True)
        weights = jnp.exp2(scores - top)
        maxima.append(top)
        sums.append(jnp.sum(weights, axis=1, keepdims=True))
        o_ref[:, span] = dot(weights.astype(BF16), kv_ref[:, over])
        yield
    st_ref[...] = spread(maxima + sums).T[:STATS]


def local_backward_steps(
    scale, place, q_ref, g_ref, st_ref, kv_ref, dq_ref, dkv_ref, bias_ref
):
    rows, width = q_ref.shape
    bias_ref[...] = causal_bias(place, rows, kv_ref.shape[0])
    stats = columns_of(st_ref[...])
    for h in range(HEADS):
        span, over = slice(h * 128, (h + 1) * 128), slice(width + h * 128, width + (h + 1) * 128)
        query, key, grad = q_ref[:, span], kv_ref[:, span], g_ref[:, span]
        scores = dot(query, key, NT) * scale + bias_ref[...]
        weights = jnp.exp2(scores - stats[:, h : h + 1])
        dweights = dot(grad, kv_ref[:, over], NT)
        dscore = (weights * (dweights - stats[:, HEADS + h : HEADS + h + 1])).astype(BF16)
        dq_ref[:, span] = dot(dscore, key) * (scale / LOG2E)
        dkv_ref[:, span] = (dot(dscore, query, TN) * (scale / LOG2E)).astype(BF16)
        dkv_ref[:, over] = dot(weights.astype(BF16), grad, TN).astype(BF16)
        yield


def local_job(kind, arrays, scale):
    rows, width = arrays[0].shape
    length = arrays[-1].shape[0]
    if kind == "forward":
        body, extra = local_forward_steps, jax.ShapeDtypeStruct((STATS, rows), F32)
    else:
        body, extra = local_backward_steps, jax.ShapeDtypeStruct((length, 2 * width), BF16)

    def steps(net, ins, outs, scratch):
        return [body(scale, net.s, *ins, *outs, *scratch)], []

    outs = [jax.ShapeDtypeStruct((rows, width), F32), extra]
    return Job(arrays, outs, [pltpu.VMEM((rows, length), F32)], steps, pltpu.VMEM, pltpu.VMEM)


def alone_kernel(job, *refs):
    place_ref, *refs = refs
    net = type("Alone", (), {"s": place_ref[0]})
    ins, outs = len(job.arrays), len(job.arrays) + len(job.outs)
    for chain in job.steps(net, refs[:ins], refs[ins:outs], refs[outs:])[0]:
        for _ in chain:
            pass


def alone(name, place, job):
    return pl.pallas_call(
        functools.partial(alone_kernel, job),
        out_shape=job.outs,
        in_specs=[pl.BlockSpec(memory_space=pltpu.SMEM)]
        + [pl.BlockSpec(memory_space=pltpu.VMEM)] * len(job.arrays),
        out_specs=[pl.BlockSpec(memory_space=pltpu.VMEM)] * len(job.outs),
        scratch_shapes=job.scratch,
        compiler_params=params(),
        name=name,
    )(place, *job.arrays)


def copy_in(pairs, sems):
    copies = [pltpu.make_async_copy(src, dst, sems.at[i]) for i, (src, dst) in enumerate(pairs)]
    for copy in copies:
        copy.start()
    return copies


def turn(values, cosine, sine):
    return values * cosine + pltpu.roll(values, values.shape[1] // 2, 1) * sine


def inverse_root(values):
    return lax.rsqrt(jnp.mean(values * values, axis=1, keepdims=True) + EPSILON)


def project_kernel(x_ref, w_any, cos_ref, sin_ref, n_ref, q_ref, kv_ref, gain_ref, w_ref, sems):
    width = x_ref.shape[1]
    spans = [slice(i * width, (i + 1) * width) for i in range(3)] + [slice(3 * width, 3 * width + 128)]
    copies = copy_in([(w_any.at[:, s], w_ref.at[:, s]) for s in spans], sems)
    x = x_ref[...].astype(F32)
    copies[3].wait()
    gain_ref[...] = w_ref[:, spans[3]].astype(F32).T[:8]
    normed = (x * inverse_root(x) * gain_ref[:1]).astype(BF16)
    n_ref[...] = normed
    cosine, sine = cos_ref[...], sin_ref[...]
    for i in range(3):
        copies[i].wait()
        product = dot(normed, w_ref[:, spans[i]])
        for h in range(HEADS):
            span = slice(h * 128, (h + 1) * 128)
            part = product[:, span]
            part = part if i == 2 else turn(part, cosine, sine)
            if i == 0:
                q_ref[:, span] = part.astype(BF16)
            else:
                over = slice((i - 1) * width + h * 128, (i - 1) * width + (h + 1) * 128)
                kv_ref[:, over] = part.astype(BF16)


def in_vmem(count):
    return [pl.BlockSpec(memory_space=pltpu.VMEM)] * count


def project(tokens, first_weights, cosine, sine):
    rows, width = tokens.shape
    columns = first_weights.shape[1]
    return pl.pallas_call(
        project_kernel,
        out_shape=[
            jax.ShapeDtypeStruct((rows, width), BF16),
            jax.ShapeDtypeStruct((rows, width), BF16),
            jax.ShapeDtypeStruct((rows, 2 * width), BF16),
            jax.ShapeDtypeStruct((8, width), F32),
        ],
        in_specs=in_vmem(1) + [pl.BlockSpec(memory_space=pl.ANY)] + in_vmem(2),
        out_specs=in_vmem(4),
        scratch_shapes=[
            pltpu.VMEM((width, columns), BF16),
            pltpu.SemaphoreType.DMA((4,)),
        ],
        compiler_params=params(),
        name="project",
    )(tokens, first_weights, cosine, sine)


def middle_kernel(
    live_ref, x_ref, g_ref, gain_ref, lo_ref, ls_ref, po_ref, ps_ref, out_any, gate_any, up_any, down_any,
    mixed_ref, gm_ref, al_ref, n_ref, gml_ref, ga_ref, st_ref, hid_ref, gg_ref, gu_ref, gain_grad_ref,
    att_ref, acc_ref, gn_ref, out_ref, gate_ref, up_ref, down_ref, sems,
):
    rows, width = x_ref.shape
    copies = copy_in(
        [(out_any, out_ref), (gate_any, gate_ref), (up_any, up_ref), (down_any, down_ref)], sems
    )
    live = live_ref[0] > 0
    peers = ps_ref.shape[0]
    local_max, local_sum = ls_ref[:HEADS], ls_ref[HEADS:]
    peer_max = [jnp.where(live, ps_ref[p, :HEADS], LOW) for p in range(peers)]
    peer_sum = [jnp.where(live, ps_ref[p, HEADS:], 0.0) for p in range(peers)]
    top = functools.reduce(jnp.maximum, peer_max, local_max)
    shares = [jnp.exp2(m - top) for m in [local_max] + peer_max]
    total = functools.reduce(
        jnp.add, [s * t for s, t in zip(shares, [local_sum] + peer_sum)]
    )
    log_total = top + jnp.log2(total)
    shares = columns_of(jnp.concatenate([s / total for s in shares], axis=0))
    for h in range(HEADS):
        span = slice(h * 128, (h + 1) * 128)
        part = lo_ref[:, span] * shares[:, h : h + 1]
        for p in range(peers):
            column = shares[:, (p + 1) * HEADS + h : (p + 1) * HEADS + h + 1]
            part += jnp.where(live, po_ref[p, :, span].astype(F32), 0.0) * column
        att_ref[:, span] = part
    attention_low = att_ref[...].astype(BF16)
    al_ref[...] = attention_low
    copies[0].wait()
    mid = x_ref[...].astype(F32) + dot(attention_low, out_ref[...])
    gm_ref[...] = mid
    root = inverse_root(mid)
    n_ref[...] = (mid * root * gain_ref[1:2]).astype(BF16)
    for copy in copies[1:]:
        copy.wait()
    grad = g_ref[...]
    acc_ref[...] = jnp.zeros_like(acc_ref)
    gn_ref[...] = jnp.zeros_like(gn_ref)
    hidden_width = gate_ref.shape[1]
    step = 256
    for start in range(0, hidden_width, step):
        span = slice(start, min(start + step, hidden_width))
        norm_two = n_ref[...]
        gate = dot(norm_two, gate_ref[:, span])
        upward = dot(norm_two, up_ref[:, span])
        grad_hidden = dot(grad, down_ref[span, :], NT)
        sigmoid = 1.0 / (1.0 + jnp.exp(-gate))
        silu = gate * sigmoid
        hidden = (silu * upward).astype(BF16)
        grad_gate = (grad_hidden * upward * (sigmoid * (1.0 + gate * (1.0 - sigmoid)))).astype(BF16)
        grad_up = (grad_hidden * silu).astype(BF16)
        hid_ref[:, span] = hidden
        gg_ref[:, span] = grad_gate
        gu_ref[:, span] = grad_up
        acc_ref[...] += dot(hidden, down_ref[span, :])
        gn_ref[...] += dot(grad_gate, gate_ref[:, span], NT) + dot(grad_up, up_ref[:, span], NT)
    mid = gm_ref[...]
    mixed_ref[...] = mid + acc_ref[...]
    normed = mid * root
    grad_norm = gn_ref[...]
    gain_grad_ref[...] = jnp.broadcast_to(
        jnp.sum(grad_norm * normed, axis=0, keepdims=True), gain_grad_ref.shape
    )
    scaled = grad_norm * gain_ref[1:2]
    grad_mid = grad.astype(F32) + root * (
        scaled - normed * jnp.mean(normed * scaled, axis=1, keepdims=True)
    )
    gm_ref[...] = grad_mid
    grad_mid_low = grad_mid.astype(BF16)
    gml_ref[...] = grad_mid_low
    grad_attention = dot(grad_mid_low, out_ref[...], NT).astype(BF16)
    ga_ref[...] = grad_attention
    products = grad_attention.astype(F32) * att_ref[...]
    dots = [
        jnp.sum(products[:, h * 128 : (h + 1) * 128], axis=1, keepdims=True) for h in range(HEADS)
    ]
    st_ref[...] = jnp.concatenate([log_total, spread(dots).T[:HEADS]], axis=0)


def middle(live, tokens, grads, gains, local, peers, weights):
    rows, width = tokens.shape
    hidden_width = weights[1].shape[1]
    full = lambda columns, kind: jax.ShapeDtypeStruct((rows, columns), kind)
    return pl.pallas_call(
        middle_kernel,
        out_shape=[
            full(width, F32),
            full(width, F32),
            full(width, BF16),
            full(width, BF16),
            full(width, BF16),
            full(width, BF16),
            jax.ShapeDtypeStruct((STATS, rows), F32),
            full(hidden_width, BF16),
            full(hidden_width, BF16),
            full(hidden_width, BF16),
            jax.ShapeDtypeStruct((8, width), F32),
        ],
        in_specs=[pl.BlockSpec(memory_space=pltpu.SMEM)]
        + in_vmem(7)
        + [pl.BlockSpec(memory_space=pl.ANY)] * 4,
        out_specs=in_vmem(11),
        scratch_shapes=[pltpu.VMEM((rows, width), F32)] * 3
        + [pltpu.VMEM(w.shape, BF16) for w in weights]
        + [pltpu.SemaphoreType.DMA((4,))],
        compiler_params=params(),
        name="middle",
    )(live, tokens, grads, gains, *local, *peers, *weights)


def final_kernel(
    live_ref, x_ref, gm_ref, gain_ref, ggain_ref, n_ref, dq_ref, pd_ref, dkv_ref, cos_ref, sin_ref, w_any,
    gx_ref, late_ref, in_ref, w_ref, sems,
):
    rows, width = x_ref.shape
    copies = copy_in([(w_any.at[:, : 3 * width], w_ref)], sems)
    live = live_ref[0] > 0
    cosine, sine = cos_ref[...], -sin_ref[...]
    for h in range(HEADS):
        span = slice(h * 128, (h + 1) * 128)
        part = dq_ref[:, span]
        for p in range(pd_ref.shape[0]):
            part += jnp.where(live, pd_ref[p, :, span].astype(F32), 0.0)
        in_ref[:, span] = turn(part, cosine, sine).astype(BF16)
        over = slice(width + h * 128, width + (h + 1) * 128)
        in_ref[:, over] = turn(dkv_ref[:, span], cosine, sine).astype(BF16)
    in_ref[:, 2 * width :] = dkv_ref[:, width:].astype(BF16)
    normed_low = n_ref[...]
    for i in range(3):
        span = slice(i * width, (i + 1) * width)
        late_ref[:, span] = dot(normed_low, in_ref[:, span], TN).astype(BF16)
    copies[0].wait()
    grad_norm = dot(in_ref[...], w_ref[...], NT)
    x = x_ref[...].astype(F32)
    root = inverse_root(x)
    normed = x * root
    gains = jnp.concatenate(
        [
            jnp.sum(grad_norm * normed, axis=0, keepdims=True),
            ggain_ref[:1],
            jnp.zeros((126, width), F32),
        ],
        axis=0,
    )
    late_ref[:, 3 * width :] = gains.T.astype(BF16)
    scaled = grad_norm * gain_ref[:1]
    gx_ref[...] = gm_ref[...] + root * (
        scaled - normed * jnp.mean(normed * scaled, axis=1, keepdims=True)
    )


def final(live, *arrays):
    rows, width = arrays[0].shape
    columns = arrays[-1].shape[1]
    return pl.pallas_call(
        final_kernel,
        out_shape=[
            jax.ShapeDtypeStruct((rows, width), F32),
            jax.ShapeDtypeStruct((width, columns), BF16),
        ],
        in_specs=[pl.BlockSpec(memory_space=pltpu.SMEM)]
        + in_vmem(len(arrays) - 1)
        + [pl.BlockSpec(memory_space=pl.ANY)],
        out_specs=in_vmem(2),
        scratch_shapes=[
            pltpu.VMEM((rows, 3 * width), BF16),
            pltpu.VMEM((width, 3 * width), BF16),
            pltpu.SemaphoreType.DMA((1,)),
        ],
        compiler_params=params(),
        name="final",
    )(live, *arrays)


REACH = {"all": ("seq", "mem"), "line": "mem", "square": "seq"}


def gather_plain(array, reach):
    return lax.all_gather(array, REACH[reach], axis=0)


def scatter_plain(array, reach):
    return lax.psum_scatter(array, REACH[reach], scatter_dimension=0, tiled=True).astype(F32)


def return_plain(array):
    return lax.all_to_all(array, "mem", split_axis=0, concat_axis=0, tiled=True)


def join_peers(outs, stats):
    top = jnp.max(stats[:, :HEADS], axis=0)
    shares = jnp.exp2(stats[:, :HEADS] - top)
    total = jnp.sum(stats[:, HEADS:] * shares, axis=0)
    wide = jnp.repeat(jnp.swapaxes(shares, 1, 2), outs.shape[-1] // HEADS, axis=2)
    joined = jnp.sum(outs.astype(F32) * wide, axis=0).astype(BF16)
    return joined[None], jnp.concatenate([top, total], axis=0)[None]


def per_device(
    sizes,
    tokens,
    cached_keys,
    cached_values,
    knn_index,
    has_memory,
    w_query,
    w_key,
    w_value,
    w_out,
    gain_attn,
    w_gate,
    w_up,
    w_down,
    gain_ffn,
    cotangent,
):
    near = sizes["seq"] == 4 and sizes["mem"] % 2 == 0 and 4 <= sizes["mem"] <= 16
    inputs, grad_out = tokens[0], cotangent[0]
    rows, width = inputs.shape
    hidden_width = w_gate.shape[1]
    head_width = width // HEADS
    scale = head_width ** (-0.5) * LOG2E
    mem_dev = cached_keys.shape[1]
    place = lax.axis_index("seq").astype(jnp.int32)[None]
    base = (lax.axis_index("mem") * mem_dev).astype(jnp.int32)[None]

    gains = jnp.concatenate(
        [gain_attn[:, None], gain_ffn[:, None], jnp.zeros((w_query.shape[0], 126), BF16)], axis=1
    )
    first_shard = jnp.concatenate([w_query, w_key, w_value, gains], axis=1)
    flag_rows = jnp.broadcast_to(has_memory[:, None], (8, 128))
    index_shard = jnp.concatenate([knn_index[0], flag_rows], axis=0)
    if near:
        jobs = [
            gather_job(sizes, index_shard, row_halves, "line"),
            gather_job(sizes, first_shard, row_halves, "all"),
        ]
        (shared,), (first_weights,) = together(1, "first", sizes, jobs)
    else:
        first_weights, shared = gather_plain(first_shard, "all"), gather_plain(index_shard, "line")
    first_weights = first_weights.reshape(-1, first_shard.shape[1])
    all_index, flags = shared[:, :rows], shared[:, rows, 0]
    segments = flags.shape[0]
    order = jnp.argsort(jnp.where(flags > 0, 0, 1), stable=True)[: segments // 2].astype(jnp.int32)

    positions = lax.axis_index("seq") * rows + jnp.arange(rows)
    cosine, sine = angles_for(positions, head_width)
    cosine = jnp.concatenate([cosine, cosine], axis=1)
    sine = jnp.concatenate([-sine, sine], axis=1)
    norm_one, queries, keys_values, gain_rows = project(inputs, first_weights, cosine, sine)
    if near:
        jobs = [
            gather_job(sizes, queries, row_halves, "line", PIECES),
            gather_job(sizes, keys_values, row_halves, "square"),
            gather_job(sizes, w_out, row_halves, "all"),
            mask_job(all_index, mem_dev),
        ]
        (all_queries,), (segment_kv,), (out_weight,), (bits,) = together(2, "second", sizes, jobs)
    else:
        all_queries = gather_plain(queries, "line")
        segment_kv = gather_plain(keys_values, "square")
        out_weight = gather_plain(w_out, "all")
        bits = mask_bits(base, all_index, mem_dev)
    segment_kv = segment_kv.reshape(-1, 2 * width)

    owner_out, owner_stats = owner_forward(
        order, all_queries, bits, cached_keys, cached_values, scale
    )
    local_work = local_job("forward", [queries, segment_kv], scale)
    if near:
        jobs = [
            return_job(sizes, [owner_out, owner_stats]),
            gather_job(sizes, w_gate, row_halves, "all"),
            gather_job(sizes, w_up, row_halves, "all"),
            gather_job(sizes, w_down, column_halves, "all"),
            local_work,
        ]
        peers, (gate_weight,), (up_weight,), (down_weight,), local = together(
            3, "third", sizes, jobs
        )
    else:
        peers = join_peers(return_plain(owner_out), return_plain(owner_stats))
        gate_weight, up_weight = gather_plain(w_gate, "all"), gather_plain(w_up, "all")
        down_weight = gather_plain(w_down, "all")
        local = alone("local_forward", place, local_work)
    weights = [
        out_weight.reshape(width, width),
        gate_weight.reshape(width, hidden_width),
        up_weight.reshape(width, hidden_width),
        down_weight.reshape(hidden_width, width),
    ]
    (
        mixed,
        grad_mid,
        attention_low,
        norm_two,
        grad_mid_low,
        grad_attention,
        back_stats,
        hidden,
        grad_gate,
        grad_upward,
        gain_two_grad,
    ) = middle(has_memory, inputs, grad_out, gain_rows, local, peers, weights)
    local_work = local_job(
        "backward", [queries, grad_attention, back_stats, segment_kv], scale
    )
    if near:
        jobs = [
            gather_job(sizes, grad_attention, row_halves, "line", PIECES),
            gather_job(sizes, back_stats, row_halves, "line"),
            local_work,
        ]
        (all_grads,), (all_stats,), (local_dq, local_dkv) = together(4, "fourth", sizes, jobs)
    else:
        all_grads, all_stats = gather_plain(grad_attention, "line"), gather_plain(back_stats, "line")
        local_dq, local_dkv = alone("local_backward", place, local_work)
    owner_grads = owner_backward(
        order, all_queries, all_grads, all_stats, bits, cached_keys, cached_values, scale
    )

    early = [
        dot(attention_low, grad_mid_low, TN).astype(BF16),
        dot(norm_two, grad_gate, TN).astype(BF16),
        dot(norm_two, grad_upward, TN).astype(BF16),
        dot(hidden, grad_out, TN).astype(BF16),
    ]
    if near:
        jobs = [
            return_job(sizes, [owner_grads]),
            scatter_job(sizes, local_dkv, row_halves, False),
            *[scatter_job(sizes, grad, row_halves) for grad in early[:3]],
            scatter_job(sizes, early[3], column_halves),
        ]
        (peer_grads,), (grad_kv,), *early_sums = together(5, "fifth", sizes, jobs)
        grad_kv = grad_kv.reshape(rows, 2 * width)
        early_sums = [total for (total,) in early_sums]
    else:
        peer_grads = jnp.sum(return_plain(owner_grads).astype(F32), axis=0, keepdims=True)
        grad_kv = scatter_plain(local_dkv, "square")
        early_sums = [scatter_plain(grad, "all") for grad in early]
    grad_inputs, late = final(
        has_memory, inputs, grad_mid, gain_rows, gain_two_grad, norm_one, local_dq, peer_grads, grad_kv,
        cosine, sine, first_weights,
    )
    if near:
        ((late_sum,),) = together(6, "sixth", sizes, [scatter_job(sizes, late, row_halves)])
    else:
        late_sum = scatter_plain(late, "all")
    return (
        mixed[None],
        grad_inputs[None],
        late_sum[:, :width],
        late_sum[:, width : 2 * width],
        late_sum[:, 2 * width : 3 * width],
        early_sums[0],
        late_sum[:, 3 * width],
        early_sums[1],
        early_sums[2],
        early_sums[3],
        late_sum[:, 3 * width + 1],
    )


def solution(mesh):
    rows, owned, feature = P("mem", "seq", None), P(None, "mem", None), P(("seq", "mem"), None)
    gain = P(("seq", "mem"))
    return jax.shard_map(
        functools.partial(per_device, dict(mesh.shape)),
        mesh=mesh,
        in_specs=(
            (rows, owned, owned, rows, P("mem"))
            + (feature,) * 4
            + (gain,)
            + (feature,) * 3
            + (gain, rows)
        ),
        out_specs=(rows, rows) + (feature,) * 4 + (gain,) + (feature,) * 3 + (gain,),
        check_vma=False,
    )
```

```python
import functools

import jax
import jax.numpy as jnp
from jax import lax
from jax.experimental import pallas as pl
from jax.experimental.pallas import tpu as pltpu
from jax.sharding import PartitionSpec as P

HEADS = 8
EPSILON = 1e-05
FLOOR = -1e30
LOW = -1e29
LOG2E = 1.4426950408889634
STATS = 16
PIECES = 4
ORDERS = {
    ("first", 4): (
        7, 0, 7, 8, 9, 1, 7, 8, 2, 10, 10, 3, 9, 11, 11, 12, 4, 10, 13, 12, 8, 13, 9, 11, 6, 5,
        13, 12,
    ),
    ("second", 4): (
        0, 30, 14, 21, 37, 44, 29, 1, 7, 51, 28, 29, 29, 46, 38, 2, 39, 29, 29, 51, 29, 22, 15,
        45, 52, 53, 16, 9, 8, 31, 3, 28, 23, 48, 29, 24, 4, 29, 32, 47, 40, 29, 29, 33, 17, 29,
        41, 10, 29, 18, 29, 29, 25, 29, 54, 11, 29, 29, 5, 44, 55, 50, 45, 6, 29, 29, 29, 29, 19,
        29, 12, 29, 30, 34, 29, 29, 43, 49, 28, 55, 35, 29, 26, 38, 29, 31, 42, 52, 29, 37, 20,
        44, 28, 28, 30, 51, 28, 29, 13, 33, 56, 39, 41, 28, 32, 27, 57, 47, 29, 29, 28, 29, 46,
        56, 50, 42, 49, 40, 34, 29, 57, 45, 29, 38, 37, 29, 53, 31, 28, 56, 48, 35, 46, 43, 54,
        55, 39, 36, 28, 32, 28, 57, 47, 48, 40, 36, 41, 53, 52, 34, 49, 50, 36, 54, 33, 35, 43,
        42,
    ),
    ("third", 4): (
        21, 28, 40, 46, 35, 47, 37, 38, 42, 49, 43, 35, 40, 38, 49, 14, 7, 0, 41, 35, 39, 41, 46,
        16, 15, 50, 35, 37, 48, 35, 8, 49, 9, 36, 42, 23, 45, 41, 29, 39, 37, 2, 46, 36, 35, 38,
        35, 18, 40, 46, 43, 22, 1, 30, 52, 46, 41, 36, 45, 43, 47, 38, 41, 32, 44, 3, 4, 25, 17,
        36, 37, 36, 42, 35, 37, 49, 43, 31, 45, 43, 49, 35, 36, 11, 44, 45, 10, 24, 45, 36, 42,
        36, 42, 36, 39, 48, 36, 47, 39, 52, 38, 12, 36, 36, 39, 50, 51, 44, 36, 35, 48, 35, 36,
        47, 5, 19, 47, 26, 52, 50, 36, 33, 36, 36, 27, 36, 51, 36, 36, 36, 36, 44, 40, 35, 20, 52,
        6, 51, 13, 36, 35, 35, 34, 36, 35, 51, 44, 48, 52, 48, 36, 36, 40, 36, 36, 51, 35, 35, 50,
        35, 35, 35, 35, 35, 35, 50, 35,
    ),
    ("fourth", 4): (
        0, 0, 3, 2, 1, 0, 1, 0, 0, 1, 2, 1, 1, 2, 3, 2, 2, 3, 3, 3,
    ),
}
F32 = jnp.float32
BF16 = jnp.bfloat16
VMEM_LIMIT = 62 * 1024 * 1024
NT = (((1,), (1,)), ((), ()))
TN = (((0,), (0,)), ((), ()))


def dot(left, right, dims=(((1,), (0,)), ((), ()))):
    return lax.dot_general(left, right, dims, preferred_element_type=F32)


def angles_for(positions, head_width):
    exponent = jnp.arange(head_width // 2, dtype=F32) * (2.0 / head_width)
    frequency = jnp.power(10000.0, -exponent)
    turned = positions.astype(F32)[:, None] * frequency[None, :]
    return (jnp.cos(turned), jnp.sin(turned))


def params(**more):
    return pltpu.CompilerParams(vmem_limit_bytes=VMEM_LIMIT, **more)


def spread(columns, width=128):
    lanes = lax.broadcasted_iota(jnp.int32, (columns[0].shape[0], width), 1)
    result = jnp.zeros((columns[0].shape[0], width), F32)
    for place, column in enumerate(columns):
        result = jnp.where(lanes == place, column, result)
    return result


def columns_of(rows_by_stat):
    count, width = rows_by_stat.shape
    padded = jnp.concatenate([rows_by_stat, jnp.zeros((128 - count, width), F32)], axis=0)
    return padded.T


MESH = pl.DeviceIdType.MESH


class Net:
    def __init__(self, line):
        self.line = line
        self.s, self.m = lax.axis_index("seq"), lax.axis_index("mem")
        self.c, self.z = self.m % 2, self.m // 2
        self.x, self.y, self.core = (self.s ^ 1, self.m), (self.s ^ 2, self.m), (self.s, self.m ^ 1)
        self.right = (self.s, (self.m + 2) % (2 * line))
        self.left = (self.s, (self.m + 2 * line - 2) % (2 * line))

    def others(self):
        ring = 2 * self.line
        return [(self.s, lax.rem(self.m + 2 * k, ring)) for k in range(1, self.line)]

    def greet(self, others):
        barrier = pltpu.get_barrier_semaphore()
        for other in others:
            pl.semaphore_signal(barrier, inc=1, device_id=other, device_id_type=MESH)
        pl.semaphore_wait(barrier, len(others))


def remote(src, dst, sends, recvs, place, device):
    return pltpu.make_async_remote_copy(
        src_ref=src,
        dst_ref=dst,
        send_sem=sends.at[place],
        recv_sem=recvs.at[place],
        device_id=device,
        device_id_type=MESH,
    )


def row_halves(ref, part):
    half = ref.shape[-2] // 2
    return ref.at[pl.ds(part * half, half)]


def column_halves(ref, part):
    half = ref.shape[-1] // 2
    return ref.at[:, pl.ds(part * half, half)]


class Gather:
    def __init__(self, net, src, out, sends, recvs, own, index, halves, line=True, square=True, core=True):
        self.net, self.src, self.out, self.sends, self.recvs, self.own = net, src, out, sends, recvs, own
        self.index, self.halves = index, halves
        self.line, self.square, self.core = line, square, core
        self.waits_core, self.waits_own, self.seen = True, True, set()

    def slot(self, s, z):
        return self.out.at[self.index(s, z, self.net.c)]

    def wait_own(self):
        pltpu.make_async_copy(self.src, self.slot(self.net.s, self.net.z), self.own).wait()

    def wait_core(self, z):
        place = self.places()[3] + z
        self.arrived(self.out.at[self.index(self.net.s, z, 1 - self.net.c)], place)

    def send(self, block, target, place, device):
        copy = remote(block, target, self.sends, self.recvs, place, device)
        copy.start()

    def sent(self, block, place):
        remote(block, block, self.sends, self.recvs, place, self.net.core).wait_send()

    def arrived(self, block, place):
        remote(block, block, self.sends, self.recvs, place, self.net.core).wait_recv()

    def places(self):
        z = self.net.line
        right, left, square, core = 0, z, 2 * z, 8 * z
        return right, left, square, core

    def chain(self, k, from_left):
        net = self.net
        z = net.z - k if from_left else net.z + k
        present = z >= 0 if from_left else z < net.line
        self.seen.add((k, from_left))
        for stage in (self.have, self.pass_square, self.end_square) if self.square else (self.have,):
            if k == 0:
                stage(0, net.z, None)
            else:
                pl.when(present)(lambda stage=stage: stage(k, z, from_left))
            yield

    def chains(self):
        chains = [self.chain(0, True)]
        for k in range(1, self.net.line if self.line else 1):
            chains += [self.chain(k, True), self.chain(k, False)]
        return chains

    def have(self, k, z, from_left):
        net = self.net
        right, left, square, core = self.places()
        target = self.slot(net.s, z)
        block = self.src if k == 0 else target
        if k == 0:
            pltpu.make_async_copy(self.src, target, self.own).start()
        else:
            self.arrived(target, (right if from_left else left) + z)
        if self.line:
            if from_left is not False:
                pl.when(net.z < net.line - 1)(lambda: self.send(block, target, right + z, net.right))
            if from_left is not True:
                pl.when(net.z > 0)(lambda: self.send(block, target, left + z, net.left))
        if self.square:
            for kind, part, device in ((0, 0, net.x), (2, 1, net.y), (1, 0, net.y), (3, 1, net.x)):
                self.send(
                    self.halves(block, part),
                    self.halves(target, part),
                    square + kind * net.line + z,
                    device,
                )
        if self.core:
            self.send(block, target, core + z, net.core)

    def pass_square(self, k, z, from_left):
        net = self.net
        _, _, square, core = self.places()
        for kind, part, other, then, device, mirror in (
            (0, 0, net.s ^ 1, 4, net.y, 1),
            (2, 1, net.s ^ 2, 5, net.x, 2),
        ):
            block = self.halves(self.slot(other, z), part)
            self.arrived(block, square + kind * net.line + z)
            self.send(block, block, square + then * net.line + z, device)
            if self.core:
                self.send(block, block, core + mirror * net.line + z, net.core)

    def end_square(self, k, z, from_left):
        net = self.net
        _, _, square, core = self.places()
        for kind, part, other, mirror in self.last(net):
            block = self.halves(self.slot(other, z), part)
            self.arrived(block, square + kind * net.line + z)
            if self.core:
                self.send(block, block, core + mirror * net.line + z, net.core)

    def last(self, net):
        return (
            (1, 0, net.s ^ 2, 3),
            (3, 1, net.s ^ 1, 5),
            (4, 0, net.s ^ 3, 4),
            (5, 1, net.s ^ 3, 6),
        )

    def finish(self):
        net = self.net
        right, left, square, core = self.places()
        own = self.slot(net.s, net.z)
        if self.waits_own:
            self.wait_own()
        if self.core:
            for z in range(net.line if self.line else 1):
                z = z if self.line else net.z
                for mirror, part, other in (
                    (0, None, net.s),
                    (1, 0, net.s ^ 1),
                    (2, 1, net.s ^ 2),
                    (3, 0, net.s ^ 2),
                    (4, 0, net.s ^ 3),
                    (5, 1, net.s ^ 1),
                    (6, 1, net.s ^ 3),
                ):
                    if part is not None and not self.square:
                        continue
                    block = self.out.at[self.index(other, z, 1 - net.c)]
                    block = block if part is None else self.halves(block, part)
                    if self.waits_core:
                        self.arrived(block, core + mirror * net.line + z)
                    self.sent(block, core + mirror * net.line + z)
        if self.square:
            half = [self.halves(own, 0), self.halves(own, 1)]
            for z in range(net.line if self.line else 1):
                z = z if self.line else net.z
                for kind, part in ((0, 0), (1, 0), (2, 1), (3, 1), (4, 0), (5, 1)):
                    self.sent(half[part], square + kind * net.line + z)
        if self.line:
            for z in range(net.line):
                pl.when((z <= net.z) & (net.z < net.line - 1))(lambda z=z: self.sent(own, right + z))
                pl.when((z >= net.z) & (net.z > 0))(lambda z=z: self.sent(own, left + z))


class Job:
    def __init__(self, arrays, outs, scratch, steps, where=pl.ANY, out_where=pl.ANY):
        self.arrays, self.outs, self.scratch, self.steps = arrays, outs, scratch, steps
        self.where, self.out_where = where, out_where


def specs(where, arrays):
    places = where if isinstance(where, list) else [where] * len(arrays)
    return [pl.BlockSpec(memory_space=place) for place in places]


def together_kernel(line, jobs, order, *refs):
    refs = list(refs)
    take = lambda count: [refs.pop(0) for _ in range(count)]
    ins = [take(len(job.arrays)) for job in jobs]
    outs = [take(len(job.outs)) for job in jobs]
    scratch = [take(len(job.scratch)) for job in jobs]
    net = Net(line)
    net.greet([net.x, net.y, net.core] + net.others())
    chains, ends = [], []
    for job, *parts in zip(jobs, ins, outs, scratch):
        more, last = job.steps(net, *parts)
        chains += more
        ends += last
    for turn in order:
        next(chains[turn], None)
    while chains:
        chains = [chain for chain in chains if next(chain, True) is None]
    for end in ends:
        end()


def together(collective_id, name, sizes, jobs):
    line = sizes["mem"] // 2
    moved = sum(2 * a.size * a.dtype.itemsize for job in jobs for a in job.arrays)
    results = pl.pallas_call(
        functools.partial(together_kernel, line, jobs, ORDERS.get((name, line), ())),
        out_shape=[out for job in jobs for out in job.outs],
        in_specs=[s for job in jobs for s in specs(job.where, job.arrays)],
        out_specs=[s for job in jobs for s in specs(job.out_where, job.outs)],
        scratch_shapes=[s for job in jobs for s in job.scratch],
        compiler_params=params(collective_id=collective_id, has_side_effects=True),
        cost_estimate=pl.CostEstimate(flops=0, bytes_accessed=moved, transcendentals=0),
        name=name,
    )(*[a for job in jobs for a in job.arrays])
    results = list(results)
    return [[results.pop(0) for _ in job.outs] for job in jobs]


def gather_parts(net, src, out, scratch, halves, reach, pieces):
    line, rows = net.line, src.shape[0] // pieces
    index = {
        "all": lambda s, z, c: (s * line + z) * 2 + c,
        "line": lambda s, z, c: z * 2 + c,
        "square": lambda s, z, c: s,
    }[reach]
    parts = []
    for i in range(pieces):
        span = pl.ds(i * rows, rows)
        ends = (src, out) if pieces == 1 else (src.at[span], out.at[:, span])
        parts.append(
            Gather(
                net, *ends, *scratch[3 * i : 3 * i + 3], index, halves,
                line=reach != "square", square=reach != "line", core=reach != "square",
            )
        )
    return parts


def gather_semaphores(line, pieces=1):
    return ([pltpu.SemaphoreType.DMA((15 * line,))] * 2 + [pltpu.SemaphoreType.DMA]) * pieces


def gather_job(sizes, array, halves, reach, pieces=1):
    line = sizes["mem"] // 2
    slots = {"all": sizes["seq"] * sizes["mem"], "line": sizes["mem"], "square": sizes["seq"]}[reach]

    def steps(net, ins, outs, scratch):
        parts = gather_parts(net, ins[0], outs[0], scratch, halves, reach, pieces)
        return [chain for part in parts for chain in part.chains()], [part.finish for part in parts]

    out = jax.ShapeDtypeStruct((slots,) + array.shape, array.dtype)
    return Job([array], [out], gather_semaphores(line, pieces), steps)


class Scatter:
    def __init__(self, net, src, out, buffers, sems, halves, whole=True):
        self.net, self.src, self.out, self.halves = net, src, out, halves
        self.whole, self.count = whole, buffers[0].shape[1]
        self.held, self.twin, self.first, self.second, self.along = buffers
        self.sends, self.recvs, self.own = sems

    def send(self, block, target, place, device):
        remote(block, target, self.sends, self.recvs, place, device).start()

    def sent(self, block, place):
        remote(block, block, self.sends, self.recvs, place, self.net.core).wait_send()

    def arrived(self, block, place):
        remote(block, block, self.sends, self.recvs, place, self.net.core).wait_recv()

    def places(self):
        z = self.count
        return 0, 4 * z, 8 * z, 10 * z, 11 * z

    def loading(self, d):
        source = self.src.at[:, d, self.net.c] if self.whole else self.src.at[:, d]
        return pltpu.make_async_copy(source, self.held.at[:, d], self.own.at[d])

    def load(self, d):
        net = self.net
        if self.src is not None:
            self.loading(d).start()
        for s in range(4 if self.whole else 0):
            self.send(self.src.at[s, d, 1 - net.c], self.twin.at[s, d], s * self.count + d, net.core)

    def add_core(self, d):
        net = self.net
        _, first, _, _, _ = self.places()
        if self.src is not None:
            self.loading(d).wait()
        for turn in (3, 2, 1, 0):
            s = net.s ^ turn
            if self.whole:
                self.arrived(self.twin.at[s, d], s * self.count + d)
                self.held[s, d] = self.held[s, d] + self.twin[s, d]
            for part, device, slot, kind in {
                3: ((0, net.y, 1, 1), (1, net.x, 1, 3)),
                2: ((0, net.y, 0, 0),),
                1: ((1, net.x, 0, 2),),
                0: (),
            }[turn]:
                self.send(
                    self.halves(self.held.at[s, d], part),
                    self.first.at[part, slot, d],
                    first + kind * self.count + d,
                    device,
                )

    def chain(self, k):
        d = lax.rem(self.net.z + k, self.net.line) if self.whole else k
        for stage in (self.load, self.add_core, self.add_first, self.add_second, self.line_step):
            stage(d)
            yield

    def add(self, block, other):
        block[...] = block[...] + other[...]

    def add_first(self, d):
        net = self.net
        _, first, second, _, _ = self.places()
        for part, slot, kind, turn in ((0, 1, 1, 1), (1, 1, 3, 2), (0, 0, 0, 0), (1, 0, 2, 0)):
            got = self.first.at[part, slot, d]
            self.arrived(got, first + kind * self.count + d)
            block = self.halves(self.held.at[net.s ^ turn, d], part)
            self.add(block, got)
            if turn:
                device = net.x if part == 0 else net.y
                self.send(block, self.second.at[part, d], second + part * self.count + d, device)

    def add_second(self, d):
        net = self.net
        _, _, second, _, _ = self.places()
        for part in range(2):
            self.arrived(self.second.at[part, d], second + part * self.count + d)
            self.add(self.halves(self.held.at[net.s, d], part), self.second.at[part, d])

    def line_step(self, d):
        net = self.net
        _, _, _, right, left = self.places()
        block = self.held.at[net.s, d]
        if not self.whole:
            self.out[d] = block[...].astype(self.out.dtype)
            return

        def go():
            pltpu.make_async_remote_copy(
                src_ref=block,
                dst_ref=self.along.at[net.z],
                send_sem=self.sends.at[right + d],
                recv_sem=self.recvs.at[left + net.z],
                device_id=(net.s, 2 * d + net.c),
                device_id_type=MESH,
            ).start()

        pl.when(net.z != d)(go)

    def keep(self):
        net = self.net
        _, _, _, _, left = self.places()
        total = self.held[net.s, net.z].astype(F32)
        for k in range(1, net.line):
            z = lax.rem(net.z + k, net.line)
            self.arrived(self.along.at[z], left + z)
            total = total + self.along[z].astype(F32)
        self.out[...] = total

    def finish(self):
        net = self.net
        _, first, second, right, left = self.places()
        full = self.held.at[net.s, 0]
        if self.whole:
            self.keep()
        for d in range(self.count):
            for s in range(4 if self.whole else 0):
                self.sent(full, s * self.count + d)
            for kind, part in enumerate((0, 0, 1, 1)):
                self.sent(self.halves(full, part), first + kind * self.count + d)
            for part in range(2):
                self.sent(self.halves(full, part), second + part * self.count + d)
            if self.whole:
                pl.when(net.z != d)(lambda d=d: self.sent(full, right + d))


def far_first(count):
    return sorted(range(count), key=lambda k: (k == 0, -min(k, count - k)))


def scatter_scratch(count, rows, columns, halves, whole):
    half = (rows // 2, columns) if halves is row_halves else (rows, columns // 2)
    block, unused = (rows, columns), (16, 128)
    return [
        pltpu.VMEM((4, count) + block, BF16),
        pltpu.VMEM((4, count) + block if whole else unused, BF16),
        pltpu.VMEM((2, 2, count) + half, BF16),
        pltpu.VMEM((2, count) + half, BF16),
        pltpu.VMEM((count,) + block if whole else unused, BF16),
        pltpu.SemaphoreType.DMA((12 * count,)),
        pltpu.SemaphoreType.DMA((12 * count,)),
        pltpu.SemaphoreType.DMA((count,)),
    ]


def scatter_job(sizes, array, halves, whole=True):
    square, line = sizes["seq"], sizes["mem"] // 2
    columns = array.shape[1]
    if whole:
        count, rows = line, array.shape[0] // (2 * square * line)
        array = array.reshape(square, line, 2, rows, columns)
        out = jax.ShapeDtypeStruct((rows, columns), F32)
    else:
        count, rows = PIECES, array.shape[0] // (square * PIECES)
        array = array.reshape(square, count, rows, columns)
        out = jax.ShapeDtypeStruct((count, rows, columns), F32)
    scratch = scatter_scratch(count, rows, columns, halves, whole)

    def steps(net, ins, outs, scratch):
        scatter = Scatter(net, ins[0], outs[0], scratch[:5], scratch[5:], halves, whole)
        return [scatter.chain(k) for k in far_first(count)], [scatter.finish]

    return Job([array], [out], scratch, steps, out_where=pltpu.VMEM)


class Return:
    def __init__(self, net, sources, outs, scratch):
        kinds = len(sources)
        self.net, self.sources, self.outs, self.kinds = net, sources, outs, range(kinds)
        self.held, self.twin = scratch[:kinds], scratch[kinds : 2 * kinds]
        self.own, self.twin_sends, self.twin_recvs, self.sends, self.recvs = scratch[2 * kinds :]

    def loading(self, i, d):
        source = self.sources[i].at[d, self.net.c]
        return pltpu.make_async_copy(source, self.held[i].at[d], self.own.at[i, d])

    def pairing(self, i, d):
        net = self.net
        return remote(
            self.sources[i].at[d, 1 - net.c],
            self.twin[i].at[d],
            self.twin_sends.at[i],
            self.twin_recvs.at[i],
            d,
            net.core,
        )

    def giving(self, i, k, d, slot, device):
        return pltpu.make_async_remote_copy(
            src_ref=self.held[i].at[d],
            dst_ref=self.outs[i].at[slot],
            send_sem=self.sends.at[i, k],
            recv_sem=self.recvs.at[i, slot],
            device_id=device,
            device_id_type=MESH,
        )

    def keeping(self, i, d):
        return pltpu.make_async_copy(
            self.held[i].at[d], self.outs[i].at[self.net.z], self.own.at[i, d]
        )

    def chain(self, k):
        net = self.net
        d = lax.rem(net.z + k, net.line)
        for i in self.kinds:
            self.loading(i, d).start()
            self.pairing(i, d).start()
        yield
        for i in self.kinds:
            self.loading(i, d).wait()
            self.pairing(i, d).wait_recv()
        self.merge(d)
        for i in self.kinds:
            if k:
                self.giving(i, k, d, net.z, (net.s, 2 * d + net.c)).start()
            else:
                self.keeping(i, d).start()
        yield

    def merge(self, d):
        held, twin = self.held, self.twin
        if len(held) == 1:
            held[0][d] = held[0][d] + twin[0][d]
            return
        mine, theirs = held[1][d], twin[1][d]
        top = jnp.maximum(mine[:HEADS], theirs[:HEADS])
        shares = [jnp.exp2(mine[:HEADS] - top), jnp.exp2(theirs[:HEADS] - top)]
        held[1][d] = jnp.concatenate(
            [top, mine[HEADS:] * shares[0] + theirs[HEADS:] * shares[1]], axis=0
        )
        shares = columns_of(jnp.concatenate(shares, axis=0))
        for h in range(HEADS):
            span = slice(h * 128, (h + 1) * 128)
            held[0][d, :, span] = (
                held[0][d, :, span].astype(F32) * shares[:, h : h + 1]
                + twin[0][d, :, span].astype(F32) * shares[:, HEADS + h : HEADS + h + 1]
            ).astype(BF16)

    def finish(self):
        net = self.net
        for k in range(net.line):
            d = lax.rem(net.z + k, net.line)
            for i in self.kinds:
                self.pairing(i, d).wait_send()
                if k:
                    copy = self.giving(i, k, d, d, net.core)
                    copy.wait_recv()
                    copy.wait_send()
                else:
                    self.keeping(i, d).wait()


def return_job(sizes, arrays):
    line, kinds = sizes["mem"] // 2, len(arrays)
    blocks = [a.reshape((line, 2) + a.shape[1:]) for a in arrays]
    slots = [pltpu.VMEM((line,) + a.shape[1:], a.dtype) for a in arrays]
    outs = [jax.ShapeDtypeStruct((line,) + a.shape[1:], a.dtype) for a in arrays]
    scratch = slots + slots + [pltpu.SemaphoreType.DMA((kinds, line))] * 5
    def steps(net, ins, outs, scratch):
        back = Return(net, ins, outs, scratch)
        return [back.chain(k) for k in (*range(1, line), 0)], [back.finish]

    return Job(blocks, outs, scratch, steps)


class OwnerForward(Return):
    def __init__(self, net, scale, parts, ins, outs, scratch, sems):
        self.index, self.keys, self.values = ins
        self.queries, self.bits, *peers = outs
        (self.places_ref, self.words_ref, self.bias, self.key, self.value, *held) = scratch
        self.far, held = held[:2], held[2:]
        self.loads, *sems = sems
        super().__init__(net, self.far, peers, held + sems)
        self.parts, self.scale = parts, scale

    def pairing(self, i, d):
        net = self.net
        return remote(
            self.far[i].at[d],
            self.twin[i].at[d],
            self.twin_sends.at[i],
            self.twin_recvs.at[i],
            d,
            net.core,
        )

    def bring(self, z, far):
        net = self.net
        segment = 2 * z + (1 - net.c if far else net.c)
        slot = int(far)
        return [
            pltpu.make_async_copy(self.keys.at[segment], self.key.at[slot], self.loads.at[0, slot]),
            pltpu.make_async_copy(
                self.values.at[segment], self.value.at[slot], self.loads.at[1, slot]
            ),
        ]

    def mask(self, z, far):
        net = self.net
        for copy in self.bring(z, far):
            copy.start()
        segment = 2 * z + (1 - net.c if far else net.c)
        mem_dev = self.keys.shape[1]
        self.bits[segment] = mask_words(
            self.index[segment], net.m * mem_dev, mem_dev, self.places_ref, self.words_ref
        )

    def need(self, k, from_left):
        for part in self.parts:
            assert (k, from_left) in part.seen

    def attend(self, z, far):
        net = self.net
        if far:
            for part in self.parts:
                part.wait_core(z)
        segment = 2 * z + (1 - net.c if far else net.c)
        fill_bias(self.bits.at[segment], self.bias)
        for copy in self.bring(z, far):
            copy.wait()
        target = self.far if far else self.held
        owner_forward_heads(
            self.scale,
            self.queries.at[segment],
            self.key.at[int(far)],
            self.value.at[int(far)],
            self.bias,
            target[0].at[z],
            target[1].at[z],
        )
        if far:
            for i in self.kinds:
                self.pairing(i, z).start()

    def home(self, k, z):
        for i in self.kinds:
            self.pairing(i, z).wait_recv()
        self.merge(z)
        net = self.net
        for i in self.kinds:
            if k:
                self.giving(i, z, z, net.z, (net.s, 2 * z + net.c)).start()
            else:
                self.keeping(i, z).start()

    def chain(self):
        net = self.net
        for k in range(net.line):
            for from_left in (True, False) if k else (True,):
                z = net.z - k if from_left else net.z + k
                present = z >= 0 if from_left else z < net.line
                here = (lambda body: body()) if k == 0 else pl.when(present)
                here(lambda: self.mask(z, True))
                yield
                self.need(k, from_left)
                if k == 0:
                    for part in self.parts:
                        part.wait_own()
                here(lambda: self.attend(z, True))
                yield
                here(lambda: self.mask(z, False))
                yield
                here(lambda: self.attend(z, False))
                yield
                here(lambda: self.home(k, z))
                yield

    def finish(self):
        net = self.net
        for k in range(net.line):
            d = lax.rem(net.z + k, net.line)
            for i in self.kinds:
                self.pairing(i, d).wait_send()
                if k:
                    copy = self.giving(i, d, d, d, net.core)
                    copy.wait_recv()
                    copy.wait_send()
                else:
                    self.keeping(i, d).wait()


def forward_job(sizes, queries, keys_values, all_index, cached_keys, cached_values, scale):
    line = sizes["mem"] // 2
    (rows, width), (segments, _, count) = queries.shape, all_index.shape
    mem_dev = cached_keys.shape[1]
    length = sizes["seq"] * rows
    shape = jax.ShapeDtypeStruct
    outs = [
        shape((segments, rows, width), BF16),
        shape((sizes["seq"],) + keys_values.shape, BF16),
        shape((segments, rows, 128), jnp.int32),
        shape((line, rows, width), BF16),
        shape((line, STATS, rows), F32),
        shape((rows, width), F32),
        shape((STATS, rows), F32),
    ]
    partial = [pltpu.VMEM((line, rows, width), BF16), pltpu.VMEM((line, STATS, rows), F32)]
    scratch = (
        gather_semaphores(line, PIECES)
        + gather_semaphores(line)
        + [pltpu.VMEM((rows, length), F32)]
        + mask_scratch(rows, count)
        + [pltpu.VMEM((rows, mem_dev), F32)]
        + [pltpu.VMEM((2, mem_dev, width), BF16)] * 2
        + partial * 3
        + [pltpu.SemaphoreType.DMA((2, 2))]
        + [pltpu.SemaphoreType.DMA((2, line))] * 5
    )

    def steps(net, ins, outs, scratch):
        queries, keys_values, *owner_ins = ins
        all_queries, segment_kv, bits, out, stats, local_out, local_stats = outs
        scratch = list(scratch)
        take = lambda count: [scratch.pop(0) for _ in range(count)]
        parts = gather_parts(net, queries, all_queries, take(3 * PIECES), row_halves, "line", PIECES)
        (square,) = gather_parts(net, keys_values, segment_kv, take(3), row_halves, "square", 1)
        (local_bias,) = take(1)
        buffers = take(11)
        owner = OwnerForward(
            net, scale, parts, owner_ins, [all_queries, bits, out, stats], buffers, scratch
        )
        for part in parts:
            part.waits_core = part.waits_own = False
        square.waits_own = False

        def local():
            for chain in square.chains():
                yield from chain
            square.wait_own()
            yield from local_forward_steps(
                scale, net.s, queries, segment_kv, local_out, local_stats, local_bias
            )

        chains = [chain for part in parts for chain in part.chains()]
        ends = [part.finish for part in parts] + [square.finish, owner.finish]
        return chains + [local(), owner.chain()], ends

    vmem = pltpu.VMEM
    return Job(
        [queries, keys_values, all_index, cached_keys, cached_values],
        outs,
        scratch,
        steps,
        [vmem, vmem, vmem, pl.ANY, pl.ANY],
        [vmem, vmem, vmem, pl.ANY, pl.ANY, vmem, vmem],
    )


def mask_words(index, base, mem_dev, place_ref, bit_ref):
    relative = index - base
    inside = (relative >= 0) & (relative < mem_dev)
    place = jnp.where(inside, relative & 127, 0)
    bit = jnp.where(inside, lax.shift_left(jnp.ones_like(relative), relative >> 7), 0)
    place_ref[...] = place.T
    bit_ref[...] = bit.T
    sought = lax.broadcasted_iota(jnp.int32, (128, 128), 0)
    halves = []
    for start in range(0, index.shape[0], 128):

        def eight(g, words, start=start):
            group = pl.ds(pl.multiple_of(g * 8, 8), 8)
            places = place_ref[group, start : start + 128]
            bits = bit_ref[group, start : start + 128]
            for j in range(8):
                words = words | jnp.where(places[j : j + 1] == sought, bits[j : j + 1], 0)
            return words

        none = jnp.zeros((128, 128), jnp.int32)
        words = lax.fori_loop(0, index.shape[1] // 8, eight, none)
        halves.append(words.T)
    return jnp.concatenate(halves, axis=0)


def mask_scratch(rows, count):
    return [pltpu.VMEM((count, rows), jnp.int32), pltpu.VMEM((count, rows), jnp.int32)]


def mask_kernel(mem_dev, base_ref, index_ref, bits_ref, place_ref, bit_ref):
    bits_ref[0] = mask_words(index_ref[0], base_ref[0], mem_dev, place_ref, bit_ref)


def mask_bits(base, all_index, mem_dev):
    segments, rows, count = all_index.shape
    return pl.pallas_call(
        functools.partial(mask_kernel, mem_dev),
        grid_spec=pltpu.PrefetchScalarGridSpec(
            num_scalar_prefetch=1,
            grid=(segments,),
            in_specs=[pl.BlockSpec((1, rows, count), lambda g, b: (g, 0, 0))],
            out_specs=pl.BlockSpec((1, rows, 128), lambda g, b: (g, 0, 0)),
            scratch_shapes=mask_scratch(rows, count),
        ),
        out_shape=jax.ShapeDtypeStruct((segments, rows, 128), jnp.int32),
        compiler_params=params(),
        name="mask_bits",
    )(base, all_index)


def mask_job(all_index, mem_dev):
    segments, rows, count = all_index.shape

    def steps(net, ins, outs, scratch):
        def chain():
            for g in range(segments):
                outs[0][g] = mask_words(ins[0][g], net.m * mem_dev, mem_dev, *scratch)
                yield

        return [chain()], []

    out = jax.ShapeDtypeStruct((segments, rows, 128), jnp.int32)
    return Job([all_index], [out], mask_scratch(rows, count), steps, pltpu.VMEM, pltpu.VMEM)


def fill_bias(bits_ref, bias_ref):
    bits = bits_ref[...].reshape(bits_ref.shape[-2:])
    for b in range(bias_ref.shape[1] // 128):
        bias_ref[:, b * 128 : (b + 1) * 128] = jnp.where(((bits >> b) & 1) != 0, 0.0, FLOOR)


def owner_backward_heads(scale, q_ref, g_ref, st_ref, k_ref, v_ref, bias_ref, dq_ref):
    stats = columns_of(st_ref[...])
    lanes = lax.broadcasted_iota(jnp.int32, stats.shape, 1)

    def two(i, carry):
        for h in (2 * i, 2 * i + 1):
            span = pl.ds(pl.multiple_of(h * 128, 128), 128)
            total = jnp.sum(jnp.where(lanes == h, stats, 0.0), axis=1, keepdims=True)
            dots = jnp.sum(jnp.where(lanes == HEADS + h, stats, 0.0), axis=1, keepdims=True)
            scores = dot(q_ref[:, span], k_ref[:, span], NT) * scale + bias_ref[...]
            weights = jnp.exp2(scores - total)
            dscore = weights * (dot(g_ref[:, span], v_ref[:, span], NT) - dots)
            dq_ref[:, span] = (
                dot(dscore.astype(BF16), k_ref[:, span]) * (scale / LOG2E)
            ).astype(BF16)
        return carry

    lax.fori_loop(0, HEADS // 2, two, 0)


def owner_forward_heads(scale, q_ref, k_ref, v_ref, bias_ref, o_ref, st_ref):
    rows = q_ref.shape[0]
    lanes = lax.broadcasted_iota(jnp.int32, (rows, 128), 1)

    def two(i, stats):
        for h in (2 * i, 2 * i + 1):
            span = pl.ds(pl.multiple_of(h * 128, 128), 128)
            scores = dot(q_ref[:, span], k_ref[:, span], NT) * scale + bias_ref[...]
            top = jnp.maximum(jnp.max(scores, axis=1, keepdims=True), LOW)
            weights = jnp.exp2(scores - top)
            total = jnp.sum(weights, axis=1, keepdims=True)
            stats = jnp.where(lanes == h, top, jnp.where(lanes == HEADS + h, total, stats))
            o_ref[:, span] = dot(weights.astype(BF16), v_ref[:, span]).astype(BF16)
        return stats

    stats = lax.fori_loop(0, HEADS // 2, two, jnp.zeros((rows, 128), F32))
    st_ref[...] = stats.T[:STATS]


def owner_forward_kernel(scale, order_ref, q_ref, bits_ref, k_ref, v_ref, o_ref, st_ref, bias_ref):
    del order_ref
    fill_bias(bits_ref, bias_ref)
    maxima, sums = [], []
    for h in range(HEADS):
        span = slice(h * 128, (h + 1) * 128)
        scores = dot(q_ref[0, :, span], k_ref[0, :, span], NT) * scale + bias_ref[...]
        top = jnp.maximum(jnp.max(scores, axis=1, keepdims=True), LOW)
        weights = jnp.exp2(scores - top)
        maxima.append(top)
        sums.append(jnp.sum(weights, axis=1, keepdims=True))
        o_ref[0, :, span] = dot(weights.astype(BF16), v_ref[0, :, span]).astype(BF16)
    st_ref[0] = spread(maxima + sums).T[:STATS]


def owner_forward(order, queries, bits, cached_keys, cached_values, scale):
    segments, rows, width = queries.shape
    mem_dev = cached_keys.shape[1]
    active = order.shape[0]
    picked = lambda a, o: (o[a], 0, 0)
    return pl.pallas_call(
        functools.partial(owner_forward_kernel, scale),
        grid_spec=pltpu.PrefetchScalarGridSpec(
            num_scalar_prefetch=1,
            grid=(active,),
            in_specs=[
                pl.BlockSpec((1, rows, width), picked),
                pl.BlockSpec((1, rows, 128), picked),
                pl.BlockSpec((1, mem_dev, width), picked),
                pl.BlockSpec((1, mem_dev, width), picked),
            ],
            out_specs=[
                pl.BlockSpec((1, rows, width), picked),
                pl.BlockSpec((1, STATS, rows), picked),
            ],
            scratch_shapes=[pltpu.VMEM((rows, mem_dev), F32)],
        ),
        out_shape=[
            jax.ShapeDtypeStruct((segments, rows, width), BF16),
            jax.ShapeDtypeStruct((segments, STATS, rows), F32),
        ],
        compiler_params=params(),
        name="owner_forward",
    )(order, queries, bits, cached_keys, cached_values)


def owner_backward_kernel(
    scale, order_ref, q_ref, g_ref, st_ref, bits_ref, k_ref, v_ref, dq_ref, bias_ref
):
    del order_ref
    fill_bias(bits_ref, bias_ref)
    stats = columns_of(st_ref[0])
    for h in range(HEADS):
        span = slice(h * 128, (h + 1) * 128)
        scores = dot(q_ref[0, :, span], k_ref[0, :, span], NT) * scale + bias_ref[...]
        weights = jnp.exp2(scores - stats[:, h : h + 1])
        dweights = dot(g_ref[0, :, span], v_ref[0, :, span], NT)
        dscore = weights * (dweights - stats[:, HEADS + h : HEADS + h + 1])
        dq_ref[0, :, span] = (
            dot(dscore.astype(BF16), k_ref[0, :, span]) * (scale / LOG2E)
        ).astype(BF16)


def owner_backward(order, queries, grads, stats, bits, cached_keys, cached_values, scale):
    segments, rows, width = queries.shape
    mem_dev = cached_keys.shape[1]
    active = order.shape[0]
    picked = lambda a, o: (o[a], 0, 0)
    return pl.pallas_call(
        functools.partial(owner_backward_kernel, scale),
        grid_spec=pltpu.PrefetchScalarGridSpec(
            num_scalar_prefetch=1,
            grid=(active,),
            in_specs=[
                pl.BlockSpec((1, rows, width), picked),
                pl.BlockSpec((1, rows, width), picked),
                pl.BlockSpec((1, STATS, rows), picked),
                pl.BlockSpec((1, rows, 128), picked),
                pl.BlockSpec((1, mem_dev, width), picked),
                pl.BlockSpec((1, mem_dev, width), picked),
            ],
            out_specs=pl.BlockSpec((1, rows, width), picked),
            scratch_shapes=[pltpu.VMEM((rows, mem_dev), F32)],
        ),
        out_shape=jax.ShapeDtypeStruct((segments, rows, width), BF16),
        compiler_params=params(),
        name="owner_backward",
    )(order, queries, grads, stats, bits, cached_keys, cached_values)


def causal_bias(place, rows, keys):
    row = place * rows + lax.broadcasted_iota(jnp.int32, (rows, keys), 0)
    return jnp.where(lax.broadcasted_iota(jnp.int32, (rows, keys), 1) <= row, 0.0, FLOOR)


def columns_at(kv_ref, span):
    block = kv_ref[:, span] if len(kv_ref.shape) == 2 else kv_ref[:, :, span]
    return block.reshape(-1, block.shape[-1])


def local_forward_steps(scale, place, q_ref, kv_ref, o_ref, st_ref, bias_ref):
    rows, width = q_ref.shape
    bias_ref[...] = causal_bias(place, rows, bias_ref.shape[1])
    maxima, sums = [], []
    for h in range(HEADS):
        span, over = slice(h * 128, (h + 1) * 128), slice(width + h * 128, width + (h + 1) * 128)
        scores = dot(q_ref[:, span], columns_at(kv_ref, span), NT) * scale + bias_ref[...]
        top = jnp.max(scores, axis=1, keepdims=True)
        weights = jnp.exp2(scores - top)
        maxima.append(top)
        sums.append(jnp.sum(weights, axis=1, keepdims=True))
        o_ref[:, span] = dot(weights.astype(BF16), columns_at(kv_ref, over))
        yield
    st_ref[...] = spread(maxima + sums).T[:STATS]


def local_backward_steps(
    scale, place, q_ref, g_ref, st_ref, kv_ref, dq_ref, dkv_ref, bias_ref
):
    rows, width = q_ref.shape
    bias_ref[...] = causal_bias(place, rows, bias_ref.shape[1])
    stats = columns_of(st_ref[...])
    for h in range(HEADS):
        span, over = slice(h * 128, (h + 1) * 128), slice(width + h * 128, width + (h + 1) * 128)
        query, key, grad = q_ref[:, span], columns_at(kv_ref, span), g_ref[:, span]
        scores = dot(query, key, NT) * scale + bias_ref[...]
        weights = jnp.exp2(scores - stats[:, h : h + 1])
        dweights = dot(grad, columns_at(kv_ref, over), NT)
        dscore = (weights * (dweights - stats[:, HEADS + h : HEADS + h + 1])).astype(BF16)
        dq_ref[:, span] = dot(dscore, key) * (scale / LOG2E)
        dkey = (dot(dscore, query, TN) * (scale / LOG2E)).astype(BF16)
        dvalue = dot(weights.astype(BF16), grad, TN).astype(BF16)
        lead = dkv_ref.shape[:-1]
        dkv_ref[(*[slice(None)] * len(lead), span)] = dkey.reshape(lead + (128,))
        dkv_ref[(*[slice(None)] * len(lead), over)] = dvalue.reshape(lead + (128,))
        yield


class OwnerBackward(OwnerForward):
    def __init__(self, net, scale, parts, stats_part, ins, outs, scratch, sems):
        self.sources_in = ins
        self.grads, self.stats, peers = outs
        *self.buffers, self.bias, far, held, twin = scratch
        self.loads, *sems = sems
        self.far = [far]
        Return.__init__(self, net, self.far, [peers], [held, twin, *sems])
        self.parts, self.scale, self.stats_part = [*parts, stats_part], scale, stats_part

    def bring(self, z, far):
        segment = 2 * z + (1 - self.net.c if far else self.net.c)
        sources = [source.at[segment] for source in (*self.sources_in, self.grads)]
        return [
            pltpu.make_async_copy(source, buffer, self.loads.at[i])
            for i, (source, buffer) in enumerate(zip(sources, self.buffers))
        ]

    def mask(self, z, far):
        if far:
            for part in self.parts:
                part.wait_core(z)
        for copy in self.bring(z, far):
            copy.start()

    def attend(self, z, far):
        net = self.net
        for copy in self.bring(z, far):
            copy.wait()
        keys, values, queries, bits, grads = self.buffers
        fill_bias(bits, self.bias)
        segment = 2 * z + (1 - net.c if far else net.c)
        owner_backward_heads(
            self.scale,
            queries,
            grads,
            self.stats.at[segment],
            keys,
            values,
            self.bias,
            (self.far[0] if far else self.held[0]).at[z],
        )
        if far:
            self.pairing(0, z).start()

    def chain(self):
        net = self.net
        for k in range(net.line):
            for from_left in (True, False) if k else (True,):
                z = net.z - k if from_left else net.z + k
                present = z >= 0 if from_left else z < net.line
                here = (lambda body: body()) if k == 0 else pl.when(present)
                self.need(k, from_left)
                if k == 0:
                    for part in self.parts:
                        part.wait_own()
                here(lambda: self.mask(z, True))
                yield
                here(lambda: self.attend(z, True))
                here(lambda: self.mask(z, False))
                yield
                here(lambda: self.attend(z, False))
                yield
                here(lambda: self.home(k, z))
                yield


def backward_job(
    sizes, queries, grads, stats, segment_kv, all_queries, bits, cached_keys, cached_values, scale
):
    square, line = sizes["seq"], sizes["mem"] // 2
    segments, rows, width = all_queries.shape
    mem_dev = cached_keys.shape[1]
    length = square * rows
    shape = jax.ShapeDtypeStruct
    outs = [
        shape((segments, rows, width), BF16),
        shape((line, rows, width), BF16),
        shape((rows, width), F32),
        shape((PIECES, rows // PIECES, 2 * width), F32),
    ]
    keys_scratch = scatter_scratch(PIECES, rows // PIECES, 2 * width, row_halves, False)
    scratch = (
        gather_semaphores(line, PIECES)
        + gather_semaphores(line)
        + [pltpu.VMEM((segments, STATS, rows), F32), pltpu.VMEM((rows, length), F32)]
        + keys_scratch
        + [pltpu.VMEM((mem_dev, width), BF16)] * 2
        + [
            pltpu.VMEM((rows, width), BF16),
            pltpu.VMEM((rows, 128), jnp.int32),
            pltpu.VMEM((rows, width), BF16),
            pltpu.VMEM((rows, mem_dev), F32),
        ]
        + [pltpu.VMEM((line, rows, width), BF16)] * 3
        + [pltpu.SemaphoreType.DMA((5,))]
        + [pltpu.SemaphoreType.DMA((1, line))] * 5
    )

    def steps(net, ins, outs, scratch):
        queries, grads, stats, segment_kv, all_queries, bits, keys, values = ins
        all_grads, peers, local_dq, grad_kv = outs
        scratch = list(scratch)
        take = lambda count: [scratch.pop(0) for _ in range(count)]
        parts = gather_parts(net, grads, all_grads, take(3 * PIECES), row_halves, "line", PIECES)
        stats_sems = take(3)
        all_stats, local_bias = take(2)
        (stats_part,) = gather_parts(net, stats, all_stats, stats_sems, row_halves, "line", 1)
        keys_scratch = take(8)
        buffers = take(9)
        scatter = Scatter(
            net, None, grad_kv, keys_scratch[:5], keys_scratch[5:], row_halves, False
        )
        owner = OwnerBackward(
            net, scale, parts, stats_part, [keys, values, all_queries, bits],
            [all_grads, all_stats, peers], buffers, scratch,
        )
        for part in [*parts, stats_part]:
            part.waits_core = part.waits_own = False

        def local():
            yield from local_backward_steps(
                scale, net.s, queries, grads, stats, segment_kv, local_dq, scatter.held, local_bias
            )
            stages = (scatter.add_core, scatter.add_first, scatter.add_second, scatter.line_step)
            for wave in range(PIECES + 3):
                for lag in (3, 2, 1, 0):
                    if 0 <= wave - lag < PIECES:
                        stages[lag](wave - lag)
                        yield

        chains = [chain for part in [*parts, stats_part] for chain in part.chains()]
        ends = [part.finish for part in [*parts, stats_part]] + [scatter.finish, owner.finish]
        return chains + [local(), owner.chain()], ends

    vmem = pltpu.VMEM
    return Job(
        [queries, grads, stats, segment_kv, all_queries, bits, cached_keys, cached_values],
        outs,
        scratch,
        steps,
        [vmem] * 4 + [pl.ANY] * 4,
        [pl.ANY, pl.ANY, vmem, vmem],
    )


def local_job(kind, arrays, scale):
    rows, width = arrays[0].shape
    length = arrays[-1].shape[0]
    if kind == "forward":
        body, extra = local_forward_steps, jax.ShapeDtypeStruct((STATS, rows), F32)
    else:
        body, extra = local_backward_steps, jax.ShapeDtypeStruct((length, 2 * width), BF16)

    def steps(net, ins, outs, scratch):
        return [body(scale, net.s, *ins, *outs, *scratch)], []

    outs = [jax.ShapeDtypeStruct((rows, width), F32), extra]
    return Job(arrays, outs, [pltpu.VMEM((rows, length), F32)], steps, pltpu.VMEM, pltpu.VMEM)


def alone_kernel(job, *refs):
    place_ref, *refs = refs
    net = type("Alone", (), {"s": place_ref[0]})
    ins, outs = len(job.arrays), len(job.arrays) + len(job.outs)
    for chain in job.steps(net, refs[:ins], refs[ins:outs], refs[outs:])[0]:
        for _ in chain:
            pass


def alone(name, place, job):
    return pl.pallas_call(
        functools.partial(alone_kernel, job),
        out_shape=job.outs,
        in_specs=[pl.BlockSpec(memory_space=pltpu.SMEM)]
        + [pl.BlockSpec(memory_space=pltpu.VMEM)] * len(job.arrays),
        out_specs=[pl.BlockSpec(memory_space=pltpu.VMEM)] * len(job.outs),
        scratch_shapes=job.scratch,
        compiler_params=params(),
        name=name,
    )(place, *job.arrays)


def copy_in(pairs, sems):
    copies = [pltpu.make_async_copy(src, dst, sems.at[i]) for i, (src, dst) in enumerate(pairs)]
    for copy in copies:
        copy.start()
    return copies


def turn(values, cosine, sine):
    return values * cosine + pltpu.roll(values, values.shape[1] // 2, 1) * sine


def inverse_root(values):
    return lax.rsqrt(jnp.mean(values * values, axis=1, keepdims=True) + EPSILON)


def project_kernel(x_ref, w_any, cos_ref, sin_ref, n_ref, q_ref, kv_ref, gain_ref, w_ref, sems):
    width = x_ref.shape[1]
    spans = [slice(i * width, (i + 1) * width) for i in range(3)] + [slice(3 * width, 3 * width + 128)]
    copies = copy_in([(w_any.at[:, s], w_ref.at[:, s]) for s in spans], sems)
    x = x_ref[...].astype(F32)
    copies[3].wait()
    gain_ref[...] = w_ref[:, spans[3]].astype(F32).T[:8]
    normed = (x * inverse_root(x) * gain_ref[:1]).astype(BF16)
    n_ref[...] = normed
    cosine, sine = cos_ref[...], sin_ref[...]
    for i in range(3):
        copies[i].wait()
        product = dot(normed, w_ref[:, spans[i]])
        for h in range(HEADS):
            span = slice(h * 128, (h + 1) * 128)
            part = product[:, span]
            part = part if i == 2 else turn(part, cosine, sine)
            if i == 0:
                q_ref[:, span] = part.astype(BF16)
            else:
                over = slice((i - 1) * width + h * 128, (i - 1) * width + (h + 1) * 128)
                kv_ref[:, over] = part.astype(BF16)


def in_vmem(count):
    return [pl.BlockSpec(memory_space=pltpu.VMEM)] * count


def project(tokens, first_weights, cosine, sine):
    rows, width = tokens.shape
    columns = first_weights.shape[1]
    return pl.pallas_call(
        project_kernel,
        out_shape=[
            jax.ShapeDtypeStruct((rows, width), BF16),
            jax.ShapeDtypeStruct((rows, width), BF16),
            jax.ShapeDtypeStruct((rows, 2 * width), BF16),
            jax.ShapeDtypeStruct((8, width), F32),
        ],
        in_specs=in_vmem(1) + [pl.BlockSpec(memory_space=pl.ANY)] + in_vmem(2),
        out_specs=in_vmem(4),
        scratch_shapes=[
            pltpu.VMEM((width, columns), BF16),
            pltpu.SemaphoreType.DMA((4,)),
        ],
        compiler_params=params(),
        name="project",
    )(tokens, first_weights, cosine, sine)


def middle_kernel(
    live_ref, x_ref, g_ref, gain_ref, lo_ref, ls_ref, po_ref, ps_ref, out_any, gate_any, up_any, down_any,
    mixed_ref, gm_ref, al_ref, n_ref, gml_ref, ga_ref, st_ref, hid_ref, gg_ref, gu_ref, gain_grad_ref,
    att_ref, acc_ref, gn_ref, out_ref, gate_ref, up_ref, down_ref, sems,
):
    rows, width = x_ref.shape
    copies = copy_in(
        [(out_any, out_ref), (gate_any, gate_ref), (up_any, up_ref), (down_any, down_ref)], sems
    )
    live = live_ref[0] > 0
    peers = ps_ref.shape[0]
    local_max, local_sum = ls_ref[:HEADS], ls_ref[HEADS:]
    peer_max = [jnp.where(live, ps_ref[p, :HEADS], LOW) for p in range(peers)]
    peer_sum = [jnp.where(live, ps_ref[p, HEADS:], 0.0) for p in range(peers)]
    top = functools.reduce(jnp.maximum, peer_max, local_max)
    shares = [jnp.exp2(m - top) for m in [local_max] + peer_max]
    total = functools.reduce(
        jnp.add, [s * t for s, t in zip(shares, [local_sum] + peer_sum)]
    )
    log_total = top + jnp.log2(total)
    shares = columns_of(jnp.concatenate([s / total for s in shares], axis=0))
    for h in range(HEADS):
        span = slice(h * 128, (h + 1) * 128)
        part = lo_ref[:, span] * shares[:, h : h + 1]
        for p in range(peers):
            column = shares[:, (p + 1) * HEADS + h : (p + 1) * HEADS + h + 1]
            part += jnp.where(live, po_ref[p, :, span].astype(F32), 0.0) * column
        att_ref[:, span] = part
    attention_low = att_ref[...].astype(BF16)
    al_ref[...] = attention_low
    copies[0].wait()
    mid = x_ref[...].astype(F32) + dot(attention_low, out_ref[...])
    gm_ref[...] = mid
    root = inverse_root(mid)
    n_ref[...] = (mid * root * gain_ref[1:2]).astype(BF16)
    for copy in copies[1:]:
        copy.wait()
    grad = g_ref[...]
    acc_ref[...] = jnp.zeros_like(acc_ref)
    gn_ref[...] = jnp.zeros_like(gn_ref)
    hidden_width = gate_ref.shape[1]
    step = 256
    for start in range(0, hidden_width, step):
        span = slice(start, min(start + step, hidden_width))
        norm_two = n_ref[...]
        gate = dot(norm_two, gate_ref[:, span])
        upward = dot(norm_two, up_ref[:, span])
        grad_hidden = dot(grad, down_ref[span, :], NT)
        sigmoid = 1.0 / (1.0 + jnp.exp(-gate))
        silu = gate * sigmoid
        hidden = (silu * upward).astype(BF16)
        grad_gate = (grad_hidden * upward * (sigmoid * (1.0 + gate * (1.0 - sigmoid)))).astype(BF16)
        grad_up = (grad_hidden * silu).astype(BF16)
        hid_ref[:, span] = hidden
        gg_ref[:, span] = grad_gate
        gu_ref[:, span] = grad_up
        acc_ref[...] += dot(hidden, down_ref[span, :])
        gn_ref[...] += dot(grad_gate, gate_ref[:, span], NT) + dot(grad_up, up_ref[:, span], NT)
    mid = gm_ref[...]
    mixed_ref[...] = mid + acc_ref[...]
    normed = mid * root
    grad_norm = gn_ref[...]
    gain_grad_ref[...] = jnp.broadcast_to(
        jnp.sum(grad_norm * normed, axis=0, keepdims=True), gain_grad_ref.shape
    )
    scaled = grad_norm * gain_ref[1:2]
    grad_mid = grad.astype(F32) + root * (
        scaled - normed * jnp.mean(normed * scaled, axis=1, keepdims=True)
    )
    gm_ref[...] = grad_mid
    grad_mid_low = grad_mid.astype(BF16)
    gml_ref[...] = grad_mid_low
    grad_attention = dot(grad_mid_low, out_ref[...], NT).astype(BF16)
    ga_ref[...] = grad_attention
    products = grad_attention.astype(F32) * att_ref[...]
    dots = [
        jnp.sum(products[:, h * 128 : (h + 1) * 128], axis=1, keepdims=True) for h in range(HEADS)
    ]
    st_ref[...] = jnp.concatenate([log_total, spread(dots).T[:HEADS]], axis=0)


def middle(live, tokens, grads, gains, local, peers, weights):
    rows, width = tokens.shape
    hidden_width = weights[1].shape[1]
    full = lambda columns, kind: jax.ShapeDtypeStruct((rows, columns), kind)
    return pl.pallas_call(
        middle_kernel,
        out_shape=[
            full(width, F32),
            full(width, F32),
            full(width, BF16),
            full(width, BF16),
            full(width, BF16),
            full(width, BF16),
            jax.ShapeDtypeStruct((STATS, rows), F32),
            full(hidden_width, BF16),
            full(hidden_width, BF16),
            full(hidden_width, BF16),
            jax.ShapeDtypeStruct((8, width), F32),
        ],
        in_specs=[pl.BlockSpec(memory_space=pltpu.SMEM)]
        + in_vmem(7)
        + [pl.BlockSpec(memory_space=pl.ANY)] * 4,
        out_specs=in_vmem(11),
        scratch_shapes=[pltpu.VMEM((rows, width), F32)] * 3
        + [pltpu.VMEM(w.shape, BF16) for w in weights]
        + [pltpu.SemaphoreType.DMA((4,))],
        compiler_params=params(),
        name="middle",
    )(live, tokens, grads, gains, *local, *peers, *weights)


def final_kernel(
    live_ref, x_ref, gm_ref, gain_ref, ggain_ref, n_ref, dq_ref, pd_ref, dkv_ref, cos_ref, sin_ref, w_any,
    gx_ref, late_ref, in_ref, w_ref, sems,
):
    rows, width = x_ref.shape
    copies = copy_in([(w_any.at[:, : 3 * width], w_ref)], sems)
    live = live_ref[0] > 0
    cosine, sine = cos_ref[...], -sin_ref[...]
    for h in range(HEADS):
        span = slice(h * 128, (h + 1) * 128)
        part = dq_ref[:, span]
        for p in range(pd_ref.shape[0]):
            part += jnp.where(live, pd_ref[p, :, span].astype(F32), 0.0)
        in_ref[:, span] = turn(part, cosine, sine).astype(BF16)
        over = slice(width + h * 128, width + (h + 1) * 128)
        in_ref[:, over] = turn(dkv_ref[:, span], cosine, sine).astype(BF16)
    in_ref[:, 2 * width :] = dkv_ref[:, width:].astype(BF16)
    normed_low = n_ref[...]
    for i in range(3):
        span = slice(i * width, (i + 1) * width)
        late_ref[:, span] = dot(normed_low, in_ref[:, span], TN).astype(BF16)
    copies[0].wait()
    grad_norm = dot(in_ref[...], w_ref[...], NT)
    x = x_ref[...].astype(F32)
    root = inverse_root(x)
    normed = x * root
    gains = jnp.concatenate(
        [
            jnp.sum(grad_norm * normed, axis=0, keepdims=True),
            ggain_ref[:1],
            jnp.zeros((126, width), F32),
        ],
        axis=0,
    )
    late_ref[:, 3 * width :] = gains.T.astype(BF16)
    scaled = grad_norm * gain_ref[:1]
    gx_ref[...] = gm_ref[...] + root * (
        scaled - normed * jnp.mean(normed * scaled, axis=1, keepdims=True)
    )


def final(live, *arrays):
    rows, width = arrays[0].shape
    columns = arrays[-1].shape[1]
    return pl.pallas_call(
        final_kernel,
        out_shape=[
            jax.ShapeDtypeStruct((rows, width), F32),
            jax.ShapeDtypeStruct((width, columns), BF16),
        ],
        in_specs=[pl.BlockSpec(memory_space=pltpu.SMEM)]
        + in_vmem(len(arrays) - 1)
        + [pl.BlockSpec(memory_space=pl.ANY)],
        out_specs=in_vmem(2),
        scratch_shapes=[
            pltpu.VMEM((rows, 3 * width), BF16),
            pltpu.VMEM((width, 3 * width), BF16),
            pltpu.SemaphoreType.DMA((1,)),
        ],
        compiler_params=params(),
        name="final",
    )(live, *arrays)


REACH = {"all": ("seq", "mem"), "line": "mem", "square": "seq"}


def gather_plain(array, reach):
    return lax.all_gather(array, REACH[reach], axis=0)


def scatter_plain(array, reach):
    return lax.psum_scatter(array, REACH[reach], scatter_dimension=0, tiled=True).astype(F32)


def return_plain(array):
    return lax.all_to_all(array, "mem", split_axis=0, concat_axis=0, tiled=True)


def join_peers(outs, stats):
    top = jnp.max(stats[:, :HEADS], axis=0)
    shares = jnp.exp2(stats[:, :HEADS] - top)
    total = jnp.sum(stats[:, HEADS:] * shares, axis=0)
    wide = jnp.repeat(jnp.swapaxes(shares, 1, 2), outs.shape[-1] // HEADS, axis=2)
    joined = jnp.sum(outs.astype(F32) * wide, axis=0).astype(BF16)
    return joined[None], jnp.concatenate([top, total], axis=0)[None]


def per_device(
    sizes,
    tokens,
    cached_keys,
    cached_values,
    knn_index,
    has_memory,
    w_query,
    w_key,
    w_value,
    w_out,
    gain_attn,
    w_gate,
    w_up,
    w_down,
    gain_ffn,
    cotangent,
):
    near = sizes["seq"] == 4 and sizes["mem"] % 2 == 0 and 4 <= sizes["mem"] <= 16
    inputs, grad_out = tokens[0], cotangent[0]
    rows, width = inputs.shape
    hidden_width = w_gate.shape[1]
    head_width = width // HEADS
    scale = head_width ** (-0.5) * LOG2E
    mem_dev = cached_keys.shape[1]
    place = lax.axis_index("seq").astype(jnp.int32)[None]
    base = (lax.axis_index("mem") * mem_dev).astype(jnp.int32)[None]

    gains = jnp.concatenate(
        [gain_attn[:, None], gain_ffn[:, None], jnp.zeros((w_query.shape[0], 126), BF16)], axis=1
    )
    first_shard = jnp.concatenate([w_query, w_key, w_value, gains], axis=1)
    flag_rows = jnp.broadcast_to(has_memory[:, None], (8, 128))
    index_shard = jnp.concatenate([knn_index[0], flag_rows], axis=0)
    if near:
        jobs = [
            gather_job(sizes, index_shard, row_halves, "line"),
            gather_job(sizes, first_shard, row_halves, "all"),
        ]
        (shared,), (first_weights,) = together(1, "first", sizes, jobs)
    else:
        first_weights, shared = gather_plain(first_shard, "all"), gather_plain(index_shard, "line")
    first_weights = first_weights.reshape(-1, first_shard.shape[1])
    all_index, flags = shared[:, :rows], shared[:, rows, 0]
    segments = flags.shape[0]
    order = jnp.argsort(jnp.where(flags > 0, 0, 1), stable=True)[: segments // 2].astype(jnp.int32)

    positions = lax.axis_index("seq") * rows + jnp.arange(rows)
    cosine, sine = angles_for(positions, head_width)
    cosine = jnp.concatenate([cosine, cosine], axis=1)
    sine = jnp.concatenate([-sine, sine], axis=1)
    norm_one, queries, keys_values, gain_rows = project(inputs, first_weights, cosine, sine)
    if near:
        jobs = [
            forward_job(
                sizes, queries, keys_values, all_index, cached_keys, cached_values, scale
            ),
            gather_job(sizes, w_out, row_halves, "all"),
            gather_job(sizes, w_gate, row_halves, "all"),
            gather_job(sizes, w_up, row_halves, "all"),
            gather_job(sizes, w_down, column_halves, "all"),
        ]
        results, (out_weight,), (gate_weight,), (up_weight,), (down_weight,) = together(
            2, "second", sizes, jobs
        )
        all_queries, segment_kv, bits, *peers = results[:5]
        local = results[5:]
        segment_kv = segment_kv.reshape(-1, 2 * width)
    else:
        all_queries = gather_plain(queries, "line")
        segment_kv = gather_plain(keys_values, "square").reshape(-1, 2 * width)
        bits = mask_bits(base, all_index, mem_dev)
        owner_out, owner_stats = owner_forward(
            order, all_queries, bits, cached_keys, cached_values, scale
        )
        peers = join_peers(return_plain(owner_out), return_plain(owner_stats))
        local = alone("local_forward", place, local_job("forward", [queries, segment_kv], scale))
        out_weight, gate_weight = gather_plain(w_out, "all"), gather_plain(w_gate, "all")
        up_weight, down_weight = gather_plain(w_up, "all"), gather_plain(w_down, "all")
    weights = [
        out_weight.reshape(width, width),
        gate_weight.reshape(width, hidden_width),
        up_weight.reshape(width, hidden_width),
        down_weight.reshape(hidden_width, width),
    ]
    (
        mixed,
        grad_mid,
        attention_low,
        norm_two,
        grad_mid_low,
        grad_attention,
        back_stats,
        hidden,
        grad_gate,
        grad_upward,
        gain_two_grad,
    ) = middle(has_memory, inputs, grad_out, gain_rows, local, peers, weights)
    early = [
        dot(attention_low, grad_mid_low, TN).astype(BF16),
        dot(norm_two, grad_gate, TN).astype(BF16),
        dot(norm_two, grad_upward, TN).astype(BF16),
        dot(hidden, grad_out, TN).astype(BF16),
    ]
    if near:
        jobs = [
            backward_job(
                sizes, queries, grad_attention, back_stats, segment_kv,
                all_queries, bits, cached_keys, cached_values, scale,
            ),
            *[scatter_job(sizes, grad, row_halves) for grad in early[:3]],
            scatter_job(sizes, early[3], column_halves),
        ]
        (_, peer_grads, local_dq, grad_kv), *early_sums = together(3, "third", sizes, jobs)
        grad_kv = grad_kv.reshape(rows, 2 * width)
        early_sums = [total for (total,) in early_sums]
    else:
        all_grads, all_stats = gather_plain(grad_attention, "line"), gather_plain(back_stats, "line")
        local_work = local_job(
            "backward", [queries, grad_attention, back_stats, segment_kv], scale
        )
        local_dq, local_dkv = alone("local_backward", place, local_work)
        owner_grads = owner_backward(
            order, all_queries, all_grads, all_stats, bits, cached_keys, cached_values, scale
        )
        peer_grads = jnp.sum(return_plain(owner_grads).astype(F32), axis=0, keepdims=True)
        grad_kv = scatter_plain(local_dkv, "square")
        early_sums = [scatter_plain(grad, "all") for grad in early]
    grad_inputs, late = final(
        has_memory, inputs, grad_mid, gain_rows, gain_two_grad, norm_one, local_dq, peer_grads, grad_kv,
        cosine, sine, first_weights,
    )
    if near:
        ((late_sum,),) = together(4, "fourth", sizes, [scatter_job(sizes, late, row_halves)])
    else:
        late_sum = scatter_plain(late, "all")
    return (
        mixed[None],
        grad_inputs[None],
        late_sum[:, :width],
        late_sum[:, width : 2 * width],
        late_sum[:, 2 * width : 3 * width],
        early_sums[0],
        late_sum[:, 3 * width],
        early_sums[1],
        early_sums[2],
        early_sums[3],
        late_sum[:, 3 * width + 1],
    )


def solution(mesh):
    rows, owned, feature = P("mem", "seq", None), P(None, "mem", None), P(("seq", "mem"), None)
    gain = P(("seq", "mem"))
    return jax.shard_map(
        functools.partial(per_device, dict(mesh.shape)),
        mesh=mesh,
        in_specs=(
            (rows, owned, owned, rows, P("mem"))
            + (feature,) * 4
            + (gain,)
            + (feature,) * 3
            + (gain, rows)
        ),
        out_specs=(rows, rows) + (feature,) * 4 + (gain,) + (feature,) * 3 + (gain,),
        check_vma=False,
    )
```

```python
import functools

import jax
import jax.numpy as jnp
from jax import lax
from jax.experimental import pallas as pl
from jax.experimental.pallas import tpu as pltpu
from jax.sharding import PartitionSpec as P

HEADS = 8
EPSILON = 1e-05
FLOOR = -1e30
LOW = -1e29
LOG2E = 1.4426950408889634
STATS = 16
PIECES = 4
SPANS = [(0, 4), (4, 8)]
ORDERS = {
    ("first", 4): (
        8, 0, 7, 9, 10, 7, 2, 9, 1, 7, 8, 11, 12, 7, 10, 7, 4, 3, 7, 9, 7, 8, 11, 7, 12, 14, 13,
        7, 7, 5, 14, 7, 15, 13, 10, 15, 11, 7, 13, 6, 12, 15, 7, 15, 15, 16, 16, 16, 16, 16, 16,
        14, 7, 16, 16, 16,
    ),
    ("second", 4): (
        30, 37, 30, 7, 0, 44, 14, 51, 21, 9, 28, 29, 31, 29, 8, 29, 30, 29, 29, 33, 38, 1, 29, 15,
        46, 22, 39, 29, 32, 35, 28, 11, 29, 29, 16, 29, 23, 13, 33, 34, 45, 17, 2, 29, 19, 29, 60,
        10, 29, 41, 3, 29, 29, 24, 29, 29, 47, 60, 29, 29, 32, 29, 31, 52, 28, 40, 29, 29, 49, 51,
        28, 29, 12, 62, 63, 4, 18, 29, 25, 48, 53, 29, 59, 29, 32, 40, 29, 29, 38, 5, 58, 6, 44,
        39, 54, 29, 28, 28, 29, 26, 35, 58, 37, 29, 27, 42, 29, 28, 29, 53, 29, 47, 61, 31, 35,
        28, 34, 61, 28, 56, 33, 36, 61, 54, 41, 28, 51, 45, 39, 50, 20, 29, 52, 46, 29, 60, 29,
        40, 54, 29, 47, 55, 50, 34, 42, 29, 37, 38, 28, 43, 56, 59, 61, 44, 29, 45, 64, 29, 58,
        52, 36, 64, 59, 29, 64, 43, 55, 42, 64, 49, 57, 59, 56, 36, 67, 65, 53, 60, 67, 50, 67,
        65, 49, 57, 64, 46, 48, 55, 41, 43, 63, 64, 67, 65, 58, 67, 67, 65, 57, 67, 64, 63, 48,
        65, 58, 62, 64, 60, 61, 59, 65, 65, 63, 67, 67, 65, 64, 65, 66, 66, 66, 66, 66, 66, 66,
        66, 66,
    ),
    ("third", 4): (
        21, 40, 50, 14, 28, 35, 40, 37, 50, 7, 0, 45, 35, 42, 23, 39, 49, 35, 36, 45, 30, 51, 40,
        38, 35, 49, 22, 41, 16, 8, 36, 9, 41, 1, 44, 35, 36, 38, 10, 35, 39, 25, 2, 49, 43, 37, 3,
        29, 36, 18, 24, 50, 51, 15, 27, 48, 41, 36, 49, 45, 4, 39, 38, 36, 37, 49, 26, 31, 47, 36,
        35, 44, 50, 51, 20, 50, 36, 36, 46, 45, 11, 45, 35, 42, 36, 40, 48, 36, 5, 37, 52, 36, 17,
        36, 40, 39, 53, 46, 44, 41, 35, 39, 12, 36, 36, 51, 37, 56, 51, 53, 47, 38, 56, 42, 41,
        36, 36, 36, 44, 36, 35, 35, 19, 36, 54, 36, 48, 32, 46, 63, 52, 36, 38, 36, 36, 36, 36,
        36, 62, 42, 33, 42, 43, 63, 53, 36, 55, 35, 36, 54, 61, 36, 48, 52, 36, 36, 35, 44, 35,
        52, 6, 56, 35, 46, 34, 48, 61, 43, 40, 36, 56, 57, 57, 36, 36, 57, 46, 60, 54, 55, 13, 36,
        36, 54, 35, 36, 47, 36, 35, 43, 43, 36, 60, 47, 35, 36, 47, 58, 58, 61, 60, 36, 35, 53,
        55, 35, 63, 35, 35, 58, 57, 62, 55, 58, 59, 60, 62, 53, 62, 35, 54, 52, 44, 61, 63, 35,
        55, 52, 56, 48, 59, 59, 57, 59,
    ),
    ("fourth", 4): (
        0, 0, 1, 2, 0, 2, 3, 0, 0, 2, 1, 2, 2, 1, 3, 4, 1, 1, 3, 4, 4, 4, 3, 3, 3,
    ),
}
F32 = jnp.float32
BF16 = jnp.bfloat16
VMEM_LIMIT = 62 * 1024 * 1024
NT = (((1,), (1,)), ((), ()))
TN = (((0,), (0,)), ((), ()))


def dot(left, right, dims=(((1,), (0,)), ((), ()))):
    return lax.dot_general(left, right, dims, preferred_element_type=F32)


def angles_for(positions, head_width):
    exponent = jnp.arange(head_width // 2, dtype=F32) * (2.0 / head_width)
    frequency = jnp.power(10000.0, -exponent)
    turned = positions.astype(F32)[:, None] * frequency[None, :]
    return (jnp.cos(turned), jnp.sin(turned))


def params(**more):
    return pltpu.CompilerParams(vmem_limit_bytes=VMEM_LIMIT, **more)


def spread(columns, width=128):
    lanes = lax.broadcasted_iota(jnp.int32, (columns[0].shape[0], width), 1)
    result = jnp.zeros((columns[0].shape[0], width), F32)
    for place, column in enumerate(columns):
        result = jnp.where(lanes == place, column, result)
    return result


def columns_of(rows_by_stat):
    count, width = rows_by_stat.shape
    padded = jnp.concatenate([rows_by_stat, jnp.zeros((128 - count, width), F32)], axis=0)
    return padded.T


MESH = pl.DeviceIdType.MESH


class Net:
    def __init__(self, line):
        self.line = line
        self.s, self.m = lax.axis_index("seq"), lax.axis_index("mem")
        self.c, self.z = self.m % 2, self.m // 2
        self.x, self.y, self.core = (self.s ^ 1, self.m), (self.s ^ 2, self.m), (self.s, self.m ^ 1)
        self.right = (self.s, (self.m + 2) % (2 * line))
        self.left = (self.s, (self.m + 2 * line - 2) % (2 * line))

    def others(self):
        ring = 2 * self.line
        return [(self.s, lax.rem(self.m + 2 * k, ring)) for k in range(1, self.line)]

    def greet(self, others):
        barrier = pltpu.get_barrier_semaphore()
        for other in others:
            pl.semaphore_signal(barrier, inc=1, device_id=other, device_id_type=MESH)
        pl.semaphore_wait(barrier, len(others))


def remote(src, dst, sends, recvs, place, device):
    return pltpu.make_async_remote_copy(
        src_ref=src,
        dst_ref=dst,
        send_sem=sends.at[place],
        recv_sem=recvs.at[place],
        device_id=device,
        device_id_type=MESH,
    )


def row_halves(ref, part):
    half = ref.shape[-2] // 2
    return ref.at[pl.ds(part * half, half)]


def column_halves(ref, part):
    half = ref.shape[-1] // 2
    return ref.at[:, pl.ds(part * half, half)]


class Gather:
    def __init__(self, net, src, out, sends, recvs, own, index, halves, line=True, square=True, core=True):
        self.net, self.src, self.out, self.sends, self.recvs, self.own = net, src, out, sends, recvs, own
        self.index, self.halves = index, halves
        self.line, self.square, self.core = line, square, core
        self.waits_core, self.waits_own, self.seen = True, True, set()

    def slot(self, s, z):
        return self.out.at[self.index(s, z, self.net.c)]

    def wait_own(self):
        pltpu.make_async_copy(self.src, self.slot(self.net.s, self.net.z), self.own).wait()

    def wait_core(self, z):
        place = self.places()[3] + z
        self.arrived(self.out.at[self.index(self.net.s, z, 1 - self.net.c)], place)

    def send(self, block, target, place, device):
        copy = remote(block, target, self.sends, self.recvs, place, device)
        copy.start()

    def sent(self, block, place):
        remote(block, block, self.sends, self.recvs, place, self.net.core).wait_send()

    def arrived(self, block, place):
        remote(block, block, self.sends, self.recvs, place, self.net.core).wait_recv()

    def places(self):
        z = self.net.line
        right, left, square, core = 0, z, 2 * z, 8 * z
        return right, left, square, core

    def chain(self, k, from_left):
        net = self.net
        z = net.z - k if from_left else net.z + k
        present = z >= 0 if from_left else z < net.line
        self.seen.add((k, from_left))
        for stage in (self.have, self.pass_square, self.end_square) if self.square else (self.have,):
            if k == 0:
                stage(0, net.z, None)
            else:
                pl.when(present)(lambda stage=stage: stage(k, z, from_left))
            yield

    def chains(self):
        chains = [self.chain(0, True)]
        for k in range(1, self.net.line if self.line else 1):
            chains += [self.chain(k, True), self.chain(k, False)]
        return chains

    def have(self, k, z, from_left):
        net = self.net
        right, left, square, core = self.places()
        target = self.slot(net.s, z)
        block = self.src if k == 0 else target
        if k == 0:
            pltpu.make_async_copy(self.src, target, self.own).start()
        else:
            self.arrived(target, (right if from_left else left) + z)
        if self.line:
            if from_left is not False:
                pl.when(net.z < net.line - 1)(lambda: self.send(block, target, right + z, net.right))
            if from_left is not True:
                pl.when(net.z > 0)(lambda: self.send(block, target, left + z, net.left))
        if self.square:
            for kind, part, device in ((0, 0, net.x), (2, 1, net.y), (1, 0, net.y), (3, 1, net.x)):
                self.send(
                    self.halves(block, part),
                    self.halves(target, part),
                    square + kind * net.line + z,
                    device,
                )
        if self.core:
            self.send(block, target, core + z, net.core)

    def pass_square(self, k, z, from_left):
        net = self.net
        _, _, square, core = self.places()
        for kind, part, other, then, device, mirror in (
            (0, 0, net.s ^ 1, 4, net.y, 1),
            (2, 1, net.s ^ 2, 5, net.x, 2),
        ):
            block = self.halves(self.slot(other, z), part)
            self.arrived(block, square + kind * net.line + z)
            self.send(block, block, square + then * net.line + z, device)
            if self.core:
                self.send(block, block, core + mirror * net.line + z, net.core)

    def end_square(self, k, z, from_left):
        net = self.net
        _, _, square, core = self.places()
        for kind, part, other, mirror in self.last(net):
            block = self.halves(self.slot(other, z), part)
            self.arrived(block, square + kind * net.line + z)
            if self.core:
                self.send(block, block, core + mirror * net.line + z, net.core)

    def last(self, net):
        return (
            (1, 0, net.s ^ 2, 3),
            (3, 1, net.s ^ 1, 5),
            (4, 0, net.s ^ 3, 4),
            (5, 1, net.s ^ 3, 6),
        )

    def closing(self):
        net = self.net
        right, left, square, core = self.places()
        own = self.slot(net.s, net.z)
        half = [self.halves(own, 0), self.halves(own, 1)] if self.square else []
        for z in range(net.line) if self.line else [net.z]:
            if self.core:
                for mirror, part, other in (
                    (0, None, net.s),
                    (1, 0, net.s ^ 1),
                    (2, 1, net.s ^ 2),
                    (3, 0, net.s ^ 2),
                    (4, 0, net.s ^ 3),
                    (5, 1, net.s ^ 1),
                    (6, 1, net.s ^ 3),
                ):
                    if part is not None and not self.square:
                        continue
                    block = self.out.at[self.index(other, z, 1 - net.c)]
                    block = block if part is None else self.halves(block, part)
                    if self.waits_core:
                        self.arrived(block, core + mirror * net.line + z)
                    self.sent(block, core + mirror * net.line + z)
                yield
            if self.square:
                for kind, part in ((0, 0), (1, 0), (2, 1), (3, 1), (4, 0), (5, 1)):
                    self.sent(half[part], square + kind * net.line + z)
                yield
            if self.line:
                pl.when((z <= net.z) & (net.z < net.line - 1))(lambda: self.sent(own, right + z))
                pl.when((z >= net.z) & (net.z > 0))(lambda: self.sent(own, left + z))
        if self.waits_own:
            self.wait_own()
        yield


class Job:
    def __init__(self, arrays, outs, scratch, steps, where=pl.ANY, out_where=pl.ANY):
        self.arrays, self.outs, self.scratch, self.steps = arrays, outs, scratch, steps
        self.where, self.out_where = where, out_where


def specs(where, arrays):
    places = where if isinstance(where, list) else [where] * len(arrays)
    return [pl.BlockSpec(memory_space=place) for place in places]


def together_kernel(line, jobs, order, *refs):
    refs = list(refs)
    take = lambda count: [refs.pop(0) for _ in range(count)]
    ins = [take(len(job.arrays)) for job in jobs]
    outs = [take(len(job.outs)) for job in jobs]
    scratch = [take(len(job.scratch)) for job in jobs]
    net = Net(line)
    net.greet([net.x, net.y, net.core] + net.others())
    chains, ends = [], []
    for job, *parts in zip(jobs, ins, outs, scratch):
        more, last = job.steps(net, *parts)
        chains += more
        ends += last
    for turn in order:
        next((chains + ends)[turn], None)
    while chains:
        chains = [chain for chain in chains if next(chain, True) is None]
    for end in ends:
        for _ in end:
            pass


def together(collective_id, name, sizes, jobs):
    line = sizes["mem"] // 2
    moved = sum(2 * a.size * a.dtype.itemsize for job in jobs for a in job.arrays)
    results = pl.pallas_call(
        functools.partial(together_kernel, line, jobs, ORDERS.get((name, line), ())),
        out_shape=[out for job in jobs for out in job.outs],
        in_specs=[s for job in jobs for s in specs(job.where, job.arrays)],
        out_specs=[s for job in jobs for s in specs(job.out_where, job.outs)],
        scratch_shapes=[s for job in jobs for s in job.scratch],
        compiler_params=params(collective_id=collective_id, has_side_effects=True),
        cost_estimate=pl.CostEstimate(flops=0, bytes_accessed=moved, transcendentals=0),
        name=name,
    )(*[a for job in jobs for a in job.arrays])
    results = list(results)
    return [[results.pop(0) for _ in job.outs] for job in jobs]


def gather_parts(net, src, out, scratch, halves, reach, pieces):
    line, rows = net.line, src.shape[0] // pieces
    index = {
        "all": lambda s, z, c: (s * line + z) * 2 + c,
        "line": lambda s, z, c: z * 2 + c,
        "square": lambda s, z, c: s,
    }[reach]
    parts = []
    for i in range(pieces):
        span = pl.ds(i * rows, rows)
        ends = (src, out) if pieces == 1 else (src.at[span], out.at[:, span])
        parts.append(
            Gather(
                net, *ends, *scratch[3 * i : 3 * i + 3], index, halves,
                line=reach != "square", square=reach != "line", core=reach != "square",
            )
        )
    return parts


def gather_semaphores(line, pieces=1):
    return ([pltpu.SemaphoreType.DMA((15 * line,))] * 2 + [pltpu.SemaphoreType.DMA]) * pieces


def gather_job(sizes, array, halves, reach, pieces=1):
    line = sizes["mem"] // 2
    slots = {"all": sizes["seq"] * sizes["mem"], "line": sizes["mem"], "square": sizes["seq"]}[reach]

    def steps(net, ins, outs, scratch):
        parts = gather_parts(net, ins[0], outs[0], scratch, halves, reach, pieces)
        return [chain for part in parts for chain in part.chains()], [part.closing() for part in parts]

    out = jax.ShapeDtypeStruct((slots,) + array.shape, array.dtype)
    return Job([array], [out], gather_semaphores(line, pieces), steps)


class Scatter:
    def __init__(self, net, src, out, buffers, sems, halves, whole=True):
        self.net, self.src, self.out, self.halves = net, src, out, halves
        self.whole, self.count = whole, buffers[0].shape[1]
        self.held, self.twin, self.first, self.second, self.along = buffers
        self.sends, self.recvs, self.own = sems

    def send(self, block, target, place, device):
        remote(block, target, self.sends, self.recvs, place, device).start()

    def sent(self, block, place):
        remote(block, block, self.sends, self.recvs, place, self.net.core).wait_send()

    def arrived(self, block, place):
        remote(block, block, self.sends, self.recvs, place, self.net.core).wait_recv()

    def places(self):
        z = self.count
        return 0, 4 * z, 8 * z, 10 * z, 11 * z

    def loading(self, d):
        source = self.src.at[:, d, self.net.c] if self.whole else self.src.at[:, d]
        return pltpu.make_async_copy(source, self.held.at[:, d], self.own.at[d])

    def load(self, d):
        net = self.net
        if self.src is not None:
            self.loading(d).start()
        for s in range(4 if self.whole else 0):
            self.send(self.src.at[s, d, 1 - net.c], self.twin.at[s, d], s * self.count + d, net.core)

    def add_core(self, d):
        net = self.net
        _, first, _, _, _ = self.places()
        if self.src is not None:
            self.loading(d).wait()
        for turn in (3, 2, 1, 0):
            s = net.s ^ turn
            if self.whole:
                self.arrived(self.twin.at[s, d], s * self.count + d)
                self.held[s, d] = self.held[s, d] + self.twin[s, d]
            for part, device, slot, kind in {
                3: ((0, net.y, 1, 1), (1, net.x, 1, 3)),
                2: ((0, net.y, 0, 0),),
                1: ((1, net.x, 0, 2),),
                0: (),
            }[turn]:
                self.send(
                    self.halves(self.held.at[s, d], part),
                    self.first.at[part, slot, d],
                    first + kind * self.count + d,
                    device,
                )

    def chain(self, k):
        d = lax.rem(self.net.z + k, self.net.line) if self.whole else k
        for stage in (self.load, self.add_core, self.add_first, self.add_second, self.line_step):
            stage(d)
            yield
        if self.whole and k == 0:
            self.keep()
            yield

    def add(self, block, other):
        block[...] = block[...] + other[...]

    def add_first(self, d):
        net = self.net
        _, first, second, _, _ = self.places()
        for part, slot, kind, turn in ((0, 1, 1, 1), (1, 1, 3, 2), (0, 0, 0, 0), (1, 0, 2, 0)):
            got = self.first.at[part, slot, d]
            self.arrived(got, first + kind * self.count + d)
            block = self.halves(self.held.at[net.s ^ turn, d], part)
            self.add(block, got)
            if turn:
                device = net.x if part == 0 else net.y
                self.send(block, self.second.at[part, d], second + part * self.count + d, device)

    def add_second(self, d):
        net = self.net
        _, _, second, _, _ = self.places()
        for part in range(2):
            self.arrived(self.second.at[part, d], second + part * self.count + d)
            self.add(self.halves(self.held.at[net.s, d], part), self.second.at[part, d])

    def line_step(self, d):
        net = self.net
        _, _, _, right, left = self.places()
        block = self.held.at[net.s, d]
        if not self.whole:
            self.out[0][d] = block[...].astype(F32)
            return

        def go():
            pltpu.make_async_remote_copy(
                src_ref=block,
                dst_ref=self.along.at[net.z],
                send_sem=self.sends.at[right + d],
                recv_sem=self.recvs.at[left + net.z],
                device_id=(net.s, 2 * d + net.c),
                device_id_type=MESH,
            ).start()

        pl.when(net.z != d)(go)

    def keep(self):
        net = self.net
        _, _, _, _, left = self.places()
        total = self.held[net.s, net.z].astype(F32)
        for k in range(1, net.line):
            z = lax.rem(net.z + k, net.line)
            self.arrived(self.along.at[z], left + z)
            total = total + self.along[z].astype(F32)
        start = 0
        for out in self.out:
            out[...] = total[:, start : start + out.shape[-1]]
            start += out.shape[-1]

    def closing(self):
        net = self.net
        _, first, second, right, _ = self.places()
        full = self.held.at[net.s, 0]
        for k in far_first(self.count):
            d = lax.rem(net.z + k, net.line) if self.whole else k
            for s in range(4 if self.whole else 0):
                self.sent(full, s * self.count + d)
            for kind, part in enumerate((0, 0, 1, 1)):
                self.sent(self.halves(full, part), first + kind * self.count + d)
            for part in range(2):
                self.sent(self.halves(full, part), second + part * self.count + d)
            if self.whole and k:
                self.sent(full, right + d)
            yield


def far_first(count):
    return sorted(range(count), key=lambda k: (k == 0, -min(k, count - k)))


def scatter_scratch(count, rows, columns, halves, whole):
    half = (rows // 2, columns) if halves is row_halves else (rows, columns // 2)
    block, unused = (rows, columns), (16, 128)
    return [
        pltpu.VMEM((4, count) + block, BF16),
        pltpu.VMEM((4, count) + block if whole else unused, BF16),
        pltpu.VMEM((2, 2, count) + half, BF16),
        pltpu.VMEM((2, count) + half, BF16),
        pltpu.VMEM((count,) + block if whole else unused, BF16),
        pltpu.SemaphoreType.DMA((12 * count,)),
        pltpu.SemaphoreType.DMA((12 * count,)),
        pltpu.SemaphoreType.DMA((count,)),
    ]


def scatter_job(sizes, array, halves, whole=True):
    square, line = sizes["seq"], sizes["mem"] // 2
    columns = array.shape[1]
    if whole:
        count, rows = line, array.shape[0] // (2 * square * line)
        array = array.reshape(square, line, 2, rows, columns)
        outs = [jax.ShapeDtypeStruct((rows, w), F32) for w in [columns]]
    else:
        count, rows = PIECES, array.shape[0] // (square * PIECES)
        array = array.reshape(square, count, rows, columns)
        outs = [jax.ShapeDtypeStruct((count, rows, columns), F32)]
    scratch = scatter_scratch(count, rows, columns, halves, whole)

    def steps(net, ins, outs, scratch):
        scatter = Scatter(net, ins[0], outs, scratch[:5], scratch[5:], halves, whole)
        return [scatter.chain(k) for k in far_first(count)], [scatter.closing()]

    return Job([array], outs, scratch, steps, out_where=pltpu.VMEM)


class Return:
    def __init__(self, net, sources, outs, scratch):
        kinds = len(sources)
        self.net, self.sources, self.outs, self.kinds = net, sources, outs, range(kinds)
        self.held, self.twin = scratch[:kinds], scratch[kinds : 2 * kinds]
        self.own, self.twin_sends, self.twin_recvs, self.sends, self.recvs = scratch[2 * kinds :]

    def loading(self, i, d):
        source = self.sources[i].at[d, self.net.c]
        return pltpu.make_async_copy(source, self.held[i].at[d], self.own.at[i, d])

    def pairing(self, i, d):
        net = self.net
        return remote(
            self.sources[i].at[d, 1 - net.c],
            self.twin[i].at[d],
            self.twin_sends.at[i],
            self.twin_recvs.at[i],
            d,
            net.core,
        )

    def giving(self, i, k, d, slot, device):
        return pltpu.make_async_remote_copy(
            src_ref=self.held[i].at[d],
            dst_ref=self.outs[i].at[slot],
            send_sem=self.sends.at[i, k],
            recv_sem=self.recvs.at[i, slot],
            device_id=device,
            device_id_type=MESH,
        )

    def keeping(self, i, d):
        return pltpu.make_async_copy(
            self.held[i].at[d], self.outs[i].at[self.net.z], self.own.at[i, d]
        )

    def merge(self, d):
        held, twin = self.held, self.twin
        if len(held) == 1:
            held[0][d] = held[0][d] + twin[0][d]
            return
        mine, theirs = held[1][d], twin[1][d]
        top = jnp.maximum(mine[:HEADS], theirs[:HEADS])
        shares = [jnp.exp2(mine[:HEADS] - top), jnp.exp2(theirs[:HEADS] - top)]
        held[1][d] = jnp.concatenate(
            [top, mine[HEADS:] * shares[0] + theirs[HEADS:] * shares[1]], axis=0
        )
        shares = columns_of(jnp.concatenate(shares, axis=0))
        for h in range(HEADS):
            span = slice(h * 128, (h + 1) * 128)
            held[0][d, :, span] = (
                held[0][d, :, span].astype(F32) * shares[:, h : h + 1]
                + twin[0][d, :, span].astype(F32) * shares[:, HEADS + h : HEADS + h + 1]
            ).astype(BF16)


def index_job(sizes, index, mem_dev):
    line = sizes["mem"] // 2
    segments = 2 * line
    rows, count = index.shape
    out = jax.ShapeDtypeStruct((segments, rows, 128), jnp.int32)
    scratch = gather_semaphores(line) + mask_scratch(rows, count)
    scratch = scratch + [pltpu.VMEM((segments, rows, count), jnp.int32)]

    def steps(net, ins, outs, scratch):
        *sems, places_ref, words_ref, all_index = scratch
        (part,) = gather_parts(net, ins[0], all_index, sems, row_halves, "line", 1)
        part.waits_core = part.waits_own = False

        def words(z, far):
            if far:
                part.wait_core(z)
            segment = 2 * z + (1 - net.c if far else net.c)
            outs[0][segment] = mask_words(
                all_index[segment], net.m * mem_dev, mem_dev, places_ref, words_ref
            )

        def masks():
            for k in range(line):
                for from_left in (True, False) if k else (True,):
                    z = net.z - k if from_left else net.z + k
                    present = z >= 0 if from_left else z < line
                    here = (lambda body: body()) if k == 0 else pl.when(present)
                    need([part], k, from_left)
                    if k == 0:
                        part.wait_own()
                    for far in (False, True):
                        here(lambda: words(z, far))
                        yield

        return part.chains() + [masks()], [part.closing()]

    return Job([index], [out], scratch, steps, pltpu.VMEM, pltpu.VMEM)


def need(parts, k, from_left):
    for part in parts:
        assert (k, from_left) in part.seen


class OwnerForward(Return):
    def __init__(self, net, scale, parts, ins, outs, scratch, sems):
        self.bits, self.keys, self.values = ins
        self.queries, *peers = outs
        self.bias, self.kept, self.key, self.value, *held = scratch
        self.far, held = held[:2], held[2:]
        self.loads, *sems = sems
        super().__init__(net, self.far, peers, held + sems)
        self.parts, self.scale = parts, scale

    def pairing(self, i, d):
        net = self.net
        return remote(
            self.far[i].at[d],
            self.twin[i].at[d],
            self.twin_sends.at[i],
            self.twin_recvs.at[i],
            d,
            net.core,
        )

    def bring(self, z, far):
        net = self.net
        segment = 2 * z + (1 - net.c if far else net.c)
        slot = int(far)
        return [
            pltpu.make_async_copy(self.keys.at[segment], self.key.at[slot], self.loads.at[0, slot]),
            pltpu.make_async_copy(
                self.values.at[segment], self.value.at[slot], self.loads.at[1, slot]
            ),
        ]

    def attend(self, z, far, span):
        net = self.net
        segment = 2 * z + (1 - net.c if far else net.c)
        if span[0] == 0:
            if far:
                for part in self.parts:
                    part.wait_core(z)
            fill_bias(self.bits.at[segment], self.bias)
            for copy in self.bring(z, far):
                copy.wait()
        target = self.far if far else self.held
        owner_forward_heads(
            span,
            self.scale,
            self.queries.at[segment],
            self.key.at[int(far)],
            self.value.at[int(far)],
            self.bias,
            self.kept,
            target[0].at[z],
            target[1].at[z],
        )
        if far and span[1] == HEADS:
            for i in self.kinds:
                self.pairing(i, z).start()

    def home(self, k, z):
        for i in self.kinds:
            self.pairing(i, z).wait_recv()
        self.merge(z)
        net = self.net
        for i in self.kinds:
            if k:
                self.giving(i, z, z, net.z, (net.s, 2 * z + net.c)).start()
            else:
                self.keeping(i, z).start()

    def chain(self):
        net = self.net
        for k in range(net.line):
            for from_left in (True, False) if k else (True,):
                z = net.z - k if from_left else net.z + k
                present = z >= 0 if from_left else z < net.line
                here = (lambda body: body()) if k == 0 else pl.when(present)
                need(self.parts, k, from_left)
                if k == 0:
                    for part in self.parts:
                        part.wait_own()

                def start():
                    for copy in self.bring(z, True) + self.bring(z, False):
                        copy.start()

                here(start)
                yield
                for far in (True, False):
                    for span in SPANS:
                        here(lambda: self.attend(z, far, span))
                        yield
                here(lambda: self.home(k, z))
                yield

    def closing(self):
        net = self.net
        for k in range(net.line):
            d = lax.rem(net.z + k, net.line)
            for i in self.kinds:
                self.pairing(i, d).wait_send()
                if k:
                    copy = self.giving(i, d, d, d, net.core)
                    copy.wait_recv()
                    copy.wait_send()
                else:
                    self.keeping(i, d).wait()
            yield


def forward_job(sizes, queries, keys_values, bits, cached_keys, cached_values, scale):
    line = sizes["mem"] // 2
    (rows, width), segments = queries.shape, bits.shape[0]
    mem_dev = cached_keys.shape[1]
    length = sizes["seq"] * rows
    shape = jax.ShapeDtypeStruct
    outs = [
        shape((segments, rows, width), BF16),
        shape((sizes["seq"],) + keys_values.shape, BF16),
        shape((line, rows, width), BF16),
        shape((line, STATS, rows), F32),
        shape((rows, width), F32),
        shape((STATS, rows), F32),
    ]
    partial = [pltpu.VMEM((line, rows, width), BF16), pltpu.VMEM((line, STATS, rows), F32)]
    scratch = (
        gather_semaphores(line, PIECES)
        + gather_semaphores(line)
        + [pltpu.VMEM((rows, length), F32)]
        + [pltpu.VMEM((rows, mem_dev), F32), pltpu.VMEM((rows, 128), F32)]
        + [pltpu.VMEM((2, mem_dev, width), BF16)] * 2
        + partial * 3
        + [pltpu.SemaphoreType.DMA((2, 2))]
        + [pltpu.SemaphoreType.DMA((2, line))] * 5
    )

    def steps(net, ins, outs, scratch):
        queries, keys_values, *owner_ins = ins
        all_queries, segment_kv, out, stats, local_out, local_stats = outs
        scratch = list(scratch)
        take = lambda count: [scratch.pop(0) for _ in range(count)]
        parts = gather_parts(net, queries, all_queries, take(3 * PIECES), row_halves, "line", PIECES)
        (square,) = gather_parts(net, keys_values, segment_kv, take(3), row_halves, "square", 1)
        (local_bias,) = take(1)
        buffers = take(10)
        owner = OwnerForward(
            net, scale, parts, owner_ins, [all_queries, out, stats], buffers, scratch
        )
        for part in parts:
            part.waits_core = part.waits_own = False
        square.waits_own = False

        def local():
            for chain in square.chains():
                yield from chain
            square.wait_own()
            yield from local_forward_steps(
                scale, net.s, queries, segment_kv, local_out, local_stats, local_bias
            )

        chains = [chain for part in parts for chain in part.chains()]
        ends = [part.closing() for part in parts] + [square.closing(), owner.closing()]
        return chains + [local(), owner.chain()], ends

    vmem = pltpu.VMEM
    return Job(
        [queries, keys_values, bits, cached_keys, cached_values],
        outs,
        scratch,
        steps,
        [vmem, vmem, vmem, pl.ANY, pl.ANY],
        [vmem, vmem, pl.ANY, pl.ANY, vmem, vmem],
    )


def mask_words(index, base, mem_dev, place_ref, bit_ref):
    relative = index - base
    inside = (relative >= 0) & (relative < mem_dev)
    place = jnp.where(inside, relative & 127, 0)
    bit = jnp.where(inside, lax.shift_left(jnp.ones_like(relative), relative >> 7), 0)
    place_ref[...] = place.T
    bit_ref[...] = bit.T
    sought = lax.broadcasted_iota(jnp.int32, (128, 128), 0)
    halves = []
    for start in range(0, index.shape[0], 128):

        def eight(g, words, start=start):
            group = pl.ds(pl.multiple_of(g * 8, 8), 8)
            places = place_ref[group, start : start + 128]
            bits = bit_ref[group, start : start + 128]
            for j in range(8):
                words = words | jnp.where(places[j : j + 1] == sought, bits[j : j + 1], 0)
            return words

        none = jnp.zeros((128, 128), jnp.int32)
        words = lax.fori_loop(0, index.shape[1] // 8, eight, none)
        halves.append(words.T)
    return jnp.concatenate(halves, axis=0)


def mask_scratch(rows, count):
    return [pltpu.VMEM((count, rows), jnp.int32), pltpu.VMEM((count, rows), jnp.int32)]


def mask_kernel(mem_dev, base_ref, index_ref, bits_ref, place_ref, bit_ref):
    bits_ref[0] = mask_words(index_ref[0], base_ref[0], mem_dev, place_ref, bit_ref)


def mask_bits(base, all_index, mem_dev):
    segments, rows, count = all_index.shape
    return pl.pallas_call(
        functools.partial(mask_kernel, mem_dev),
        grid_spec=pltpu.PrefetchScalarGridSpec(
            num_scalar_prefetch=1,
            grid=(segments,),
            in_specs=[pl.BlockSpec((1, rows, count), lambda g, b: (g, 0, 0))],
            out_specs=pl.BlockSpec((1, rows, 128), lambda g, b: (g, 0, 0)),
            scratch_shapes=mask_scratch(rows, count),
        ),
        out_shape=jax.ShapeDtypeStruct((segments, rows, 128), jnp.int32),
        compiler_params=params(),
        name="mask_bits",
    )(base, all_index)


def fill_bias(bits_ref, bias_ref):
    bits = bits_ref[...].reshape(bits_ref.shape[-2:])
    for b in range(bias_ref.shape[1] // 128):
        bias_ref[:, b * 128 : (b + 1) * 128] = jnp.where(((bits >> b) & 1) != 0, 0.0, FLOOR)


def owner_backward_heads(span, scale, q_ref, g_ref, st_ref, k_ref, v_ref, bias_ref, dq_ref):
    stats = columns_of(st_ref[...])
    lanes = lax.broadcasted_iota(jnp.int32, stats.shape, 1)

    def two(i, carry):
        for h in (2 * i, 2 * i + 1):
            lane = pl.ds(pl.multiple_of(h * 128, 128), 128)
            total = jnp.sum(jnp.where(lanes == h, stats, 0.0), axis=1, keepdims=True)
            dots = jnp.sum(jnp.where(lanes == HEADS + h, stats, 0.0), axis=1, keepdims=True)
            scores = dot(q_ref[:, lane], k_ref[:, lane], NT) * scale + bias_ref[...]
            weights = jnp.exp2(scores - total)
            dscore = weights * (dot(g_ref[:, lane], v_ref[:, lane], NT) - dots)
            dq_ref[:, lane] = (
                dot(dscore.astype(BF16), k_ref[:, lane]) * (scale / LOG2E)
            ).astype(BF16)
        return carry

    lax.fori_loop(span[0] // 2, span[1] // 2, two, 0)


def owner_forward_heads(span, scale, q_ref, k_ref, v_ref, bias_ref, stats_ref, o_ref, st_ref):
    rows = q_ref.shape[0]
    lanes = lax.broadcasted_iota(jnp.int32, (rows, 128), 1)

    def two(i, stats):
        for h in (2 * i, 2 * i + 1):
            lane = pl.ds(pl.multiple_of(h * 128, 128), 128)
            scores = dot(q_ref[:, lane], k_ref[:, lane], NT) * scale + bias_ref[...]
            top = jnp.maximum(jnp.max(scores, axis=1, keepdims=True), LOW)
            weights = jnp.exp2(scores - top)
            total = jnp.sum(weights, axis=1, keepdims=True)
            stats = jnp.where(lanes == h, top, jnp.where(lanes == HEADS + h, total, stats))
            o_ref[:, lane] = dot(weights.astype(BF16), v_ref[:, lane]).astype(BF16)
        return stats

    start = stats_ref[...] if span[0] else jnp.zeros((rows, 128), F32)
    stats = lax.fori_loop(span[0] // 2, span[1] // 2, two, start)
    if span[1] == HEADS:
        st_ref[...] = stats.T[:STATS]
    else:
        stats_ref[...] = stats


def owner_forward_kernel(scale, order_ref, q_ref, bits_ref, k_ref, v_ref, o_ref, st_ref, bias_ref):
    del order_ref
    fill_bias(bits_ref, bias_ref)
    maxima, sums = [], []
    for h in range(HEADS):
        span = slice(h * 128, (h + 1) * 128)
        scores = dot(q_ref[0, :, span], k_ref[0, :, span], NT) * scale + bias_ref[...]
        top = jnp.maximum(jnp.max(scores, axis=1, keepdims=True), LOW)
        weights = jnp.exp2(scores - top)
        maxima.append(top)
        sums.append(jnp.sum(weights, axis=1, keepdims=True))
        o_ref[0, :, span] = dot(weights.astype(BF16), v_ref[0, :, span]).astype(BF16)
    st_ref[0] = spread(maxima + sums).T[:STATS]


def owner_forward(order, queries, bits, cached_keys, cached_values, scale):
    segments, rows, width = queries.shape
    mem_dev = cached_keys.shape[1]
    active = order.shape[0]
    picked = lambda a, o: (o[a], 0, 0)
    return pl.pallas_call(
        functools.partial(owner_forward_kernel, scale),
        grid_spec=pltpu.PrefetchScalarGridSpec(
            num_scalar_prefetch=1,
            grid=(active,),
            in_specs=[
                pl.BlockSpec((1, rows, width), picked),
                pl.BlockSpec((1, rows, 128), picked),
                pl.BlockSpec((1, mem_dev, width), picked),
                pl.BlockSpec((1, mem_dev, width), picked),
            ],
            out_specs=[
                pl.BlockSpec((1, rows, width), picked),
                pl.BlockSpec((1, STATS, rows), picked),
            ],
            scratch_shapes=[pltpu.VMEM((rows, mem_dev), F32)],
        ),
        out_shape=[
            jax.ShapeDtypeStruct((segments, rows, width), BF16),
            jax.ShapeDtypeStruct((segments, STATS, rows), F32),
        ],
        compiler_params=params(),
        name="owner_forward",
    )(order, queries, bits, cached_keys, cached_values)


def owner_backward_kernel(
    scale, order_ref, q_ref, g_ref, st_ref, bits_ref, k_ref, v_ref, dq_ref, bias_ref
):
    del order_ref
    fill_bias(bits_ref, bias_ref)
    stats = columns_of(st_ref[0])
    for h in range(HEADS):
        span = slice(h * 128, (h + 1) * 128)
        scores = dot(q_ref[0, :, span], k_ref[0, :, span], NT) * scale + bias_ref[...]
        weights = jnp.exp2(scores - stats[:, h : h + 1])
        dweights = dot(g_ref[0, :, span], v_ref[0, :, span], NT)
        dscore = weights * (dweights - stats[:, HEADS + h : HEADS + h + 1])
        dq_ref[0, :, span] = (
            dot(dscore.astype(BF16), k_ref[0, :, span]) * (scale / LOG2E)
        ).astype(BF16)


def owner_backward(order, queries, grads, stats, bits, cached_keys, cached_values, scale):
    segments, rows, width = queries.shape
    mem_dev = cached_keys.shape[1]
    active = order.shape[0]
    picked = lambda a, o: (o[a], 0, 0)
    return pl.pallas_call(
        functools.partial(owner_backward_kernel, scale),
        grid_spec=pltpu.PrefetchScalarGridSpec(
            num_scalar_prefetch=1,
            grid=(active,),
            in_specs=[
                pl.BlockSpec((1, rows, width), picked),
                pl.BlockSpec((1, rows, width), picked),
                pl.BlockSpec((1, STATS, rows), picked),
                pl.BlockSpec((1, rows, 128), picked),
                pl.BlockSpec((1, mem_dev, width), picked),
                pl.BlockSpec((1, mem_dev, width), picked),
            ],
            out_specs=pl.BlockSpec((1, rows, width), picked),
            scratch_shapes=[pltpu.VMEM((rows, mem_dev), F32)],
        ),
        out_shape=jax.ShapeDtypeStruct((segments, rows, width), BF16),
        compiler_params=params(),
        name="owner_backward",
    )(order, queries, grads, stats, bits, cached_keys, cached_values)


def causal_bias(place, rows, keys):
    row = place * rows + lax.broadcasted_iota(jnp.int32, (rows, keys), 0)
    return jnp.where(lax.broadcasted_iota(jnp.int32, (rows, keys), 1) <= row, 0.0, FLOOR)


def columns_at(kv_ref, span):
    block = kv_ref[:, span] if len(kv_ref.shape) == 2 else kv_ref[:, :, span]
    return block.reshape(-1, block.shape[-1])


def local_forward_steps(scale, place, q_ref, kv_ref, o_ref, st_ref, bias_ref):
    rows, width = q_ref.shape
    bias_ref[...] = causal_bias(place, rows, bias_ref.shape[1])
    maxima, sums = [], []
    for h in range(HEADS):
        span, over = slice(h * 128, (h + 1) * 128), slice(width + h * 128, width + (h + 1) * 128)
        scores = dot(q_ref[:, span], columns_at(kv_ref, span), NT) * scale + bias_ref[...]
        top = jnp.max(scores, axis=1, keepdims=True)
        weights = jnp.exp2(scores - top)
        maxima.append(top)
        sums.append(jnp.sum(weights, axis=1, keepdims=True))
        o_ref[:, span] = dot(weights.astype(BF16), columns_at(kv_ref, over))
        yield
    st_ref[...] = spread(maxima + sums).T[:STATS]


def local_backward_steps(
    scale, place, q_ref, g_ref, st_ref, kv_ref, dq_ref, dkv_ref, bias_ref
):
    rows, width = q_ref.shape
    bias_ref[...] = causal_bias(place, rows, bias_ref.shape[1])
    stats = columns_of(st_ref[...])
    for h in range(HEADS):
        span, over = slice(h * 128, (h + 1) * 128), slice(width + h * 128, width + (h + 1) * 128)
        query, key, grad = q_ref[:, span], columns_at(kv_ref, span), g_ref[:, span]
        scores = dot(query, key, NT) * scale + bias_ref[...]
        weights = jnp.exp2(scores - stats[:, h : h + 1])
        dweights = dot(grad, columns_at(kv_ref, over), NT)
        dscore = (weights * (dweights - stats[:, HEADS + h : HEADS + h + 1])).astype(BF16)
        dq_ref[:, span] = dot(dscore, key) * (scale / LOG2E)
        dkey = (dot(dscore, query, TN) * (scale / LOG2E)).astype(BF16)
        dvalue = dot(weights.astype(BF16), grad, TN).astype(BF16)
        lead = dkv_ref.shape[:-1]
        dkv_ref[(*[slice(None)] * len(lead), span)] = dkey.reshape(lead + (128,))
        dkv_ref[(*[slice(None)] * len(lead), over)] = dvalue.reshape(lead + (128,))
        yield


class OwnerBackward(OwnerForward):
    def __init__(self, net, scale, parts, stats_part, ins, outs, scratch, sems):
        self.sources_in = ins
        self.grads, self.stats, peers = outs
        *self.buffers, self.bias, far, held, twin = scratch
        self.loads, *sems = sems
        self.far = [far]
        Return.__init__(self, net, self.far, [peers], [held, twin, *sems])
        self.parts, self.scale, self.stats_part = [*parts, stats_part], scale, stats_part

    def bring(self, z, far):
        segment = 2 * z + (1 - self.net.c if far else self.net.c)
        sources = [source.at[segment] for source in (*self.sources_in, self.grads)]
        return [
            pltpu.make_async_copy(source, buffer, self.loads.at[i])
            for i, (source, buffer) in enumerate(zip(sources, self.buffers))
        ]

    def mask(self, z, far):
        if far:
            for part in self.parts:
                part.wait_core(z)
        for copy in self.bring(z, far):
            copy.start()

    def attend(self, z, far, span):
        net = self.net
        keys, values, queries, bits, grads = self.buffers
        if span[0] == 0:
            for copy in self.bring(z, far):
                copy.wait()
            fill_bias(bits, self.bias)
        segment = 2 * z + (1 - net.c if far else net.c)
        owner_backward_heads(
            span,
            self.scale,
            queries,
            grads,
            self.stats.at[segment],
            keys,
            values,
            self.bias,
            (self.far[0] if far else self.held[0]).at[z],
        )
        if far and span[1] == HEADS:
            self.pairing(0, z).start()

    def chain(self):
        net = self.net
        for k in range(net.line):
            for from_left in (True, False) if k else (True,):
                z = net.z - k if from_left else net.z + k
                present = z >= 0 if from_left else z < net.line
                here = (lambda body: body()) if k == 0 else pl.when(present)
                need(self.parts, k, from_left)
                if k == 0:
                    for part in self.parts:
                        part.wait_own()
                here(lambda: self.mask(z, True))
                yield
                for far in (True, False):
                    for span in SPANS:

                        def part():
                            self.attend(z, far, span)
                            if far and span[1] == HEADS:
                                self.mask(z, False)

                        here(part)
                        yield
                here(lambda: self.home(k, z))
                yield


def backward_job(
    sizes, queries, grads, stats, segment_kv, all_queries, bits, cached_keys, cached_values, scale
):
    square, line = sizes["seq"], sizes["mem"] // 2
    segments, rows, width = all_queries.shape
    mem_dev = cached_keys.shape[1]
    length = square * rows
    shape = jax.ShapeDtypeStruct
    outs = [
        shape((segments, rows, width), BF16),
        shape((line, rows, width), BF16),
        shape((rows, width), F32),
        shape((PIECES, rows // PIECES, 2 * width), F32),
    ]
    keys_scratch = scatter_scratch(PIECES, rows // PIECES, 2 * width, row_halves, False)
    scratch = (
        gather_semaphores(line, PIECES)
        + gather_semaphores(line)
        + [pltpu.VMEM((segments, STATS, rows), F32), pltpu.VMEM((rows, length), F32)]
        + keys_scratch
        + [pltpu.VMEM((mem_dev, width), BF16)] * 2
        + [
            pltpu.VMEM((rows, width), BF16),
            pltpu.VMEM((rows, 128), jnp.int32),
            pltpu.VMEM((rows, width), BF16),
            pltpu.VMEM((rows, mem_dev), F32),
        ]
        + [pltpu.VMEM((line, rows, width), BF16)] * 3
        + [pltpu.SemaphoreType.DMA((5,))]
        + [pltpu.SemaphoreType.DMA((1, line))] * 5
    )

    def steps(net, ins, outs, scratch):
        queries, grads, stats, segment_kv, all_queries, bits, keys, values = ins
        all_grads, peers, local_dq, grad_kv = outs
        scratch = list(scratch)
        take = lambda count: [scratch.pop(0) for _ in range(count)]
        parts = gather_parts(net, grads, all_grads, take(3 * PIECES), row_halves, "line", PIECES)
        stats_sems = take(3)
        all_stats, local_bias = take(2)
        (stats_part,) = gather_parts(net, stats, all_stats, stats_sems, row_halves, "line", 1)
        keys_scratch = take(8)
        buffers = take(9)
        scatter = Scatter(
            net, None, [grad_kv], keys_scratch[:5], keys_scratch[5:], row_halves, False
        )
        owner = OwnerBackward(
            net, scale, parts, stats_part, [keys, values, all_queries, bits],
            [all_grads, all_stats, peers], buffers, scratch,
        )
        for part in [*parts, stats_part]:
            part.waits_core = part.waits_own = False

        def local():
            yield from local_backward_steps(
                scale, net.s, queries, grads, stats, segment_kv, local_dq, scatter.held, local_bias
            )
            stages = (scatter.add_core, scatter.add_first, scatter.add_second, scatter.line_step)
            for wave in range(PIECES + 3):
                for lag in (3, 2, 1, 0):
                    if 0 <= wave - lag < PIECES:
                        stages[lag](wave - lag)
                        yield

        chains = [chain for part in [*parts, stats_part] for chain in part.chains()]
        ends = [part.closing() for part in [*parts, stats_part]]
        ends += [scatter.closing(), owner.closing()]
        return chains + [local(), owner.chain()], ends

    vmem = pltpu.VMEM
    return Job(
        [queries, grads, stats, segment_kv, all_queries, bits, cached_keys, cached_values],
        outs,
        scratch,
        steps,
        [vmem] * 4 + [pl.ANY] * 4,
        [pl.ANY, pl.ANY, vmem, vmem],
    )


def local_job(kind, arrays, scale):
    rows, width = arrays[0].shape
    length = arrays[-1].shape[0]
    if kind == "forward":
        body, extra = local_forward_steps, jax.ShapeDtypeStruct((STATS, rows), F32)
    else:
        body, extra = local_backward_steps, jax.ShapeDtypeStruct((length, 2 * width), BF16)

    def steps(net, ins, outs, scratch):
        return [body(scale, net.s, *ins, *outs, *scratch)], []

    outs = [jax.ShapeDtypeStruct((rows, width), F32), extra]
    return Job(arrays, outs, [pltpu.VMEM((rows, length), F32)], steps, pltpu.VMEM, pltpu.VMEM)


def alone_kernel(job, *refs):
    place_ref, *refs = refs
    net = type("Alone", (), {"s": place_ref[0]})
    ins, outs = len(job.arrays), len(job.arrays) + len(job.outs)
    for chain in job.steps(net, refs[:ins], refs[ins:outs], refs[outs:])[0]:
        for _ in chain:
            pass


def alone(name, place, job):
    return pl.pallas_call(
        functools.partial(alone_kernel, job),
        out_shape=job.outs,
        in_specs=[pl.BlockSpec(memory_space=pltpu.SMEM)]
        + [pl.BlockSpec(memory_space=pltpu.VMEM)] * len(job.arrays),
        out_specs=[pl.BlockSpec(memory_space=pltpu.VMEM)] * len(job.outs),
        scratch_shapes=job.scratch,
        compiler_params=params(),
        name=name,
    )(place, *job.arrays)


def copy_in(pairs, sems):
    copies = [pltpu.make_async_copy(src, dst, sems.at[i]) for i, (src, dst) in enumerate(pairs)]
    for copy in copies:
        copy.start()
    return copies


def turn(values, cosine, sine):
    return values * cosine + pltpu.roll(values, values.shape[1] // 2, 1) * sine


def inverse_root(values):
    return lax.rsqrt(jnp.mean(values * values, axis=1, keepdims=True) + EPSILON)


def project_kernel(x_ref, w_any, cos_ref, sin_ref, n_ref, q_ref, kv_ref, gain_ref, w_ref, sems):
    width = x_ref.shape[1]
    spans = [slice(i * width, (i + 1) * width) for i in range(3)] + [slice(3 * width, 3 * width + 128)]
    copies = copy_in([(w_any.at[:, s], w_ref.at[:, s]) for s in spans], sems)
    x = x_ref[...].astype(F32)
    copies[3].wait()
    gain_ref[...] = w_ref[:, spans[3]].astype(F32).T[:8]
    normed = (x * inverse_root(x) * gain_ref[:1]).astype(BF16)
    n_ref[...] = normed
    cosine, sine = cos_ref[...], sin_ref[...]
    for i in range(3):
        copies[i].wait()
        product = dot(normed, w_ref[:, spans[i]])
        for h in range(HEADS):
            span = slice(h * 128, (h + 1) * 128)
            part = product[:, span]
            part = part if i == 2 else turn(part, cosine, sine)
            if i == 0:
                q_ref[:, span] = part.astype(BF16)
            else:
                over = slice((i - 1) * width + h * 128, (i - 1) * width + (h + 1) * 128)
                kv_ref[:, over] = part.astype(BF16)


def in_vmem(count):
    return [pl.BlockSpec(memory_space=pltpu.VMEM)] * count


def project(tokens, first_weights, cosine, sine):
    rows, width = tokens.shape
    columns = first_weights.shape[1]
    return pl.pallas_call(
        project_kernel,
        out_shape=[
            jax.ShapeDtypeStruct((rows, width), BF16),
            jax.ShapeDtypeStruct((rows, width), BF16),
            jax.ShapeDtypeStruct((rows, 2 * width), BF16),
            jax.ShapeDtypeStruct((8, width), F32),
        ],
        in_specs=in_vmem(1) + [pl.BlockSpec(memory_space=pl.ANY)] + in_vmem(2),
        out_specs=in_vmem(4),
        scratch_shapes=[
            pltpu.VMEM((width, columns), BF16),
            pltpu.SemaphoreType.DMA((4,)),
        ],
        compiler_params=params(),
        name="project",
    )(tokens, first_weights, cosine, sine)


def middle_kernel(
    live_ref, x_ref, g_ref, gain_ref, lo_ref, ls_ref, po_ref, ps_ref, out_any, gate_any, up_any, down_any,
    mixed_ref, gm_ref, ga_ref, st_ref, gain_grad_ref, wo_any, wg_any, wu_any, wd_any,
    att_ref, acc_ref, gn_ref, n_ref, nt_ref, out_ref, gate_ref, up_ref, down_ref, side_ref, tall_ref, sems, writes,
):
    rows, width = x_ref.shape
    copies = copy_in(
        [(out_any, out_ref), (gate_any, gate_ref), (up_any, up_ref), (down_any, down_ref)], sems
    )
    live = live_ref[0] > 0
    peers = ps_ref.shape[0]
    local_max, local_sum = ls_ref[:HEADS], ls_ref[HEADS:]
    peer_max = [jnp.where(live, ps_ref[p, :HEADS], LOW) for p in range(peers)]
    peer_sum = [jnp.where(live, ps_ref[p, HEADS:], 0.0) for p in range(peers)]
    top = functools.reduce(jnp.maximum, peer_max, local_max)
    shares = [jnp.exp2(m - top) for m in [local_max] + peer_max]
    total = functools.reduce(
        jnp.add, [s * t for s, t in zip(shares, [local_sum] + peer_sum)]
    )
    log_total = top + jnp.log2(total)
    shares = columns_of(jnp.concatenate([s / total for s in shares], axis=0))
    for h in range(HEADS):
        span = slice(h * 128, (h + 1) * 128)
        part = lo_ref[:, span] * shares[:, h : h + 1]
        for p in range(peers):
            column = shares[:, (p + 1) * HEADS + h : (p + 1) * HEADS + h + 1]
            part += jnp.where(live, po_ref[p, :, span].astype(F32), 0.0) * column
        att_ref[:, span] = part
    attention_low = att_ref[...].astype(BF16)
    copies[0].wait()
    mid = x_ref[...].astype(F32) + dot(attention_low, out_ref[...])
    gm_ref[...] = mid
    root = inverse_root(mid)
    n_ref[...] = (mid * root * gain_ref[1:2]).astype(BF16)
    for copy in copies[1:]:
        copy.wait()
    nt_ref[...] = n_ref[...].T
    grad = g_ref[...]
    acc_ref[...] = jnp.zeros_like(acc_ref)
    gn_ref[...] = jnp.zeros_like(gn_ref)
    hidden_width = gate_ref.shape[1]
    step = 512
    pending = [[], []]

    def write(slot, product, buffer, target, place):
        buffer[...] = product.astype(BF16)
        copy = pltpu.make_async_copy(buffer, target, writes.at[slot, place])
        copy.start()
        pending[slot].append(copy)

    for turn_of, start in enumerate(range(0, hidden_width, step)):
        span = slice(start, min(start + step, hidden_width))
        slot = turn_of % 2
        while pending[slot]:
            pending[slot].pop().wait()
        norm_two = n_ref[...]
        gate = dot(norm_two, gate_ref[:, span])
        upward = dot(norm_two, up_ref[:, span])
        grad_hidden = dot(grad, down_ref[span, :], NT)
        sigmoid = 1.0 / (1.0 + jnp.exp(-gate))
        silu = gate * sigmoid
        hidden = (silu * upward).astype(BF16)
        grad_gate = (grad_hidden * upward * (sigmoid * (1.0 + gate * (1.0 - sigmoid)))).astype(BF16)
        grad_up = (grad_hidden * silu).astype(BF16)
        write(slot, dot(nt_ref[...], grad_gate), side_ref.at[slot, 0, :, : span.stop - start], wg_any.at[:, span], 0)
        write(slot, dot(nt_ref[...], grad_up), side_ref.at[slot, 1, :, : span.stop - start], wu_any.at[:, span], 1)
        write(slot, dot(hidden, grad, TN), tall_ref.at[slot, : span.stop - start], wd_any.at[span, :], 2)
        acc_ref[...] += dot(hidden, down_ref[span, :])
        gn_ref[...] += dot(grad_gate, gate_ref[:, span], NT) + dot(grad_up, up_ref[:, span], NT)
    mid = gm_ref[...]
    mixed_ref[...] = mid + acc_ref[...]
    normed = mid * root
    grad_norm = gn_ref[...]
    gain_grad_ref[...] = jnp.broadcast_to(
        jnp.sum(grad_norm * normed, axis=0, keepdims=True), gain_grad_ref.shape
    )
    scaled = grad_norm * gain_ref[1:2]
    grad_mid = grad.astype(F32) + root * (
        scaled - normed * jnp.mean(normed * scaled, axis=1, keepdims=True)
    )
    gm_ref[...] = grad_mid
    grad_mid_low = grad_mid.astype(BF16)
    nt_ref[...] = att_ref[...].astype(BF16).T
    for start in range(0, width, step):
        span = slice(start, start + step)
        slot = start // step % 2
        while pending[slot]:
            pending[slot].pop().wait()
        write(slot, dot(nt_ref[...], grad_mid_low[:, span]), side_ref.at[slot, 0], wo_any.at[:, span], 0)
    grad_attention = dot(grad_mid_low, out_ref[...], NT).astype(BF16)
    ga_ref[...] = grad_attention
    products = grad_attention.astype(F32) * att_ref[...]
    dots = [
        jnp.sum(products[:, h * 128 : (h + 1) * 128], axis=1, keepdims=True) for h in range(HEADS)
    ]
    st_ref[...] = jnp.concatenate([log_total, spread(dots).T[:HEADS]], axis=0)
    for copy in pending[0] + pending[1]:
        copy.wait()


def middle(live, tokens, grads, gains, local, peers, weights):
    rows, width = tokens.shape
    hidden_width = weights[1].shape[1]
    full = lambda columns, kind: jax.ShapeDtypeStruct((rows, columns), kind)
    return pl.pallas_call(
        middle_kernel,
        out_shape=[
            full(width, F32),
            full(width, F32),
            full(width, BF16),
            jax.ShapeDtypeStruct((STATS, rows), F32),
            jax.ShapeDtypeStruct((8, width), F32),
        ]
        + [jax.ShapeDtypeStruct(w.shape, BF16) for w in weights],
        in_specs=[pl.BlockSpec(memory_space=pltpu.SMEM)]
        + in_vmem(7)
        + [pl.BlockSpec(memory_space=pl.ANY)] * 4,
        out_specs=in_vmem(5) + [pl.BlockSpec(memory_space=pl.ANY)] * 4,
        scratch_shapes=[pltpu.VMEM((rows, width), F32)] * 3
        + [pltpu.VMEM((rows, width), BF16), pltpu.VMEM((width, rows), BF16)]
        + [pltpu.VMEM(w.shape, BF16) for w in weights]
        + [
            pltpu.VMEM((2, 2, width, 512), BF16),
            pltpu.VMEM((2, 512, width), BF16),
            pltpu.SemaphoreType.DMA((4,)),
            pltpu.SemaphoreType.DMA((2, 3)),
        ],
        compiler_params=params(),
        name="middle",
    )(live, tokens, grads, gains, *local, *peers, *weights)


def final_kernel(
    live_ref, x_ref, gm_ref, gain_ref, ggain_ref, n_ref, dq_ref, pd_ref, dkv_ref, cos_ref, sin_ref, w_any,
    *rest,
):
    rows, width = x_ref.shape
    ready, (gx_ref, late_ref), given = rest[:4], rest[4:6], rest[6:10]
    in_ref, w_ref, sems = rest[10:]
    copies = copy_in([(w_any.at[:, : 3 * width], w_ref)], sems)
    for source, target in zip(ready, given):
        target[...] = source[...]
    live = live_ref[0] > 0
    cosine, sine = cos_ref[...], -sin_ref[...]
    for h in range(HEADS):
        span = slice(h * 128, (h + 1) * 128)
        part = dq_ref[:, span]
        for p in range(pd_ref.shape[0]):
            part += jnp.where(live, pd_ref[p, :, span].astype(F32), 0.0)
        in_ref[:, span] = turn(part, cosine, sine).astype(BF16)
        over = slice(width + h * 128, width + (h + 1) * 128)
        in_ref[:, over] = turn(dkv_ref[:, span], cosine, sine).astype(BF16)
    in_ref[:, 2 * width :] = dkv_ref[:, width:].astype(BF16)
    normed_low = n_ref[...]
    for i in range(3):
        span = slice(i * width, (i + 1) * width)
        late_ref[:, span] = dot(normed_low, in_ref[:, span], TN).astype(BF16)
    copies[0].wait()
    grad_norm = dot(in_ref[...], w_ref[...], NT)
    x = x_ref[...].astype(F32)
    root = inverse_root(x)
    normed = x * root
    gains = jnp.concatenate(
        [
            jnp.sum(grad_norm * normed, axis=0, keepdims=True),
            ggain_ref[:1],
            jnp.zeros((126, width), F32),
        ],
        axis=0,
    )
    late_ref[:, 3 * width :] = gains.T.astype(BF16)
    scaled = grad_norm * gain_ref[:1]
    gx_ref[...] = gm_ref[...] + root * (
        scaled - normed * jnp.mean(normed * scaled, axis=1, keepdims=True)
    )


def final(live, *arrays, early):
    rows, width = arrays[0].shape
    columns = arrays[-1].shape[1]
    results = pl.pallas_call(
        final_kernel,
        out_shape=[
            jax.ShapeDtypeStruct((rows, width), F32),
            jax.ShapeDtypeStruct((width, columns), BF16),
        ]
        + [jax.ShapeDtypeStruct(e.shape, e.dtype) for e in early],
        in_specs=[pl.BlockSpec(memory_space=pltpu.SMEM)]
        + in_vmem(len(arrays) - 1)
        + [pl.BlockSpec(memory_space=pl.ANY)]
        + in_vmem(len(early)),
        out_specs=in_vmem(2 + len(early)),
        scratch_shapes=[
            pltpu.VMEM((rows, 3 * width), BF16),
            pltpu.VMEM((width, 3 * width), BF16),
            pltpu.SemaphoreType.DMA((1,)),
        ],
        compiler_params=params(),
        name="final",
    )(live, *arrays, *early)
    return results[0], results[1], results[2:]


def deliver_kernel(late_ref, *outs):
    width = outs[0].shape[1]
    for i in range(3):
        outs[i][...] = late_ref[:, i * width : (i + 1) * width]
    gains = late_ref[:, 3 * width :]
    rows = gains.shape[0]
    square = jnp.concatenate([gains, jnp.zeros((128 - rows, 128), F32)], axis=0).T
    for i in range(2):
        outs[3 + i][...] = square[i : i + 1, :rows]


def deliver(late_sum, width):
    rows = late_sum.shape[0]
    shapes = [(rows, width)] * 3 + [(1, rows)] * 2
    *sums, gain_one, gain_two = pl.pallas_call(
        deliver_kernel,
        out_shape=[jax.ShapeDtypeStruct(shape, F32) for shape in shapes],
        in_specs=in_vmem(1),
        out_specs=in_vmem(5),
        compiler_params=params(),
        name="deliver",
    )(late_sum)
    return sums, gain_one.reshape(rows), gain_two.reshape(rows)


REACH = {"all": ("seq", "mem"), "line": "mem", "square": "seq"}


def gather_plain(array, reach):
    return lax.all_gather(array, REACH[reach], axis=0)


def scatter_plain(array, reach):
    return lax.psum_scatter(array, REACH[reach], scatter_dimension=0, tiled=True).astype(F32)


def return_plain(array):
    return lax.all_to_all(array, "mem", split_axis=0, concat_axis=0, tiled=True)


def join_peers(outs, stats):
    top = jnp.max(stats[:, :HEADS], axis=0)
    shares = jnp.exp2(stats[:, :HEADS] - top)
    total = jnp.sum(stats[:, HEADS:] * shares, axis=0)
    wide = jnp.repeat(jnp.swapaxes(shares, 1, 2), outs.shape[-1] // HEADS, axis=2)
    joined = jnp.sum(outs.astype(F32) * wide, axis=0).astype(BF16)
    return joined[None], jnp.concatenate([top, total], axis=0)[None]


def per_device(
    sizes,
    tokens,
    cached_keys,
    cached_values,
    knn_index,
    has_memory,
    w_query,
    w_key,
    w_value,
    w_out,
    gain_attn,
    w_gate,
    w_up,
    w_down,
    gain_ffn,
    cotangent,
):
    near = sizes["seq"] == 4 and sizes["mem"] % 2 == 0 and 4 <= sizes["mem"] <= 16
    inputs, grad_out = tokens[0], cotangent[0]
    rows, width = inputs.shape
    hidden_width = w_gate.shape[1]
    head_width = width // HEADS
    scale = head_width ** (-0.5) * LOG2E
    mem_dev = cached_keys.shape[1]
    place = lax.axis_index("seq").astype(jnp.int32)[None]
    base = (lax.axis_index("mem") * mem_dev).astype(jnp.int32)[None]

    gains = jnp.concatenate(
        [gain_attn[:, None], gain_ffn[:, None], jnp.zeros((w_query.shape[0], 126), BF16)], axis=1
    )
    first_shard = jnp.concatenate([w_query, w_key, w_value, gains], axis=1)
    if near:
        jobs = [
            index_job(sizes, knn_index[0], mem_dev),
            gather_job(sizes, first_shard, row_halves, "all"),
        ]
        (bits,), (first_weights,) = together(1, "first", sizes, jobs)
    else:
        first_weights = gather_plain(first_shard, "all")
        bits = mask_bits(base, gather_plain(knn_index[0], "line"), mem_dev)
        flags = lax.all_gather(has_memory, "mem", axis=0, tiled=True)
        order = jnp.argsort(jnp.where(flags > 0, 0, 1), stable=True)
        order = order[: flags.shape[0] // 2].astype(jnp.int32)
    first_weights = first_weights.reshape(-1, first_shard.shape[1])

    positions = lax.axis_index("seq") * rows + jnp.arange(rows)
    cosine, sine = angles_for(positions, head_width)
    cosine = jnp.concatenate([cosine, cosine], axis=1)
    sine = jnp.concatenate([-sine, sine], axis=1)
    norm_one, queries, keys_values, gain_rows = project(inputs, first_weights, cosine, sine)
    if near:
        jobs = [
            forward_job(
                sizes, queries, keys_values, bits, cached_keys, cached_values, scale
            ),
            gather_job(sizes, w_out, row_halves, "all"),
            gather_job(sizes, w_gate, row_halves, "all"),
            gather_job(sizes, w_up, row_halves, "all"),
            gather_job(sizes, w_down, column_halves, "all"),
        ]
        results, (out_weight,), (gate_weight,), (up_weight,), (down_weight,) = together(
            2, "second", sizes, jobs
        )
        all_queries, segment_kv, *peers = results[:4]
        local = results[4:]
        segment_kv = segment_kv.reshape(-1, 2 * width)
    else:
        all_queries = gather_plain(queries, "line")
        segment_kv = gather_plain(keys_values, "square").reshape(-1, 2 * width)
        owner_out, owner_stats = owner_forward(
            order, all_queries, bits, cached_keys, cached_values, scale
        )
        peers = join_peers(return_plain(owner_out), return_plain(owner_stats))
        local = alone("local_forward", place, local_job("forward", [queries, segment_kv], scale))
        out_weight, gate_weight = gather_plain(w_out, "all"), gather_plain(w_gate, "all")
        up_weight, down_weight = gather_plain(w_up, "all"), gather_plain(w_down, "all")
    weights = [
        out_weight.reshape(width, width),
        gate_weight.reshape(width, hidden_width),
        up_weight.reshape(width, hidden_width),
        down_weight.reshape(hidden_width, width),
    ]
    mixed, grad_mid, grad_attention, back_stats, gain_two_grad, *early = middle(
        has_memory, inputs, grad_out, gain_rows, local, peers, weights
    )
    if near:
        jobs = [
            backward_job(
                sizes, queries, grad_attention, back_stats, segment_kv,
                all_queries, bits, cached_keys, cached_values, scale,
            ),
            *[scatter_job(sizes, grad, row_halves) for grad in early[:3]],
            scatter_job(sizes, early[3], column_halves),
        ]
        (_, peer_grads, local_dq, grad_kv), *early_sums = together(3, "third", sizes, jobs)
        grad_kv = grad_kv.reshape(rows, 2 * width)
        early_sums = [total for (total,) in early_sums]
    else:
        all_grads, all_stats = gather_plain(grad_attention, "line"), gather_plain(back_stats, "line")
        local_work = local_job(
            "backward", [queries, grad_attention, back_stats, segment_kv], scale
        )
        local_dq, local_dkv = alone("local_backward", place, local_work)
        owner_grads = owner_backward(
            order, all_queries, all_grads, all_stats, bits, cached_keys, cached_values, scale
        )
        peer_grads = jnp.sum(return_plain(owner_grads).astype(F32), axis=0, keepdims=True)
        grad_kv = scatter_plain(local_dkv, "square")
        early_sums = [scatter_plain(grad, "all") for grad in early]
    grad_inputs, late, early_sums = final(
        has_memory, inputs, grad_mid, gain_rows, gain_two_grad, norm_one, local_dq, peer_grads, grad_kv,
        cosine, sine, first_weights, early=early_sums,
    )
    if near:
        ((late_sum,),) = together(4, "fourth", sizes, [scatter_job(sizes, late, row_halves)])
    else:
        late_sum = scatter_plain(late, "all")
    late_sums, gain_one_sum, gain_two_sum = deliver(late_sum, width)
    return (
        mixed[None],
        grad_inputs[None],
        *late_sums,
        early_sums[0],
        gain_one_sum,
        *early_sums[1:],
        gain_two_sum,
    )


def solution(mesh):
    rows, owned, feature = P("mem", "seq", None), P(None, "mem", None), P(("seq", "mem"), None)
    gain = P(("seq", "mem"))
    return jax.shard_map(
        functools.partial(per_device, dict(mesh.shape)),
        mesh=mesh,
        in_specs=(
            (rows, owned, owned, rows, P("mem"))
            + (feature,) * 4
            + (gain,)
            + (feature,) * 3
            + (gain, rows)
        ),
        out_specs=(rows, rows) + (feature,) * 4 + (gain,) + (feature,) * 3 + (gain,),
        check_vma=False,
    )
```

```python
import functools

import jax
import jax.numpy as jnp
from jax import lax
from jax.experimental import pallas as pl
from jax.experimental.pallas import tpu as pltpu
from jax.sharding import PartitionSpec as P

HEADS = 8
EPSILON = 1e-05
FLOOR = -1e30
LOW = -1e29
LOG2E = 1.4426950408889634
STATS = 16
PIECES = 4
SPANS = [(0, 4), (4, 8)]
ORDERS = {
    ("first", 4): (
        8, 0, 7, 9, 10, 7, 2, 9, 1, 7, 8, 11, 12, 7, 10, 7, 4, 3, 7, 9, 7, 8, 11, 7, 12, 14, 13,
        7, 7, 5, 14, 7, 15, 13, 10, 15, 11, 7, 13, 6, 12, 15, 7, 15, 15, 16, 16, 16, 16, 16, 16,
        14, 7, 16, 16, 16,
    ),
    ("second", 4): (
        30, 7, 21, 44, 0, 28, 14, 29, 29, 29, 9, 32, 31, 45, 30, 29, 22, 1, 16, 29, 8, 23, 34, 28,
        29, 46, 44, 15, 47, 29, 29, 33, 2, 51, 29, 48, 29, 37, 34, 17, 3, 29, 52, 29, 29, 29, 31,
        29, 45, 24, 29, 11, 10, 28, 29, 29, 26, 49, 4, 29, 38, 28, 44, 28, 19, 12, 29, 5, 18, 59,
        62, 28, 35, 51, 29, 53, 58, 25, 49, 30, 29, 39, 52, 29, 35, 29, 46, 50, 28, 29, 29, 29,
        40, 29, 13, 58, 60, 47, 32, 59, 29, 35, 36, 20, 29, 29, 45, 38, 55, 42, 48, 27, 29, 54, 6,
        61, 49, 33, 29, 53, 60, 50, 56, 29, 29, 36, 40, 29, 41, 47, 37, 60, 31, 66, 32, 33, 39,
        51, 29, 28, 42, 29, 29, 54, 62, 28, 59, 29, 38, 46, 41, 64, 29, 56, 40, 55, 63, 52, 34,
        42, 37, 29, 66, 28, 54, 56, 48, 64, 58, 39, 57, 50, 43, 65, 57, 41, 64, 66, 36, 53, 64,
        65, 61, 66, 58, 65, 43, 55, 66, 65, 58, 61, 28, 67, 63, 43, 64, 65, 66, 65, 57, 66, 64,
        64, 65, 59, 67, 61, 67, 60, 65, 67, 66, 67, 64, 66, 67, 64, 59, 63, 60, 61, 67, 63, 67,
        65, 67,
    ),
    ("third", 4): (
        45, 37, 28, 49, 0, 35, 21, 47, 35, 42, 45, 35, 7, 14, 35, 39, 41, 38, 49, 1, 50, 44, 51,
        42, 35, 39, 23, 2, 36, 35, 45, 37, 36, 43, 29, 8, 36, 38, 49, 16, 41, 50, 22, 39, 36, 25,
        3, 40, 45, 15, 9, 10, 36, 30, 42, 36, 24, 37, 49, 36, 45, 51, 35, 36, 41, 38, 40, 49, 17,
        36, 50, 37, 4, 27, 35, 5, 35, 37, 39, 36, 46, 31, 36, 36, 42, 42, 38, 36, 41, 43, 19, 32,
        18, 40, 41, 26, 36, 11, 38, 36, 44, 50, 35, 50, 51, 46, 36, 36, 55, 33, 36, 36, 35, 48,
        36, 39, 60, 36, 12, 47, 43, 57, 36, 36, 44, 36, 57, 36, 36, 56, 36, 6, 51, 35, 51, 53, 36,
        36, 36, 36, 46, 61, 43, 36, 36, 36, 35, 36, 52, 13, 20, 35, 54, 34, 46, 63, 40, 63, 61,
        47, 43, 46, 44, 35, 52, 35, 57, 60, 40, 36, 36, 35, 47, 47, 62, 53, 35, 59, 36, 58, 35,
        53, 36, 53, 36, 52, 44, 36, 48, 61, 55, 40, 35, 62, 56, 63, 57, 56, 54, 35, 36, 54, 58,
        35, 61, 44, 48, 35, 35, 48, 63, 52, 59, 56, 52, 55, 62, 54, 56, 48, 52, 55, 59, 55, 62,
        60, 48, 54, 58, 57, 58, 59, 53, 60,
    ),
    ("fourth", 4): (
        0, 0, 1, 2, 0, 2, 3, 0, 0, 2, 1, 2, 2, 1, 3, 4, 1, 1, 3, 4, 4, 4, 3, 3, 3,
    ),
}
F32 = jnp.float32
BF16 = jnp.bfloat16
VMEM_LIMIT = 62 * 1024 * 1024
NT = (((1,), (1,)), ((), ()))
TN = (((0,), (0,)), ((), ()))


def dot(left, right, dims=(((1,), (0,)), ((), ()))):
    return lax.dot_general(left, right, dims, preferred_element_type=F32)


def rope_tables(positions, head_width):
    lane = jnp.arange(head_width)
    half = head_width // 2
    exponent = (lane % half).astype(F32) * (2.0 / head_width)
    frequency = jnp.power(10000.0, -exponent)
    turned = positions.astype(F32)[:, None] * frequency[None, :]
    sine = jnp.sin(turned)
    return jnp.cos(turned), jnp.where(lane[None, :] < half, -sine, sine)


def params(**more):
    return pltpu.CompilerParams(vmem_limit_bytes=VMEM_LIMIT, **more)


def spread(columns, width=128):
    lanes = lax.broadcasted_iota(jnp.int32, (columns[0].shape[0], width), 1)
    result = jnp.zeros((columns[0].shape[0], width), F32)
    for place, column in enumerate(columns):
        result = jnp.where(lanes == place, column, result)
    return result


def columns_of(rows_by_stat):
    count, width = rows_by_stat.shape
    padded = jnp.concatenate([rows_by_stat, jnp.zeros((128 - count, width), F32)], axis=0)
    return padded.T


MESH = pl.DeviceIdType.MESH


class Net:
    def __init__(self, line):
        self.line = line
        self.s, self.m = lax.axis_index("seq"), lax.axis_index("mem")
        self.c, self.z = self.m % 2, self.m // 2
        self.x, self.y, self.core = (self.s ^ 1, self.m), (self.s ^ 2, self.m), (self.s, self.m ^ 1)
        self.right = (self.s, (self.m + 2) % (2 * line))
        self.left = (self.s, (self.m + 2 * line - 2) % (2 * line))

    def others(self):
        ring = 2 * self.line
        return [(self.s, lax.rem(self.m + 2 * k, ring)) for k in range(1, self.line)]

    def greet(self, others):
        barrier = pltpu.get_barrier_semaphore()
        for other in others:
            pl.semaphore_signal(barrier, inc=1, device_id=other, device_id_type=MESH)
        pl.semaphore_wait(barrier, len(others))


def remote(src, dst, sends, recvs, place, device):
    return pltpu.make_async_remote_copy(
        src_ref=src,
        dst_ref=dst,
        send_sem=sends.at[place],
        recv_sem=recvs.at[place],
        device_id=device,
        device_id_type=MESH,
    )


def row_halves(ref, part):
    half = ref.shape[-2] // 2
    return ref.at[pl.ds(part * half, half)]


def column_halves(ref, part):
    half = ref.shape[-1] // 2
    return ref.at[:, pl.ds(part * half, half)]


class Gather:
    def __init__(self, net, src, out, sends, recvs, own, index, halves, line=True, square=True, core=True):
        self.net, self.src, self.out, self.sends, self.recvs, self.own = net, src, out, sends, recvs, own
        self.index, self.halves = index, halves
        self.line, self.square, self.core = line, square, core
        self.waits_core, self.waits_own, self.seen = True, True, set()

    def slot(self, s, z):
        return self.out.at[self.index(s, z, self.net.c)]

    def wait_own(self):
        pltpu.make_async_copy(self.src, self.slot(self.net.s, self.net.z), self.own).wait()

    def wait_core(self, z):
        place = self.places()[3] + z
        self.arrived(self.out.at[self.index(self.net.s, z, 1 - self.net.c)], place)

    def send(self, block, target, place, device):
        copy = remote(block, target, self.sends, self.recvs, place, device)
        copy.start()

    def sent(self, block, place):
        remote(block, block, self.sends, self.recvs, place, self.net.core).wait_send()

    def arrived(self, block, place):
        remote(block, block, self.sends, self.recvs, place, self.net.core).wait_recv()

    def places(self):
        z = self.net.line
        right, left, square, core = 0, z, 2 * z, 8 * z
        return right, left, square, core

    def chain(self, k, from_left):
        net = self.net
        z = net.z - k if from_left else net.z + k
        present = z >= 0 if from_left else z < net.line
        self.seen.add((k, from_left))
        for stage in (self.have, self.pass_square, self.end_square) if self.square else (self.have,):
            if k == 0:
                stage(0, net.z, None)
            else:
                pl.when(present)(lambda stage=stage: stage(k, z, from_left))
            yield

    def chains(self):
        chains = [self.chain(0, True)]
        for k in range(1, self.net.line if self.line else 1):
            chains += [self.chain(k, True), self.chain(k, False)]
        return chains

    def have(self, k, z, from_left):
        net = self.net
        right, left, square, core = self.places()
        target = self.slot(net.s, z)
        block = self.src if k == 0 else target
        if k == 0:
            pltpu.make_async_copy(self.src, target, self.own).start()
        else:
            self.arrived(target, (right if from_left else left) + z)
        if self.line:
            if from_left is not False:
                pl.when(net.z < net.line - 1)(lambda: self.send(block, target, right + z, net.right))
            if from_left is not True:
                pl.when(net.z > 0)(lambda: self.send(block, target, left + z, net.left))
        if self.square:
            for kind, part, device in ((0, 0, net.x), (2, 1, net.y), (1, 0, net.y), (3, 1, net.x)):
                self.send(
                    self.halves(block, part),
                    self.halves(target, part),
                    square + kind * net.line + z,
                    device,
                )
        if self.core:
            self.send(block, target, core + z, net.core)

    def pass_square(self, k, z, from_left):
        net = self.net
        _, _, square, core = self.places()
        for kind, part, other, then, device, mirror in (
            (0, 0, net.s ^ 1, 4, net.y, 1),
            (2, 1, net.s ^ 2, 5, net.x, 2),
        ):
            block = self.halves(self.slot(other, z), part)
            self.arrived(block, square + kind * net.line + z)
            self.send(block, block, square + then * net.line + z, device)
            if self.core:
                self.send(block, block, core + mirror * net.line + z, net.core)

    def end_square(self, k, z, from_left):
        net = self.net
        _, _, square, core = self.places()
        for kind, part, other, mirror in self.last(net):
            block = self.halves(self.slot(other, z), part)
            self.arrived(block, square + kind * net.line + z)
            if self.core:
                self.send(block, block, core + mirror * net.line + z, net.core)

    def last(self, net):
        return (
            (1, 0, net.s ^ 2, 3),
            (3, 1, net.s ^ 1, 5),
            (4, 0, net.s ^ 3, 4),
            (5, 1, net.s ^ 3, 6),
        )

    def closing(self):
        net = self.net
        right, left, square, core = self.places()
        own = self.slot(net.s, net.z)
        half = [self.halves(own, 0), self.halves(own, 1)] if self.square else []
        for z in range(net.line) if self.line else [net.z]:
            if self.core:
                for mirror, part, other in (
                    (0, None, net.s),
                    (1, 0, net.s ^ 1),
                    (2, 1, net.s ^ 2),
                    (3, 0, net.s ^ 2),
                    (4, 0, net.s ^ 3),
                    (5, 1, net.s ^ 1),
                    (6, 1, net.s ^ 3),
                ):
                    if part is not None and not self.square:
                        continue
                    block = self.out.at[self.index(other, z, 1 - net.c)]
                    block = block if part is None else self.halves(block, part)
                    if self.waits_core:
                        self.arrived(block, core + mirror * net.line + z)
                    self.sent(block, core + mirror * net.line + z)
                yield
            if self.square:
                for kind, part in ((0, 0), (1, 0), (2, 1), (3, 1), (4, 0), (5, 1)):
                    self.sent(half[part], square + kind * net.line + z)
                yield
            if self.line:
                pl.when((z <= net.z) & (net.z < net.line - 1))(lambda: self.sent(own, right + z))
                pl.when((z >= net.z) & (net.z > 0))(lambda: self.sent(own, left + z))
        if self.waits_own:
            self.wait_own()
        yield


class Job:
    def __init__(self, arrays, outs, scratch, steps, where=pl.ANY, out_where=pl.ANY):
        self.arrays, self.outs, self.scratch, self.steps = arrays, outs, scratch, steps
        self.where, self.out_where = where, out_where


def specs(where, arrays):
    places = where if isinstance(where, list) else [where] * len(arrays)
    return [pl.BlockSpec(memory_space=place) for place in places]


def together_kernel(line, jobs, order, *refs):
    refs = list(refs)
    take = lambda count: [refs.pop(0) for _ in range(count)]
    ins = [take(len(job.arrays)) for job in jobs]
    outs = [take(len(job.outs)) for job in jobs]
    scratch = [take(len(job.scratch)) for job in jobs]
    net = Net(line)
    net.greet([net.x, net.y, net.core] + net.others())
    chains, ends = [], []
    for job, *parts in zip(jobs, ins, outs, scratch):
        more, last = job.steps(net, *parts)
        chains += more
        ends += last
    for turn in order:
        next((chains + ends)[turn], None)
    while chains:
        chains = [chain for chain in chains if next(chain, True) is None]
    for end in ends:
        for _ in end:
            pass


def together(collective_id, name, sizes, jobs):
    line = sizes["mem"] // 2
    moved = sum(2 * a.size * a.dtype.itemsize for job in jobs for a in job.arrays)
    results = pl.pallas_call(
        functools.partial(together_kernel, line, jobs, ORDERS.get((name, line), ())),
        out_shape=[out for job in jobs for out in job.outs],
        in_specs=[s for job in jobs for s in specs(job.where, job.arrays)],
        out_specs=[s for job in jobs for s in specs(job.out_where, job.outs)],
        scratch_shapes=[s for job in jobs for s in job.scratch],
        compiler_params=params(collective_id=collective_id, has_side_effects=True),
        cost_estimate=pl.CostEstimate(flops=0, bytes_accessed=moved, transcendentals=0),
        name=name,
    )(*[a for job in jobs for a in job.arrays])
    results = list(results)
    return [[results.pop(0) for _ in job.outs] for job in jobs]


def gather_parts(net, src, out, scratch, halves, reach, pieces):
    line, rows = net.line, src.shape[0] // pieces
    index = {
        "all": lambda s, z, c: (s * line + z) * 2 + c,
        "line": lambda s, z, c: z * 2 + c,
        "square": lambda s, z, c: s,
    }[reach]
    parts = []
    for i in range(pieces):
        span = pl.ds(i * rows, rows)
        ends = (src, out) if pieces == 1 else (src.at[span], out.at[:, span])
        parts.append(
            Gather(
                net, *ends, *scratch[3 * i : 3 * i + 3], index, halves,
                line=reach != "square", square=reach != "line", core=reach != "square",
            )
        )
    return parts


def gather_semaphores(line, pieces=1):
    return ([pltpu.SemaphoreType.DMA((15 * line,))] * 2 + [pltpu.SemaphoreType.DMA]) * pieces


def gather_job(sizes, array, halves, reach, pieces=1):
    line = sizes["mem"] // 2
    slots = {"all": sizes["seq"] * sizes["mem"], "line": sizes["mem"], "square": sizes["seq"]}[reach]

    def steps(net, ins, outs, scratch):
        parts = gather_parts(net, ins[0], outs[0], scratch, halves, reach, pieces)
        return [chain for part in parts for chain in part.chains()], [part.closing() for part in parts]

    out = jax.ShapeDtypeStruct((slots,) + array.shape, array.dtype)
    return Job([array], [out], gather_semaphores(line, pieces), steps, pltpu.VMEM)


class Scatter:
    def __init__(self, net, src, out, buffers, sems, halves, whole=True):
        self.net, self.src, self.out, self.halves = net, src, out, halves
        self.whole, self.count = whole, buffers[0].shape[1]
        self.held, self.twin, self.first, self.second, self.along = buffers
        self.sends, self.recvs, self.own = sems

    def send(self, block, target, place, device):
        remote(block, target, self.sends, self.recvs, place, device).start()

    def sent(self, block, place):
        remote(block, block, self.sends, self.recvs, place, self.net.core).wait_send()

    def arrived(self, block, place):
        remote(block, block, self.sends, self.recvs, place, self.net.core).wait_recv()

    def places(self):
        z = self.count
        return 0, 4 * z, 8 * z, 10 * z, 11 * z

    def loading(self, d):
        source = self.src.at[:, d, self.net.c] if self.whole else self.src.at[:, d]
        return pltpu.make_async_copy(source, self.held.at[:, d], self.own.at[d])

    def load(self, d):
        net = self.net
        if self.src is not None:
            self.loading(d).start()
        for s in range(4 if self.whole else 0):
            self.send(self.src.at[s, d, 1 - net.c], self.twin.at[s, d], s * self.count + d, net.core)

    def add_core(self, d):
        net = self.net
        _, first, _, _, _ = self.places()
        if self.src is not None:
            self.loading(d).wait()
        for turn in (3, 2, 1, 0):
            s = net.s ^ turn
            if self.whole:
                self.arrived(self.twin.at[s, d], s * self.count + d)
                self.held[s, d] = self.held[s, d] + self.twin[s, d]
            for part, device, slot, kind in {
                3: ((0, net.y, 1, 1), (1, net.x, 1, 3)),
                2: ((0, net.y, 0, 0),),
                1: ((1, net.x, 0, 2),),
                0: (),
            }[turn]:
                self.send(
                    self.halves(self.held.at[s, d], part),
                    self.first.at[part, slot, d],
                    first + kind * self.count + d,
                    device,
                )

    def chain(self, k):
        d = lax.rem(self.net.z + k, self.net.line) if self.whole else k
        for stage in (self.load, self.add_core, self.add_first, self.add_second, self.line_step):
            stage(d)
            yield
        if self.whole and k == 0:
            self.keep()
            yield

    def add(self, block, other):
        block[...] = block[...] + other[...]

    def add_first(self, d):
        net = self.net
        _, first, second, _, _ = self.places()
        for part, slot, kind, turn in ((0, 1, 1, 1), (1, 1, 3, 2), (0, 0, 0, 0), (1, 0, 2, 0)):
            got = self.first.at[part, slot, d]
            self.arrived(got, first + kind * self.count + d)
            block = self.halves(self.held.at[net.s ^ turn, d], part)
            self.add(block, got)
            if turn:
                device = net.x if part == 0 else net.y
                self.send(block, self.second.at[part, d], second + part * self.count + d, device)

    def add_second(self, d):
        net = self.net
        _, _, second, _, _ = self.places()
        for part in range(2):
            self.arrived(self.second.at[part, d], second + part * self.count + d)
            self.add(self.halves(self.held.at[net.s, d], part), self.second.at[part, d])

    def line_step(self, d):
        net = self.net
        _, _, _, right, left = self.places()
        block = self.held.at[net.s, d]
        if not self.whole:
            self.out[0][d] = block[...].astype(F32)
            return

        def go():
            pltpu.make_async_remote_copy(
                src_ref=block,
                dst_ref=self.along.at[net.z],
                send_sem=self.sends.at[right + d],
                recv_sem=self.recvs.at[left + net.z],
                device_id=(net.s, 2 * d + net.c),
                device_id_type=MESH,
            ).start()

        pl.when(net.z != d)(go)

    def keep(self):
        net = self.net
        _, _, _, _, left = self.places()
        total = self.held[net.s, net.z].astype(F32)
        for k in range(1, net.line):
            z = lax.rem(net.z + k, net.line)
            self.arrived(self.along.at[z], left + z)
            total = total + self.along[z].astype(F32)
        start = 0
        for out in self.out:
            out[...] = total[:, start : start + out.shape[-1]]
            start += out.shape[-1]

    def closing(self):
        net = self.net
        _, first, second, right, _ = self.places()
        full = self.held.at[net.s, 0]
        for k in far_first(self.count):
            d = lax.rem(net.z + k, net.line) if self.whole else k
            for s in range(4 if self.whole else 0):
                self.sent(full, s * self.count + d)
            for kind, part in enumerate((0, 0, 1, 1)):
                self.sent(self.halves(full, part), first + kind * self.count + d)
            for part in range(2):
                self.sent(self.halves(full, part), second + part * self.count + d)
            if self.whole and k:
                self.sent(full, right + d)
            yield


def far_first(count):
    return sorted(range(count), key=lambda k: (k == 0, -min(k, count - k)))


def scatter_scratch(count, rows, columns, halves, whole):
    half = (rows // 2, columns) if halves is row_halves else (rows, columns // 2)
    block, unused = (rows, columns), (16, 128)
    return [
        pltpu.VMEM((4, count) + block, BF16),
        pltpu.VMEM((4, count) + block if whole else unused, BF16),
        pltpu.VMEM((2, 2, count) + half, BF16),
        pltpu.VMEM((2, count) + half, BF16),
        pltpu.VMEM((count,) + block if whole else unused, BF16),
        pltpu.SemaphoreType.DMA((12 * count,)),
        pltpu.SemaphoreType.DMA((12 * count,)),
        pltpu.SemaphoreType.DMA((count,)),
    ]


def scatter_job(sizes, array, halves, whole=True):
    square, line = sizes["seq"], sizes["mem"] // 2
    columns = array.shape[1]
    if whole:
        count, rows = line, array.shape[0] // (2 * square * line)
        array = array.reshape(square, line, 2, rows, columns)
        outs = [jax.ShapeDtypeStruct((rows, w), F32) for w in [columns]]
    else:
        count, rows = PIECES, array.shape[0] // (square * PIECES)
        array = array.reshape(square, count, rows, columns)
        outs = [jax.ShapeDtypeStruct((count, rows, columns), F32)]
    scratch = scatter_scratch(count, rows, columns, halves, whole)

    def steps(net, ins, outs, scratch):
        scatter = Scatter(net, ins[0], outs, scratch[:5], scratch[5:], halves, whole)
        return [scatter.chain(k) for k in far_first(count)], [scatter.closing()]

    return Job([array], outs, scratch, steps, out_where=pltpu.VMEM)


class Return:
    def __init__(self, net, sources, outs, scratch):
        kinds = len(sources)
        self.net, self.sources, self.outs, self.kinds = net, sources, outs, range(kinds)
        self.held, self.twin = scratch[:kinds], scratch[kinds : 2 * kinds]
        self.own, self.twin_sends, self.twin_recvs, self.sends, self.recvs = scratch[2 * kinds :]

    def loading(self, i, d):
        source = self.sources[i].at[d, self.net.c]
        return pltpu.make_async_copy(source, self.held[i].at[d], self.own.at[i, d])

    def pairing(self, i, d):
        net = self.net
        return remote(
            self.sources[i].at[d, 1 - net.c],
            self.twin[i].at[d],
            self.twin_sends.at[i],
            self.twin_recvs.at[i],
            d,
            net.core,
        )

    def giving(self, i, k, d, slot, device):
        return pltpu.make_async_remote_copy(
            src_ref=self.held[i].at[d],
            dst_ref=self.outs[i].at[slot],
            send_sem=self.sends.at[i, k],
            recv_sem=self.recvs.at[i, slot],
            device_id=device,
            device_id_type=MESH,
        )

    def keeping(self, i, d):
        return pltpu.make_async_copy(
            self.held[i].at[d], self.outs[i].at[self.net.z], self.own.at[i, d]
        )

    def merge(self, d):
        held, twin = self.held, self.twin
        if len(held) == 1:
            held[0][d] = held[0][d] + twin[0][d]
            return
        mine, theirs = held[1][d], twin[1][d]
        top = jnp.maximum(mine[:HEADS], theirs[:HEADS])
        shares = [jnp.exp2(mine[:HEADS] - top), jnp.exp2(theirs[:HEADS] - top)]
        held[1][d] = jnp.concatenate(
            [top, mine[HEADS:] * shares[0] + theirs[HEADS:] * shares[1]], axis=0
        )
        shares = columns_of(jnp.concatenate(shares, axis=0))
        for h in range(HEADS):
            span = slice(h * 128, (h + 1) * 128)
            held[0][d, :, span] = (
                held[0][d, :, span].astype(F32) * shares[:, h : h + 1]
                + twin[0][d, :, span].astype(F32) * shares[:, HEADS + h : HEADS + h + 1]
            ).astype(BF16)


def index_job(sizes, index, mem_dev):
    line = sizes["mem"] // 2
    segments = 2 * line
    rows, count = index.shape
    out = jax.ShapeDtypeStruct((segments, rows, 128), jnp.int32)
    scratch = gather_semaphores(line) + mask_scratch(rows, count)
    scratch = scratch + [pltpu.VMEM((segments, rows, count), jnp.int32)]

    def steps(net, ins, outs, scratch):
        *sems, places_ref, words_ref, all_index = scratch
        (part,) = gather_parts(net, ins[0], all_index, sems, row_halves, "line", 1)
        part.waits_core = part.waits_own = False

        def words(z, far):
            if far:
                part.wait_core(z)
            segment = 2 * z + (1 - net.c if far else net.c)
            outs[0][segment] = mask_words(
                all_index[segment], net.m * mem_dev, mem_dev, places_ref, words_ref
            )

        def masks():
            for k in range(line):
                for from_left in (True, False) if k else (True,):
                    z = net.z - k if from_left else net.z + k
                    present = z >= 0 if from_left else z < line
                    here = (lambda body: body()) if k == 0 else pl.when(present)
                    need([part], k, from_left)
                    if k == 0:
                        part.wait_own()
                    for far in (False, True):
                        here(lambda: words(z, far))
                        yield

        return part.chains() + [masks()], [part.closing()]

    return Job([index], [out], scratch, steps, pltpu.VMEM, pltpu.VMEM)


def need(parts, k, from_left):
    for part in parts:
        assert (k, from_left) in part.seen


class OwnerForward(Return):
    def __init__(self, net, scale, parts, ins, outs, scratch, sems):
        self.bits, self.keys, self.values = ins
        self.queries, *peers = outs
        self.bias, self.kept, self.key, self.value, *held = scratch
        self.far, held = held[:2], held[2:]
        self.loads, *sems = sems
        super().__init__(net, self.far, peers, held + sems)
        self.parts, self.scale = parts, scale

    def pairing(self, i, d):
        net = self.net
        return remote(
            self.far[i].at[d],
            self.twin[i].at[d],
            self.twin_sends.at[i],
            self.twin_recvs.at[i],
            d,
            net.core,
        )

    def bring(self, z, far):
        net = self.net
        segment = 2 * z + (1 - net.c if far else net.c)
        slot = int(far)
        return [
            pltpu.make_async_copy(self.keys.at[segment], self.key.at[slot], self.loads.at[0, slot]),
            pltpu.make_async_copy(
                self.values.at[segment], self.value.at[slot], self.loads.at[1, slot]
            ),
        ]

    def attend(self, z, far, span):
        net = self.net
        segment = 2 * z + (1 - net.c if far else net.c)
        if span[0] == 0:
            if far:
                for part in self.parts:
                    part.wait_core(z)
            fill_bias(self.bits.at[segment], self.bias)
            for copy in self.bring(z, far):
                copy.wait()
        target = self.far if far else self.held
        owner_forward_heads(
            span,
            self.scale,
            self.queries.at[segment],
            self.key.at[int(far)],
            self.value.at[int(far)],
            self.bias,
            self.kept,
            target[0].at[z],
            target[1].at[z],
        )
        if far and span[1] == HEADS:
            for i in self.kinds:
                self.pairing(i, z).start()

    def home(self, k, z):
        for i in self.kinds:
            self.pairing(i, z).wait_recv()
        self.merge(z)
        net = self.net
        for i in self.kinds:
            if k:
                self.giving(i, z, z, net.z, (net.s, 2 * z + net.c)).start()
            else:
                self.keeping(i, z).start()

    def chain(self):
        net = self.net
        for k in range(net.line):
            for from_left in (True, False) if k else (True,):
                z = net.z - k if from_left else net.z + k
                present = z >= 0 if from_left else z < net.line
                here = (lambda body: body()) if k == 0 else pl.when(present)
                need(self.parts, k, from_left)
                if k == 0:
                    for part in self.parts:
                        part.wait_own()

                def start():
                    for copy in self.bring(z, True) + self.bring(z, False):
                        copy.start()

                here(start)
                yield
                for far in (True, False):
                    for span in SPANS:
                        here(lambda: self.attend(z, far, span))
                        yield
                here(lambda: self.home(k, z))
                yield

    def closing(self):
        net = self.net
        for k in range(net.line):
            d = lax.rem(net.z + k, net.line)
            for i in self.kinds:
                self.pairing(i, d).wait_send()
                if k:
                    copy = self.giving(i, d, d, d, net.core)
                    copy.wait_recv()
                    copy.wait_send()
                else:
                    self.keeping(i, d).wait()
            yield


def forward_job(sizes, queries, keys_values, bits, cached_keys, cached_values, scale):
    line = sizes["mem"] // 2
    (rows, width), segments = queries.shape, bits.shape[0]
    mem_dev = cached_keys.shape[1]
    length = sizes["seq"] * rows
    shape = jax.ShapeDtypeStruct
    outs = [
        shape((segments, rows, width), BF16),
        shape((sizes["seq"],) + keys_values.shape, BF16),
        shape((line, rows, width), BF16),
        shape((line, STATS, rows), F32),
        shape((rows, width), F32),
        shape((STATS, rows), F32),
    ]
    partial = [pltpu.VMEM((line, rows, width), BF16), pltpu.VMEM((line, STATS, rows), F32)]
    scratch = (
        gather_semaphores(line, PIECES)
        + gather_semaphores(line)
        + [pltpu.VMEM((rows, length), F32)]
        + [pltpu.VMEM((rows, mem_dev), F32), pltpu.VMEM((rows, 128), F32)]
        + [pltpu.VMEM((2, mem_dev, width), BF16)] * 2
        + partial * 3
        + [pltpu.SemaphoreType.DMA((2, 2))]
        + [pltpu.SemaphoreType.DMA((2, line))] * 5
    )

    def steps(net, ins, outs, scratch):
        queries, keys_values, *owner_ins = ins
        all_queries, segment_kv, out, stats, local_out, local_stats = outs
        scratch = list(scratch)
        take = lambda count: [scratch.pop(0) for _ in range(count)]
        parts = gather_parts(net, queries, all_queries, take(3 * PIECES), row_halves, "line", PIECES)
        (square,) = gather_parts(net, keys_values, segment_kv, take(3), row_halves, "square", 1)
        (local_bias,) = take(1)
        buffers = take(10)
        owner = OwnerForward(
            net, scale, parts, owner_ins, [all_queries, out, stats], buffers, scratch
        )
        for part in parts:
            part.waits_core = part.waits_own = False
        square.waits_own = False

        def local():
            for chain in square.chains():
                yield from chain
            square.wait_own()
            yield from local_forward_steps(
                scale, net.s, queries, segment_kv, local_out, local_stats, local_bias
            )

        chains = [chain for part in parts for chain in part.chains()]
        ends = [part.closing() for part in parts] + [square.closing(), owner.closing()]
        return chains + [local(), owner.chain()], ends

    vmem = pltpu.VMEM
    return Job(
        [queries, keys_values, bits, cached_keys, cached_values],
        outs,
        scratch,
        steps,
        [vmem, vmem, vmem, pl.ANY, pl.ANY],
        [vmem, vmem, pl.ANY, pl.ANY, vmem, vmem],
    )


def mask_words(index, base, mem_dev, place_ref, bit_ref):
    relative = index - base
    inside = (relative >= 0) & (relative < mem_dev)
    place = jnp.where(inside, relative & 127, 0)
    bit = jnp.where(inside, lax.shift_left(jnp.ones_like(relative), relative >> 7), 0)
    place_ref[...] = place.T
    bit_ref[...] = bit.T
    sought = lax.broadcasted_iota(jnp.int32, (128, 128), 0)
    halves = []
    for start in range(0, index.shape[0], 128):

        def eight(g, words, start=start):
            group = pl.ds(pl.multiple_of(g * 8, 8), 8)
            places = place_ref[group, start : start + 128]
            bits = bit_ref[group, start : start + 128]
            for j in range(8):
                words = words | jnp.where(places[j : j + 1] == sought, bits[j : j + 1], 0)
            return words

        none = jnp.zeros((128, 128), jnp.int32)
        words = lax.fori_loop(0, index.shape[1] // 8, eight, none)
        halves.append(words.T)
    return jnp.concatenate(halves, axis=0)


def mask_scratch(rows, count):
    return [pltpu.VMEM((count, rows), jnp.int32), pltpu.VMEM((count, rows), jnp.int32)]


def mask_kernel(mem_dev, base_ref, index_ref, bits_ref, place_ref, bit_ref):
    bits_ref[0] = mask_words(index_ref[0], base_ref[0], mem_dev, place_ref, bit_ref)


def mask_bits(base, all_index, mem_dev):
    segments, rows, count = all_index.shape
    return pl.pallas_call(
        functools.partial(mask_kernel, mem_dev),
        grid_spec=pltpu.PrefetchScalarGridSpec(
            num_scalar_prefetch=1,
            grid=(segments,),
            in_specs=[pl.BlockSpec((1, rows, count), lambda g, b: (g, 0, 0))],
            out_specs=pl.BlockSpec((1, rows, 128), lambda g, b: (g, 0, 0)),
            scratch_shapes=mask_scratch(rows, count),
        ),
        out_shape=jax.ShapeDtypeStruct((segments, rows, 128), jnp.int32),
        compiler_params=params(),
        name="mask_bits",
    )(base, all_index)


def fill_bias(bits_ref, bias_ref):
    bits = bits_ref[...].reshape(bits_ref.shape[-2:])
    for b in range(bias_ref.shape[1] // 128):
        bias_ref[:, b * 128 : (b + 1) * 128] = jnp.where(((bits >> b) & 1) != 0, 0.0, FLOOR)


def owner_backward_heads(span, scale, q_ref, g_ref, st_ref, k_ref, v_ref, bias_ref, dq_ref):
    stats = columns_of(st_ref[...])
    lanes = lax.broadcasted_iota(jnp.int32, stats.shape, 1)

    def two(i, carry):
        for h in (2 * i, 2 * i + 1):
            lane = pl.ds(pl.multiple_of(h * 128, 128), 128)
            total = jnp.sum(jnp.where(lanes == h, stats, 0.0), axis=1, keepdims=True)
            dots = jnp.sum(jnp.where(lanes == HEADS + h, stats, 0.0), axis=1, keepdims=True)
            scores = dot(q_ref[:, lane], k_ref[:, lane], NT) * scale + bias_ref[...]
            weights = jnp.exp2(scores - total)
            dscore = weights * (dot(g_ref[:, lane], v_ref[:, lane], NT) - dots)
            dq_ref[:, lane] = (
                dot(dscore.astype(BF16), k_ref[:, lane]) * (scale / LOG2E)
            ).astype(BF16)
        return carry

    lax.fori_loop(span[0] // 2, span[1] // 2, two, 0)


def owner_forward_heads(span, scale, q_ref, k_ref, v_ref, bias_ref, stats_ref, o_ref, st_ref):
    rows = q_ref.shape[0]
    lanes = lax.broadcasted_iota(jnp.int32, (rows, 128), 1)

    def two(i, stats):
        for h in (2 * i, 2 * i + 1):
            lane = pl.ds(pl.multiple_of(h * 128, 128), 128)
            scores = dot(q_ref[:, lane], k_ref[:, lane], NT) * scale + bias_ref[...]
            top = jnp.maximum(jnp.max(scores, axis=1, keepdims=True), LOW)
            weights = jnp.exp2(scores - top)
            total = jnp.sum(weights, axis=1, keepdims=True)
            stats = jnp.where(lanes == h, top, jnp.where(lanes == HEADS + h, total, stats))
            o_ref[:, lane] = dot(weights.astype(BF16), v_ref[:, lane]).astype(BF16)
        return stats

    start = stats_ref[...] if span[0] else jnp.zeros((rows, 128), F32)
    stats = lax.fori_loop(span[0] // 2, span[1] // 2, two, start)
    if span[1] == HEADS:
        st_ref[...] = stats.T[:STATS]
    else:
        stats_ref[...] = stats


def owner_forward_kernel(scale, order_ref, q_ref, bits_ref, k_ref, v_ref, o_ref, st_ref, bias_ref):
    del order_ref
    fill_bias(bits_ref, bias_ref)
    maxima, sums = [], []
    for h in range(HEADS):
        span = slice(h * 128, (h + 1) * 128)
        scores = dot(q_ref[0, :, span], k_ref[0, :, span], NT) * scale + bias_ref[...]
        top = jnp.maximum(jnp.max(scores, axis=1, keepdims=True), LOW)
        weights = jnp.exp2(scores - top)
        maxima.append(top)
        sums.append(jnp.sum(weights, axis=1, keepdims=True))
        o_ref[0, :, span] = dot(weights.astype(BF16), v_ref[0, :, span]).astype(BF16)
    st_ref[0] = spread(maxima + sums).T[:STATS]


def owner_forward(order, queries, bits, cached_keys, cached_values, scale):
    segments, rows, width = queries.shape
    mem_dev = cached_keys.shape[1]
    active = order.shape[0]
    picked = lambda a, o: (o[a], 0, 0)
    return pl.pallas_call(
        functools.partial(owner_forward_kernel, scale),
        grid_spec=pltpu.PrefetchScalarGridSpec(
            num_scalar_prefetch=1,
            grid=(active,),
            in_specs=[
                pl.BlockSpec((1, rows, width), picked),
                pl.BlockSpec((1, rows, 128), picked),
                pl.BlockSpec((1, mem_dev, width), picked),
                pl.BlockSpec((1, mem_dev, width), picked),
            ],
            out_specs=[
                pl.BlockSpec((1, rows, width), picked),
                pl.BlockSpec((1, STATS, rows), picked),
            ],
            scratch_shapes=[pltpu.VMEM((rows, mem_dev), F32)],
        ),
        out_shape=[
            jax.ShapeDtypeStruct((segments, rows, width), BF16),
            jax.ShapeDtypeStruct((segments, STATS, rows), F32),
        ],
        compiler_params=params(),
        name="owner_forward",
    )(order, queries, bits, cached_keys, cached_values)


def owner_backward_kernel(
    scale, order_ref, q_ref, g_ref, st_ref, bits_ref, k_ref, v_ref, dq_ref, bias_ref
):
    del order_ref
    fill_bias(bits_ref, bias_ref)
    stats = columns_of(st_ref[0])
    for h in range(HEADS):
        span = slice(h * 128, (h + 1) * 128)
        scores = dot(q_ref[0, :, span], k_ref[0, :, span], NT) * scale + bias_ref[...]
        weights = jnp.exp2(scores - stats[:, h : h + 1])
        dweights = dot(g_ref[0, :, span], v_ref[0, :, span], NT)
        dscore = weights * (dweights - stats[:, HEADS + h : HEADS + h + 1])
        dq_ref[0, :, span] = (
            dot(dscore.astype(BF16), k_ref[0, :, span]) * (scale / LOG2E)
        ).astype(BF16)


def owner_backward(order, queries, grads, stats, bits, cached_keys, cached_values, scale):
    segments, rows, width = queries.shape
    mem_dev = cached_keys.shape[1]
    active = order.shape[0]
    picked = lambda a, o: (o[a], 0, 0)
    return pl.pallas_call(
        functools.partial(owner_backward_kernel, scale),
        grid_spec=pltpu.PrefetchScalarGridSpec(
            num_scalar_prefetch=1,
            grid=(active,),
            in_specs=[
                pl.BlockSpec((1, rows, width), picked),
                pl.BlockSpec((1, rows, width), picked),
                pl.BlockSpec((1, STATS, rows), picked),
                pl.BlockSpec((1, rows, 128), picked),
                pl.BlockSpec((1, mem_dev, width), picked),
                pl.BlockSpec((1, mem_dev, width), picked),
            ],
            out_specs=pl.BlockSpec((1, rows, width), picked),
            scratch_shapes=[pltpu.VMEM((rows, mem_dev), F32)],
        ),
        out_shape=jax.ShapeDtypeStruct((segments, rows, width), BF16),
        compiler_params=params(),
        name="owner_backward",
    )(order, queries, grads, stats, bits, cached_keys, cached_values)


def causal_bias(place, rows, keys):
    row = place * rows + lax.broadcasted_iota(jnp.int32, (rows, keys), 0)
    return jnp.where(lax.broadcasted_iota(jnp.int32, (rows, keys), 1) <= row, 0.0, FLOOR)


def columns_at(kv_ref, span):
    block = kv_ref[:, span] if len(kv_ref.shape) == 2 else kv_ref[:, :, span]
    return block.reshape(-1, block.shape[-1])


def local_forward_steps(scale, place, q_ref, kv_ref, o_ref, st_ref, bias_ref):
    rows, width = q_ref.shape
    bias_ref[...] = causal_bias(place, rows, bias_ref.shape[1])
    maxima, sums = [], []
    for h in range(HEADS):
        span, over = slice(h * 128, (h + 1) * 128), slice(width + h * 128, width + (h + 1) * 128)
        scores = dot(q_ref[:, span], columns_at(kv_ref, span), NT) * scale + bias_ref[...]
        top = jnp.max(scores, axis=1, keepdims=True)
        weights = jnp.exp2(scores - top)
        maxima.append(top)
        sums.append(jnp.sum(weights, axis=1, keepdims=True))
        o_ref[:, span] = dot(weights.astype(BF16), columns_at(kv_ref, over))
        yield
    st_ref[...] = spread(maxima + sums).T[:STATS]


def local_backward_steps(
    scale, place, q_ref, g_ref, st_ref, kv_ref, dq_ref, dkv_ref, bias_ref
):
    rows, width = q_ref.shape
    bias_ref[...] = causal_bias(place, rows, bias_ref.shape[1])
    stats = columns_of(st_ref[...])
    for h in range(HEADS):
        span, over = slice(h * 128, (h + 1) * 128), slice(width + h * 128, width + (h + 1) * 128)
        query, key, grad = q_ref[:, span], columns_at(kv_ref, span), g_ref[:, span]
        scores = dot(query, key, NT) * scale + bias_ref[...]
        weights = jnp.exp2(scores - stats[:, h : h + 1])
        dweights = dot(grad, columns_at(kv_ref, over), NT)
        dscore = (weights * (dweights - stats[:, HEADS + h : HEADS + h + 1])).astype(BF16)
        dq_ref[:, span] = dot(dscore, key) * (scale / LOG2E)
        dkey = (dot(dscore, query, TN) * (scale / LOG2E)).astype(BF16)
        dvalue = dot(weights.astype(BF16), grad, TN).astype(BF16)
        lead = dkv_ref.shape[:-1]
        dkv_ref[(*[slice(None)] * len(lead), span)] = dkey.reshape(lead + (128,))
        dkv_ref[(*[slice(None)] * len(lead), over)] = dvalue.reshape(lead + (128,))
        yield


class OwnerBackward(OwnerForward):
    def __init__(self, net, scale, parts, stats_part, ins, outs, scratch, sems):
        self.sources_in = ins
        self.grads, self.stats, peers = outs
        *self.buffers, self.bias, far, held, twin = scratch
        self.loads, *sems = sems
        self.far = [far]
        Return.__init__(self, net, self.far, [peers], [held, twin, *sems])
        self.parts, self.scale, self.stats_part = [*parts, stats_part], scale, stats_part

    def bring(self, z, far):
        segment = 2 * z + (1 - self.net.c if far else self.net.c)
        sources = [source.at[segment] for source in (*self.sources_in, self.grads)]
        return [
            pltpu.make_async_copy(source, buffer, self.loads.at[i])
            for i, (source, buffer) in enumerate(zip(sources, self.buffers))
        ]

    def mask(self, z, far):
        if far:
            for part in self.parts:
                part.wait_core(z)
        for copy in self.bring(z, far):
            copy.start()

    def attend(self, z, far, span):
        net = self.net
        keys, values, queries, bits, grads = self.buffers
        if span[0] == 0:
            for copy in self.bring(z, far):
                copy.wait()
            fill_bias(bits, self.bias)
        segment = 2 * z + (1 - net.c if far else net.c)
        owner_backward_heads(
            span,
            self.scale,
            queries,
            grads,
            self.stats.at[segment],
            keys,
            values,
            self.bias,
            (self.far[0] if far else self.held[0]).at[z],
        )
        if far and span[1] == HEADS:
            self.pairing(0, z).start()

    def chain(self):
        net = self.net
        for k in range(net.line):
            for from_left in (True, False) if k else (True,):
                z = net.z - k if from_left else net.z + k
                present = z >= 0 if from_left else z < net.line
                here = (lambda body: body()) if k == 0 else pl.when(present)
                need(self.parts, k, from_left)
                if k == 0:
                    for part in self.parts:
                        part.wait_own()
                here(lambda: self.mask(z, True))
                yield
                for far in (True, False):
                    for span in SPANS:

                        def part():
                            self.attend(z, far, span)
                            if far and span[1] == HEADS:
                                self.mask(z, False)

                        here(part)
                        yield
                here(lambda: self.home(k, z))
                yield


def backward_job(
    sizes, queries, grads, stats, segment_kv, all_queries, bits, cached_keys, cached_values, scale
):
    square, line = sizes["seq"], sizes["mem"] // 2
    segments, rows, width = all_queries.shape
    mem_dev = cached_keys.shape[1]
    length = square * rows
    shape = jax.ShapeDtypeStruct
    outs = [
        shape((segments, rows, width), BF16),
        shape((line, rows, width), BF16),
        shape((rows, width), F32),
        shape((PIECES, rows // PIECES, 2 * width), F32),
    ]
    keys_scratch = scatter_scratch(PIECES, rows // PIECES, 2 * width, row_halves, False)
    scratch = (
        gather_semaphores(line, PIECES)
        + gather_semaphores(line)
        + [pltpu.VMEM((segments, STATS, rows), F32), pltpu.VMEM((rows, length), F32)]
        + keys_scratch
        + [pltpu.VMEM((mem_dev, width), BF16)] * 2
        + [
            pltpu.VMEM((rows, width), BF16),
            pltpu.VMEM((rows, 128), jnp.int32),
            pltpu.VMEM((rows, width), BF16),
            pltpu.VMEM((rows, mem_dev), F32),
        ]
        + [pltpu.VMEM((line, rows, width), BF16)] * 3
        + [pltpu.SemaphoreType.DMA((5,))]
        + [pltpu.SemaphoreType.DMA((1, line))] * 5
    )

    def steps(net, ins, outs, scratch):
        queries, grads, stats, segment_kv, all_queries, bits, keys, values = ins
        all_grads, peers, local_dq, grad_kv = outs
        scratch = list(scratch)
        take = lambda count: [scratch.pop(0) for _ in range(count)]
        parts = gather_parts(net, grads, all_grads, take(3 * PIECES), row_halves, "line", PIECES)
        stats_sems = take(3)
        all_stats, local_bias = take(2)
        (stats_part,) = gather_parts(net, stats, all_stats, stats_sems, row_halves, "line", 1)
        keys_scratch = take(8)
        buffers = take(9)
        scatter = Scatter(
            net, None, [grad_kv], keys_scratch[:5], keys_scratch[5:], row_halves, False
        )
        owner = OwnerBackward(
            net, scale, parts, stats_part, [keys, values, all_queries, bits],
            [all_grads, all_stats, peers], buffers, scratch,
        )
        for part in [*parts, stats_part]:
            part.waits_core = part.waits_own = False

        def local():
            yield from local_backward_steps(
                scale, net.s, queries, grads, stats, segment_kv, local_dq, scatter.held, local_bias
            )
            stages = (scatter.add_core, scatter.add_first, scatter.add_second, scatter.line_step)
            for wave in range(PIECES + 3):
                for lag in (3, 2, 1, 0):
                    if 0 <= wave - lag < PIECES:
                        stages[lag](wave - lag)
                        yield

        chains = [chain for part in [*parts, stats_part] for chain in part.chains()]
        ends = [part.closing() for part in [*parts, stats_part]]
        ends += [scatter.closing(), owner.closing()]
        return chains + [local(), owner.chain()], ends

    vmem = pltpu.VMEM
    return Job(
        [queries, grads, stats, segment_kv, all_queries, bits, cached_keys, cached_values],
        outs,
        scratch,
        steps,
        [vmem] * 4 + [pl.ANY] * 4,
        [pl.ANY, pl.ANY, vmem, vmem],
    )


def local_job(kind, arrays, scale):
    rows, width = arrays[0].shape
    length = arrays[-1].shape[0]
    if kind == "forward":
        body, extra = local_forward_steps, jax.ShapeDtypeStruct((STATS, rows), F32)
    else:
        body, extra = local_backward_steps, jax.ShapeDtypeStruct((length, 2 * width), BF16)

    def steps(net, ins, outs, scratch):
        return [body(scale, net.s, *ins, *outs, *scratch)], []

    outs = [jax.ShapeDtypeStruct((rows, width), F32), extra]
    return Job(arrays, outs, [pltpu.VMEM((rows, length), F32)], steps, pltpu.VMEM, pltpu.VMEM)


def alone_kernel(job, *refs):
    place_ref, *refs = refs
    net = type("Alone", (), {"s": place_ref[0]})
    ins, outs = len(job.arrays), len(job.arrays) + len(job.outs)
    for chain in job.steps(net, refs[:ins], refs[ins:outs], refs[outs:])[0]:
        for _ in chain:
            pass


def alone(name, place, job):
    return pl.pallas_call(
        functools.partial(alone_kernel, job),
        out_shape=job.outs,
        in_specs=[pl.BlockSpec(memory_space=pltpu.SMEM)]
        + [pl.BlockSpec(memory_space=pltpu.VMEM)] * len(job.arrays),
        out_specs=[pl.BlockSpec(memory_space=pltpu.VMEM)] * len(job.outs),
        scratch_shapes=job.scratch,
        compiler_params=params(),
        name=name,
    )(place, *job.arrays)


def copy_in(pairs, sems):
    copies = [pltpu.make_async_copy(src, dst, sems.at[i]) for i, (src, dst) in enumerate(pairs)]
    for copy in copies:
        copy.start()
    return copies


def turn(values, cosine, sine):
    return values * cosine + pltpu.roll(values, values.shape[1] // 2, 1) * sine


def inverse_root(values):
    return lax.rsqrt(jnp.mean(values * values, axis=1, keepdims=True) + EPSILON)


def project_kernel(x_ref, w_any, cos_ref, sin_ref, n_ref, q_ref, kv_ref, gain_ref, w_ref, sems):
    width = x_ref.shape[1]
    spans = [slice(i * width, (i + 1) * width) for i in range(3)]
    gains = slice(3 * width, 3 * width + 128)
    copies = copy_in([(w_any.at[:, s], w_ref.at[:, s]) for s in [gains, *spans]], sems)
    x = x_ref[...].astype(F32)
    copies[0].wait()
    gain_ref[...] = w_ref[:, gains].astype(F32).T[:8]
    normed = (x * inverse_root(x) * gain_ref[:1]).astype(BF16)
    n_ref[...] = normed
    cosine, sine = cos_ref[...], sin_ref[...]
    for i in range(3):
        copies[1 + i].wait()
        product = dot(normed, w_ref[:, spans[i]])
        for h in range(HEADS):
            span = slice(h * 128, (h + 1) * 128)
            part = product[:, span]
            part = part if i == 2 else turn(part, cosine, sine)
            if i == 0:
                q_ref[:, span] = part.astype(BF16)
            else:
                over = slice((i - 1) * width + h * 128, (i - 1) * width + (h + 1) * 128)
                kv_ref[:, over] = part.astype(BF16)


def in_vmem(count):
    return [pl.BlockSpec(memory_space=pltpu.VMEM)] * count


def project(tokens, first_weights, cosine, sine):
    rows, width = tokens.shape
    columns = first_weights.shape[1]
    return pl.pallas_call(
        project_kernel,
        out_shape=[
            jax.ShapeDtypeStruct((rows, width), BF16),
            jax.ShapeDtypeStruct((rows, width), BF16),
            jax.ShapeDtypeStruct((rows, 2 * width), BF16),
            jax.ShapeDtypeStruct((8, width), F32),
        ],
        in_specs=in_vmem(1) + [pl.BlockSpec(memory_space=pl.ANY)] + in_vmem(2),
        out_specs=in_vmem(4),
        scratch_shapes=[
            pltpu.VMEM((width, columns), BF16),
            pltpu.SemaphoreType.DMA((4,)),
        ],
        compiler_params=params(),
        name="project",
    )(tokens, first_weights, cosine, sine)


def middle_kernel(
    live_ref, x_ref, g_ref, gain_ref, lo_ref, ls_ref, po_ref, ps_ref, out_any, gate_any, up_any, down_any,
    mixed_ref, gm_ref, ga_ref, st_ref, gain_grad_ref, wo_any, wg_any, wu_any, wd_any,
    att_ref, acc_ref, gn_ref, n_ref, nt_ref, out_ref, gate_ref, up_ref, down_ref, side_ref, tall_ref, sems, writes,
):
    rows, width = x_ref.shape
    copies = copy_in(
        [(out_any, out_ref), (gate_any, gate_ref), (up_any, up_ref), (down_any, down_ref)], sems
    )
    live = live_ref[0] > 0
    peers = ps_ref.shape[0]
    local_max, local_sum = ls_ref[:HEADS], ls_ref[HEADS:]
    peer_max = [jnp.where(live, ps_ref[p, :HEADS], LOW) for p in range(peers)]
    peer_sum = [jnp.where(live, ps_ref[p, HEADS:], 0.0) for p in range(peers)]
    top = functools.reduce(jnp.maximum, peer_max, local_max)
    shares = [jnp.exp2(m - top) for m in [local_max] + peer_max]
    total = functools.reduce(
        jnp.add, [s * t for s, t in zip(shares, [local_sum] + peer_sum)]
    )
    log_total = top + jnp.log2(total)
    shares = columns_of(jnp.concatenate([s / total for s in shares], axis=0))
    for h in range(HEADS):
        span = slice(h * 128, (h + 1) * 128)
        part = lo_ref[:, span] * shares[:, h : h + 1]
        for p in range(peers):
            column = shares[:, (p + 1) * HEADS + h : (p + 1) * HEADS + h + 1]
            part += jnp.where(live, po_ref[p, :, span].astype(F32), 0.0) * column
        att_ref[:, span] = part
    attention_low = att_ref[...].astype(BF16)
    copies[0].wait()
    mid = x_ref[...].astype(F32) + dot(attention_low, out_ref[...])
    gm_ref[...] = mid
    root = inverse_root(mid)
    n_ref[...] = (mid * root * gain_ref[1:2]).astype(BF16)
    for copy in copies[1:]:
        copy.wait()
    nt_ref[...] = n_ref[...].T
    grad = g_ref[...]
    acc_ref[...] = jnp.zeros_like(acc_ref)
    gn_ref[...] = jnp.zeros_like(gn_ref)
    hidden_width = gate_ref.shape[1]
    step = 512
    pending = [[], []]

    def write(slot, product, buffer, target, place):
        buffer[...] = product.astype(BF16)
        copy = pltpu.make_async_copy(buffer, target, writes.at[slot, place])
        copy.start()
        pending[slot].append(copy)

    for turn_of, start in enumerate(range(0, hidden_width, step)):
        span = slice(start, min(start + step, hidden_width))
        slot = turn_of % 2
        while pending[slot]:
            pending[slot].pop().wait()
        norm_two = n_ref[...]
        gate = dot(norm_two, gate_ref[:, span])
        upward = dot(norm_two, up_ref[:, span])
        grad_hidden = dot(grad, down_ref[span, :], NT)
        sigmoid = 1.0 / (1.0 + jnp.exp(-gate))
        silu = gate * sigmoid
        hidden = (silu * upward).astype(BF16)
        grad_gate = (grad_hidden * upward * (sigmoid * (1.0 + gate * (1.0 - sigmoid)))).astype(BF16)
        grad_up = (grad_hidden * silu).astype(BF16)
        write(slot, dot(nt_ref[...], grad_gate), side_ref.at[slot, 0, :, : span.stop - start], wg_any.at[:, span], 0)
        write(slot, dot(nt_ref[...], grad_up), side_ref.at[slot, 1, :, : span.stop - start], wu_any.at[:, span], 1)
        write(slot, dot(hidden, grad, TN), tall_ref.at[slot, : span.stop - start], wd_any.at[span, :], 2)
        acc_ref[...] += dot(hidden, down_ref[span, :])
        gn_ref[...] += dot(grad_gate, gate_ref[:, span], NT) + dot(grad_up, up_ref[:, span], NT)
    mid = gm_ref[...]
    mixed_ref[...] = mid + acc_ref[...]
    normed = mid * root
    grad_norm = gn_ref[...]
    gain_grad_ref[...] = jnp.broadcast_to(
        jnp.sum(grad_norm * normed, axis=0, keepdims=True), gain_grad_ref.shape
    )
    scaled = grad_norm * gain_ref[1:2]
    grad_mid = grad.astype(F32) + root * (
        scaled - normed * jnp.mean(normed * scaled, axis=1, keepdims=True)
    )
    gm_ref[...] = grad_mid
    grad_mid_low = grad_mid.astype(BF16)
    nt_ref[...] = att_ref[...].astype(BF16).T
    for start in range(0, width, step):
        span = slice(start, start + step)
        slot = start // step % 2
        while pending[slot]:
            pending[slot].pop().wait()
        write(slot, dot(nt_ref[...], grad_mid_low[:, span]), side_ref.at[slot, 0], wo_any.at[:, span], 0)
    grad_attention = dot(grad_mid_low, out_ref[...], NT).astype(BF16)
    ga_ref[...] = grad_attention
    products = grad_attention.astype(F32) * att_ref[...]
    dots = [
        jnp.sum(products[:, h * 128 : (h + 1) * 128], axis=1, keepdims=True) for h in range(HEADS)
    ]
    st_ref[...] = jnp.concatenate([log_total, spread(dots).T[:HEADS]], axis=0)
    for copy in pending[0] + pending[1]:
        copy.wait()


def middle(live, tokens, grads, gains, local, peers, weights):
    rows, width = tokens.shape
    hidden_width = weights[1].shape[1]
    full = lambda columns, kind: jax.ShapeDtypeStruct((rows, columns), kind)
    return pl.pallas_call(
        middle_kernel,
        out_shape=[
            full(width, F32),
            full(width, F32),
            full(width, BF16),
            jax.ShapeDtypeStruct((STATS, rows), F32),
            jax.ShapeDtypeStruct((8, width), F32),
        ]
        + [jax.ShapeDtypeStruct(w.shape, BF16) for w in weights],
        in_specs=[pl.BlockSpec(memory_space=pltpu.SMEM)]
        + in_vmem(7)
        + [pl.BlockSpec(memory_space=pl.ANY)] * 4,
        out_specs=in_vmem(5) + [pl.BlockSpec(memory_space=pl.ANY)] * 4,
        scratch_shapes=[pltpu.VMEM((rows, width), F32)] * 3
        + [pltpu.VMEM((rows, width), BF16), pltpu.VMEM((width, rows), BF16)]
        + [pltpu.VMEM(w.shape, BF16) for w in weights]
        + [
            pltpu.VMEM((2, 2, width, 512), BF16),
            pltpu.VMEM((2, 512, width), BF16),
            pltpu.SemaphoreType.DMA((4,)),
            pltpu.SemaphoreType.DMA((2, 3)),
        ],
        compiler_params=params(),
        name="middle",
    )(live, tokens, grads, gains, *local, *peers, *weights)


def final_kernel(
    live_ref, x_ref, gm_ref, gain_ref, ggain_ref, n_ref, dq_ref, pd_ref, dkv_ref, cos_ref, sin_ref, w_any,
    *rest,
):
    rows, width = x_ref.shape
    ready, (gx_ref, late_ref), given = rest[:4], rest[4:6], rest[6:10]
    in_ref, w_ref, made_ref, sems, writes = rest[10:]
    copies = copy_in([(w_any.at[:, : 3 * width], w_ref)], sems)

    def write(i, span):
        copy = pltpu.make_async_copy(made_ref.at[:, span], late_ref.at[:, span], writes.at[i])
        copy.start()
        copies.append(copy)

    for source, target in zip(ready, given):
        target[...] = source[...]
    live = live_ref[0] > 0
    cosine, sine = cos_ref[...], -sin_ref[...]
    for h in range(HEADS):
        span = slice(h * 128, (h + 1) * 128)
        part = dq_ref[:, span]
        for p in range(pd_ref.shape[0]):
            part += jnp.where(live, pd_ref[p, :, span].astype(F32), 0.0)
        in_ref[:, span] = turn(part, cosine, sine).astype(BF16)
        over = slice(width + h * 128, width + (h + 1) * 128)
        in_ref[:, over] = turn(dkv_ref[:, span], cosine, sine).astype(BF16)
    in_ref[:, 2 * width :] = dkv_ref[:, width:].astype(BF16)
    flipped = n_ref[...].T
    for i in range(3):
        span = slice(i * width, (i + 1) * width)
        made_ref[:, span] = dot(flipped, in_ref[:, span]).astype(BF16)
        write(i, span)
    copies[0].wait()
    grad_norm = dot(in_ref[...], w_ref[...], NT)
    x = x_ref[...].astype(F32)
    root = inverse_root(x)
    normed = x * root
    gains = jnp.concatenate(
        [
            jnp.sum(grad_norm * normed, axis=0, keepdims=True),
            ggain_ref[:1],
            jnp.zeros((126, width), F32),
        ],
        axis=0,
    )
    made_ref[:, 3 * width :] = gains.T.astype(BF16)
    write(3, slice(3 * width, made_ref.shape[1]))
    scaled = grad_norm * gain_ref[:1]
    gx_ref[...] = gm_ref[...] + root * (
        scaled - normed * jnp.mean(normed * scaled, axis=1, keepdims=True)
    )
    for copy in copies[1:]:
        copy.wait()


def final(live, *arrays, early):
    rows, width = arrays[0].shape
    columns = arrays[-1].shape[1]
    results = pl.pallas_call(
        final_kernel,
        out_shape=[
            jax.ShapeDtypeStruct((rows, width), F32),
            jax.ShapeDtypeStruct((width, columns), BF16),
        ]
        + [jax.ShapeDtypeStruct(e.shape, e.dtype) for e in early],
        in_specs=[pl.BlockSpec(memory_space=pltpu.SMEM)]
        + in_vmem(len(arrays) - 1)
        + [pl.BlockSpec(memory_space=pl.ANY)]
        + in_vmem(len(early)),
        out_specs=in_vmem(1) + [pl.BlockSpec(memory_space=pl.ANY)] + in_vmem(len(early)),
        scratch_shapes=[
            pltpu.VMEM((rows, 3 * width), BF16),
            pltpu.VMEM((width, 3 * width), BF16),
            pltpu.VMEM((width, columns), BF16),
            pltpu.SemaphoreType.DMA((1,)),
            pltpu.SemaphoreType.DMA((4,)),
        ],
        compiler_params=params(),
        name="final",
    )(live, *arrays, *early)
    return results[0], results[1], results[2:]


def deliver_kernel(late_ref, *outs):
    width = outs[0].shape[1]
    for i in range(3):
        outs[i][...] = late_ref[:, i * width : (i + 1) * width]
    gains = late_ref[:, 3 * width :]
    rows = gains.shape[0]
    square = jnp.concatenate([gains, jnp.zeros((128 - rows, 128), F32)], axis=0).T
    for i in range(2):
        outs[3 + i][...] = square[i : i + 1, :rows]


def deliver(late_sum, width):
    rows = late_sum.shape[0]
    shapes = [(rows, width)] * 3 + [(1, rows)] * 2
    *sums, gain_one, gain_two = pl.pallas_call(
        deliver_kernel,
        out_shape=[jax.ShapeDtypeStruct(shape, F32) for shape in shapes],
        in_specs=in_vmem(1),
        out_specs=in_vmem(5),
        compiler_params=params(),
        name="deliver",
    )(late_sum)
    return sums, gain_one.reshape(rows), gain_two.reshape(rows)


REACH = {"all": ("seq", "mem"), "line": "mem", "square": "seq"}


def gather_plain(array, reach):
    return lax.all_gather(array, REACH[reach], axis=0)


def scatter_plain(array, reach):
    return lax.psum_scatter(array, REACH[reach], scatter_dimension=0, tiled=True).astype(F32)


def return_plain(array):
    return lax.all_to_all(array, "mem", split_axis=0, concat_axis=0, tiled=True)


def join_peers(outs, stats):
    top = jnp.max(stats[:, :HEADS], axis=0)
    shares = jnp.exp2(stats[:, :HEADS] - top)
    total = jnp.sum(stats[:, HEADS:] * shares, axis=0)
    wide = jnp.repeat(jnp.swapaxes(shares, 1, 2), outs.shape[-1] // HEADS, axis=2)
    joined = jnp.sum(outs.astype(F32) * wide, axis=0).astype(BF16)
    return joined[None], jnp.concatenate([top, total], axis=0)[None]


def per_device(
    sizes,
    tokens,
    cached_keys,
    cached_values,
    knn_index,
    has_memory,
    w_query,
    w_key,
    w_value,
    w_out,
    gain_attn,
    w_gate,
    w_up,
    w_down,
    gain_ffn,
    cotangent,
):
    near = sizes["seq"] == 4 and sizes["mem"] % 2 == 0 and 4 <= sizes["mem"] <= 16
    inputs, grad_out = tokens[0], cotangent[0]
    rows, width = inputs.shape
    hidden_width = w_gate.shape[1]
    head_width = width // HEADS
    scale = head_width ** (-0.5) * LOG2E
    mem_dev = cached_keys.shape[1]
    place = lax.axis_index("seq").astype(jnp.int32)[None]
    base = (lax.axis_index("mem") * mem_dev).astype(jnp.int32)[None]

    gains = jnp.concatenate(
        [gain_attn[:, None], gain_ffn[:, None], jnp.zeros((w_query.shape[0], 126), BF16)], axis=1
    )
    first_shard = jnp.concatenate([w_query, w_key, w_value, gains], axis=1)
    if near:
        jobs = [
            index_job(sizes, knn_index[0], mem_dev),
            gather_job(sizes, first_shard, row_halves, "all"),
        ]
        (bits,), (first_weights,) = together(1, "first", sizes, jobs)
    else:
        first_weights = gather_plain(first_shard, "all")
        bits = mask_bits(base, gather_plain(knn_index[0], "line"), mem_dev)
        flags = lax.all_gather(has_memory, "mem", axis=0, tiled=True)
        order = jnp.argsort(jnp.where(flags > 0, 0, 1), stable=True)
        order = order[: flags.shape[0] // 2].astype(jnp.int32)
    first_weights = first_weights.reshape(-1, first_shard.shape[1])

    positions = lax.axis_index("seq") * rows + jnp.arange(rows)
    cosine, sine = rope_tables(positions, head_width)
    norm_one, queries, keys_values, gain_rows = project(inputs, first_weights, cosine, sine)
    if near:
        jobs = [
            forward_job(
                sizes, queries, keys_values, bits, cached_keys, cached_values, scale
            ),
            gather_job(sizes, w_out, row_halves, "all"),
            gather_job(sizes, w_gate, row_halves, "all"),
            gather_job(sizes, w_up, row_halves, "all"),
            gather_job(sizes, w_down, column_halves, "all"),
        ]
        results, (out_weight,), (gate_weight,), (up_weight,), (down_weight,) = together(
            2, "second", sizes, jobs
        )
        all_queries, segment_kv, *peers = results[:4]
        local = results[4:]
        segment_kv = segment_kv.reshape(-1, 2 * width)
    else:
        all_queries = gather_plain(queries, "line")
        segment_kv = gather_plain(keys_values, "square").reshape(-1, 2 * width)
        owner_out, owner_stats = owner_forward(
            order, all_queries, bits, cached_keys, cached_values, scale
        )
        peers = join_peers(return_plain(owner_out), return_plain(owner_stats))
        local = alone("local_forward", place, local_job("forward", [queries, segment_kv], scale))
        out_weight, gate_weight = gather_plain(w_out, "all"), gather_plain(w_gate, "all")
        up_weight, down_weight = gather_plain(w_up, "all"), gather_plain(w_down, "all")
    weights = [
        out_weight.reshape(width, width),
        gate_weight.reshape(width, hidden_width),
        up_weight.reshape(width, hidden_width),
        down_weight.reshape(hidden_width, width),
    ]
    mixed, grad_mid, grad_attention, back_stats, gain_two_grad, *early = middle(
        has_memory, inputs, grad_out, gain_rows, local, peers, weights
    )
    if near:
        jobs = [
            backward_job(
                sizes, queries, grad_attention, back_stats, segment_kv,
                all_queries, bits, cached_keys, cached_values, scale,
            ),
            *[scatter_job(sizes, grad, row_halves) for grad in early[:3]],
            scatter_job(sizes, early[3], column_halves),
        ]
        (_, peer_grads, local_dq, grad_kv), *early_sums = together(3, "third", sizes, jobs)
        grad_kv = grad_kv.reshape(rows, 2 * width)
        early_sums = [total for (total,) in early_sums]
    else:
        all_grads, all_stats = gather_plain(grad_attention, "line"), gather_plain(back_stats, "line")
        local_work = local_job(
            "backward", [queries, grad_attention, back_stats, segment_kv], scale
        )
        local_dq, local_dkv = alone("local_backward", place, local_work)
        owner_grads = owner_backward(
            order, all_queries, all_grads, all_stats, bits, cached_keys, cached_values, scale
        )
        peer_grads = jnp.sum(return_plain(owner_grads).astype(F32), axis=0, keepdims=True)
        grad_kv = scatter_plain(local_dkv, "square")
        early_sums = [scatter_plain(grad, "all") for grad in early]
    grad_inputs, late, early_sums = final(
        has_memory, inputs, grad_mid, gain_rows, gain_two_grad, norm_one, local_dq, peer_grads, grad_kv,
        cosine, sine, first_weights, early=early_sums,
    )
    if near:
        ((late_sum,),) = together(4, "fourth", sizes, [scatter_job(sizes, late, row_halves)])
    else:
        late_sum = scatter_plain(late, "all")
    late_sums, gain_one_sum, gain_two_sum = deliver(late_sum, width)
    return (
        mixed[None],
        grad_inputs[None],
        *late_sums,
        early_sums[0],
        gain_one_sum,
        *early_sums[1:],
        gain_two_sum,
    )


def solution(mesh):
    rows, owned, feature = P("mem", "seq", None), P(None, "mem", None), P(("seq", "mem"), None)
    gain = P(("seq", "mem"))
    return jax.shard_map(
        functools.partial(per_device, dict(mesh.shape)),
        mesh=mesh,
        in_specs=(
            (rows, owned, owned, rows, P("mem"))
            + (feature,) * 4
            + (gain,)
            + (feature,) * 3
            + (gain, rows)
        ),
        out_specs=(rows, rows) + (feature,) * 4 + (gain,) + (feature,) * 3 + (gain,),
        check_vma=False,
    )
```

```python
import functools

import jax
import jax.numpy as jnp
from jax import lax
from jax.experimental import pallas as pl
from jax.experimental.pallas import tpu as pltpu
from jax.sharding import PartitionSpec as P

HEADS = 8
EPSILON = 1e-05
FLOOR = -1e30
LOW = -1e29
LOG2E = 1.4426950408889634
STATS = 16
PIECES = 4
SPANS = [(0, 4), (4, 8)]
ORDERS = {
    ("first", 4): (
        8, 0, 7, 9, 10, 7, 2, 9, 1, 7, 8, 11, 12, 7, 10, 7, 4, 3, 7, 9, 7, 8, 11, 7, 12, 14, 13,
        7, 7, 5, 14, 7, 15, 13, 10, 15, 11, 7, 13, 6, 12, 15, 7, 15, 15, 16, 16, 16, 16, 16, 16,
        14, 7, 16, 16, 16,
    ),
    ("second", 4): (
        28, 30, 44, 0, 21, 7, 46, 37, 14, 29, 29, 29, 31, 51, 29, 29, 15, 1, 38, 8, 23, 9, 32, 29,
        2, 22, 33, 29, 45, 28, 16, 29, 3, 35, 29, 17, 5, 11, 52, 29, 40, 47, 29, 51, 29, 24, 29,
        29, 54, 30, 53, 29, 29, 29, 10, 34, 4, 29, 29, 39, 29, 33, 29, 18, 29, 29, 31, 19, 42, 29,
        28, 13, 28, 25, 29, 48, 46, 29, 58, 60, 47, 29, 29, 6, 28, 55, 29, 58, 60, 49, 28, 54, 62,
        56, 35, 34, 40, 26, 32, 60, 29, 38, 12, 37, 20, 29, 29, 41, 29, 61, 48, 51, 55, 52, 53,
        29, 32, 59, 29, 36, 56, 33, 29, 27, 29, 31, 45, 34, 49, 42, 50, 28, 37, 44, 29, 29, 35,
        54, 59, 47, 57, 29, 39, 38, 29, 28, 50, 48, 46, 28, 52, 29, 30, 28, 61, 53, 64, 41, 40,
        36, 63, 45, 58, 56, 64, 43, 42, 49, 59, 57, 67, 55, 28, 64, 64, 64, 61, 64, 43, 36, 50,
        44, 39, 67, 41, 57, 67, 65, 65, 65, 65, 65, 61, 64, 65, 67, 66, 58, 64, 66, 43, 67, 63,
        63, 58, 67, 60, 66, 63, 67, 67, 66, 60, 61, 66, 59, 66, 64, 67, 66, 66, 65, 65, 62, 66,
        65, 59,
    ),
    ("third", 4): (
        51, 21, 41, 38, 0, 14, 42, 35, 35, 51, 35, 45, 35, 28, 7, 41, 42, 40, 46, 35, 36, 22, 23,
        35, 2, 50, 51, 1, 36, 45, 49, 15, 16, 37, 41, 36, 8, 9, 35, 29, 49, 36, 51, 30, 51, 37,
        36, 45, 50, 36, 36, 4, 41, 41, 42, 18, 39, 49, 25, 36, 43, 11, 17, 45, 45, 36, 43, 50, 35,
        32, 36, 49, 24, 35, 49, 48, 36, 36, 43, 36, 37, 39, 46, 42, 50, 48, 3, 50, 36, 42, 36, 38,
        62, 31, 52, 26, 47, 43, 40, 35, 56, 43, 10, 37, 44, 5, 37, 36, 36, 36, 36, 46, 47, 27, 53,
        39, 36, 36, 33, 57, 35, 19, 59, 36, 20, 36, 53, 36, 36, 38, 36, 36, 6, 40, 46, 13, 35, 34,
        46, 48, 36, 36, 36, 47, 35, 61, 55, 63, 35, 12, 38, 39, 36, 61, 47, 55, 54, 52, 38, 36,
        57, 36, 39, 36, 60, 40, 36, 35, 36, 36, 56, 36, 36, 35, 54, 63, 36, 44, 36, 35, 47, 35,
        54, 60, 35, 58, 61, 52, 62, 36, 55, 44, 35, 35, 57, 40, 44, 53, 57, 56, 63, 52, 60, 55,
        61, 58, 60, 52, 62, 56, 58, 62, 56, 48, 63, 44, 52, 35, 54, 48, 58, 40, 53, 55, 44, 35,
        35, 48, 59, 53, 59, 57, 54, 59,
    ),
    ("fourth", 4): (
        0, 0, 1, 2, 0, 2, 3, 0, 0, 2, 1, 2, 2, 1, 3, 4, 1, 1, 3, 4, 4, 4, 3, 3, 3,
    ),
}
F32 = jnp.float32
BF16 = jnp.bfloat16
VMEM_LIMIT = 62 * 1024 * 1024
NT = (((1,), (1,)), ((), ()))
TN = (((0,), (0,)), ((), ()))


def dot(left, right, dims=(((1,), (0,)), ((), ()))):
    return lax.dot_general(left, right, dims, preferred_element_type=F32)


def rope_tables(positions, head_width):
    lane = jnp.arange(head_width)
    half = head_width // 2
    exponent = (lane % half).astype(F32) * (2.0 / head_width)
    frequency = jnp.power(10000.0, -exponent)
    turned = positions.astype(F32)[:, None] * frequency[None, :]
    sine = jnp.sin(turned)
    return jnp.cos(turned), jnp.where(lane[None, :] < half, -sine, sine)


def params(**more):
    return pltpu.CompilerParams(vmem_limit_bytes=VMEM_LIMIT, **more)


def spread(columns, width=128):
    lanes = lax.broadcasted_iota(jnp.int32, (columns[0].shape[0], width), 1)
    result = jnp.zeros((columns[0].shape[0], width), F32)
    for place, column in enumerate(columns):
        result = jnp.where(lanes == place, column, result)
    return result


def columns_of(rows_by_stat):
    count, width = rows_by_stat.shape
    padded = jnp.concatenate([rows_by_stat, jnp.zeros((128 - count, width), F32)], axis=0)
    return padded.T


MESH = pl.DeviceIdType.MESH


class Net:
    def __init__(self, line):
        self.line = line
        self.s, self.m = lax.axis_index("seq"), lax.axis_index("mem")
        self.c, self.z = self.m % 2, self.m // 2
        self.x, self.y, self.core = (self.s ^ 1, self.m), (self.s ^ 2, self.m), (self.s, self.m ^ 1)
        self.right = (self.s, (self.m + 2) % (2 * line))
        self.left = (self.s, (self.m + 2 * line - 2) % (2 * line))

    def others(self):
        ring = 2 * self.line
        return [(self.s, lax.rem(self.m + 2 * k, ring)) for k in range(1, self.line)]

    def greet(self, others):
        barrier = pltpu.get_barrier_semaphore()
        for other in others:
            pl.semaphore_signal(barrier, inc=1, device_id=other, device_id_type=MESH)
        pl.semaphore_wait(barrier, len(others))


def remote(src, dst, sends, recvs, place, device):
    return pltpu.make_async_remote_copy(
        src_ref=src,
        dst_ref=dst,
        send_sem=sends.at[place],
        recv_sem=recvs.at[place],
        device_id=device,
        device_id_type=MESH,
    )


def row_halves(ref, part):
    half = ref.shape[-2] // 2
    return ref.at[pl.ds(part * half, half)]


def column_halves(ref, part):
    half = ref.shape[-1] // 2
    return ref.at[:, pl.ds(part * half, half)]


class Gather:
    def __init__(self, net, src, out, sends, recvs, own, index, halves, line=True, square=True, core=True):
        self.net, self.src, self.out, self.sends, self.recvs, self.own = net, src, out, sends, recvs, own
        self.index, self.halves = index, halves
        self.line, self.square, self.core = line, square, core
        self.waits_core, self.waits_own, self.seen = True, True, set()

    def slot(self, s, z):
        return self.out.at[self.index(s, z, self.net.c)]

    def wait_own(self):
        pltpu.make_async_copy(self.src, self.slot(self.net.s, self.net.z), self.own).wait()

    def wait_core(self, z):
        place = self.places()[3] + z
        self.arrived(self.out.at[self.index(self.net.s, z, 1 - self.net.c)], place)

    def send(self, block, target, place, device):
        copy = remote(block, target, self.sends, self.recvs, place, device)
        copy.start()

    def sent(self, block, place):
        remote(block, block, self.sends, self.recvs, place, self.net.core).wait_send()

    def arrived(self, block, place):
        remote(block, block, self.sends, self.recvs, place, self.net.core).wait_recv()

    def places(self):
        z = self.net.line
        right, left, square, core = 0, z, 2 * z, 8 * z
        return right, left, square, core

    def chain(self, k, from_left):
        net = self.net
        z = net.z - k if from_left else net.z + k
        present = z >= 0 if from_left else z < net.line
        self.seen.add((k, from_left))
        for stage in (self.have, self.pass_square, self.end_square) if self.square else (self.have,):
            if k == 0:
                stage(0, net.z, None)
            else:
                pl.when(present)(lambda stage=stage: stage(k, z, from_left))
            yield

    def chains(self):
        chains = [self.chain(0, True)]
        for k in range(1, self.net.line if self.line else 1):
            chains += [self.chain(k, True), self.chain(k, False)]
        return chains

    def have(self, k, z, from_left):
        net = self.net
        right, left, square, core = self.places()
        target = self.slot(net.s, z)
        block = self.src if k == 0 else target
        if k == 0:
            pltpu.make_async_copy(self.src, target, self.own).start()
        else:
            self.arrived(target, (right if from_left else left) + z)
        if self.line:
            if from_left is not False:
                pl.when(net.z < net.line - 1)(lambda: self.send(block, target, right + z, net.right))
            if from_left is not True:
                pl.when(net.z > 0)(lambda: self.send(block, target, left + z, net.left))
        if self.square:
            for kind, part, device in ((0, 0, net.x), (2, 1, net.y), (1, 0, net.y), (3, 1, net.x)):
                self.send(
                    self.halves(block, part),
                    self.halves(target, part),
                    square + kind * net.line + z,
                    device,
                )
        if self.core:
            self.send(block, target, core + z, net.core)

    def pass_square(self, k, z, from_left):
        net = self.net
        _, _, square, core = self.places()
        for kind, part, other, then, device, mirror in (
            (0, 0, net.s ^ 1, 4, net.y, 1),
            (2, 1, net.s ^ 2, 5, net.x, 2),
        ):
            block = self.halves(self.slot(other, z), part)
            self.arrived(block, square + kind * net.line + z)
            self.send(block, block, square + then * net.line + z, device)
            if self.core:
                self.send(block, block, core + mirror * net.line + z, net.core)

    def end_square(self, k, z, from_left):
        net = self.net
        _, _, square, core = self.places()
        for kind, part, other, mirror in self.last(net):
            block = self.halves(self.slot(other, z), part)
            self.arrived(block, square + kind * net.line + z)
            if self.core:
                self.send(block, block, core + mirror * net.line + z, net.core)

    def last(self, net):
        return (
            (1, 0, net.s ^ 2, 3),
            (3, 1, net.s ^ 1, 5),
            (4, 0, net.s ^ 3, 4),
            (5, 1, net.s ^ 3, 6),
        )

    def closing(self):
        net = self.net
        right, left, square, core = self.places()
        own = self.slot(net.s, net.z)
        half = [self.halves(own, 0), self.halves(own, 1)] if self.square else []
        for z in range(net.line) if self.line else [net.z]:
            if self.core:
                for mirror, part, other in (
                    (0, None, net.s),
                    (1, 0, net.s ^ 1),
                    (2, 1, net.s ^ 2),
                    (3, 0, net.s ^ 2),
                    (4, 0, net.s ^ 3),
                    (5, 1, net.s ^ 1),
                    (6, 1, net.s ^ 3),
                ):
                    if part is not None and not self.square:
                        continue
                    block = self.out.at[self.index(other, z, 1 - net.c)]
                    block = block if part is None else self.halves(block, part)
                    if self.waits_core:
                        self.arrived(block, core + mirror * net.line + z)
                    self.sent(block, core + mirror * net.line + z)
                yield
            if self.square:
                for kind, part in ((0, 0), (1, 0), (2, 1), (3, 1), (4, 0), (5, 1)):
                    self.sent(half[part], square + kind * net.line + z)
                yield
            if self.line:
                pl.when((z <= net.z) & (net.z < net.line - 1))(lambda: self.sent(own, right + z))
                pl.when((z >= net.z) & (net.z > 0))(lambda: self.sent(own, left + z))
        if self.waits_own:
            self.wait_own()
        yield


class Job:
    def __init__(self, arrays, outs, scratch, steps, where=pl.ANY, out_where=pl.ANY):
        self.arrays, self.outs, self.scratch, self.steps = arrays, outs, scratch, steps
        self.where, self.out_where = where, out_where


def specs(where, arrays):
    places = where if isinstance(where, list) else [where] * len(arrays)
    return [pl.BlockSpec(memory_space=place) for place in places]


def together_kernel(line, jobs, order, *refs):
    refs = list(refs)
    take = lambda count: [refs.pop(0) for _ in range(count)]
    ins = [take(len(job.arrays)) for job in jobs]
    outs = [take(len(job.outs)) for job in jobs]
    scratch = [take(len(job.scratch)) for job in jobs]
    net = Net(line)
    net.greet([net.x, net.y, net.core] + net.others())
    chains, ends = [], []
    for job, *parts in zip(jobs, ins, outs, scratch):
        more, last = job.steps(net, *parts)
        chains += more
        ends += last
    for turn in order:
        next((chains + ends)[turn], None)
    while chains:
        chains = [chain for chain in chains if next(chain, True) is None]
    for end in ends:
        for _ in end:
            pass


def together(collective_id, name, sizes, jobs):
    line = sizes["mem"] // 2
    moved = sum(2 * a.size * a.dtype.itemsize for job in jobs for a in job.arrays)
    results = pl.pallas_call(
        functools.partial(together_kernel, line, jobs, ORDERS.get((name, line), ())),
        out_shape=[out for job in jobs for out in job.outs],
        in_specs=[s for job in jobs for s in specs(job.where, job.arrays)],
        out_specs=[s for job in jobs for s in specs(job.out_where, job.outs)],
        scratch_shapes=[s for job in jobs for s in job.scratch],
        compiler_params=params(collective_id=collective_id, has_side_effects=True),
        cost_estimate=pl.CostEstimate(flops=0, bytes_accessed=moved, transcendentals=0),
        name=name,
    )(*[a for job in jobs for a in job.arrays])
    results = list(results)
    return [[results.pop(0) for _ in job.outs] for job in jobs]


def gather_parts(net, src, out, scratch, halves, reach, pieces):
    line, rows = net.line, src.shape[0] // pieces
    index = {
        "all": lambda s, z, c: (s * line + z) * 2 + c,
        "line": lambda s, z, c: z * 2 + c,
        "square": lambda s, z, c: s,
    }[reach]
    parts = []
    for i in range(pieces):
        span = pl.ds(i * rows, rows)
        ends = (src, out) if pieces == 1 else (src.at[span], out.at[:, span])
        parts.append(
            Gather(
                net, *ends, *scratch[3 * i : 3 * i + 3], index, halves,
                line=reach != "square", square=reach != "line", core=reach != "square",
            )
        )
    return parts


def gather_semaphores(line, pieces=1):
    return ([pltpu.SemaphoreType.DMA((15 * line,))] * 2 + [pltpu.SemaphoreType.DMA]) * pieces


def gather_job(sizes, array, halves, reach, pieces=1):
    line = sizes["mem"] // 2
    slots = {"all": sizes["seq"] * sizes["mem"], "line": sizes["mem"], "square": sizes["seq"]}[reach]

    def steps(net, ins, outs, scratch):
        parts = gather_parts(net, ins[0], outs[0], scratch, halves, reach, pieces)
        return [chain for part in parts for chain in part.chains()], [part.closing() for part in parts]

    out = jax.ShapeDtypeStruct((slots,) + array.shape, array.dtype)
    return Job([array], [out], gather_semaphores(line, pieces), steps, pltpu.VMEM)


class Scatter:
    def __init__(self, net, src, out, buffers, sems, halves, whole=True):
        self.net, self.src, self.out, self.halves = net, src, out, halves
        self.whole, self.count = whole, buffers[0].shape[1]
        self.held, self.twin, self.first, self.second, self.along = buffers
        self.sends, self.recvs, self.own = sems

    def send(self, block, target, place, device):
        remote(block, target, self.sends, self.recvs, place, device).start()

    def sent(self, block, place):
        remote(block, block, self.sends, self.recvs, place, self.net.core).wait_send()

    def arrived(self, block, place):
        remote(block, block, self.sends, self.recvs, place, self.net.core).wait_recv()

    def places(self):
        z = self.count
        return 0, 4 * z, 8 * z, 10 * z, 11 * z

    def loading(self, d):
        source = self.src.at[:, d, self.net.c] if self.whole else self.src.at[:, d]
        return pltpu.make_async_copy(source, self.held.at[:, d], self.own.at[d])

    def load(self, d):
        net = self.net
        if self.src is not None:
            self.loading(d).start()
        for s in range(4 if self.whole else 0):
            self.send(self.src.at[s, d, 1 - net.c], self.twin.at[s, d], s * self.count + d, net.core)

    def add_core(self, d):
        net = self.net
        _, first, _, _, _ = self.places()
        if self.src is not None:
            self.loading(d).wait()
        for turn in (3, 2, 1, 0):
            s = net.s ^ turn
            if self.whole:
                self.arrived(self.twin.at[s, d], s * self.count + d)
                self.held[s, d] = self.held[s, d] + self.twin[s, d]
            for part, device, slot, kind in {
                3: ((0, net.y, 1, 1), (1, net.x, 1, 3)),
                2: ((0, net.y, 0, 0),),
                1: ((1, net.x, 0, 2),),
                0: (),
            }[turn]:
                self.send(
                    self.halves(self.held.at[s, d], part),
                    self.first.at[part, slot, d],
                    first + kind * self.count + d,
                    device,
                )

    def chain(self, k):
        d = lax.rem(self.net.z + k, self.net.line) if self.whole else k
        for stage in (self.load, self.add_core, self.add_first, self.add_second, self.line_step):
            stage(d)
            yield
        if self.whole and k == 0:
            self.keep()
            yield

    def add(self, block, other):
        block[...] = block[...] + other[...]

    def add_first(self, d):
        net = self.net
        _, first, second, _, _ = self.places()
        for part, slot, kind, turn in ((0, 1, 1, 1), (1, 1, 3, 2), (0, 0, 0, 0), (1, 0, 2, 0)):
            got = self.first.at[part, slot, d]
            self.arrived(got, first + kind * self.count + d)
            block = self.halves(self.held.at[net.s ^ turn, d], part)
            self.add(block, got)
            if turn:
                device = net.x if part == 0 else net.y
                self.send(block, self.second.at[part, d], second + part * self.count + d, device)

    def add_second(self, d):
        net = self.net
        _, _, second, _, _ = self.places()
        for part in range(2):
            self.arrived(self.second.at[part, d], second + part * self.count + d)
            self.add(self.halves(self.held.at[net.s, d], part), self.second.at[part, d])

    def line_step(self, d):
        net = self.net
        _, _, _, right, left = self.places()
        block = self.held.at[net.s, d]
        if not self.whole:
            self.out[0][d] = block[...].astype(F32)
            return

        def go():
            pltpu.make_async_remote_copy(
                src_ref=block,
                dst_ref=self.along.at[net.z],
                send_sem=self.sends.at[right + d],
                recv_sem=self.recvs.at[left + net.z],
                device_id=(net.s, 2 * d + net.c),
                device_id_type=MESH,
            ).start()

        pl.when(net.z != d)(go)

    def keep(self):
        net = self.net
        _, _, _, _, left = self.places()
        total = self.held[net.s, net.z].astype(F32)
        for k in range(1, net.line):
            z = lax.rem(net.z + k, net.line)
            self.arrived(self.along.at[z], left + z)
            total = total + self.along[z].astype(F32)
        start = 0
        for out in self.out:
            out[...] = total[:, start : start + out.shape[-1]]
            start += out.shape[-1]

    def closing(self):
        net = self.net
        _, first, second, right, _ = self.places()
        full = self.held.at[net.s, 0]
        for k in far_first(self.count):
            d = lax.rem(net.z + k, net.line) if self.whole else k
            for s in range(4 if self.whole else 0):
                self.sent(full, s * self.count + d)
            for kind, part in enumerate((0, 0, 1, 1)):
                self.sent(self.halves(full, part), first + kind * self.count + d)
            for part in range(2):
                self.sent(self.halves(full, part), second + part * self.count + d)
            if self.whole and k:
                self.sent(full, right + d)
            yield


def far_first(count):
    return sorted(range(count), key=lambda k: (k == 0, -min(k, count - k)))


def scatter_scratch(count, rows, columns, halves, whole):
    half = (rows // 2, columns) if halves is row_halves else (rows, columns // 2)
    block, unused = (rows, columns), (16, 128)
    return [
        pltpu.VMEM((4, count) + block, BF16),
        pltpu.VMEM((4, count) + block if whole else unused, BF16),
        pltpu.VMEM((2, 2, count) + half, BF16),
        pltpu.VMEM((2, count) + half, BF16),
        pltpu.VMEM((count,) + block if whole else unused, BF16),
        pltpu.SemaphoreType.DMA((12 * count,)),
        pltpu.SemaphoreType.DMA((12 * count,)),
        pltpu.SemaphoreType.DMA((count,)),
    ]


def scatter_job(sizes, array, halves, whole=True):
    square, line = sizes["seq"], sizes["mem"] // 2
    columns = array.shape[1]
    if whole:
        count, rows = line, array.shape[0] // (2 * square * line)
        array = array.reshape(square, line, 2, rows, columns)
        outs = [jax.ShapeDtypeStruct((rows, w), F32) for w in [columns]]
    else:
        count, rows = PIECES, array.shape[0] // (square * PIECES)
        array = array.reshape(square, count, rows, columns)
        outs = [jax.ShapeDtypeStruct((count, rows, columns), F32)]
    scratch = scatter_scratch(count, rows, columns, halves, whole)

    def steps(net, ins, outs, scratch):
        scatter = Scatter(net, ins[0], outs, scratch[:5], scratch[5:], halves, whole)
        return [scatter.chain(k) for k in far_first(count)], [scatter.closing()]

    return Job([array], outs, scratch, steps, out_where=pltpu.VMEM)


class Return:
    def __init__(self, net, sources, outs, scratch):
        kinds = len(sources)
        self.net, self.sources, self.outs, self.kinds = net, sources, outs, range(kinds)
        self.held, self.twin = scratch[:kinds], scratch[kinds : 2 * kinds]
        self.own, self.twin_sends, self.twin_recvs, self.sends, self.recvs = scratch[2 * kinds :]

    def loading(self, i, d):
        source = self.sources[i].at[d, self.net.c]
        return pltpu.make_async_copy(source, self.held[i].at[d], self.own.at[i, d])

    def pairing(self, i, d):
        net = self.net
        return remote(
            self.sources[i].at[d, 1 - net.c],
            self.twin[i].at[d],
            self.twin_sends.at[i],
            self.twin_recvs.at[i],
            d,
            net.core,
        )

    def giving(self, i, k, d, slot, device):
        return pltpu.make_async_remote_copy(
            src_ref=self.held[i].at[d],
            dst_ref=self.outs[i].at[slot],
            send_sem=self.sends.at[i, k],
            recv_sem=self.recvs.at[i, slot],
            device_id=device,
            device_id_type=MESH,
        )

    def keeping(self, i, d):
        return pltpu.make_async_copy(
            self.held[i].at[d], self.outs[i].at[self.net.z], self.own.at[i, d]
        )

    def merge(self, d):
        held, twin = self.held, self.twin
        if len(held) == 1:
            held[0][d] = held[0][d] + twin[0][d]
            return
        mine, theirs = held[1][d], twin[1][d]
        top = jnp.maximum(mine[:HEADS], theirs[:HEADS])
        shares = [jnp.exp2(mine[:HEADS] - top), jnp.exp2(theirs[:HEADS] - top)]
        held[1][d] = jnp.concatenate(
            [top, mine[HEADS:] * shares[0] + theirs[HEADS:] * shares[1]], axis=0
        )
        shares = columns_of(jnp.concatenate(shares, axis=0))
        for h in range(HEADS):
            span = slice(h * 128, (h + 1) * 128)
            held[0][d, :, span] = (
                held[0][d, :, span].astype(F32) * shares[:, h : h + 1]
                + twin[0][d, :, span].astype(F32) * shares[:, HEADS + h : HEADS + h + 1]
            ).astype(BF16)


def index_job(sizes, index, mem_dev):
    line = sizes["mem"] // 2
    segments = 2 * line
    rows, count = index.shape
    out = jax.ShapeDtypeStruct((segments, rows, 128), jnp.int32)
    scratch = gather_semaphores(line) + mask_scratch(rows, count)
    scratch = scratch + [pltpu.VMEM((segments, rows, count), jnp.int32)]

    def steps(net, ins, outs, scratch):
        *sems, places_ref, words_ref, all_index = scratch
        (part,) = gather_parts(net, ins[0], all_index, sems, row_halves, "line", 1)
        part.waits_core = part.waits_own = False

        def words(z, far):
            if far:
                part.wait_core(z)
            segment = 2 * z + (1 - net.c if far else net.c)
            outs[0][segment] = mask_words(
                all_index[segment], net.m * mem_dev, mem_dev, places_ref, words_ref
            )

        def masks():
            for k in range(line):
                for from_left in (True, False) if k else (True,):
                    z = net.z - k if from_left else net.z + k
                    present = z >= 0 if from_left else z < line
                    here = (lambda body: body()) if k == 0 else pl.when(present)
                    need([part], k, from_left)
                    if k == 0:
                        part.wait_own()
                    for far in (False, True):
                        here(lambda: words(z, far))
                        yield

        return part.chains() + [masks()], [part.closing()]

    return Job([index], [out], scratch, steps, pltpu.VMEM, pltpu.VMEM)


def need(parts, k, from_left):
    for part in parts:
        assert (k, from_left) in part.seen


class OwnerForward(Return):
    def __init__(self, net, scale, parts, ins, outs, scratch, sems):
        self.bits, self.keys, self.values = ins
        self.queries, *peers = outs
        self.bias, self.kept, self.key, self.value, *held = scratch
        self.far, held = held[:2], held[2:]
        self.loads, *sems = sems
        super().__init__(net, self.far, peers, held + sems)
        self.parts, self.scale = parts, scale

    def pairing(self, i, d):
        net = self.net
        return remote(
            self.far[i].at[d],
            self.twin[i].at[d],
            self.twin_sends.at[i],
            self.twin_recvs.at[i],
            d,
            net.core,
        )

    def bring(self, z, far):
        net = self.net
        segment = 2 * z + (1 - net.c if far else net.c)
        slot = int(far)
        return [
            pltpu.make_async_copy(self.keys.at[segment], self.key.at[slot], self.loads.at[0, slot]),
            pltpu.make_async_copy(
                self.values.at[segment], self.value.at[slot], self.loads.at[1, slot]
            ),
        ]

    def attend(self, z, far, span):
        net = self.net
        segment = 2 * z + (1 - net.c if far else net.c)
        if span[0] == 0:
            if far:
                for part in self.parts:
                    part.wait_core(z)
            fill_bias(self.bits.at[segment], self.bias)
            for copy in self.bring(z, far):
                copy.wait()
        target = self.far if far else self.held
        owner_forward_heads(
            span,
            self.scale,
            self.queries.at[segment],
            self.key.at[int(far)],
            self.value.at[int(far)],
            self.bias,
            self.kept,
            target[0].at[z],
            target[1].at[z],
        )
        if far and span[1] == HEADS:
            for i in self.kinds:
                self.pairing(i, z).start()

    def home(self, k, z):
        for i in self.kinds:
            self.pairing(i, z).wait_recv()
        self.merge(z)
        net = self.net
        for i in self.kinds:
            if k:
                self.giving(i, z, z, net.z, (net.s, 2 * z + net.c)).start()
            else:
                self.keeping(i, z).start()

    def chain(self):
        net = self.net
        for k in range(net.line):
            for from_left in (True, False) if k else (True,):
                z = net.z - k if from_left else net.z + k
                present = z >= 0 if from_left else z < net.line
                here = (lambda body: body()) if k == 0 else pl.when(present)
                need(self.parts, k, from_left)
                if k == 0:
                    for part in self.parts:
                        part.wait_own()

                def start():
                    for copy in self.bring(z, True) + self.bring(z, False):
                        copy.start()

                here(start)
                yield
                for far in (True, False):
                    for span in SPANS:
                        here(lambda: self.attend(z, far, span))
                        yield
                here(lambda: self.home(k, z))
                yield

    def closing(self):
        net = self.net
        for k in range(net.line):
            d = lax.rem(net.z + k, net.line)
            for i in self.kinds:
                self.pairing(i, d).wait_send()
                if k:
                    copy = self.giving(i, d, d, d, net.core)
                    copy.wait_recv()
                    copy.wait_send()
                else:
                    self.keeping(i, d).wait()
            yield


def forward_job(sizes, queries, keys_values, bits, cached_keys, cached_values, scale):
    line = sizes["mem"] // 2
    (rows, width), segments = queries.shape, bits.shape[0]
    mem_dev = cached_keys.shape[1]
    length = sizes["seq"] * rows
    shape = jax.ShapeDtypeStruct
    outs = [
        shape((segments, rows, width), BF16),
        shape((sizes["seq"],) + keys_values.shape, BF16),
        shape((line, rows, width), BF16),
        shape((line, STATS, rows), F32),
        shape((rows, width), F32),
        shape((STATS, rows), F32),
    ]
    partial = [pltpu.VMEM((line, rows, width), BF16), pltpu.VMEM((line, STATS, rows), F32)]
    scratch = (
        gather_semaphores(line, PIECES)
        + gather_semaphores(line)
        + [pltpu.VMEM((rows, length), F32)]
        + [pltpu.VMEM((rows, mem_dev), F32), pltpu.VMEM((rows, 128), F32)]
        + [pltpu.VMEM((2, mem_dev, width), BF16)] * 2
        + partial * 3
        + [pltpu.SemaphoreType.DMA((2, 2))]
        + [pltpu.SemaphoreType.DMA((2, line))] * 5
    )

    def steps(net, ins, outs, scratch):
        queries, keys_values, *owner_ins = ins
        all_queries, segment_kv, out, stats, local_out, local_stats = outs
        scratch = list(scratch)
        take = lambda count: [scratch.pop(0) for _ in range(count)]
        parts = gather_parts(net, queries, all_queries, take(3 * PIECES), row_halves, "line", PIECES)
        (square,) = gather_parts(net, keys_values, segment_kv, take(3), row_halves, "square", 1)
        (local_bias,) = take(1)
        buffers = take(10)
        owner = OwnerForward(
            net, scale, parts, owner_ins, [all_queries, out, stats], buffers, scratch
        )
        for part in parts:
            part.waits_core = part.waits_own = False
        square.waits_own = False

        def local():
            for chain in square.chains():
                yield from chain
            square.wait_own()
            yield from local_forward_steps(
                scale, net.s, queries, segment_kv, local_out, local_stats, local_bias
            )

        chains = [chain for part in parts for chain in part.chains()]
        ends = [part.closing() for part in parts] + [square.closing(), owner.closing()]
        return chains + [local(), owner.chain()], ends

    vmem = pltpu.VMEM
    return Job(
        [queries, keys_values, bits, cached_keys, cached_values],
        outs,
        scratch,
        steps,
        [vmem, vmem, vmem, pl.ANY, pl.ANY],
        [vmem, vmem, pl.ANY, pl.ANY, vmem, vmem],
    )


def mask_words(index, base, mem_dev, place_ref, bit_ref):
    relative = index - base
    inside = (relative >= 0) & (relative < mem_dev)
    place = jnp.where(inside, relative & 127, 0)
    bit = jnp.where(inside, lax.shift_left(jnp.ones_like(relative), relative >> 7), 0)
    place_ref[...] = place.T
    bit_ref[...] = bit.T
    sought = lax.broadcasted_iota(jnp.int32, (128, 128), 0)
    halves = []
    for start in range(0, index.shape[0], 128):

        def eight(g, words, start=start):
            group = pl.ds(pl.multiple_of(g * 8, 8), 8)
            places = place_ref[group, start : start + 128]
            bits = bit_ref[group, start : start + 128]
            for j in range(8):
                words = words | jnp.where(places[j : j + 1] == sought, bits[j : j + 1], 0)
            return words

        none = jnp.zeros((128, 128), jnp.int32)
        words = lax.fori_loop(0, index.shape[1] // 8, eight, none)
        halves.append(words.T)
    return jnp.concatenate(halves, axis=0)


def mask_scratch(rows, count):
    return [pltpu.VMEM((count, rows), jnp.int32), pltpu.VMEM((count, rows), jnp.int32)]


def mask_kernel(mem_dev, base_ref, index_ref, bits_ref, place_ref, bit_ref):
    bits_ref[0] = mask_words(index_ref[0], base_ref[0], mem_dev, place_ref, bit_ref)


def mask_bits(base, all_index, mem_dev):
    segments, rows, count = all_index.shape
    return pl.pallas_call(
        functools.partial(mask_kernel, mem_dev),
        grid_spec=pltpu.PrefetchScalarGridSpec(
            num_scalar_prefetch=1,
            grid=(segments,),
            in_specs=[pl.BlockSpec((1, rows, count), lambda g, b: (g, 0, 0))],
            out_specs=pl.BlockSpec((1, rows, 128), lambda g, b: (g, 0, 0)),
            scratch_shapes=mask_scratch(rows, count),
        ),
        out_shape=jax.ShapeDtypeStruct((segments, rows, 128), jnp.int32),
        compiler_params=params(),
        name="mask_bits",
    )(base, all_index)


def fill_bias(bits_ref, bias_ref):
    bits = bits_ref[...].reshape(bits_ref.shape[-2:])
    for b in range(bias_ref.shape[1] // 128):
        bias_ref[:, b * 128 : (b + 1) * 128] = jnp.where(((bits >> b) & 1) != 0, 0.0, FLOOR)


def owner_backward_heads(span, scale, q_ref, g_ref, st_ref, k_ref, v_ref, bias_ref, dq_ref):
    stats = columns_of(st_ref[...])
    lanes = lax.broadcasted_iota(jnp.int32, stats.shape, 1)

    def two(i, carry):
        for h in (2 * i, 2 * i + 1):
            lane = pl.ds(pl.multiple_of(h * 128, 128), 128)
            total = jnp.sum(jnp.where(lanes == h, stats, 0.0), axis=1, keepdims=True)
            dots = jnp.sum(jnp.where(lanes == HEADS + h, stats, 0.0), axis=1, keepdims=True)
            scores = dot(q_ref[:, lane], k_ref[:, lane], NT) * scale + bias_ref[...]
            weights = jnp.exp2(scores - total)
            dscore = weights * (dot(g_ref[:, lane], v_ref[:, lane], NT) - dots)
            dq_ref[:, lane] = (
                dot(dscore.astype(BF16), k_ref[:, lane]) * (scale / LOG2E)
            ).astype(BF16)
        return carry

    lax.fori_loop(span[0] // 2, span[1] // 2, two, 0)


def owner_forward_heads(span, scale, q_ref, k_ref, v_ref, bias_ref, stats_ref, o_ref, st_ref):
    rows = q_ref.shape[0]
    lanes = lax.broadcasted_iota(jnp.int32, (rows, 128), 1)

    def two(i, stats):
        for h in (2 * i, 2 * i + 1):
            lane = pl.ds(pl.multiple_of(h * 128, 128), 128)
            scores = dot(q_ref[:, lane], k_ref[:, lane], NT) * scale + bias_ref[...]
            top = jnp.maximum(jnp.max(scores, axis=1, keepdims=True), LOW)
            weights = jnp.exp2(scores - top)
            total = jnp.sum(weights, axis=1, keepdims=True)
            stats = jnp.where(lanes == h, top, jnp.where(lanes == HEADS + h, total, stats))
            o_ref[:, lane] = dot(weights.astype(BF16), v_ref[:, lane]).astype(BF16)
        return stats

    start = stats_ref[...] if span[0] else jnp.zeros((rows, 128), F32)
    stats = lax.fori_loop(span[0] // 2, span[1] // 2, two, start)
    if span[1] == HEADS:
        st_ref[...] = stats.T[:STATS]
    else:
        stats_ref[...] = stats


def owner_forward_kernel(scale, order_ref, q_ref, bits_ref, k_ref, v_ref, o_ref, st_ref, bias_ref):
    del order_ref
    fill_bias(bits_ref, bias_ref)
    maxima, sums = [], []
    for h in range(HEADS):
        span = slice(h * 128, (h + 1) * 128)
        scores = dot(q_ref[0, :, span], k_ref[0, :, span], NT) * scale + bias_ref[...]
        top = jnp.maximum(jnp.max(scores, axis=1, keepdims=True), LOW)
        weights = jnp.exp2(scores - top)
        maxima.append(top)
        sums.append(jnp.sum(weights, axis=1, keepdims=True))
        o_ref[0, :, span] = dot(weights.astype(BF16), v_ref[0, :, span]).astype(BF16)
    st_ref[0] = spread(maxima + sums).T[:STATS]


def owner_forward(order, queries, bits, cached_keys, cached_values, scale):
    segments, rows, width = queries.shape
    mem_dev = cached_keys.shape[1]
    active = order.shape[0]
    picked = lambda a, o: (o[a], 0, 0)
    return pl.pallas_call(
        functools.partial(owner_forward_kernel, scale),
        grid_spec=pltpu.PrefetchScalarGridSpec(
            num_scalar_prefetch=1,
            grid=(active,),
            in_specs=[
                pl.BlockSpec((1, rows, width), picked),
                pl.BlockSpec((1, rows, 128), picked),
                pl.BlockSpec((1, mem_dev, width), picked),
                pl.BlockSpec((1, mem_dev, width), picked),
            ],
            out_specs=[
                pl.BlockSpec((1, rows, width), picked),
                pl.BlockSpec((1, STATS, rows), picked),
            ],
            scratch_shapes=[pltpu.VMEM((rows, mem_dev), F32)],
        ),
        out_shape=[
            jax.ShapeDtypeStruct((segments, rows, width), BF16),
            jax.ShapeDtypeStruct((segments, STATS, rows), F32),
        ],
        compiler_params=params(),
        name="owner_forward",
    )(order, queries, bits, cached_keys, cached_values)


def owner_backward_kernel(
    scale, order_ref, q_ref, g_ref, st_ref, bits_ref, k_ref, v_ref, dq_ref, bias_ref
):
    del order_ref
    fill_bias(bits_ref, bias_ref)
    stats = columns_of(st_ref[0])
    for h in range(HEADS):
        span = slice(h * 128, (h + 1) * 128)
        scores = dot(q_ref[0, :, span], k_ref[0, :, span], NT) * scale + bias_ref[...]
        weights = jnp.exp2(scores - stats[:, h : h + 1])
        dweights = dot(g_ref[0, :, span], v_ref[0, :, span], NT)
        dscore = weights * (dweights - stats[:, HEADS + h : HEADS + h + 1])
        dq_ref[0, :, span] = (
            dot(dscore.astype(BF16), k_ref[0, :, span]) * (scale / LOG2E)
        ).astype(BF16)


def owner_backward(order, queries, grads, stats, bits, cached_keys, cached_values, scale):
    segments, rows, width = queries.shape
    mem_dev = cached_keys.shape[1]
    active = order.shape[0]
    picked = lambda a, o: (o[a], 0, 0)
    return pl.pallas_call(
        functools.partial(owner_backward_kernel, scale),
        grid_spec=pltpu.PrefetchScalarGridSpec(
            num_scalar_prefetch=1,
            grid=(active,),
            in_specs=[
                pl.BlockSpec((1, rows, width), picked),
                pl.BlockSpec((1, rows, width), picked),
                pl.BlockSpec((1, STATS, rows), picked),
                pl.BlockSpec((1, rows, 128), picked),
                pl.BlockSpec((1, mem_dev, width), picked),
                pl.BlockSpec((1, mem_dev, width), picked),
            ],
            out_specs=pl.BlockSpec((1, rows, width), picked),
            scratch_shapes=[pltpu.VMEM((rows, mem_dev), F32)],
        ),
        out_shape=jax.ShapeDtypeStruct((segments, rows, width), BF16),
        compiler_params=params(),
        name="owner_backward",
    )(order, queries, grads, stats, bits, cached_keys, cached_values)


def causal_bias(place, rows, keys):
    row = place * rows + lax.broadcasted_iota(jnp.int32, (rows, keys), 0)
    return jnp.where(lax.broadcasted_iota(jnp.int32, (rows, keys), 1) <= row, 0.0, FLOOR)


def columns_at(kv_ref, span):
    block = kv_ref[:, span] if len(kv_ref.shape) == 2 else kv_ref[:, :, span]
    return block.reshape(-1, block.shape[-1])


def local_forward_steps(scale, place, q_ref, kv_ref, o_ref, st_ref, bias_ref):
    rows, width = q_ref.shape
    bias_ref[...] = causal_bias(place, rows, bias_ref.shape[1])
    maxima, sums = [], []
    for h in range(HEADS):
        span, over = slice(h * 128, (h + 1) * 128), slice(width + h * 128, width + (h + 1) * 128)
        scores = dot(q_ref[:, span], columns_at(kv_ref, span), NT) * scale + bias_ref[...]
        top = jnp.max(scores, axis=1, keepdims=True)
        weights = jnp.exp2(scores - top)
        maxima.append(top)
        sums.append(jnp.sum(weights, axis=1, keepdims=True))
        o_ref[:, span] = dot(weights.astype(BF16), columns_at(kv_ref, over))
        yield
    st_ref[...] = spread(maxima + sums).T[:STATS]


def local_backward_steps(
    scale, place, q_ref, g_ref, st_ref, kv_ref, dq_ref, dkv_ref, bias_ref
):
    rows, width = q_ref.shape
    bias_ref[...] = causal_bias(place, rows, bias_ref.shape[1])
    stats = columns_of(st_ref[...])
    for h in range(HEADS):
        span, over = slice(h * 128, (h + 1) * 128), slice(width + h * 128, width + (h + 1) * 128)
        query, key, grad = q_ref[:, span], columns_at(kv_ref, span), g_ref[:, span]
        scores = dot(query, key, NT) * scale + bias_ref[...]
        weights = jnp.exp2(scores - stats[:, h : h + 1])
        dweights = dot(grad, columns_at(kv_ref, over), NT)
        dscore = (weights * (dweights - stats[:, HEADS + h : HEADS + h + 1])).astype(BF16)
        dq_ref[:, span] = dot(dscore, key) * (scale / LOG2E)
        dkey = (dot(dscore, query, TN) * (scale / LOG2E)).astype(BF16)
        dvalue = dot(weights.astype(BF16), grad, TN).astype(BF16)
        lead = dkv_ref.shape[:-1]
        dkv_ref[(*[slice(None)] * len(lead), span)] = dkey.reshape(lead + (128,))
        dkv_ref[(*[slice(None)] * len(lead), over)] = dvalue.reshape(lead + (128,))
        yield


class OwnerBackward(OwnerForward):
    def __init__(self, net, scale, parts, stats_part, ins, outs, scratch, sems):
        self.sources_in = ins
        self.grads, self.stats, peers = outs
        *self.buffers, self.bias, far, held, twin = scratch
        self.loads, *sems = sems
        self.far = [far]
        Return.__init__(self, net, self.far, [peers], [held, twin, *sems])
        self.parts, self.scale, self.stats_part = [*parts, stats_part], scale, stats_part

    def bring(self, z, far):
        segment = 2 * z + (1 - self.net.c if far else self.net.c)
        sources = [source.at[segment] for source in (*self.sources_in, self.grads)]
        return [
            pltpu.make_async_copy(source, buffer, self.loads.at[i])
            for i, (source, buffer) in enumerate(zip(sources, self.buffers))
        ]

    def mask(self, z, far):
        if far:
            for part in self.parts:
                part.wait_core(z)
        for copy in self.bring(z, far):
            copy.start()

    def attend(self, z, far, span):
        net = self.net
        keys, values, queries, bits, grads = self.buffers
        if span[0] == 0:
            for copy in self.bring(z, far):
                copy.wait()
            fill_bias(bits, self.bias)
        segment = 2 * z + (1 - net.c if far else net.c)
        owner_backward_heads(
            span,
            self.scale,
            queries,
            grads,
            self.stats.at[segment],
            keys,
            values,
            self.bias,
            (self.far[0] if far else self.held[0]).at[z],
        )
        if far and span[1] == HEADS:
            self.pairing(0, z).start()

    def chain(self):
        net = self.net
        for k in range(net.line):
            for from_left in (True, False) if k else (True,):
                z = net.z - k if from_left else net.z + k
                present = z >= 0 if from_left else z < net.line
                here = (lambda body: body()) if k == 0 else pl.when(present)
                need(self.parts, k, from_left)
                if k == 0:
                    for part in self.parts:
                        part.wait_own()
                here(lambda: self.mask(z, True))
                yield
                for far in (True, False):
                    for span in SPANS:

                        def part():
                            self.attend(z, far, span)
                            if far and span[1] == HEADS:
                                self.mask(z, False)

                        here(part)
                        yield
                here(lambda: self.home(k, z))
                yield


def backward_job(
    sizes, queries, grads, stats, segment_kv, all_queries, bits, cached_keys, cached_values, scale
):
    square, line = sizes["seq"], sizes["mem"] // 2
    segments, rows, width = all_queries.shape
    mem_dev = cached_keys.shape[1]
    length = square * rows
    shape = jax.ShapeDtypeStruct
    outs = [
        shape((segments, rows, width), BF16),
        shape((line, rows, width), BF16),
        shape((rows, width), F32),
        shape((PIECES, rows // PIECES, 2 * width), F32),
    ]
    keys_scratch = scatter_scratch(PIECES, rows // PIECES, 2 * width, row_halves, False)
    scratch = (
        gather_semaphores(line, PIECES)
        + gather_semaphores(line)
        + [pltpu.VMEM((segments, STATS, rows), F32), pltpu.VMEM((rows, length), F32)]
        + keys_scratch
        + [pltpu.VMEM((mem_dev, width), BF16)] * 2
        + [
            pltpu.VMEM((rows, width), BF16),
            pltpu.VMEM((rows, 128), jnp.int32),
            pltpu.VMEM((rows, width), BF16),
            pltpu.VMEM((rows, mem_dev), F32),
        ]
        + [pltpu.VMEM((line, rows, width), BF16)] * 3
        + [pltpu.SemaphoreType.DMA((5,))]
        + [pltpu.SemaphoreType.DMA((1, line))] * 5
    )

    def steps(net, ins, outs, scratch):
        queries, grads, stats, segment_kv, all_queries, bits, keys, values = ins
        all_grads, peers, local_dq, grad_kv = outs
        scratch = list(scratch)
        take = lambda count: [scratch.pop(0) for _ in range(count)]
        parts = gather_parts(net, grads, all_grads, take(3 * PIECES), row_halves, "line", PIECES)
        stats_sems = take(3)
        all_stats, local_bias = take(2)
        (stats_part,) = gather_parts(net, stats, all_stats, stats_sems, row_halves, "line", 1)
        keys_scratch = take(8)
        buffers = take(9)
        scatter = Scatter(
            net, None, [grad_kv], keys_scratch[:5], keys_scratch[5:], row_halves, False
        )
        owner = OwnerBackward(
            net, scale, parts, stats_part, [keys, values, all_queries, bits],
            [all_grads, all_stats, peers], buffers, scratch,
        )
        for part in [*parts, stats_part]:
            part.waits_core = part.waits_own = False

        def local():
            yield from local_backward_steps(
                scale, net.s, queries, grads, stats, segment_kv, local_dq, scatter.held, local_bias
            )
            stages = (scatter.add_core, scatter.add_first, scatter.add_second, scatter.line_step)
            for wave in range(PIECES + 3):
                for lag in (3, 2, 1, 0):
                    if 0 <= wave - lag < PIECES:
                        stages[lag](wave - lag)
                        yield

        chains = [chain for part in [*parts, stats_part] for chain in part.chains()]
        ends = [part.closing() for part in [*parts, stats_part]]
        ends += [scatter.closing(), owner.closing()]
        return chains + [local(), owner.chain()], ends

    vmem = pltpu.VMEM
    return Job(
        [queries, grads, stats, segment_kv, all_queries, bits, cached_keys, cached_values],
        outs,
        scratch,
        steps,
        [vmem] * 4 + [pl.ANY] * 4,
        [pl.ANY, pl.ANY, vmem, vmem],
    )


def local_job(kind, arrays, scale):
    rows, width = arrays[0].shape
    length = arrays[-1].shape[0]
    if kind == "forward":
        body, extra = local_forward_steps, jax.ShapeDtypeStruct((STATS, rows), F32)
    else:
        body, extra = local_backward_steps, jax.ShapeDtypeStruct((length, 2 * width), BF16)

    def steps(net, ins, outs, scratch):
        return [body(scale, net.s, *ins, *outs, *scratch)], []

    outs = [jax.ShapeDtypeStruct((rows, width), F32), extra]
    return Job(arrays, outs, [pltpu.VMEM((rows, length), F32)], steps, pltpu.VMEM, pltpu.VMEM)


def alone_kernel(job, *refs):
    place_ref, *refs = refs
    net = type("Alone", (), {"s": place_ref[0]})
    ins, outs = len(job.arrays), len(job.arrays) + len(job.outs)
    for chain in job.steps(net, refs[:ins], refs[ins:outs], refs[outs:])[0]:
        for _ in chain:
            pass


def alone(name, place, job):
    return pl.pallas_call(
        functools.partial(alone_kernel, job),
        out_shape=job.outs,
        in_specs=[pl.BlockSpec(memory_space=pltpu.SMEM)]
        + [pl.BlockSpec(memory_space=pltpu.VMEM)] * len(job.arrays),
        out_specs=[pl.BlockSpec(memory_space=pltpu.VMEM)] * len(job.outs),
        scratch_shapes=job.scratch,
        compiler_params=params(),
        name=name,
    )(place, *job.arrays)


def copy_in(pairs, sems):
    copies = [pltpu.make_async_copy(src, dst, sems.at[i]) for i, (src, dst) in enumerate(pairs)]
    for copy in copies:
        copy.start()
    return copies


def turn(values, cosine, sine):
    return values * cosine + pltpu.roll(values, values.shape[1] // 2, 1) * sine


def inverse_root(values):
    return lax.rsqrt(jnp.mean(values * values, axis=1, keepdims=True) + EPSILON)


def project_kernel(x_ref, w_any, cos_ref, sin_ref, n_ref, q_ref, kv_ref, gain_ref, w_ref, sems):
    width = x_ref.shape[1]
    spans = [slice(i * width, (i + 1) * width) for i in range(3)]
    gains = slice(3 * width, 3 * width + 128)
    copies = copy_in([(w_any.at[:, s], w_ref.at[:, s]) for s in [gains, *spans]], sems)
    x = x_ref[...].astype(F32)
    copies[0].wait()
    gain_ref[...] = w_ref[:, gains].astype(F32).T[:8]
    normed = (x * inverse_root(x) * gain_ref[:1]).astype(BF16)
    n_ref[...] = normed
    cosine, sine = cos_ref[...], sin_ref[...]
    for i in range(3):
        copies[1 + i].wait()
        product = dot(normed, w_ref[:, spans[i]])
        for h in range(HEADS):
            span = slice(h * 128, (h + 1) * 128)
            part = product[:, span]
            part = part if i == 2 else turn(part, cosine, sine)
            if i == 0:
                q_ref[:, span] = part.astype(BF16)
            else:
                over = slice((i - 1) * width + h * 128, (i - 1) * width + (h + 1) * 128)
                kv_ref[:, over] = part.astype(BF16)


def in_vmem(count):
    return [pl.BlockSpec(memory_space=pltpu.VMEM)] * count


def project(tokens, first_weights, cosine, sine):
    rows, width = tokens.shape
    columns = first_weights.shape[1]
    return pl.pallas_call(
        project_kernel,
        out_shape=[
            jax.ShapeDtypeStruct((rows, width), BF16),
            jax.ShapeDtypeStruct((rows, width), BF16),
            jax.ShapeDtypeStruct((rows, 2 * width), BF16),
            jax.ShapeDtypeStruct((8, width), F32),
        ],
        in_specs=in_vmem(1) + [pl.BlockSpec(memory_space=pl.ANY)] + in_vmem(2),
        out_specs=in_vmem(4),
        scratch_shapes=[
            pltpu.VMEM((width, columns), BF16),
            pltpu.SemaphoreType.DMA((4,)),
        ],
        compiler_params=params(),
        name="project",
    )(tokens, first_weights, cosine, sine)


def middle_kernel(
    live_ref, x_ref, g_ref, gain_ref, lo_ref, ls_ref, po_ref, ps_ref, out_any, gate_any, up_any, down_any,
    mixed_ref, gm_ref, ga_ref, st_ref, gain_grad_ref, wo_any, wg_any, wu_any, wd_any,
    att_ref, acc_ref, gn_ref, n_ref, nt_ref, out_ref, gate_ref, up_ref, down_ref, side_ref, tall_ref, sems, writes,
):
    rows, width = x_ref.shape
    copies = copy_in(
        [(out_any, out_ref), (gate_any, gate_ref), (up_any, up_ref), (down_any, down_ref)], sems
    )
    live = live_ref[0] > 0
    peers = ps_ref.shape[0]
    local_max, local_sum = ls_ref[:HEADS], ls_ref[HEADS:]
    peer_max = [jnp.where(live, ps_ref[p, :HEADS], LOW) for p in range(peers)]
    peer_sum = [jnp.where(live, ps_ref[p, HEADS:], 0.0) for p in range(peers)]
    top = functools.reduce(jnp.maximum, peer_max, local_max)
    shares = [jnp.exp2(m - top) for m in [local_max] + peer_max]
    total = functools.reduce(
        jnp.add, [s * t for s, t in zip(shares, [local_sum] + peer_sum)]
    )
    log_total = top + jnp.log2(total)
    shares = columns_of(jnp.concatenate([s / total for s in shares], axis=0))
    for h in range(HEADS):
        span = slice(h * 128, (h + 1) * 128)
        part = lo_ref[:, span] * shares[:, h : h + 1]
        for p in range(peers):
            column = shares[:, (p + 1) * HEADS + h : (p + 1) * HEADS + h + 1]
            part += jnp.where(live, po_ref[p, :, span].astype(F32), 0.0) * column
        att_ref[:, span] = part
    attention_low = att_ref[...].astype(BF16)
    copies[0].wait()
    mid = x_ref[...].astype(F32) + dot(attention_low, out_ref[...])
    gm_ref[...] = mid
    root = inverse_root(mid)
    n_ref[...] = (mid * root * gain_ref[1:2]).astype(BF16)
    for copy in copies[1:]:
        copy.wait()
    nt_ref[...] = n_ref[...].T
    grad = g_ref[...]
    acc_ref[...] = jnp.zeros_like(acc_ref)
    gn_ref[...] = jnp.zeros_like(gn_ref)
    hidden_width = gate_ref.shape[1]
    step = 512
    pending = [[], []]

    def write(slot, product, buffer, target, place):
        buffer[...] = product.astype(BF16)
        copy = pltpu.make_async_copy(buffer, target, writes.at[slot, place])
        copy.start()
        pending[slot].append(copy)

    for turn_of, start in enumerate(range(0, hidden_width, step)):
        span = slice(start, min(start + step, hidden_width))
        slot = turn_of % 2
        while pending[slot]:
            pending[slot].pop().wait()
        norm_two = n_ref[...]
        gate = dot(norm_two, gate_ref[:, span])
        upward = dot(norm_two, up_ref[:, span])
        grad_hidden = dot(grad, down_ref[span, :], NT)
        sigmoid = 1.0 / (1.0 + jnp.exp(-gate))
        silu = gate * sigmoid
        hidden = (silu * upward).astype(BF16)
        grad_gate = (grad_hidden * upward * (sigmoid * (1.0 + gate * (1.0 - sigmoid)))).astype(BF16)
        grad_up = (grad_hidden * silu).astype(BF16)
        write(slot, dot(nt_ref[...], grad_gate), side_ref.at[slot, 0, :, : span.stop - start], wg_any.at[:, span], 0)
        write(slot, dot(nt_ref[...], grad_up), side_ref.at[slot, 1, :, : span.stop - start], wu_any.at[:, span], 1)
        write(slot, dot(hidden, grad, TN), tall_ref.at[slot, : span.stop - start], wd_any.at[span, :], 2)
        acc_ref[...] += dot(hidden, down_ref[span, :])
        gn_ref[...] += dot(grad_gate, gate_ref[:, span], NT) + dot(grad_up, up_ref[:, span], NT)
    mid = gm_ref[...]
    mixed_ref[...] = mid + acc_ref[...]
    normed = mid * root
    grad_norm = gn_ref[...]
    gain_grad_ref[...] = jnp.broadcast_to(
        jnp.sum(grad_norm * normed, axis=0, keepdims=True), gain_grad_ref.shape
    )
    scaled = grad_norm * gain_ref[1:2]
    grad_mid = grad.astype(F32) + root * (
        scaled - normed * jnp.mean(normed * scaled, axis=1, keepdims=True)
    )
    gm_ref[...] = grad_mid
    grad_mid_low = grad_mid.astype(BF16)
    nt_ref[...] = att_ref[...].astype(BF16).T
    for start in range(0, width, step):
        span = slice(start, start + step)
        slot = start // step % 2
        while pending[slot]:
            pending[slot].pop().wait()
        write(slot, dot(nt_ref[...], grad_mid_low[:, span]), side_ref.at[slot, 0], wo_any.at[:, span], 0)
    grad_attention = dot(grad_mid_low, out_ref[...], NT).astype(BF16)
    ga_ref[...] = grad_attention
    products = grad_attention.astype(F32) * att_ref[...]
    dots = [
        jnp.sum(products[:, h * 128 : (h + 1) * 128], axis=1, keepdims=True) for h in range(HEADS)
    ]
    st_ref[...] = jnp.concatenate([log_total, spread(dots).T[:HEADS]], axis=0)
    for copy in pending[0] + pending[1]:
        copy.wait()


def middle(live, tokens, grads, gains, local, peers, weights):
    rows, width = tokens.shape
    hidden_width = weights[1].shape[1]
    full = lambda columns, kind: jax.ShapeDtypeStruct((rows, columns), kind)
    return pl.pallas_call(
        middle_kernel,
        out_shape=[
            full(width, F32),
            full(width, F32),
            full(width, BF16),
            jax.ShapeDtypeStruct((STATS, rows), F32),
            jax.ShapeDtypeStruct((8, width), F32),
        ]
        + [jax.ShapeDtypeStruct(w.shape, BF16) for w in weights],
        in_specs=[pl.BlockSpec(memory_space=pltpu.SMEM)]
        + in_vmem(7)
        + [pl.BlockSpec(memory_space=pl.ANY)] * 4,
        out_specs=in_vmem(5) + [pl.BlockSpec(memory_space=pl.ANY)] * 4,
        scratch_shapes=[pltpu.VMEM((rows, width), F32)] * 3
        + [pltpu.VMEM((rows, width), BF16), pltpu.VMEM((width, rows), BF16)]
        + [pltpu.VMEM(w.shape, BF16) for w in weights]
        + [
            pltpu.VMEM((2, 2, width, 512), BF16),
            pltpu.VMEM((2, 512, width), BF16),
            pltpu.SemaphoreType.DMA((4,)),
            pltpu.SemaphoreType.DMA((2, 3)),
        ],
        compiler_params=params(),
        name="middle",
    )(live, tokens, grads, gains, *local, *peers, *weights)


def final_kernel(
    live_ref, x_ref, gm_ref, gain_ref, ggain_ref, n_ref, dq_ref, pd_ref, dkv_ref, cos_ref, sin_ref, w_any,
    *rest,
):
    rows, width = x_ref.shape
    ready, (gx_ref, late_ref), given = rest[:4], rest[4:6], rest[6:10]
    in_ref, w_ref, made_ref, sems, writes = rest[10:]
    copies = copy_in([(w_any.at[:, : 3 * width], w_ref)], sems)

    def write(i, span):
        copy = pltpu.make_async_copy(made_ref.at[:, span], late_ref.at[:, span], writes.at[i])
        copy.start()
        copies.append(copy)

    for source, target in zip(ready, given):
        target[...] = source[...]
    live = live_ref[0] > 0
    cosine, sine = cos_ref[...], -sin_ref[...]
    for h in range(HEADS):
        span = slice(h * 128, (h + 1) * 128)
        part = dq_ref[:, span]
        for p in range(pd_ref.shape[0]):
            part += jnp.where(live, pd_ref[p, :, span].astype(F32), 0.0)
        in_ref[:, span] = turn(part, cosine, sine).astype(BF16)
        over = slice(width + h * 128, width + (h + 1) * 128)
        in_ref[:, over] = turn(dkv_ref[:, span], cosine, sine).astype(BF16)
    in_ref[:, 2 * width :] = dkv_ref[:, width:].astype(BF16)
    flipped = n_ref[...].T
    for i in range(3):
        span = slice(i * width, (i + 1) * width)
        made_ref[:, span] = dot(flipped, in_ref[:, span]).astype(BF16)
        write(i, span)
    copies[0].wait()
    grad_norm = dot(in_ref[...], w_ref[...], NT)
    x = x_ref[...].astype(F32)
    root = inverse_root(x)
    normed = x * root
    gains = jnp.concatenate(
        [
            jnp.sum(grad_norm * normed, axis=0, keepdims=True),
            ggain_ref[:1],
            jnp.zeros((126, width), F32),
        ],
        axis=0,
    )
    made_ref[:, 3 * width :] = gains.T.astype(BF16)
    write(3, slice(3 * width, made_ref.shape[1]))
    scaled = grad_norm * gain_ref[:1]
    gx_ref[...] = gm_ref[...] + root * (
        scaled - normed * jnp.mean(normed * scaled, axis=1, keepdims=True)
    )
    for copy in copies[1:]:
        copy.wait()


def final(live, *arrays, early):
    rows, width = arrays[0].shape
    columns = arrays[-1].shape[1]
    results = pl.pallas_call(
        final_kernel,
        out_shape=[
            jax.ShapeDtypeStruct((rows, width), F32),
            jax.ShapeDtypeStruct((width, columns), BF16),
        ]
        + [jax.ShapeDtypeStruct(e.shape, e.dtype) for e in early],
        in_specs=[pl.BlockSpec(memory_space=pltpu.SMEM)]
        + in_vmem(len(arrays) - 1)
        + [pl.BlockSpec(memory_space=pl.ANY)]
        + in_vmem(len(early)),
        out_specs=in_vmem(1) + [pl.BlockSpec(memory_space=pl.ANY)] + in_vmem(len(early)),
        scratch_shapes=[
            pltpu.VMEM((rows, 3 * width), BF16),
            pltpu.VMEM((width, 3 * width), BF16),
            pltpu.VMEM((width, columns), BF16),
            pltpu.SemaphoreType.DMA((1,)),
            pltpu.SemaphoreType.DMA((4,)),
        ],
        compiler_params=params(),
        name="final",
    )(live, *arrays, *early)
    return results[0], results[1], results[2:]


def deliver_kernel(late_ref, *outs):
    width = outs[0].shape[1]
    for i in range(3):
        outs[i][...] = late_ref[:, i * width : (i + 1) * width]
    gains = late_ref[:, 3 * width :]
    rows = gains.shape[0]
    square = jnp.concatenate([gains, jnp.zeros((128 - rows, 128), F32)], axis=0).T
    for i in range(2):
        outs[3 + i][...] = square[i : i + 1, :rows]


def deliver(late_sum, width):
    rows = late_sum.shape[0]
    shapes = [(rows, width)] * 3 + [(1, rows)] * 2
    *sums, gain_one, gain_two = pl.pallas_call(
        deliver_kernel,
        out_shape=[jax.ShapeDtypeStruct(shape, F32) for shape in shapes],
        in_specs=in_vmem(1),
        out_specs=in_vmem(5),
        compiler_params=params(),
        name="deliver",
    )(late_sum)
    return sums, gain_one.reshape(rows), gain_two.reshape(rows)


REACH = {"all": ("seq", "mem"), "line": "mem", "square": "seq"}


def gather_plain(array, reach):
    return lax.all_gather(array, REACH[reach], axis=0)


def scatter_plain(array, reach):
    return lax.psum_scatter(array, REACH[reach], scatter_dimension=0, tiled=True).astype(F32)


def return_plain(array):
    return lax.all_to_all(array, "mem", split_axis=0, concat_axis=0, tiled=True)


def join_peers(outs, stats):
    top = jnp.max(stats[:, :HEADS], axis=0)
    shares = jnp.exp2(stats[:, :HEADS] - top)
    total = jnp.sum(stats[:, HEADS:] * shares, axis=0)
    wide = jnp.repeat(jnp.swapaxes(shares, 1, 2), outs.shape[-1] // HEADS, axis=2)
    joined = jnp.sum(outs.astype(F32) * wide, axis=0).astype(BF16)
    return joined[None], jnp.concatenate([top, total], axis=0)[None]


def per_device(
    sizes,
    tokens,
    cached_keys,
    cached_values,
    knn_index,
    has_memory,
    w_query,
    w_key,
    w_value,
    w_out,
    gain_attn,
    w_gate,
    w_up,
    w_down,
    gain_ffn,
    cotangent,
):
    near = sizes["seq"] == 4 and sizes["mem"] % 2 == 0 and 4 <= sizes["mem"] <= 16
    inputs, grad_out = tokens[0], cotangent[0]
    rows, width = inputs.shape
    hidden_width = w_gate.shape[1]
    head_width = width // HEADS
    scale = head_width ** (-0.5) * LOG2E
    mem_dev = cached_keys.shape[1]
    place = lax.axis_index("seq").astype(jnp.int32)[None]
    base = (lax.axis_index("mem") * mem_dev).astype(jnp.int32)[None]

    gains = jnp.concatenate(
        [gain_attn[:, None], gain_ffn[:, None], jnp.zeros((w_query.shape[0], 126), BF16)], axis=1
    )
    first_shard = jnp.concatenate([w_query, w_key, w_value, gains], axis=1)
    if near:
        jobs = [
            index_job(sizes, knn_index[0], mem_dev),
            gather_job(sizes, first_shard, row_halves, "all"),
        ]
        (bits,), (first_weights,) = together(1, "first", sizes, jobs)
    else:
        first_weights = gather_plain(first_shard, "all")
        bits = mask_bits(base, gather_plain(knn_index[0], "line"), mem_dev)
        flags = lax.all_gather(has_memory, "mem", axis=0, tiled=True)
        order = jnp.argsort(jnp.where(flags > 0, 0, 1), stable=True)
        order = order[: flags.shape[0] // 2].astype(jnp.int32)
    first_weights = first_weights.reshape(-1, first_shard.shape[1])

    positions = lax.axis_index("seq") * rows + jnp.arange(rows)
    cosine, sine = rope_tables(positions, head_width)
    norm_one, queries, keys_values, gain_rows = project(inputs, first_weights, cosine, sine)
    if near:
        jobs = [
            forward_job(
                sizes, queries, keys_values, bits, cached_keys, cached_values, scale
            ),
            gather_job(sizes, w_out, row_halves, "all"),
            gather_job(sizes, w_gate, row_halves, "all"),
            gather_job(sizes, w_up, row_halves, "all"),
            gather_job(sizes, w_down, column_halves, "all"),
        ]
        results, (out_weight,), (gate_weight,), (up_weight,), (down_weight,) = together(
            2, "second", sizes, jobs
        )
        all_queries, segment_kv, *peers = results[:4]
        local = results[4:]
        segment_kv = segment_kv.reshape(-1, 2 * width)
    else:
        all_queries = gather_plain(queries, "line")
        segment_kv = gather_plain(keys_values, "square").reshape(-1, 2 * width)
        owner_out, owner_stats = owner_forward(
            order, all_queries, bits, cached_keys, cached_values, scale
        )
        peers = join_peers(return_plain(owner_out), return_plain(owner_stats))
        local = alone("local_forward", place, local_job("forward", [queries, segment_kv], scale))
        out_weight, gate_weight = gather_plain(w_out, "all"), gather_plain(w_gate, "all")
        up_weight, down_weight = gather_plain(w_up, "all"), gather_plain(w_down, "all")
    weights = [
        out_weight.reshape(width, width),
        gate_weight.reshape(width, hidden_width),
        up_weight.reshape(width, hidden_width),
        down_weight.reshape(hidden_width, width),
    ]
    mixed, grad_mid, grad_attention, back_stats, gain_two_grad, *early = middle(
        has_memory, inputs, grad_out, gain_rows, local, peers, weights
    )
    if near:
        jobs = [
            backward_job(
                sizes, queries, grad_attention, back_stats, segment_kv,
                all_queries, bits, cached_keys, cached_values, scale,
            ),
            *[scatter_job(sizes, grad, row_halves) for grad in early[:3]],
            scatter_job(sizes, early[3], column_halves),
        ]
        (_, peer_grads, local_dq, grad_kv), *early_sums = together(3, "third", sizes, jobs)
        grad_kv = grad_kv.reshape(rows, 2 * width)
        early_sums = [total for (total,) in early_sums]
    else:
        all_grads, all_stats = gather_plain(grad_attention, "line"), gather_plain(back_stats, "line")
        local_work = local_job(
            "backward", [queries, grad_attention, back_stats, segment_kv], scale
        )
        local_dq, local_dkv = alone("local_backward", place, local_work)
        owner_grads = owner_backward(
            order, all_queries, all_grads, all_stats, bits, cached_keys, cached_values, scale
        )
        peer_grads = jnp.sum(return_plain(owner_grads).astype(F32), axis=0, keepdims=True)
        grad_kv = scatter_plain(local_dkv, "square")
        early_sums = [scatter_plain(grad, "all") for grad in early]
    grad_inputs, late, early_sums = final(
        has_memory, inputs, grad_mid, gain_rows, gain_two_grad, norm_one, local_dq, peer_grads, grad_kv,
        cosine, sine, first_weights, early=early_sums,
    )
    if near:
        ((late_sum,),) = together(4, "fourth", sizes, [scatter_job(sizes, late, row_halves)])
    else:
        late_sum = scatter_plain(late, "all")
    late_sums, gain_one_sum, gain_two_sum = deliver(late_sum, width)
    return (
        mixed[None],
        grad_inputs[None],
        *late_sums,
        early_sums[0],
        gain_one_sum,
        *early_sums[1:],
        gain_two_sum,
    )


def solution(mesh):
    rows, owned, feature = P("mem", "seq", None), P(None, "mem", None), P(("seq", "mem"), None)
    gain = P(("seq", "mem"))
    return jax.shard_map(
        functools.partial(per_device, dict(mesh.shape)),
        mesh=mesh,
        in_specs=(
            (rows, owned, owned, rows, P("mem"))
            + (feature,) * 4
            + (gain,)
            + (feature,) * 3
            + (gain, rows)
        ),
        out_specs=(rows, rows) + (feature,) * 4 + (gain,) + (feature,) * 3 + (gain,),
        check_vma=False,
    )
```

```python
import functools

import jax
import jax.numpy as jnp
from jax import lax
from jax.experimental import pallas as pl
from jax.experimental.pallas import tpu as pltpu
from jax.sharding import PartitionSpec as P

HEADS = 8
EPSILON = 1e-05
FLOOR = -1e30
LOW = -1e29
LOG2E = 1.4426950408889634
STATS = 16
PIECES = 4
SPANS = [(0, 4), (4, 8)]
ORDERS = {
    ("first", 4): (
        8, 0, 7, 9, 10, 7, 2, 9, 1, 7, 8, 11, 12, 7, 10, 7, 4, 3, 7, 9, 7, 8, 11, 7, 12, 14, 13,
        7, 7, 5, 14, 7, 15, 13, 10, 15, 11, 7, 13, 6, 12, 15, 7, 15, 15, 16, 16, 16, 16, 16, 16,
        14, 7, 16, 16, 16,
    ),
    ("second", 4): (
        28, 51, 30, 44, 7, 14, 31, 0, 32, 21, 29, 9, 29, 33, 37, 15, 29, 29, 23, 22, 52, 8, 29,
        17, 53, 24, 2, 29, 1, 29, 45, 16, 29, 11, 25, 38, 29, 29, 54, 30, 28, 29, 47, 4, 10, 46,
        63, 26, 51, 32, 29, 29, 19, 29, 29, 61, 3, 35, 18, 29, 34, 40, 13, 29, 39, 29, 55, 29, 29,
        29, 29, 48, 29, 29, 29, 29, 47, 28, 6, 29, 53, 12, 5, 35, 37, 29, 32, 30, 58, 54, 60, 29,
        29, 45, 56, 49, 28, 33, 29, 28, 40, 36, 29, 28, 20, 38, 42, 29, 27, 31, 58, 60, 29, 51,
        61, 28, 29, 29, 41, 52, 60, 60, 53, 42, 61, 29, 56, 57, 49, 29, 28, 50, 54, 58, 40, 34,
        62, 39, 44, 38, 33, 29, 55, 35, 29, 31, 37, 29, 28, 46, 42, 61, 47, 52, 28, 41, 56, 43,
        36, 29, 45, 48, 55, 49, 65, 39, 67, 65, 50, 61, 64, 28, 43, 44, 64, 58, 63, 67, 34, 64,
        63, 64, 64, 59, 59, 59, 41, 36, 66, 46, 65, 66, 57, 67, 65, 67, 67, 50, 43, 66, 65, 64,
        64, 58, 66, 48, 59, 57, 67, 65, 66, 65, 66, 65, 64, 63, 65, 64, 67, 67, 67, 59, 66, 60,
        66, 66, 62,
    ),
    ("third", 4): (
        51, 41, 21, 37, 35, 28, 35, 49, 0, 51, 14, 35, 42, 7, 46, 41, 35, 35, 36, 45, 23, 35, 29,
        1, 50, 22, 42, 2, 36, 51, 48, 41, 16, 45, 15, 36, 9, 39, 30, 8, 49, 38, 43, 37, 51, 51,
        36, 41, 41, 36, 3, 36, 25, 31, 18, 45, 36, 24, 50, 35, 36, 49, 10, 4, 45, 11, 32, 43, 45,
        36, 50, 35, 42, 49, 49, 27, 36, 35, 36, 36, 36, 43, 37, 26, 50, 52, 38, 17, 40, 46, 50,
        42, 36, 42, 36, 48, 62, 47, 39, 35, 43, 56, 33, 37, 37, 56, 43, 36, 36, 36, 36, 36, 46,
        47, 35, 12, 36, 36, 36, 36, 36, 5, 36, 36, 19, 13, 38, 46, 54, 46, 54, 44, 40, 39, 35, 48,
        60, 34, 36, 36, 36, 53, 63, 36, 55, 20, 55, 47, 56, 52, 39, 38, 35, 56, 38, 48, 36, 36, 6,
        36, 39, 54, 35, 57, 35, 36, 36, 36, 36, 36, 44, 60, 48, 40, 47, 47, 62, 35, 36, 61, 36,
        53, 35, 35, 61, 52, 63, 55, 61, 40, 63, 57, 36, 53, 44, 58, 35, 35, 58, 35, 44, 62, 60,
        60, 56, 57, 53, 54, 62, 59, 44, 44, 52, 63, 58, 48, 58, 35, 40, 40, 35, 52, 53, 55, 61,
        57, 54, 57, 35, 55, 52, 59, 59, 59,
    ),
    ("fourth", 4): (
        0, 0, 1, 2, 0, 2, 3, 0, 0, 2, 1, 2, 2, 1, 3, 4, 1, 1, 3, 4, 4, 4, 3, 3, 3,
    ),
}
F32 = jnp.float32
BF16 = jnp.bfloat16
VMEM_LIMIT = 62 * 1024 * 1024
NT = (((1,), (1,)), ((), ()))
TN = (((0,), (0,)), ((), ()))


def dot(left, right, dims=(((1,), (0,)), ((), ()))):
    return lax.dot_general(left, right, dims, preferred_element_type=F32)


def rope_tables(positions, head_width):
    lane = jnp.arange(head_width)
    half = head_width // 2
    exponent = (lane % half).astype(F32) * (2.0 / head_width)
    frequency = jnp.power(10000.0, -exponent)
    turned = positions.astype(F32)[:, None] * frequency[None, :]
    sine = jnp.sin(turned)
    return jnp.cos(turned), jnp.where(lane[None, :] < half, -sine, sine)


def params(**more):
    return pltpu.CompilerParams(vmem_limit_bytes=VMEM_LIMIT, **more)


def spread(columns, width=128):
    lanes = lax.broadcasted_iota(jnp.int32, (columns[0].shape[0], width), 1)
    result = jnp.zeros((columns[0].shape[0], width), F32)
    for place, column in enumerate(columns):
        result = jnp.where(lanes == place, column, result)
    return result


def columns_of(rows_by_stat):
    count, width = rows_by_stat.shape
    padded = jnp.concatenate([rows_by_stat, jnp.zeros((128 - count, width), F32)], axis=0)
    return padded.T


MESH = pl.DeviceIdType.MESH


class Net:
    def __init__(self, line):
        self.line = line
        self.s, self.m = lax.axis_index("seq"), lax.axis_index("mem")
        self.c, self.z = self.m % 2, self.m // 2
        self.x, self.y, self.core = (self.s ^ 1, self.m), (self.s ^ 2, self.m), (self.s, self.m ^ 1)
        self.right = (self.s, (self.m + 2) % (2 * line))
        self.left = (self.s, (self.m + 2 * line - 2) % (2 * line))

    def others(self):
        ring = 2 * self.line
        return [(self.s, lax.rem(self.m + 2 * k, ring)) for k in range(1, self.line)]

    def greet(self, others):
        barrier = pltpu.get_barrier_semaphore()
        for other in others:
            pl.semaphore_signal(barrier, inc=1, device_id=other, device_id_type=MESH)
        pl.semaphore_wait(barrier, len(others))


def remote(src, dst, sends, recvs, place, device):
    return pltpu.make_async_remote_copy(
        src_ref=src,
        dst_ref=dst,
        send_sem=sends.at[place],
        recv_sem=recvs.at[place],
        device_id=device,
        device_id_type=MESH,
    )


def row_halves(ref, part):
    half = ref.shape[-2] // 2
    return ref.at[pl.ds(part * half, half)]


def column_halves(ref, part):
    half = ref.shape[-1] // 2
    return ref.at[:, pl.ds(part * half, half)]


class Gather:
    def __init__(self, net, src, out, sends, recvs, own, index, halves, line=True, square=True, core=True):
        self.net, self.src, self.out, self.sends, self.recvs, self.own = net, src, out, sends, recvs, own
        self.index, self.halves = index, halves
        self.line, self.square, self.core = line, square, core
        self.waits_core, self.waits_own, self.seen = True, True, set()

    def slot(self, s, z):
        return self.out.at[self.index(s, z, self.net.c)]

    def wait_own(self):
        pltpu.make_async_copy(self.src, self.slot(self.net.s, self.net.z), self.own).wait()

    def wait_core(self, z):
        place = self.places()[3] + z
        self.arrived(self.out.at[self.index(self.net.s, z, 1 - self.net.c)], place)

    def send(self, block, target, place, device):
        copy = remote(block, target, self.sends, self.recvs, place, device)
        copy.start()

    def sent(self, block, place):
        remote(block, block, self.sends, self.recvs, place, self.net.core).wait_send()

    def arrived(self, block, place):
        remote(block, block, self.sends, self.recvs, place, self.net.core).wait_recv()

    def places(self):
        z = self.net.line
        right, left, square, core = 0, z, 2 * z, 8 * z
        return right, left, square, core

    def chain(self, k, from_left):
        net = self.net
        z = net.z - k if from_left else net.z + k
        present = z >= 0 if from_left else z < net.line
        self.seen.add((k, from_left))
        for stage in (self.have, self.pass_square, self.end_square) if self.square else (self.have,):
            if k == 0:
                stage(0, net.z, None)
            else:
                pl.when(present)(lambda stage=stage: stage(k, z, from_left))
            yield

    def chains(self):
        chains = [self.chain(0, True)]
        for k in range(1, self.net.line if self.line else 1):
            chains += [self.chain(k, True), self.chain(k, False)]
        return chains

    def have(self, k, z, from_left):
        net = self.net
        right, left, square, core = self.places()
        target = self.slot(net.s, z)
        block = self.src if k == 0 else target
        if k == 0:
            pltpu.make_async_copy(self.src, target, self.own).start()
        else:
            self.arrived(target, (right if from_left else left) + z)
        if self.line:
            if from_left is not False:
                pl.when(net.z < net.line - 1)(lambda: self.send(block, target, right + z, net.right))
            if from_left is not True:
                pl.when(net.z > 0)(lambda: self.send(block, target, left + z, net.left))
        if self.square:
            for kind, part, device in ((0, 0, net.x), (2, 1, net.y), (1, 0, net.y), (3, 1, net.x)):
                self.send(
                    self.halves(block, part),
                    self.halves(target, part),
                    square + kind * net.line + z,
                    device,
                )
        if self.core:
            self.send(block, target, core + z, net.core)

    def pass_square(self, k, z, from_left):
        net = self.net
        _, _, square, core = self.places()
        for kind, part, other, then, device, mirror in (
            (0, 0, net.s ^ 1, 4, net.y, 1),
            (2, 1, net.s ^ 2, 5, net.x, 2),
        ):
            block = self.halves(self.slot(other, z), part)
            self.arrived(block, square + kind * net.line + z)
            self.send(block, block, square + then * net.line + z, device)
            if self.core:
                self.send(block, block, core + mirror * net.line + z, net.core)

    def end_square(self, k, z, from_left):
        net = self.net
        _, _, square, core = self.places()
        for kind, part, other, mirror in self.last(net):
            block = self.halves(self.slot(other, z), part)
            self.arrived(block, square + kind * net.line + z)
            if self.core:
                self.send(block, block, core + mirror * net.line + z, net.core)

    def last(self, net):
        return (
            (1, 0, net.s ^ 2, 3),
            (3, 1, net.s ^ 1, 5),
            (4, 0, net.s ^ 3, 4),
            (5, 1, net.s ^ 3, 6),
        )

    def closing(self):
        net = self.net
        right, left, square, core = self.places()
        own = self.slot(net.s, net.z)
        half = [self.halves(own, 0), self.halves(own, 1)] if self.square else []
        for z in range(net.line) if self.line else [net.z]:
            if self.core:
                for mirror, part, other in (
                    (0, None, net.s),
                    (1, 0, net.s ^ 1),
                    (2, 1, net.s ^ 2),
                    (3, 0, net.s ^ 2),
                    (4, 0, net.s ^ 3),
                    (5, 1, net.s ^ 1),
                    (6, 1, net.s ^ 3),
                ):
                    if part is not None and not self.square:
                        continue
                    block = self.out.at[self.index(other, z, 1 - net.c)]
                    block = block if part is None else self.halves(block, part)
                    if self.waits_core:
                        self.arrived(block, core + mirror * net.line + z)
                    self.sent(block, core + mirror * net.line + z)
                yield
            if self.square:
                for kind, part in ((0, 0), (1, 0), (2, 1), (3, 1), (4, 0), (5, 1)):
                    self.sent(half[part], square + kind * net.line + z)
                yield
            if self.line:
                pl.when((z <= net.z) & (net.z < net.line - 1))(lambda: self.sent(own, right + z))
                pl.when((z >= net.z) & (net.z > 0))(lambda: self.sent(own, left + z))
        if self.waits_own:
            self.wait_own()
        yield


class Job:
    def __init__(self, arrays, outs, scratch, steps, where=pl.ANY, out_where=pl.ANY):
        self.arrays, self.outs, self.scratch, self.steps = arrays, outs, scratch, steps
        self.where, self.out_where = where, out_where


def specs(where, arrays):
    places = where if isinstance(where, list) else [where] * len(arrays)
    return [pl.BlockSpec(memory_space=place) for place in places]


def together_kernel(line, jobs, order, *refs):
    refs = list(refs)
    take = lambda count: [refs.pop(0) for _ in range(count)]
    ins = [take(len(job.arrays)) for job in jobs]
    outs = [take(len(job.outs)) for job in jobs]
    scratch = [take(len(job.scratch)) for job in jobs]
    net = Net(line)
    net.greet([net.x, net.y, net.core] + net.others())
    chains, ends = [], []
    for job, *parts in zip(jobs, ins, outs, scratch):
        more, last = job.steps(net, *parts)
        chains += more
        ends += last
    for turn in order:
        next((chains + ends)[turn], None)
    while chains:
        chains = [chain for chain in chains if next(chain, True) is None]
    for end in ends:
        for _ in end:
            pass


def together(collective_id, name, sizes, jobs):
    line = sizes["mem"] // 2
    moved = sum(2 * a.size * a.dtype.itemsize for job in jobs for a in job.arrays)
    results = pl.pallas_call(
        functools.partial(together_kernel, line, jobs, ORDERS.get((name, line), ())),
        out_shape=[out for job in jobs for out in job.outs],
        in_specs=[s for job in jobs for s in specs(job.where, job.arrays)],
        out_specs=[s for job in jobs for s in specs(job.out_where, job.outs)],
        scratch_shapes=[s for job in jobs for s in job.scratch],
        compiler_params=params(collective_id=collective_id, has_side_effects=True),
        cost_estimate=pl.CostEstimate(flops=0, bytes_accessed=moved, transcendentals=0),
        name=name,
    )(*[a for job in jobs for a in job.arrays])
    results = list(results)
    return [[results.pop(0) for _ in job.outs] for job in jobs]


def gather_parts(net, src, out, scratch, halves, reach, pieces):
    line, rows = net.line, src.shape[0] // pieces
    index = {
        "all": lambda s, z, c: (s * line + z) * 2 + c,
        "line": lambda s, z, c: z * 2 + c,
        "square": lambda s, z, c: s,
    }[reach]
    parts = []
    for i in range(pieces):
        span = pl.ds(i * rows, rows)
        ends = (src, out) if pieces == 1 else (src.at[span], out.at[:, span])
        parts.append(
            Gather(
                net, *ends, *scratch[3 * i : 3 * i + 3], index, halves,
                line=reach != "square", square=reach != "line", core=reach != "square",
            )
        )
    return parts


def gather_semaphores(line, pieces=1):
    return ([pltpu.SemaphoreType.DMA((15 * line,))] * 2 + [pltpu.SemaphoreType.DMA]) * pieces


def gather_job(sizes, array, halves, reach, pieces=1):
    line = sizes["mem"] // 2
    slots = {"all": sizes["seq"] * sizes["mem"], "line": sizes["mem"], "square": sizes["seq"]}[reach]

    def steps(net, ins, outs, scratch):
        parts = gather_parts(net, ins[0], outs[0], scratch, halves, reach, pieces)
        return [chain for part in parts for chain in part.chains()], [part.closing() for part in parts]

    out = jax.ShapeDtypeStruct((slots,) + array.shape, array.dtype)
    return Job([array], [out], gather_semaphores(line, pieces), steps, pltpu.VMEM)


class Scatter:
    def __init__(self, net, src, out, buffers, sems, halves, whole=True):
        self.net, self.src, self.out, self.halves = net, src, out, halves
        self.whole, self.count = whole, buffers[0].shape[1]
        self.held, self.twin, self.first, self.second, self.along = buffers
        self.sends, self.recvs, self.own = sems

    def send(self, block, target, place, device):
        remote(block, target, self.sends, self.recvs, place, device).start()

    def sent(self, block, place):
        remote(block, block, self.sends, self.recvs, place, self.net.core).wait_send()

    def arrived(self, block, place):
        remote(block, block, self.sends, self.recvs, place, self.net.core).wait_recv()

    def places(self):
        z = self.count
        return 0, 4 * z, 8 * z, 10 * z, 11 * z

    def loading(self, d):
        source = self.src.at[:, d, self.net.c] if self.whole else self.src.at[:, d]
        return pltpu.make_async_copy(source, self.held.at[:, d], self.own.at[d])

    def load(self, d):
        net = self.net
        if self.src is not None:
            self.loading(d).start()
        for s in range(4 if self.whole else 0):
            self.send(self.src.at[s, d, 1 - net.c], self.twin.at[s, d], s * self.count + d, net.core)

    def add_core(self, d):
        net = self.net
        _, first, _, _, _ = self.places()
        if self.src is not None:
            self.loading(d).wait()
        for turn in (3, 2, 1, 0):
            s = net.s ^ turn
            if self.whole:
                self.arrived(self.twin.at[s, d], s * self.count + d)
                self.held[s, d] = self.held[s, d] + self.twin[s, d]
            for part, device, slot, kind in {
                3: ((0, net.y, 1, 1), (1, net.x, 1, 3)),
                2: ((0, net.y, 0, 0),),
                1: ((1, net.x, 0, 2),),
                0: (),
            }[turn]:
                self.send(
                    self.halves(self.held.at[s, d], part),
                    self.first.at[part, slot, d],
                    first + kind * self.count + d,
                    device,
                )

    def chain(self, k):
        d = lax.rem(self.net.z + k, self.net.line) if self.whole else k
        for stage in (self.load, self.add_core, self.add_first, self.add_second, self.line_step):
            stage(d)
            yield
        if self.whole and k == 0:
            self.keep()
            yield

    def add(self, block, other):
        block[...] = block[...] + other[...]

    def add_first(self, d):
        net = self.net
        _, first, second, _, _ = self.places()
        for part, slot, kind, turn in ((0, 1, 1, 1), (1, 1, 3, 2), (0, 0, 0, 0), (1, 0, 2, 0)):
            got = self.first.at[part, slot, d]
            self.arrived(got, first + kind * self.count + d)
            block = self.halves(self.held.at[net.s ^ turn, d], part)
            self.add(block, got)
            if turn:
                device = net.x if part == 0 else net.y
                self.send(block, self.second.at[part, d], second + part * self.count + d, device)

    def add_second(self, d):
        net = self.net
        _, _, second, _, _ = self.places()
        for part in range(2):
            self.arrived(self.second.at[part, d], second + part * self.count + d)
            self.add(self.halves(self.held.at[net.s, d], part), self.second.at[part, d])

    def line_step(self, d):
        net = self.net
        _, _, _, right, left = self.places()
        block = self.held.at[net.s, d]
        if not self.whole:
            self.out[0][d] = block[...].astype(F32)
            return

        def go():
            pltpu.make_async_remote_copy(
                src_ref=block,
                dst_ref=self.along.at[net.z],
                send_sem=self.sends.at[right + d],
                recv_sem=self.recvs.at[left + net.z],
                device_id=(net.s, 2 * d + net.c),
                device_id_type=MESH,
            ).start()

        pl.when(net.z != d)(go)

    def keep(self):
        net = self.net
        _, _, _, _, left = self.places()
        total = self.held[net.s, net.z].astype(F32)
        for k in range(1, net.line):
            z = lax.rem(net.z + k, net.line)
            self.arrived(self.along.at[z], left + z)
            total = total + self.along[z].astype(F32)
        start = 0
        for out in self.out:
            out[...] = total[:, start : start + out.shape[-1]]
            start += out.shape[-1]

    def closing(self):
        net = self.net
        _, first, second, right, _ = self.places()
        full = self.held.at[net.s, 0]
        for k in far_first(self.count):
            d = lax.rem(net.z + k, net.line) if self.whole else k
            for s in range(4 if self.whole else 0):
                self.sent(full, s * self.count + d)
            for kind, part in enumerate((0, 0, 1, 1)):
                self.sent(self.halves(full, part), first + kind * self.count + d)
            for part in range(2):
                self.sent(self.halves(full, part), second + part * self.count + d)
            if self.whole and k:
                self.sent(full, right + d)
            yield


def far_first(count):
    return sorted(range(count), key=lambda k: (k == 0, -min(k, count - k)))


def scatter_scratch(count, rows, columns, halves, whole):
    half = (rows // 2, columns) if halves is row_halves else (rows, columns // 2)
    block, unused = (rows, columns), (16, 128)
    return [
        pltpu.VMEM((4, count) + block, BF16),
        pltpu.VMEM((4, count) + block if whole else unused, BF16),
        pltpu.VMEM((2, 2, count) + half, BF16),
        pltpu.VMEM((2, count) + half, BF16),
        pltpu.VMEM((count,) + block if whole else unused, BF16),
        pltpu.SemaphoreType.DMA((12 * count,)),
        pltpu.SemaphoreType.DMA((12 * count,)),
        pltpu.SemaphoreType.DMA((count,)),
    ]


def scatter_job(sizes, array, halves, whole=True):
    square, line = sizes["seq"], sizes["mem"] // 2
    columns = array.shape[1]
    if whole:
        count, rows = line, array.shape[0] // (2 * square * line)
        array = array.reshape(square, line, 2, rows, columns)
        outs = [jax.ShapeDtypeStruct((rows, w), F32) for w in [columns]]
    else:
        count, rows = PIECES, array.shape[0] // (square * PIECES)
        array = array.reshape(square, count, rows, columns)
        outs = [jax.ShapeDtypeStruct((count, rows, columns), F32)]
    scratch = scatter_scratch(count, rows, columns, halves, whole)

    def steps(net, ins, outs, scratch):
        scatter = Scatter(net, ins[0], outs, scratch[:5], scratch[5:], halves, whole)
        return [scatter.chain(k) for k in far_first(count)], [scatter.closing()]

    return Job([array], outs, scratch, steps, out_where=pltpu.VMEM)


class Return:
    def __init__(self, net, sources, outs, scratch):
        kinds = len(sources)
        self.net, self.sources, self.outs, self.kinds = net, sources, outs, range(kinds)
        self.held, self.twin = scratch[:kinds], scratch[kinds : 2 * kinds]
        self.own, self.twin_sends, self.twin_recvs, self.sends, self.recvs = scratch[2 * kinds :]

    def loading(self, i, d):
        source = self.sources[i].at[d, self.net.c]
        return pltpu.make_async_copy(source, self.held[i].at[d], self.own.at[i, d])

    def pairing(self, i, d):
        net = self.net
        return remote(
            self.sources[i].at[d, 1 - net.c],
            self.twin[i].at[d],
            self.twin_sends.at[i],
            self.twin_recvs.at[i],
            d,
            net.core,
        )

    def giving(self, i, k, d, slot, device):
        return pltpu.make_async_remote_copy(
            src_ref=self.held[i].at[d],
            dst_ref=self.outs[i].at[slot],
            send_sem=self.sends.at[i, k],
            recv_sem=self.recvs.at[i, slot],
            device_id=device,
            device_id_type=MESH,
        )

    def keeping(self, i, d):
        return pltpu.make_async_copy(
            self.held[i].at[d], self.outs[i].at[self.net.z], self.own.at[i, d]
        )

    def merge(self, d):
        held, twin = self.held, self.twin
        if len(held) == 1:
            held[0][d] = held[0][d] + twin[0][d]
            return
        mine, theirs = held[1][d], twin[1][d]
        top = jnp.maximum(mine[:HEADS], theirs[:HEADS])
        shares = [jnp.exp2(mine[:HEADS] - top), jnp.exp2(theirs[:HEADS] - top)]
        held[1][d] = jnp.concatenate(
            [top, mine[HEADS:] * shares[0] + theirs[HEADS:] * shares[1]], axis=0
        )
        shares = columns_of(jnp.concatenate(shares, axis=0))
        for h in range(HEADS):
            span = slice(h * 128, (h + 1) * 128)
            held[0][d, :, span] = (
                held[0][d, :, span].astype(F32) * shares[:, h : h + 1]
                + twin[0][d, :, span].astype(F32) * shares[:, HEADS + h : HEADS + h + 1]
            ).astype(BF16)


def index_job(sizes, index, mem_dev):
    line = sizes["mem"] // 2
    segments = 2 * line
    rows, count = index.shape
    out = jax.ShapeDtypeStruct((segments, rows, 128), jnp.int32)
    scratch = gather_semaphores(line) + mask_scratch(rows, count)
    scratch = scratch + [pltpu.VMEM((segments, rows, count), jnp.int32)]

    def steps(net, ins, outs, scratch):
        *sems, places_ref, words_ref, all_index = scratch
        (part,) = gather_parts(net, ins[0], all_index, sems, row_halves, "line", 1)
        part.waits_core = part.waits_own = False

        def words(z, far):
            if far:
                part.wait_core(z)
            segment = 2 * z + (1 - net.c if far else net.c)
            outs[0][segment] = mask_words(
                all_index[segment], net.m * mem_dev, mem_dev, places_ref, words_ref
            )

        def masks():
            for k in range(line):
                for from_left in (True, False) if k else (True,):
                    z = net.z - k if from_left else net.z + k
                    present = z >= 0 if from_left else z < line
                    here = (lambda body: body()) if k == 0 else pl.when(present)
                    need([part], k, from_left)
                    if k == 0:
                        part.wait_own()
                    for far in (False, True):
                        here(lambda: words(z, far))
                        yield

        return part.chains() + [masks()], [part.closing()]

    return Job([index], [out], scratch, steps, pltpu.VMEM, pltpu.VMEM)


def need(parts, k, from_left):
    for part in parts:
        assert (k, from_left) in part.seen


class OwnerForward(Return):
    def __init__(self, net, scale, parts, ins, outs, scratch, sems):
        self.bits, self.keys, self.values = ins
        self.queries, *peers = outs
        self.bias, self.kept, self.key, self.value, *held = scratch
        self.far, held = held[:2], held[2:]
        self.loads, *sems = sems
        super().__init__(net, self.far, peers, held + sems)
        self.parts, self.scale = parts, scale

    def pairing(self, i, d):
        net = self.net
        return remote(
            self.far[i].at[d],
            self.twin[i].at[d],
            self.twin_sends.at[i],
            self.twin_recvs.at[i],
            d,
            net.core,
        )

    def bring(self, z, far):
        net = self.net
        segment = 2 * z + (1 - net.c if far else net.c)
        slot = int(far)
        return [
            pltpu.make_async_copy(self.keys.at[segment], self.key.at[slot], self.loads.at[0, slot]),
            pltpu.make_async_copy(
                self.values.at[segment], self.value.at[slot], self.loads.at[1, slot]
            ),
        ]

    def attend(self, z, far, span):
        net = self.net
        segment = 2 * z + (1 - net.c if far else net.c)
        if span[0] == 0:
            if far:
                for part in self.parts:
                    part.wait_core(z)
            fill_bias(self.bits.at[segment], self.bias)
            for copy in self.bring(z, far):
                copy.wait()
        target = self.far if far else self.held
        owner_forward_heads(
            span,
            self.scale,
            self.queries.at[segment],
            self.key.at[int(far)],
            self.value.at[int(far)],
            self.bias,
            self.kept,
            target[0].at[z],
            target[1].at[z],
        )
        if far and span[1] == HEADS:
            for i in self.kinds:
                self.pairing(i, z).start()

    def home(self, k, z):
        for i in self.kinds:
            self.pairing(i, z).wait_recv()
        self.merge(z)
        net = self.net
        for i in self.kinds:
            if k:
                self.giving(i, z, z, net.z, (net.s, 2 * z + net.c)).start()
            else:
                self.keeping(i, z).start()

    def chain(self):
        net = self.net
        for k in range(net.line):
            for from_left in (True, False) if k else (True,):
                z = net.z - k if from_left else net.z + k
                present = z >= 0 if from_left else z < net.line
                here = (lambda body: body()) if k == 0 else pl.when(present)
                need(self.parts, k, from_left)
                if k == 0:
                    for part in self.parts:
                        part.wait_own()

                def start():
                    for copy in self.bring(z, True) + self.bring(z, False):
                        copy.start()

                here(start)
                yield
                for far in (True, False):
                    for span in SPANS:
                        here(lambda: self.attend(z, far, span))
                        yield
                here(lambda: self.home(k, z))
                yield

    def closing(self):
        net = self.net
        for k in range(net.line):
            d = lax.rem(net.z + k, net.line)
            for i in self.kinds:
                self.pairing(i, d).wait_send()
                if k:
                    copy = self.giving(i, d, d, d, net.core)
                    copy.wait_recv()
                    copy.wait_send()
                else:
                    self.keeping(i, d).wait()
            yield


def forward_job(sizes, queries, keys_values, bits, cached_keys, cached_values, scale):
    line = sizes["mem"] // 2
    (rows, width), segments = queries.shape, bits.shape[0]
    mem_dev = cached_keys.shape[1]
    length = sizes["seq"] * rows
    shape = jax.ShapeDtypeStruct
    outs = [
        shape((segments, rows, width), BF16),
        shape((sizes["seq"],) + keys_values.shape, BF16),
        shape((line, rows, width), BF16),
        shape((line, STATS, rows), F32),
        shape((rows, width), F32),
        shape((STATS, rows), F32),
    ]
    partial = [pltpu.VMEM((line, rows, width), BF16), pltpu.VMEM((line, STATS, rows), F32)]
    scratch = (
        gather_semaphores(line, PIECES)
        + gather_semaphores(line)
        + [pltpu.VMEM((rows, length), F32)]
        + [pltpu.VMEM((rows, mem_dev), F32), pltpu.VMEM((rows, 128), F32)]
        + [pltpu.VMEM((2, mem_dev, width), BF16)] * 2
        + partial * 3
        + [pltpu.SemaphoreType.DMA((2, 2))]
        + [pltpu.SemaphoreType.DMA((2, line))] * 5
    )

    def steps(net, ins, outs, scratch):
        queries, keys_values, *owner_ins = ins
        all_queries, segment_kv, out, stats, local_out, local_stats = outs
        scratch = list(scratch)
        take = lambda count: [scratch.pop(0) for _ in range(count)]
        parts = gather_parts(net, queries, all_queries, take(3 * PIECES), row_halves, "line", PIECES)
        (square,) = gather_parts(net, keys_values, segment_kv, take(3), row_halves, "square", 1)
        (local_bias,) = take(1)
        buffers = take(10)
        owner = OwnerForward(
            net, scale, parts, owner_ins, [all_queries, out, stats], buffers, scratch
        )
        for part in parts:
            part.waits_core = part.waits_own = False
        square.waits_own = False

        def local():
            for chain in square.chains():
                yield from chain
            square.wait_own()
            yield from local_forward_steps(
                scale, net.s, queries, segment_kv, local_out, local_stats, local_bias
            )

        chains = [chain for part in parts for chain in part.chains()]
        ends = [part.closing() for part in parts] + [square.closing(), owner.closing()]
        return chains + [local(), owner.chain()], ends

    vmem = pltpu.VMEM
    return Job(
        [queries, keys_values, bits, cached_keys, cached_values],
        outs,
        scratch,
        steps,
        [vmem, vmem, vmem, pl.ANY, pl.ANY],
        [vmem, vmem, pl.ANY, pl.ANY, vmem, vmem],
    )


def mask_words(index, base, mem_dev, place_ref, bit_ref):
    relative = index - base
    inside = (relative >= 0) & (relative < mem_dev)
    place = jnp.where(inside, relative & 127, 0)
    bit = jnp.where(inside, lax.shift_left(jnp.ones_like(relative), relative >> 7), 0)
    place_ref[...] = place.T
    bit_ref[...] = bit.T
    sought = lax.broadcasted_iota(jnp.int32, (128, 128), 0)
    halves = []
    for start in range(0, index.shape[0], 128):

        def eight(g, words, start=start):
            group = pl.ds(pl.multiple_of(g * 8, 8), 8)
            places = place_ref[group, start : start + 128]
            bits = bit_ref[group, start : start + 128]
            for j in range(8):
                words = words | jnp.where(places[j : j + 1] == sought, bits[j : j + 1], 0)
            return words

        none = jnp.zeros((128, 128), jnp.int32)
        words = lax.fori_loop(0, index.shape[1] // 8, eight, none)
        halves.append(words.T)
    return jnp.concatenate(halves, axis=0)


def mask_scratch(rows, count):
    return [pltpu.VMEM((count, rows), jnp.int32), pltpu.VMEM((count, rows), jnp.int32)]


def mask_kernel(mem_dev, base_ref, index_ref, bits_ref, place_ref, bit_ref):
    bits_ref[0] = mask_words(index_ref[0], base_ref[0], mem_dev, place_ref, bit_ref)


def mask_bits(base, all_index, mem_dev):
    segments, rows, count = all_index.shape
    return pl.pallas_call(
        functools.partial(mask_kernel, mem_dev),
        grid_spec=pltpu.PrefetchScalarGridSpec(
            num_scalar_prefetch=1,
            grid=(segments,),
            in_specs=[pl.BlockSpec((1, rows, count), lambda g, b: (g, 0, 0))],
            out_specs=pl.BlockSpec((1, rows, 128), lambda g, b: (g, 0, 0)),
            scratch_shapes=mask_scratch(rows, count),
        ),
        out_shape=jax.ShapeDtypeStruct((segments, rows, 128), jnp.int32),
        compiler_params=params(),
        name="mask_bits",
    )(base, all_index)


def fill_bias(bits_ref, bias_ref):
    bits = bits_ref[...].reshape(bits_ref.shape[-2:])
    for b in range(bias_ref.shape[1] // 128):
        bias_ref[:, b * 128 : (b + 1) * 128] = jnp.where(((bits >> b) & 1) != 0, 0.0, FLOOR)


def owner_backward_heads(span, scale, q_ref, g_ref, st_ref, k_ref, v_ref, bias_ref, dq_ref):
    stats = columns_of(st_ref[...])
    lanes = lax.broadcasted_iota(jnp.int32, stats.shape, 1)

    def two(i, carry):
        for h in (2 * i, 2 * i + 1):
            lane = pl.ds(pl.multiple_of(h * 128, 128), 128)
            total = jnp.sum(jnp.where(lanes == h, stats, 0.0), axis=1, keepdims=True)
            dots = jnp.sum(jnp.where(lanes == HEADS + h, stats, 0.0), axis=1, keepdims=True)
            scores = dot(q_ref[:, lane], k_ref[:, lane], NT) * scale + bias_ref[...]
            weights = jnp.exp2(scores - total)
            dscore = weights * (dot(g_ref[:, lane], v_ref[:, lane], NT) - dots)
            dq_ref[:, lane] = (
                dot(dscore.astype(BF16), k_ref[:, lane]) * (scale / LOG2E)
            ).astype(BF16)
        return carry

    lax.fori_loop(span[0] // 2, span[1] // 2, two, 0)


def owner_forward_heads(span, scale, q_ref, k_ref, v_ref, bias_ref, stats_ref, o_ref, st_ref):
    rows = q_ref.shape[0]
    lanes = lax.broadcasted_iota(jnp.int32, (rows, 128), 1)

    def two(i, stats):
        for h in (2 * i, 2 * i + 1):
            lane = pl.ds(pl.multiple_of(h * 128, 128), 128)
            scores = dot(q_ref[:, lane], k_ref[:, lane], NT) * scale + bias_ref[...]
            top = jnp.maximum(jnp.max(scores, axis=1, keepdims=True), LOW)
            weights = jnp.exp2(scores - top)
            total = jnp.sum(weights, axis=1, keepdims=True)
            stats = jnp.where(lanes == h, top, jnp.where(lanes == HEADS + h, total, stats))
            o_ref[:, lane] = dot(weights.astype(BF16), v_ref[:, lane]).astype(BF16)
        return stats

    start = stats_ref[...] if span[0] else jnp.zeros((rows, 128), F32)
    stats = lax.fori_loop(span[0] // 2, span[1] // 2, two, start)
    if span[1] == HEADS:
        st_ref[...] = stats.T[:STATS]
    else:
        stats_ref[...] = stats


def owner_forward_kernel(scale, order_ref, q_ref, bits_ref, k_ref, v_ref, o_ref, st_ref, bias_ref):
    del order_ref
    fill_bias(bits_ref, bias_ref)
    maxima, sums = [], []
    for h in range(HEADS):
        span = slice(h * 128, (h + 1) * 128)
        scores = dot(q_ref[0, :, span], k_ref[0, :, span], NT) * scale + bias_ref[...]
        top = jnp.maximum(jnp.max(scores, axis=1, keepdims=True), LOW)
        weights = jnp.exp2(scores - top)
        maxima.append(top)
        sums.append(jnp.sum(weights, axis=1, keepdims=True))
        o_ref[0, :, span] = dot(weights.astype(BF16), v_ref[0, :, span]).astype(BF16)
    st_ref[0] = spread(maxima + sums).T[:STATS]


def owner_forward(order, queries, bits, cached_keys, cached_values, scale):
    segments, rows, width = queries.shape
    mem_dev = cached_keys.shape[1]
    active = order.shape[0]
    picked = lambda a, o: (o[a], 0, 0)
    return pl.pallas_call(
        functools.partial(owner_forward_kernel, scale),
        grid_spec=pltpu.PrefetchScalarGridSpec(
            num_scalar_prefetch=1,
            grid=(active,),
            in_specs=[
                pl.BlockSpec((1, rows, width), picked),
                pl.BlockSpec((1, rows, 128), picked),
                pl.BlockSpec((1, mem_dev, width), picked),
                pl.BlockSpec((1, mem_dev, width), picked),
            ],
            out_specs=[
                pl.BlockSpec((1, rows, width), picked),
                pl.BlockSpec((1, STATS, rows), picked),
            ],
            scratch_shapes=[pltpu.VMEM((rows, mem_dev), F32)],
        ),
        out_shape=[
            jax.ShapeDtypeStruct((segments, rows, width), BF16),
            jax.ShapeDtypeStruct((segments, STATS, rows), F32),
        ],
        compiler_params=params(),
        name="owner_forward",
    )(order, queries, bits, cached_keys, cached_values)


def owner_backward_kernel(
    scale, order_ref, q_ref, g_ref, st_ref, bits_ref, k_ref, v_ref, dq_ref, bias_ref
):
    del order_ref
    fill_bias(bits_ref, bias_ref)
    stats = columns_of(st_ref[0])
    for h in range(HEADS):
        span = slice(h * 128, (h + 1) * 128)
        scores = dot(q_ref[0, :, span], k_ref[0, :, span], NT) * scale + bias_ref[...]
        weights = jnp.exp2(scores - stats[:, h : h + 1])
        dweights = dot(g_ref[0, :, span], v_ref[0, :, span], NT)
        dscore = weights * (dweights - stats[:, HEADS + h : HEADS + h + 1])
        dq_ref[0, :, span] = (
            dot(dscore.astype(BF16), k_ref[0, :, span]) * (scale / LOG2E)
        ).astype(BF16)


def owner_backward(order, queries, grads, stats, bits, cached_keys, cached_values, scale):
    segments, rows, width = queries.shape
    mem_dev = cached_keys.shape[1]
    active = order.shape[0]
    picked = lambda a, o: (o[a], 0, 0)
    return pl.pallas_call(
        functools.partial(owner_backward_kernel, scale),
        grid_spec=pltpu.PrefetchScalarGridSpec(
            num_scalar_prefetch=1,
            grid=(active,),
            in_specs=[
                pl.BlockSpec((1, rows, width), picked),
                pl.BlockSpec((1, rows, width), picked),
                pl.BlockSpec((1, STATS, rows), picked),
                pl.BlockSpec((1, rows, 128), picked),
                pl.BlockSpec((1, mem_dev, width), picked),
                pl.BlockSpec((1, mem_dev, width), picked),
            ],
            out_specs=pl.BlockSpec((1, rows, width), picked),
            scratch_shapes=[pltpu.VMEM((rows, mem_dev), F32)],
        ),
        out_shape=jax.ShapeDtypeStruct((segments, rows, width), BF16),
        compiler_params=params(),
        name="owner_backward",
    )(order, queries, grads, stats, bits, cached_keys, cached_values)


def causal_bias(place, rows, keys):
    row = place * rows + lax.broadcasted_iota(jnp.int32, (rows, keys), 0)
    return jnp.where(lax.broadcasted_iota(jnp.int32, (rows, keys), 1) <= row, 0.0, FLOOR)


def columns_at(kv_ref, span):
    block = kv_ref[:, span] if len(kv_ref.shape) == 2 else kv_ref[:, :, span]
    return block.reshape(-1, block.shape[-1])


def local_forward_steps(scale, place, q_ref, kv_ref, o_ref, st_ref, bias_ref):
    rows, width = q_ref.shape
    bias_ref[...] = causal_bias(place, rows, bias_ref.shape[1])
    maxima, sums = [], []
    for h in range(HEADS):
        span, over = slice(h * 128, (h + 1) * 128), slice(width + h * 128, width + (h + 1) * 128)
        scores = dot(q_ref[:, span], columns_at(kv_ref, span), NT) * scale + bias_ref[...]
        top = jnp.max(scores, axis=1, keepdims=True)
        weights = jnp.exp2(scores - top)
        maxima.append(top)
        sums.append(jnp.sum(weights, axis=1, keepdims=True))
        o_ref[:, span] = dot(weights.astype(BF16), columns_at(kv_ref, over))
        yield
    st_ref[...] = spread(maxima + sums).T[:STATS]


def local_backward_steps(
    scale, place, q_ref, g_ref, st_ref, kv_ref, dq_ref, dkv_ref, bias_ref
):
    rows, width = q_ref.shape
    bias_ref[...] = causal_bias(place, rows, bias_ref.shape[1])
    stats = columns_of(st_ref[...])
    for h in range(HEADS):
        span, over = slice(h * 128, (h + 1) * 128), slice(width + h * 128, width + (h + 1) * 128)
        query, key, grad = q_ref[:, span], columns_at(kv_ref, span), g_ref[:, span]
        scores = dot(query, key, NT) * scale + bias_ref[...]
        weights = jnp.exp2(scores - stats[:, h : h + 1])
        dweights = dot(grad, columns_at(kv_ref, over), NT)
        dscore = (weights * (dweights - stats[:, HEADS + h : HEADS + h + 1])).astype(BF16)
        dq_ref[:, span] = dot(dscore, key) * (scale / LOG2E)
        dkey = (dot(dscore, query, TN) * (scale / LOG2E)).astype(BF16)
        dvalue = dot(weights.astype(BF16), grad, TN).astype(BF16)
        lead = dkv_ref.shape[:-1]
        dkv_ref[(*[slice(None)] * len(lead), span)] = dkey.reshape(lead + (128,))
        dkv_ref[(*[slice(None)] * len(lead), over)] = dvalue.reshape(lead + (128,))
        yield


class OwnerBackward(OwnerForward):
    def __init__(self, net, scale, parts, stats_part, ins, outs, scratch, sems):
        self.sources_in = ins
        self.grads, self.stats, peers = outs
        *self.buffers, self.bias, far, held, twin = scratch
        self.loads, *sems = sems
        self.far = [far]
        Return.__init__(self, net, self.far, [peers], [held, twin, *sems])
        self.parts, self.scale, self.stats_part = [*parts, stats_part], scale, stats_part

    def bring(self, z, far):
        segment = 2 * z + (1 - self.net.c if far else self.net.c)
        sources = [source.at[segment] for source in (*self.sources_in, self.grads)]
        return [
            pltpu.make_async_copy(source, buffer, self.loads.at[i])
            for i, (source, buffer) in enumerate(zip(sources, self.buffers))
        ]

    def mask(self, z, far):
        if far:
            for part in self.parts:
                part.wait_core(z)
        for copy in self.bring(z, far):
            copy.start()

    def attend(self, z, far, span):
        net = self.net
        keys, values, queries, bits, grads = self.buffers
        if span[0] == 0:
            for copy in self.bring(z, far):
                copy.wait()
            fill_bias(bits, self.bias)
        segment = 2 * z + (1 - net.c if far else net.c)
        owner_backward_heads(
            span,
            self.scale,
            queries,
            grads,
            self.stats.at[segment],
            keys,
            values,
            self.bias,
            (self.far[0] if far else self.held[0]).at[z],
        )
        if far and span[1] == HEADS:
            self.pairing(0, z).start()

    def chain(self):
        net = self.net
        for k in range(net.line):
            for from_left in (True, False) if k else (True,):
                z = net.z - k if from_left else net.z + k
                present = z >= 0 if from_left else z < net.line
                here = (lambda body: body()) if k == 0 else pl.when(present)
                need(self.parts, k, from_left)
                if k == 0:
                    for part in self.parts:
                        part.wait_own()
                here(lambda: self.mask(z, True))
                yield
                for far in (True, False):
                    for span in SPANS:

                        def part():
                            self.attend(z, far, span)
                            if far and span[1] == HEADS:
                                self.mask(z, False)

                        here(part)
                        yield
                here(lambda: self.home(k, z))
                yield


def backward_job(
    sizes, queries, grads, stats, segment_kv, all_queries, bits, cached_keys, cached_values, scale
):
    square, line = sizes["seq"], sizes["mem"] // 2
    segments, rows, width = all_queries.shape
    mem_dev = cached_keys.shape[1]
    length = square * rows
    shape = jax.ShapeDtypeStruct
    outs = [
        shape((segments, rows, width), BF16),
        shape((line, rows, width), BF16),
        shape((rows, width), F32),
        shape((PIECES, rows // PIECES, 2 * width), F32),
    ]
    keys_scratch = scatter_scratch(PIECES, rows // PIECES, 2 * width, row_halves, False)
    scratch = (
        gather_semaphores(line, PIECES)
        + gather_semaphores(line)
        + [pltpu.VMEM((segments, STATS, rows), F32), pltpu.VMEM((rows, length), F32)]
        + keys_scratch
        + [pltpu.VMEM((mem_dev, width), BF16)] * 2
        + [
            pltpu.VMEM((rows, width), BF16),
            pltpu.VMEM((rows, 128), jnp.int32),
            pltpu.VMEM((rows, width), BF16),
            pltpu.VMEM((rows, mem_dev), F32),
        ]
        + [pltpu.VMEM((line, rows, width), BF16)] * 3
        + [pltpu.SemaphoreType.DMA((5,))]
        + [pltpu.SemaphoreType.DMA((1, line))] * 5
    )

    def steps(net, ins, outs, scratch):
        queries, grads, stats, segment_kv, all_queries, bits, keys, values = ins
        all_grads, peers, local_dq, grad_kv = outs
        scratch = list(scratch)
        take = lambda count: [scratch.pop(0) for _ in range(count)]
        parts = gather_parts(net, grads, all_grads, take(3 * PIECES), row_halves, "line", PIECES)
        stats_sems = take(3)
        all_stats, local_bias = take(2)
        (stats_part,) = gather_parts(net, stats, all_stats, stats_sems, row_halves, "line", 1)
        keys_scratch = take(8)
        buffers = take(9)
        scatter = Scatter(
            net, None, [grad_kv], keys_scratch[:5], keys_scratch[5:], row_halves, False
        )
        owner = OwnerBackward(
            net, scale, parts, stats_part, [keys, values, all_queries, bits],
            [all_grads, all_stats, peers], buffers, scratch,
        )
        for part in [*parts, stats_part]:
            part.waits_core = part.waits_own = False

        def local():
            yield from local_backward_steps(
                scale, net.s, queries, grads, stats, segment_kv, local_dq, scatter.held, local_bias
            )
            stages = (scatter.add_core, scatter.add_first, scatter.add_second, scatter.line_step)
            for wave in range(PIECES + 3):
                for lag in (3, 2, 1, 0):
                    if 0 <= wave - lag < PIECES:
                        stages[lag](wave - lag)
                        yield

        chains = [chain for part in [*parts, stats_part] for chain in part.chains()]
        ends = [part.closing() for part in [*parts, stats_part]]
        ends += [scatter.closing(), owner.closing()]
        return chains + [local(), owner.chain()], ends

    vmem = pltpu.VMEM
    return Job(
        [queries, grads, stats, segment_kv, all_queries, bits, cached_keys, cached_values],
        outs,
        scratch,
        steps,
        [vmem] * 4 + [pl.ANY] * 4,
        [pl.ANY, pl.ANY, vmem, vmem],
    )


def local_job(kind, arrays, scale):
    rows, width = arrays[0].shape
    length = arrays[-1].shape[0]
    if kind == "forward":
        body, extra = local_forward_steps, jax.ShapeDtypeStruct((STATS, rows), F32)
    else:
        body, extra = local_backward_steps, jax.ShapeDtypeStruct((length, 2 * width), BF16)

    def steps(net, ins, outs, scratch):
        return [body(scale, net.s, *ins, *outs, *scratch)], []

    outs = [jax.ShapeDtypeStruct((rows, width), F32), extra]
    return Job(arrays, outs, [pltpu.VMEM((rows, length), F32)], steps, pltpu.VMEM, pltpu.VMEM)


def alone_kernel(job, *refs):
    place_ref, *refs = refs
    net = type("Alone", (), {"s": place_ref[0]})
    ins, outs = len(job.arrays), len(job.arrays) + len(job.outs)
    for chain in job.steps(net, refs[:ins], refs[ins:outs], refs[outs:])[0]:
        for _ in chain:
            pass


def alone(name, place, job):
    return pl.pallas_call(
        functools.partial(alone_kernel, job),
        out_shape=job.outs,
        in_specs=[pl.BlockSpec(memory_space=pltpu.SMEM)]
        + [pl.BlockSpec(memory_space=pltpu.VMEM)] * len(job.arrays),
        out_specs=[pl.BlockSpec(memory_space=pltpu.VMEM)] * len(job.outs),
        scratch_shapes=job.scratch,
        compiler_params=params(),
        name=name,
    )(place, *job.arrays)


def copy_in(pairs, sems):
    copies = [pltpu.make_async_copy(src, dst, sems.at[i]) for i, (src, dst) in enumerate(pairs)]
    for copy in copies:
        copy.start()
    return copies


def turn(values, cosine, sine):
    return values * cosine + pltpu.roll(values, values.shape[1] // 2, 1) * sine


def inverse_root(values):
    return lax.rsqrt(jnp.mean(values * values, axis=1, keepdims=True) + EPSILON)


def project_kernel(x_ref, w_any, cos_ref, sin_ref, n_ref, q_ref, kv_ref, gain_ref, w_ref, sems):
    width = x_ref.shape[1]
    spans = [slice(i * width, (i + 1) * width) for i in range(3)]
    gains = slice(3 * width, 3 * width + 128)
    copies = copy_in([(w_any.at[:, s], w_ref.at[:, s]) for s in [gains, *spans]], sems)
    x = x_ref[...].astype(F32)
    copies[0].wait()
    gain_ref[...] = w_ref[:, gains].astype(F32).T[:8]
    normed = (x * inverse_root(x) * gain_ref[:1]).astype(BF16)
    n_ref[...] = normed
    cosine, sine = cos_ref[...], sin_ref[...]
    for i in range(3):
        copies[1 + i].wait()
        product = dot(normed, w_ref[:, spans[i]])
        for h in range(HEADS):
            span = slice(h * 128, (h + 1) * 128)
            part = product[:, span]
            part = part if i == 2 else turn(part, cosine, sine)
            if i == 0:
                q_ref[:, span] = part.astype(BF16)
            else:
                over = slice((i - 1) * width + h * 128, (i - 1) * width + (h + 1) * 128)
                kv_ref[:, over] = part.astype(BF16)


def in_vmem(count):
    return [pl.BlockSpec(memory_space=pltpu.VMEM)] * count


def project(tokens, first_weights, cosine, sine):
    rows, width = tokens.shape
    columns = first_weights.shape[1]
    return pl.pallas_call(
        project_kernel,
        out_shape=[
            jax.ShapeDtypeStruct((rows, width), BF16),
            jax.ShapeDtypeStruct((rows, width), BF16),
            jax.ShapeDtypeStruct((rows, 2 * width), BF16),
            jax.ShapeDtypeStruct((8, width), F32),
        ],
        in_specs=in_vmem(1) + [pl.BlockSpec(memory_space=pl.ANY)] + in_vmem(2),
        out_specs=in_vmem(4),
        scratch_shapes=[
            pltpu.VMEM((width, columns), BF16),
            pltpu.SemaphoreType.DMA((4,)),
        ],
        compiler_params=params(),
        name="project",
    )(tokens, first_weights, cosine, sine)


def middle_kernel(
    live_ref, x_ref, g_ref, gain_ref, lo_ref, ls_ref, po_ref, ps_ref, out_any, gate_any, up_any, down_any,
    mixed_ref, gm_ref, ga_ref, st_ref, gain_grad_ref, wo_any, wg_any, wu_any, wd_any,
    att_ref, acc_ref, gn_ref, n_ref, nt_ref, out_ref, gate_ref, up_ref, down_ref, side_ref, tall_ref, sems, writes,
):
    rows, width = x_ref.shape
    copies = copy_in(
        [(out_any, out_ref), (gate_any, gate_ref), (up_any, up_ref), (down_any, down_ref)], sems
    )
    live = live_ref[0] > 0
    peers = ps_ref.shape[0]
    local_max, local_sum = ls_ref[:HEADS], ls_ref[HEADS:]
    peer_max = [jnp.where(live, ps_ref[p, :HEADS], LOW) for p in range(peers)]
    peer_sum = [jnp.where(live, ps_ref[p, HEADS:], 0.0) for p in range(peers)]
    top = functools.reduce(jnp.maximum, peer_max, local_max)
    shares = [jnp.exp2(m - top) for m in [local_max] + peer_max]
    total = functools.reduce(
        jnp.add, [s * t for s, t in zip(shares, [local_sum] + peer_sum)]
    )
    log_total = top + jnp.log2(total)
    shares = columns_of(jnp.concatenate([s / total for s in shares], axis=0))
    for h in range(HEADS):
        span = slice(h * 128, (h + 1) * 128)
        part = lo_ref[:, span] * shares[:, h : h + 1]
        for p in range(peers):
            column = shares[:, (p + 1) * HEADS + h : (p + 1) * HEADS + h + 1]
            part += jnp.where(live, po_ref[p, :, span].astype(F32), 0.0) * column
        att_ref[:, span] = part
    attention_low = att_ref[...].astype(BF16)
    copies[0].wait()
    mid = x_ref[...].astype(F32) + dot(attention_low, out_ref[...])
    gm_ref[...] = mid
    root = inverse_root(mid)
    n_ref[...] = (mid * root * gain_ref[1:2]).astype(BF16)
    for copy in copies[1:]:
        copy.wait()
    nt_ref[...] = n_ref[...].T
    grad = g_ref[...]
    acc_ref[...] = jnp.zeros_like(acc_ref)
    gn_ref[...] = jnp.zeros_like(gn_ref)
    hidden_width = gate_ref.shape[1]
    step = 512
    pending = [[], []]

    def write(slot, product, buffer, target, place):
        buffer[...] = product.astype(BF16)
        copy = pltpu.make_async_copy(buffer, target, writes.at[slot, place])
        copy.start()
        pending[slot].append(copy)

    for turn_of, start in enumerate(range(0, hidden_width, step)):
        span = slice(start, min(start + step, hidden_width))
        slot = turn_of % 2
        while pending[slot]:
            pending[slot].pop().wait()
        norm_two = n_ref[...]
        gate = dot(norm_two, gate_ref[:, span])
        upward = dot(norm_two, up_ref[:, span])
        grad_hidden = dot(grad, down_ref[span, :], NT)
        sigmoid = 1.0 / (1.0 + jnp.exp(-gate))
        silu = gate * sigmoid
        hidden = (silu * upward).astype(BF16)
        grad_gate = (grad_hidden * upward * (sigmoid * (1.0 + gate * (1.0 - sigmoid)))).astype(BF16)
        grad_up = (grad_hidden * silu).astype(BF16)
        write(slot, dot(nt_ref[...], grad_gate), side_ref.at[slot, 0, :, : span.stop - start], wg_any.at[:, span], 0)
        write(slot, dot(nt_ref[...], grad_up), side_ref.at[slot, 1, :, : span.stop - start], wu_any.at[:, span], 1)
        write(slot, dot(hidden, grad, TN), tall_ref.at[slot, : span.stop - start], wd_any.at[span, :], 2)
        acc_ref[...] += dot(hidden, down_ref[span, :])
        gn_ref[...] += dot(grad_gate, gate_ref[:, span], NT) + dot(grad_up, up_ref[:, span], NT)
    mid = gm_ref[...]
    mixed_ref[...] = mid + acc_ref[...]
    normed = mid * root
    grad_norm = gn_ref[...]
    gain_grad_ref[...] = jnp.broadcast_to(
        jnp.sum(grad_norm * normed, axis=0, keepdims=True), gain_grad_ref.shape
    )
    scaled = grad_norm * gain_ref[1:2]
    grad_mid = grad.astype(F32) + root * (
        scaled - normed * jnp.mean(normed * scaled, axis=1, keepdims=True)
    )
    gm_ref[...] = grad_mid
    grad_mid_low = grad_mid.astype(BF16)
    nt_ref[...] = att_ref[...].astype(BF16).T
    for start in range(0, width, step):
        span = slice(start, start + step)
        slot = start // step % 2
        while pending[slot]:
            pending[slot].pop().wait()
        write(slot, dot(nt_ref[...], grad_mid_low[:, span]), side_ref.at[slot, 0], wo_any.at[:, span], 0)
    grad_attention = dot(grad_mid_low, out_ref[...], NT).astype(BF16)
    ga_ref[...] = grad_attention
    products = grad_attention.astype(F32) * att_ref[...]
    dots = [
        jnp.sum(products[:, h * 128 : (h + 1) * 128], axis=1, keepdims=True) for h in range(HEADS)
    ]
    st_ref[...] = jnp.concatenate([log_total, spread(dots).T[:HEADS]], axis=0)
    for copy in pending[0] + pending[1]:
        copy.wait()


def middle(live, tokens, grads, gains, local, peers, weights):
    rows, width = tokens.shape
    hidden_width = weights[1].shape[1]
    full = lambda columns, kind: jax.ShapeDtypeStruct((rows, columns), kind)
    return pl.pallas_call(
        middle_kernel,
        out_shape=[
            full(width, F32),
            full(width, F32),
            full(width, BF16),
            jax.ShapeDtypeStruct((STATS, rows), F32),
            jax.ShapeDtypeStruct((8, width), F32),
        ]
        + [jax.ShapeDtypeStruct(w.shape, BF16) for w in weights],
        in_specs=[pl.BlockSpec(memory_space=pltpu.SMEM)]
        + in_vmem(7)
        + [pl.BlockSpec(memory_space=pl.ANY)] * 4,
        out_specs=in_vmem(5) + [pl.BlockSpec(memory_space=pl.ANY)] * 4,
        scratch_shapes=[pltpu.VMEM((rows, width), F32)] * 3
        + [pltpu.VMEM((rows, width), BF16), pltpu.VMEM((width, rows), BF16)]
        + [pltpu.VMEM(w.shape, BF16) for w in weights]
        + [
            pltpu.VMEM((2, 2, width, 512), BF16),
            pltpu.VMEM((2, 512, width), BF16),
            pltpu.SemaphoreType.DMA((4,)),
            pltpu.SemaphoreType.DMA((2, 3)),
        ],
        compiler_params=params(),
        name="middle",
    )(live, tokens, grads, gains, *local, *peers, *weights)


def final_kernel(
    live_ref, x_ref, gm_ref, gain_ref, ggain_ref, n_ref, dq_ref, pd_ref, dkv_ref, cos_ref, sin_ref, w_any,
    *rest,
):
    rows, width = x_ref.shape
    ready, (gx_ref, late_ref), given = rest[:4], rest[4:6], rest[6:10]
    in_ref, w_ref, made_ref, sems, writes = rest[10:]
    copies = copy_in([(w_any.at[:, : 3 * width], w_ref)], sems)

    def write(i, span):
        copy = pltpu.make_async_copy(made_ref.at[:, span], late_ref.at[:, span], writes.at[i])
        copy.start()
        copies.append(copy)

    for source, target in zip(ready, given):
        target[...] = source[...]
    live = live_ref[0] > 0
    cosine, sine = cos_ref[...], -sin_ref[...]
    for h in range(HEADS):
        span = slice(h * 128, (h + 1) * 128)
        part = dq_ref[:, span]
        for p in range(pd_ref.shape[0]):
            part += jnp.where(live, pd_ref[p, :, span].astype(F32), 0.0)
        in_ref[:, span] = turn(part, cosine, sine).astype(BF16)
        over = slice(width + h * 128, width + (h + 1) * 128)
        in_ref[:, over] = turn(dkv_ref[:, span], cosine, sine).astype(BF16)
    in_ref[:, 2 * width :] = dkv_ref[:, width:].astype(BF16)
    flipped = n_ref[...].T
    for i in range(3):
        span = slice(i * width, (i + 1) * width)
        made_ref[:, span] = dot(flipped, in_ref[:, span]).astype(BF16)
        write(i, span)
    copies[0].wait()
    grad_norm = dot(in_ref[...], w_ref[...], NT)
    x = x_ref[...].astype(F32)
    root = inverse_root(x)
    normed = x * root
    gains = jnp.concatenate(
        [
            jnp.sum(grad_norm * normed, axis=0, keepdims=True),
            ggain_ref[:1],
            jnp.zeros((126, width), F32),
        ],
        axis=0,
    )
    made_ref[:, 3 * width :] = gains.T.astype(BF16)
    write(3, slice(3 * width, made_ref.shape[1]))
    scaled = grad_norm * gain_ref[:1]
    gx_ref[...] = gm_ref[...] + root * (
        scaled - normed * jnp.mean(normed * scaled, axis=1, keepdims=True)
    )
    for copy in copies[1:]:
        copy.wait()


def final(live, *arrays, early):
    rows, width = arrays[0].shape
    columns = arrays[-1].shape[1]
    results = pl.pallas_call(
        final_kernel,
        out_shape=[
            jax.ShapeDtypeStruct((rows, width), F32),
            jax.ShapeDtypeStruct((width, columns), BF16),
        ]
        + [jax.ShapeDtypeStruct(e.shape, e.dtype) for e in early],
        in_specs=[pl.BlockSpec(memory_space=pltpu.SMEM)]
        + in_vmem(len(arrays) - 1)
        + [pl.BlockSpec(memory_space=pl.ANY)]
        + in_vmem(len(early)),
        out_specs=in_vmem(1) + [pl.BlockSpec(memory_space=pl.ANY)] + in_vmem(len(early)),
        scratch_shapes=[
            pltpu.VMEM((rows, 3 * width), BF16),
            pltpu.VMEM((width, 3 * width), BF16),
            pltpu.VMEM((width, columns), BF16),
            pltpu.SemaphoreType.DMA((1,)),
            pltpu.SemaphoreType.DMA((4,)),
        ],
        compiler_params=params(),
        name="final",
    )(live, *arrays, *early)
    return results[0], results[1], results[2:]


def deliver_kernel(late_ref, *outs):
    width = outs[0].shape[1]
    for i in range(3):
        outs[i][...] = late_ref[:, i * width : (i + 1) * width]
    gains = late_ref[:, 3 * width :]
    rows = gains.shape[0]
    square = jnp.concatenate([gains, jnp.zeros((128 - rows, 128), F32)], axis=0).T
    for i in range(2):
        outs[3 + i][...] = square[i : i + 1, :rows]


def deliver(late_sum, width):
    rows = late_sum.shape[0]
    shapes = [(rows, width)] * 3 + [(1, rows)] * 2
    *sums, gain_one, gain_two = pl.pallas_call(
        deliver_kernel,
        out_shape=[jax.ShapeDtypeStruct(shape, F32) for shape in shapes],
        in_specs=in_vmem(1),
        out_specs=in_vmem(5),
        compiler_params=params(),
        name="deliver",
    )(late_sum)
    return sums, gain_one.reshape(rows), gain_two.reshape(rows)


REACH = {"all": ("seq", "mem"), "line": "mem", "square": "seq"}


def gather_plain(array, reach):
    return lax.all_gather(array, REACH[reach], axis=0)


def scatter_plain(array, reach):
    return lax.psum_scatter(array, REACH[reach], scatter_dimension=0, tiled=True).astype(F32)


def return_plain(array):
    return lax.all_to_all(array, "mem", split_axis=0, concat_axis=0, tiled=True)


def join_peers(outs, stats):
    top = jnp.max(stats[:, :HEADS], axis=0)
    shares = jnp.exp2(stats[:, :HEADS] - top)
    total = jnp.sum(stats[:, HEADS:] * shares, axis=0)
    wide = jnp.repeat(jnp.swapaxes(shares, 1, 2), outs.shape[-1] // HEADS, axis=2)
    joined = jnp.sum(outs.astype(F32) * wide, axis=0).astype(BF16)
    return joined[None], jnp.concatenate([top, total], axis=0)[None]


def per_device(
    sizes,
    tokens,
    cached_keys,
    cached_values,
    knn_index,
    has_memory,
    w_query,
    w_key,
    w_value,
    w_out,
    gain_attn,
    w_gate,
    w_up,
    w_down,
    gain_ffn,
    cotangent,
):
    near = sizes["seq"] == 4 and sizes["mem"] % 2 == 0 and 4 <= sizes["mem"] <= 16
    inputs, grad_out = tokens[0], cotangent[0]
    rows, width = inputs.shape
    hidden_width = w_gate.shape[1]
    head_width = width // HEADS
    scale = head_width ** (-0.5) * LOG2E
    mem_dev = cached_keys.shape[1]
    place = lax.axis_index("seq").astype(jnp.int32)[None]
    base = (lax.axis_index("mem") * mem_dev).astype(jnp.int32)[None]

    gains = jnp.concatenate(
        [gain_attn[:, None], gain_ffn[:, None], jnp.zeros((w_query.shape[0], 126), BF16)], axis=1
    )
    first_shard = jnp.concatenate([w_query, w_key, w_value, gains], axis=1)
    if near:
        jobs = [
            index_job(sizes, knn_index[0], mem_dev),
            gather_job(sizes, first_shard, row_halves, "all"),
        ]
        (bits,), (first_weights,) = together(1, "first", sizes, jobs)
    else:
        first_weights = gather_plain(first_shard, "all")
        bits = mask_bits(base, gather_plain(knn_index[0], "line"), mem_dev)
        flags = lax.all_gather(has_memory, "mem", axis=0, tiled=True)
        order = jnp.argsort(jnp.where(flags > 0, 0, 1), stable=True)
        order = order[: flags.shape[0] // 2].astype(jnp.int32)
    first_weights = first_weights.reshape(-1, first_shard.shape[1])

    positions = lax.axis_index("seq") * rows + jnp.arange(rows)
    cosine, sine = rope_tables(positions, head_width)
    norm_one, queries, keys_values, gain_rows = project(inputs, first_weights, cosine, sine)
    if near:
        jobs = [
            forward_job(
                sizes, queries, keys_values, bits, cached_keys, cached_values, scale
            ),
            gather_job(sizes, w_out, row_halves, "all"),
            gather_job(sizes, w_gate, row_halves, "all"),
            gather_job(sizes, w_up, row_halves, "all"),
            gather_job(sizes, w_down, column_halves, "all"),
        ]
        results, (out_weight,), (gate_weight,), (up_weight,), (down_weight,) = together(
            2, "second", sizes, jobs
        )
        all_queries, segment_kv, *peers = results[:4]
        local = results[4:]
        segment_kv = segment_kv.reshape(-1, 2 * width)
    else:
        all_queries = gather_plain(queries, "line")
        segment_kv = gather_plain(keys_values, "square").reshape(-1, 2 * width)
        owner_out, owner_stats = owner_forward(
            order, all_queries, bits, cached_keys, cached_values, scale
        )
        peers = join_peers(return_plain(owner_out), return_plain(owner_stats))
        local = alone("local_forward", place, local_job("forward", [queries, segment_kv], scale))
        out_weight, gate_weight = gather_plain(w_out, "all"), gather_plain(w_gate, "all")
        up_weight, down_weight = gather_plain(w_up, "all"), gather_plain(w_down, "all")
    weights = [
        out_weight.reshape(width, width),
        gate_weight.reshape(width, hidden_width),
        up_weight.reshape(width, hidden_width),
        down_weight.reshape(hidden_width, width),
    ]
    mixed, grad_mid, grad_attention, back_stats, gain_two_grad, *early = middle(
        has_memory, inputs, grad_out, gain_rows, local, peers, weights
    )
    if near:
        jobs = [
            backward_job(
                sizes, queries, grad_attention, back_stats, segment_kv,
                all_queries, bits, cached_keys, cached_values, scale,
            ),
            *[scatter_job(sizes, grad, row_halves) for grad in early[:3]],
            scatter_job(sizes, early[3], column_halves),
        ]
        (_, peer_grads, local_dq, grad_kv), *early_sums = together(3, "third", sizes, jobs)
        grad_kv = grad_kv.reshape(rows, 2 * width)
        early_sums = [total for (total,) in early_sums]
    else:
        all_grads, all_stats = gather_plain(grad_attention, "line"), gather_plain(back_stats, "line")
        local_work = local_job(
            "backward", [queries, grad_attention, back_stats, segment_kv], scale
        )
        local_dq, local_dkv = alone("local_backward", place, local_work)
        owner_grads = owner_backward(
            order, all_queries, all_grads, all_stats, bits, cached_keys, cached_values, scale
        )
        peer_grads = jnp.sum(return_plain(owner_grads).astype(F32), axis=0, keepdims=True)
        grad_kv = scatter_plain(local_dkv, "square")
        early_sums = [scatter_plain(grad, "all") for grad in early]
    grad_inputs, late, early_sums = final(
        has_memory, inputs, grad_mid, gain_rows, gain_two_grad, norm_one, local_dq, peer_grads, grad_kv,
        cosine, sine, first_weights, early=early_sums,
    )
    if near:
        ((late_sum,),) = together(4, "fourth", sizes, [scatter_job(sizes, late, row_halves)])
    else:
        late_sum = scatter_plain(late, "all")
    late_sums, gain_one_sum, gain_two_sum = deliver(late_sum, width)
    return (
        mixed[None],
        grad_inputs[None],
        *late_sums,
        early_sums[0],
        gain_one_sum,
        *early_sums[1:],
        gain_two_sum,
    )


def solution(mesh):
    rows, owned, feature = P("mem", "seq", None), P(None, "mem", None), P(("seq", "mem"), None)
    gain = P(("seq", "mem"))
    return jax.shard_map(
        functools.partial(per_device, dict(mesh.shape)),
        mesh=mesh,
        in_specs=(
            (rows, owned, owned, rows, P("mem"))
            + (feature,) * 4
            + (gain,)
            + (feature,) * 3
            + (gain, rows)
        ),
        out_specs=(rows, rows) + (feature,) * 4 + (gain,) + (feature,) * 3 + (gain,),
        check_vma=False,
    )
```
